32 devices in a mesh: dp: 4 (over z), row: 4 (over y, x), col: 2 (over core).
Axes of the slice: x: 2, y: 2, z: 4, core: 2. Of those that a mesh axis runs over, the one named last changes fastest.
Arguments:
- block_input: bfloat16 [6144, 2048], P(('dp', 'row'), 'col'), may hold values from -6 to 6
- norm1_gain: bfloat16 [2048], P('col'), may hold values from 0.5 to 1.5
- norm1_shift: bfloat16 [2048], P('col'), may hold values from -1.5 to 1.5
- qkv_weight: bfloat16 [3, 2048, 2048], P(None, 'col', 'row'), may hold values from -0.1875 to 0.1875
- qkv_bias: bfloat16 [3, 2048], P(None, ('row', 'col')), may hold values from -3 to 3
- out_weight: bfloat16 [2048, 2048], P('row', 'col'), may hold values from -0.375 to 0.375
- norm2_gain: bfloat16 [2048], P('col'), may hold values from 0.5 to 1.5
- norm2_shift: bfloat16 [2048], P('col'), may hold values from -1.5 to 1.5
- gate_up_weight: bfloat16 [2, 2048, 5632], P(None, 'col', 'row'), may hold values from -0.125 to 0.125
- down_weight: bfloat16 [5632, 2048], P('row', 'col'), may hold values from -0.078125 to 0.078125
- output_grad: bfloat16 [6144, 2048], P(('dp', 'row'), 'col'), may hold values from -6 to 6
Outputs:
- block_output: bfloat16 [6144, 2048], P(('dp', 'row'), 'col')
- input_grad: float32 [6144, 2048], P(('dp', 'row'), 'col')
- norm1_gain_grad: float32 [2048], P('col')
- norm1_shift_grad: float32 [2048], P('col')
- qkv_weight_grad: float32 [3, 2048, 2048], P(None, 'col', 'row')
- qkv_bias_grad: float32 [3, 2048], P(None, ('row', 'col'))
- out_weight_grad: float32 [2048, 2048], P('row', 'col')
- norm2_gain_grad: float32 [2048], P('col')
- norm2_shift_grad: float32 [2048], P('col')
- gate_up_weight_grad: float32 [2, 2048, 5632], P(None, 'col', 'row')
- down_weight_grad: float32 [5632, 2048], P('row', 'col')
The draws below stay inside these ranges and needn't reach their ends.
All inputs are finite; a program needn't handle non-finite values.
Results may differ from the reference program's by a relative error of at most 0.014.
Values may be sent and summed in bfloat16 or wider, within the bound.
No kernel may reach another device: no remote copies, remote signals or barrier semaphores. Data moves between devices by JAX's collectives and lax.ppermute only.
A program may use at most 256 MiB of HBM per device.

```python
import jax
import jax.numpy as jnp
from jax import lax

D = 2048
H = 32
HD = 64
FF = 5632
ROT = 16
SEQ = 1536
TOKENS = 6144
N_DP = 4


def steps_of(rng, shape, cuts, smallest, largest):
    def one(axis_at, blocks):
        draws = jax.random.uniform(jax.random.fold_in(jax.random.fold_in(rng, 6), axis_at), (blocks,), jnp.float32, smallest / len(cuts), largest / len(cuts))
        return jnp.repeat(jnp.exp(draws), shape[axis_at] // blocks).reshape((-1,) + (1,) * (len(shape) - axis_at - 1))

    loudness = one(*cuts[0])
    for cut in cuts[1:]:
        loudness = loudness * one(*cut)
    return loudness


def centred(key, dims, width, limit, split=(), held_as=jnp.bfloat16):
    values = jax.random.normal(key, dims, jnp.float32) * width
    if len(split) > 0:
        values = steps_of(key, dims, split, -0.22, 0.18) * values
    return jnp.clip(values, min=-limit, max=limit).astype(held_as)


def setup_inputs(seed: int = 0) -> dict:
    key_list = jax.random.split(jax.random.key(seed), 12)
    return {
        "block_input": centred(key_list[0], (TOKENS, D), 1.0, 6.0, ((0, 16), (1, 2))),
        "norm1_gain": jnp.clip(1.0 + 0.1 * jax.random.normal(key_list[1], (D,), jnp.float32), 0.5, 1.5).astype(jnp.bfloat16),
        "norm1_shift": centred(key_list[2], (D,), 0.3, 1.5, ((0, 2),)),
        "qkv_weight": centred(key_list[3], (3, D, H * HD), (D // 2) ** -0.5, 0.1875, ((1, 2), (2, 4))),
        "qkv_bias": centred(key_list[4], (3, H * HD), 0.5, 3.0, ((1, 8),)),
        "out_weight": centred(key_list[5], (H * HD, D), (H * HD // 8) ** -0.5, 0.375, ((0, 4), (1, 2))),
        "norm2_gain": jnp.clip(1.0 + 0.1 * jax.random.normal(key_list[6], (D,), jnp.float32), 0.5, 1.5).astype(jnp.bfloat16),
        "norm2_shift": centred(key_list[7], (D,), 0.3, 1.5, ((0, 2),)),
        "gate_up_weight": centred(key_list[8], (2, D, FF), D ** -0.5, 0.125, ((1, 2), (2, 4))),
        "down_weight": centred(key_list[9], (FF, D), FF ** -0.5, 0.078125, ((0, 4), (1, 2))),
        "output_grad": centred(key_list[10], (TOKENS, D), 1.0, 6.0, ((0, 16), (1, 2))),
    }


@jax.custom_vjp
def low(v):
    return lax.optimization_barrier(v.astype(jnp.bfloat16)).astype(jnp.float32)

@jax.custom_vjp
def low_back(v):
    return v

def low_keep(v):
    return (low(v), None)

def low_pass(kept, grad):
    return (grad,)

def back_keep(v):
    return (v, None)

def back_low(kept, grad):
    return (low(grad),)
low.defvjp(low_keep, low_pass)
low_back.defvjp(back_keep, back_low)
epsilon = 1e-05
base_rate = 10000.0
highest = lax.Precision.HIGHEST

def layer_norm(values, gain, shift):
    center = values - lax.optimization_barrier(jnp.mean(values, axis=-1, keepdims=True))
    spread = lax.optimization_barrier(jnp.mean(center * center, axis=-1, keepdims=True))
    return center * lax.rsqrt(spread + epsilon) * gain + shift

def rotary_tables(length, rotary):
    half_dims = rotary // 2
    freqs = base_rate ** (-(2.0 * jnp.arange(half_dims, dtype=jnp.float32)) / rotary)
    angles = jnp.arange(length, dtype=jnp.float32)[:, None] * freqs[None, :]
    return (jnp.cos(angles)[:, None, :], jnp.sin(angles)[:, None, :])

def rotate(heads, cosine, sine):
    half_dims = cosine.shape[-1]
    first = heads[..., :half_dims]
    second = heads[..., half_dims:2 * half_dims]
    return jnp.concatenate([first * cosine - second * sine, second * cosine + first * sine, heads[..., 2 * half_dims:]], axis=-1)

def attend(query, key, value):
    length = query.shape[0]
    block_rows = min(512, length)
    block_count = length // block_rows
    scaling = query.shape[2] ** (-0.5)
    key_places = jnp.arange(length, dtype=jnp.int32)

    def one_block(offset):
        queries = lax.dynamic_slice_in_dim(query, offset, block_rows, 0)
        raw = low_back(jnp.einsum('qhd,khd->hqk', queries, key, precision=highest))
        scores = raw * scaling
        allowed = key_places[None, :] <= (offset + jnp.arange(block_rows, dtype=jnp.int32))[:, None]
        scores = jnp.where(allowed[None], scores, -1e+30)
        weights = jnp.exp(scores - lax.optimization_barrier(jnp.max(scores, axis=-1, keepdims=True)))
        probs = low(weights / lax.optimization_barrier(jnp.sum(weights, axis=-1, keepdims=True)))
        return jnp.einsum('hqk,khd->qhd', probs, value, precision=highest)
    offsets = (jnp.arange(block_count) * block_rows).astype(jnp.int32)
    outs = lax.map(jax.checkpoint(one_block), offsets)
    return outs.reshape(length, query.shape[1] * query.shape[2])

def forward(values, norm1_gain, norm1_shift, qkv_weight, qkv_bias, out_weight, norm2_gain, norm2_shift, gate_up_weight, down_weight):
    length = values.shape[0]
    normed = low(layer_norm(values, norm1_gain, norm1_shift))
    project = low_back(jnp.einsum('td,kdf->ktf', normed, qkv_weight, precision=highest) + qkv_bias[:, None, :])
    cosine, sine = rotary_tables(length, ROT)
    query = low(rotate(project[0].reshape(length, H, HD), cosine, sine))
    key = low(rotate(project[1].reshape(length, H, HD), cosine, sine))
    value = low(project[2].reshape(length, H, HD))
    mixed = low_back(low(attend(query, key, value)))
    after = values + low_back(jnp.dot(mixed, out_weight, precision=highest))
    normed2 = low(layer_norm(after, norm2_gain, norm2_shift))
    gate_up = low_back(jnp.einsum('td,kdf->ktf', normed2, gate_up_weight, precision=highest))
    hidden = low(jax.nn.silu(gate_up[0]) * gate_up[1])
    return after + jnp.dot(hidden, down_weight, precision=highest)

def reference(block_input, norm1_gain, norm1_shift, qkv_weight, qkv_bias, out_weight, norm2_gain, norm2_shift, gate_up_weight, down_weight, output_grad):
    params = tuple((item.astype(jnp.float32) for item in (norm1_gain, norm1_shift, qkv_weight, qkv_bias, out_weight, norm2_gain, norm2_shift, gate_up_weight, down_weight)))
    inputs = block_input.astype(jnp.float32).reshape(N_DP, SEQ, D)
    cotangents = output_grad.astype(jnp.float32).reshape(N_DP, SEQ, D)
    zeros = tuple((jnp.zeros_like(item) for item in params))

    def one_sequence(totals, item):
        values, cotangent = item
        result, pullback = jax.vjp(forward, values, *params)
        grads = pullback(cotangent)
        totals = tuple((first + second for first, second in zip(totals, grads[1:])))
        return (totals, (result.astype(jnp.bfloat16), grads[0]))
    totals, (results, input_grads) = lax.scan(one_sequence, zeros, (inputs, cotangents))
    return (results.reshape(TOKENS, D), input_grads.reshape(TOKENS, D), totals[0], totals[1], totals[2], totals[3], totals[4], totals[5], totals[6], totals[7], totals[8])
```

```python
import functools

import jax
import jax.numpy as jnp
from jax import lax
from jax.experimental import pallas as pl
from jax.experimental.pallas import tpu as pltpu
from jax.sharding import PartitionSpec as P

HD = 64
ROT = 16
LANES = 128
MIB = 1 << 20

epsilon = 1e-05
base_rate = 10000.0
bf16 = jnp.bfloat16
f32 = jnp.float32

NN = (((1,), (0,)), ((), ()))
NT = (((1,), (1,)), ((), ()))
TN = (((0,), (0,)), ((), ()))


def dot(first, second, dims=NN):
    return lax.dot_general(first, second, dims, preferred_element_type=f32)


def row_permute(values, core_zero, core_one):
    pairs = [
        (row * 2 + core, (row ^ (core_one if core else core_zero)) * 2 + core)
        for row in range(4)
        for core in range(2)
    ]
    return lax.ppermute(values, ("row", "col"), pairs)


def first_way(values):
    return row_permute(values, 1, 2)


def second_way(values):
    return row_permute(values, 2, 1)


def sibling(values):
    return lax.ppermute(values, "col", [(0, 1), (1, 0)])


def grid_rows():
    return lax.axis_size("row") == 4


def places():
    row, core = lax.axis_index("row"), lax.axis_index("col")
    if grid_rows():
        one = jnp.where(core == 0, 1, 2)
        return jnp.stack([row, row ^ one, row ^ (3 - one), row ^ 3]), (0, 2, 1, 3)
    count = lax.axis_size("row")
    return jnp.arange(count), tuple(range(count))


def gather_rows(own):
    if grid_rows():
        near = first_way(own)
        side = second_way(own)
        return [own, near, side, second_way(near)]
    whole = lax.all_gather(own, "row", axis=0, tiled=True)
    return jnp.split(whole, lax.axis_size("row"), axis=0)


def scatter_rows(parts):
    if grid_rows():
        passing = first_way(parts[3])
        near = first_way(parts[1])
        side = second_way((parts[2].astype(f32) + passing.astype(f32)).astype(bf16))
        return parts[0].astype(f32) + near.astype(f32) + side.astype(f32)
    whole = jnp.concatenate(parts, axis=0)
    return lax.psum_scatter(whole, "row", scatter_dimension=0, tiled=True).astype(f32)


def sum_sequences(part):
    if lax.axis_size("dp") != 4:
        return lax.psum(part, "dp").astype(f32)
    inward = lax.ppermute(part, "dp", [(0, 1), (3, 2)])
    half = (part.astype(f32) + inward.astype(f32)).astype(bf16)
    across = lax.ppermute(half, "dp", [(1, 2), (2, 1)])
    total = (half.astype(f32) + across.astype(f32)).astype(bf16)
    outward = lax.ppermute(total, "dp", [(1, 0), (2, 3)])
    place = lax.axis_index("dp")
    return jnp.where((place == 1) | (place == 2), total, outward).astype(f32)


def width_pair(first, second):
    return lax.psum((first, second), "col")


def normalize(values):
    width = values.shape[1] * lax.axis_size("col")
    totals, squares = width_pair(jnp.sum(values, axis=-1), jnp.sum(values * values, axis=-1))
    average = totals / width
    spread = squares / width - average * average
    inverse = lax.rsqrt(spread + epsilon)[:, None]
    return ((values - average[:, None]) * inverse, inverse)


def norm_back(scaled, normed_hat, inverse):
    width = normed_hat.shape[1] * lax.axis_size("col")
    first, second = width_pair(jnp.sum(scaled, axis=-1), jnp.sum(scaled * normed_hat, axis=-1))
    return inverse * (scaled - first[:, None] / width - normed_hat * second[:, None] / width)


def rotary_tables(place, rows):
    half_dims = ROT // 2
    lane = jnp.arange(LANES) % HD
    freqs = base_rate ** (-(2.0 * (lane % half_dims).astype(f32)) / ROT)
    where = (place[:, None] * rows + jnp.arange(rows)[None, :]).astype(f32)
    angles = where[:, :, None] * freqs
    turned = lane < ROT
    cosine = jnp.where(turned, jnp.cos(angles), 1.0)
    sine = jnp.where(turned, jnp.where(lane < half_dims, -1.0, 1.0) * jnp.sin(angles), 0.0)
    return cosine, sine


def turn(values, cosine, sine):
    half_dims = ROT // 2
    lane = lax.broadcasted_iota(jnp.int32, values.shape, 1) % HD
    partner = jnp.where(
        lane < half_dims,
        pltpu.roll(values, LANES - half_dims, 1),
        pltpu.roll(values, half_dims, 1),
    )
    return values * cosine + partner * sine


def params(mib, *order):
    return pltpu.CompilerParams(vmem_limit_bytes=mib * MIB)


def cost(flops, moved, hard=0):
    return pl.CostEstimate(flops=int(flops), bytes_accessed=int(moved), transcendentals=int(hard))


def project_kernel(own, other, keep, taken, bias, cosine, sine, *rest):
    out = rest[-1]
    kind = pl.program_id(0)
    result = dot(own[...], keep[0]) + dot(other[...], taken[0]) + bias[0].astype(f32)

    @pl.when(kind < 2)
    def _():
        for at in range(0, result.shape[1], LANES):
            part = slice(at, at + LANES)
            out[0, 0, :, part] = turn(result[:, part], cosine[0], sine[0]).astype(bf16)

    @pl.when(kind == 2)
    def _():
        out[0, 0] = result.astype(bf16)


def project_piece(index, count, own, other, keep, taken, bias, cosine, sine, before):
    rows, width = own.shape
    units = keep.shape[2]
    whole = lambda k: (0, 0)
    table = pl.BlockSpec((1, rows, LANES), lambda k: (index, 0, 0))
    weight = pl.BlockSpec((1, width, units), lambda k: (k, 0, 0))
    in_specs = [
        pl.BlockSpec((rows, width), whole),
        pl.BlockSpec((rows, width), whole),
        weight,
        weight,
        pl.BlockSpec((1, 1, units), lambda k: (k, 0, 0)),
        table,
        table,
    ]
    args = [own, other, keep, taken, bias, cosine, sine]
    aliases = {}
    if before is not None:
        in_specs.append(pl.BlockSpec(memory_space=pl.ANY))
        args.append(before)
        aliases = {7: 0}
    return pl.pallas_call(
        project_kernel,
        grid=(3,),
        in_specs=in_specs,
        out_specs=pl.BlockSpec((1, 1, rows, units), lambda k: (index, k, 0, 0)),
        out_shape=jax.ShapeDtypeStruct((count, 3, rows, units), bf16),
        input_output_aliases=aliases,
        compiler_params=params(24),
        cost_estimate=cost(12 * rows * width * units, 4 * rows * width + 12 * width * units),
        name="project_piece",
    )(*args)


def causal(rows):
    keys = lax.broadcasted_iota(jnp.int32, (rows, rows), 0)
    return keys <= lax.broadcasted_iota(jnp.int32, (rows, rows), 1)


def head_lanes(values, head):
    lane = lax.broadcasted_iota(jnp.int32, values.shape, 1)
    return jnp.where((lane >= head * HD) & (lane < (head + 1) * HD), values, jnp.zeros_like(values))


def attend_kernel(slot, qkv, mixed, kept, logsum, scores):
    count, _, rows, _ = qkv.shape
    heads = LANES // HD
    scale = HD**-0.5
    for at in range(count):
        here = slot[at]
        query = qkv[here, 0] * jnp.asarray(scale, bf16)
        for head in range(heads):
            highest = None
            for past in range(at + 1):
                key = head_lanes(qkv[slot[past], 1], head)
                block = dot(key, query, NT)
                if past == at:
                    block = jnp.where(causal(rows), block, -1e30)
                scores[pl.ds(past * rows, rows), :] = block
                peak = jnp.max(block, axis=0, keepdims=True)
                highest = peak if highest is None else jnp.maximum(highest, peak)
            total = jnp.zeros((1, rows), f32)
            outs = jnp.zeros((HD, rows), f32)
            for past in range(at + 1):
                weights = jnp.exp(scores[pl.ds(past * rows, rows), :] - highest)
                total = total + jnp.sum(weights, axis=0, keepdims=True)
                value = jnp.transpose(qkv[slot[past], 2])[head * HD : (head + 1) * HD]
                outs = outs + dot(value, weights.astype(bf16))
            kept[0, here, pl.ds(head * HD, HD), :] = outs / total
            logsum[0, here, pl.ds(head, 1), :] = highest + jnp.log(total)
        mixed[here] = jnp.transpose(kept[0, here]).astype(bf16)


def attend_forward(slot, qkv):
    count, _, rows, units = qkv.shape
    pairs = units // LANES
    work = rows * rows * count * (count + 1) // 2 * units
    return pl.pallas_call(
        attend_kernel,
        grid_spec=pltpu.PrefetchScalarGridSpec(
            num_scalar_prefetch=1,
            grid=(pairs,),
            in_specs=[pl.BlockSpec((count, 3, rows, LANES), lambda p, s: (0, 0, 0, p))],
            out_specs=[
                pl.BlockSpec((count, rows, LANES), lambda p, s: (0, 0, p)),
                pl.BlockSpec((1, count, LANES, rows), lambda p, s: (p, 0, 0, 0)),
                pl.BlockSpec((1, count, 8, rows), lambda p, s: (p, 0, 0, 0)),
            ],
            scratch_shapes=[pltpu.VMEM((count * rows, rows), f32)],
        ),
        out_shape=[
            jax.ShapeDtypeStruct((count, rows, units), bf16),
            jax.ShapeDtypeStruct((pairs, count, LANES, rows), f32),
            jax.ShapeDtypeStruct((pairs, count, 8, rows), f32),
        ],
        compiler_params=params(40),
        cost_estimate=cost(16 * work, 16 * count * rows * units, work // HD),
        name="attend_forward",
    )(slot, qkv)


def attend_back_kernel(slot, qkv, grads, kept, logsum, cosine, sine, out, dq, dk, dv, inner):
    count, _, rows, _ = qkv.shape
    heads = LANES // HD
    scale = HD**-0.5
    dk[...] = jnp.zeros_like(dk)
    dv[...] = jnp.zeros_like(dv)
    for at in range(count):
        product = jnp.transpose(grads[at].astype(f32)) * kept[0, at]
        for head in range(heads):
            part = product[head * HD : (head + 1) * HD]
            inner[at, pl.ds(head, 1), :] = jnp.sum(part, axis=0, keepdims=True)
    for at in range(count):
        here = slot[at]
        query = qkv[here, 0] * jnp.asarray(scale, bf16)
        grad = grads[here]
        for head in range(heads):
            query_head = head_lanes(query, head)
            grad_head = head_lanes(grad, head)
            query_grad = jnp.zeros((HD, rows), f32)
            for past in range(at + 1):
                there = slot[past]
                key = qkv[there, 1]
                value = qkv[there, 2]
                block = dot(key, query_head, NT)
                weights = jnp.exp(block - logsum[0, here, pl.ds(head, 1), :])
                if past == at:
                    weights = jnp.where(causal(rows), weights, 0.0)
                moved = dot(value, grad_head, NT)
                raw = (weights * (moved - inner[here, pl.ds(head, 1), :])).astype(bf16)
                dv[there] += dot(weights.astype(bf16), grad_head)
                dk[there] += dot(raw, query_head)
                turned = jnp.transpose(key)[head * HD : (head + 1) * HD]
                query_grad = query_grad + dot(turned, raw)
            dq[pl.ds(head * HD, HD), :] = query_grad * scale
        out[0, here] = turn(jnp.transpose(dq[...]), cosine[here], -sine[here]).astype(bf16)
    for at in range(count):
        out[1, at] = turn(dk[at], cosine[at], -sine[at]).astype(bf16)
        out[2, at] = dv[at].astype(bf16)


def attend_backward(slot, qkv, grads, kept, logsum, cosine, sine):
    count, _, rows, units = qkv.shape
    pairs = units // LANES
    work = rows * rows * count * (count + 1) // 2 * units
    table = pl.BlockSpec((count, rows, LANES), lambda p, s: (0, 0, 0))
    return pl.pallas_call(
        attend_back_kernel,
        grid_spec=pltpu.PrefetchScalarGridSpec(
            num_scalar_prefetch=1,
            grid=(pairs,),
            in_specs=[
                pl.BlockSpec((count, 3, rows, LANES), lambda p, s: (0, 0, 0, p)),
                pl.BlockSpec((count, rows, LANES), lambda p, s: (0, 0, p)),
                pl.BlockSpec((1, count, LANES, rows), lambda p, s: (p, 0, 0, 0)),
                pl.BlockSpec((1, count, 8, rows), lambda p, s: (p, 0, 0, 0)),
                table,
                table,
            ],
            out_specs=pl.BlockSpec((3, count, rows, LANES), lambda p, s: (0, 0, 0, p)),
            scratch_shapes=[
                pltpu.VMEM((LANES, rows), f32),
                pltpu.VMEM((count, rows, LANES), f32),
                pltpu.VMEM((count, rows, LANES), f32),
                pltpu.VMEM((count, 8, rows), f32),
            ],
        ),
        out_shape=jax.ShapeDtypeStruct((3, count, rows, units), bf16),
        compiler_params=params(48),
        cost_estimate=cost(40 * work, 24 * count * rows * units, work // HD),
        name="attend_backward",
    )(slot, qkv, grads, kept, logsum, cosine, sine)


def ordered(core, own, other, out, width):
    rest = out.shape[-1] - width
    lead = core[0] == 0
    out[..., :width] = jnp.where(lead, own[...], other[...])
    out[..., width:] = jnp.where(lead, other[..., :rest], own[..., :rest])


def block_of(width):
    return 256 if width % 256 == 0 else LANES


def mixed_out_kernel(swap, core, own, other, weight, *outs):
    units = outs[-1]
    count = own.shape[0]

    @pl.when(pl.program_id(0) == 0)
    def _():
        for at in range(count):
            ordered(core, own.at[at], other.at[swap[at]], units.at[at], own.shape[2])

    for at in range(count):
        outs[at][...] = dot(units[at], weight[...]).astype(bf16)


def mixed_out(core, swap, own, other, weight):
    count, rows, units = own.shape
    width = weight.shape[1]
    block = block_of(width)
    whole = lambda k, s: (0, 0, 0)
    return pl.pallas_call(
        functools.partial(mixed_out_kernel, swap),
        grid_spec=pltpu.PrefetchScalarGridSpec(
            num_scalar_prefetch=1,
            grid=(width // block,),
            in_specs=[
                pl.BlockSpec((count, rows, units), whole),
                pl.BlockSpec((count, rows, units), whole),
                pl.BlockSpec((2 * units, block), lambda k, s: (0, k)),
            ],
            out_specs=[pl.BlockSpec((rows, block), lambda k, s: (0, k))] * count
            + [pl.BlockSpec((count, rows, 2 * units), whole)],
        ),
        out_shape=[jax.ShapeDtypeStruct((rows, width), bf16)] * count
        + [jax.ShapeDtypeStruct((count, rows, 2 * units), bf16)],
        compiler_params=params(24),
        cost_estimate=cost(4 * count * rows * units * width, 2 * count * rows * (width + 4 * units)),
        name="mixed_out",
    )(core, own, other, weight)


def hidden_kernel(own, other, grad_own, grad_other, gate_up, taken, down, down_taken, out):
    gate = dot(own[...], gate_up[0]) + dot(other[...], taken[0])
    up = dot(own[...], gate_up[1]) + dot(other[...], taken[1])
    grad = dot(grad_own[...], down[...], NT) + dot(grad_other[...], down_taken[...], NT)
    sigmoid = jax.nn.sigmoid(gate)
    silu = gate * sigmoid
    slope = sigmoid * (1.0 + gate * (1.0 - sigmoid))
    out[0] = (silu * up).astype(bf16)
    out[1] = (grad * up * slope).astype(bf16)
    out[2] = (grad * silu).astype(bf16)


def hidden_piece(own, other, grad_own, grad_other, gate_up, taken, down, down_taken):
    rows, width = own.shape
    units = gate_up.shape[2]
    block = block_of(units)
    rows_in = pl.BlockSpec((rows, width), lambda k: (0, 0))
    entry = pl.BlockSpec((2, width, block), lambda k: (0, 0, k))
    leave = pl.BlockSpec((block, width), lambda k: (k, 0))
    return pl.pallas_call(
        hidden_kernel,
        grid=(units // block,),
        in_specs=[rows_in] * 4 + [entry, entry, leave, leave],
        out_specs=pl.BlockSpec((3, rows, block), lambda k: (0, 0, k)),
        out_shape=jax.ShapeDtypeStruct((3, rows, units), bf16),
        compiler_params=params(32),
        cost_estimate=cost(12 * rows * width * units, 12 * width * units + 8 * rows * width),
        name="hidden_piece",
    )(own, other, grad_own, grad_other, gate_up, taken, down, down_taken)


def units_back_kernel(core, own, other, gate_up, down, *rest):
    branch, normed_grad, units = rest[-3:]

    @pl.when(pl.program_id(0) == 0)
    def _():
        for kind in range(3):
            ordered(core, own.at[kind], other.at[kind], units.at[kind, 0], own.shape[2])

    branch[...] = dot(units[0, 0], down[...]).astype(bf16)
    normed_grad[...] = (
        dot(units[1, 0], gate_up[0], NT) + dot(units[2, 0], gate_up[1], NT)
    ).astype(bf16)


def units_back_piece(index, count, core, own, other, gate_up, down, before):
    _, rows, half = own.shape
    total, width = down.shape
    block = block_of(width)
    halves = pl.BlockSpec((3, rows, half), lambda k, s: (0, 0, 0))
    in_specs = [
        halves,
        halves,
        pl.BlockSpec((2, block, total), lambda k, s: (0, k, 0)),
        pl.BlockSpec((total, block), lambda k, s: (0, k)),
    ]
    args = [own, other, gate_up, down]
    aliases = {}
    if before is not None:
        in_specs.append(pl.BlockSpec(memory_space=pl.ANY))
        args.append(before)
        aliases = {5: 2}
    columns = pl.BlockSpec((rows, block), lambda k, s: (0, k))
    return pl.pallas_call(
        units_back_kernel,
        grid_spec=pltpu.PrefetchScalarGridSpec(
            num_scalar_prefetch=1,
            grid=(width // block,),
            in_specs=in_specs,
            out_specs=[
                columns,
                columns,
                pl.BlockSpec((3, 1, rows, total), lambda k, s: (0, index, 0, 0)),
            ],
        ),
        out_shape=[
            jax.ShapeDtypeStruct((rows, width), bf16),
            jax.ShapeDtypeStruct((rows, width), bf16),
            jax.ShapeDtypeStruct((3, count, rows, total), bf16),
        ],
        input_output_aliases=aliases,
        compiler_params=params(40),
        cost_estimate=cost(6 * rows * width * total, 6 * width * total + 12 * rows * total),
        name="units_back_piece",
    )(core, *args)


def mixed_grad_kernel(count, *refs):
    keep, taken, out = refs[-3:]
    for at in range(count):
        out[at] = (
            dot(refs[at][...], keep[...], NT) + dot(refs[count + at][...], taken[...], NT)
        ).astype(bf16)


def mixed_back(own, other, keep, taken):
    count = len(own)
    rows, width = own[0].shape
    units = keep.shape[0]
    return pl.pallas_call(
        functools.partial(mixed_grad_kernel, count),
        out_shape=jax.ShapeDtypeStruct((count, rows, units), bf16),
        compiler_params=params(24 if count == 4 else 40),
        cost_estimate=cost(4 * count * rows * width * units, 4 * count * rows * width),
        name="mixed_back",
    )(*own, *other, keep, taken)


def project_back_kernel(swap, core, own, other, weight, *outs):
    units = outs[-1]
    count = own.shape[1]

    @pl.when(pl.program_id(0) == 0)
    def _():
        for kind in range(3):
            for at in range(count):
                ordered(
                    core,
                    own.at[kind, at],
                    other.at[kind, swap[at]],
                    units.at[kind, at],
                    own.shape[3],
                )

    for at in range(count):
        outs[at][...] = sum(dot(units[kind, at], weight[kind], NT) for kind in range(3)).astype(bf16)


def project_back(core, swap, own, other, weight):
    _, count, rows, half = own.shape
    _, width, total = weight.shape
    block = block_of(width)
    whole = lambda k, s: (0, 0, 0, 0)
    return pl.pallas_call(
        functools.partial(project_back_kernel, swap),
        grid_spec=pltpu.PrefetchScalarGridSpec(
            num_scalar_prefetch=1,
            grid=(width // block,),
            in_specs=[
                pl.BlockSpec((3, count, rows, half), whole),
                pl.BlockSpec((3, count, rows, half), whole),
                pl.BlockSpec((3, block, total), lambda k, s: (0, k, 0)),
            ],
            out_specs=[pl.BlockSpec((rows, block), lambda k, s: (0, k))] * count
            + [pl.BlockSpec((3, count, rows, total), whole)],
        ),
        out_shape=[jax.ShapeDtypeStruct((rows, width), bf16)] * count
        + [jax.ShapeDtypeStruct((3, count, rows, total), bf16)],
        compiler_params=params(40),
        cost_estimate=cost(6 * count * rows * total * width, 2 * count * rows * (width + 6 * total)),
        name="project_back",
    )(core, own, other, weight)


def halves(weight, axis, width):
    lead = lax.slice_in_dim(weight, 0, width, axis=axis)
    rest = lax.slice_in_dim(weight, width, weight.shape[axis], axis=axis)
    pad = [(0, 0)] * weight.ndim
    pad[axis] = (0, width - rest.shape[axis])
    rest = jnp.pad(rest, pad)
    first = lax.axis_index("col") == 0
    return jnp.where(first, lead, rest), jnp.where(first, rest, lead)


def shards(
    block_input,
    norm1_gain,
    norm1_shift,
    qkv_weight,
    qkv_bias,
    out_weight,
    norm2_gain,
    norm2_shift,
    gate_up_weight,
    down_weight,
    output_grad,
):
    count = lax.axis_size("row")
    rows = block_input.shape[0]
    core = lax.axis_index("col").astype(jnp.int32)[None]
    place, swap = places()
    slot = inverse_places(place)
    cosine, sine = rotary_tables(place, rows)
    half_units = out_weight.shape[0] // 2
    total_hidden = down_weight.shape[0]
    half_hidden = -(-total_hidden // (2 * LANES)) * LANES

    inputs = block_input.astype(f32)
    gain_one = norm1_gain.astype(f32)
    gain_two = norm2_gain.astype(f32)
    hat_one, inverse_one = normalize(inputs)
    normed_one = (hat_one * gain_one + norm1_shift.astype(f32)).astype(bf16)

    one_own = gather_rows(normed_one)
    qkv_keep, qkv_send = halves(qkv_weight, 2, half_units)
    qkv_taken = sibling(qkv_send)
    one_other = [sibling(one_own[swap[at]]) for at in range(count)]
    grad_own = gather_rows(output_grad)
    grad_other = [sibling(grad_own[swap[at]]) for at in range(count)]
    gate_up_keep, gate_up_send = halves(gate_up_weight, 2, half_hidden)
    gate_up_taken = sibling(gate_up_send)
    down_keep, down_send = halves(down_weight, 0, half_hidden)
    down_taken = sibling(down_send)
    out_keep, out_send = halves(out_weight, 0, half_units)
    out_taken = sibling(out_send)

    qkv = None
    for at in range(count):
        qkv = project_piece(
            at, count, one_own[at], one_other[at], qkv_keep, qkv_taken,
            qkv_bias[:, None, :], cosine, sine, qkv,
        )
    mixed, kept, logsum = attend_forward(slot, qkv)
    *branch, mixed_units = mixed_out(core, swap, mixed, sibling(mixed), out_weight)
    after = inputs + scatter_rows(branch)
    hat_two, inverse_two = normalize(after)
    normed_two = (hat_two * gain_two + norm2_shift.astype(f32)).astype(bf16)

    two_own = gather_rows(normed_two)
    two_other = [sibling(two_own[swap[at]]) for at in range(count)]
    order = (0, 3, 1, 2) if grid_rows() else tuple(range(count))
    pieces = {}
    for at in order:
        pieces[at] = hidden_piece(
            two_own[at], two_other[at], grad_own[at], grad_other[at],
            gate_up_keep, gate_up_taken, down_keep, down_taken,
        )
    others = {at: sibling(pieces[swap[at]]) for at in order}
    units = None
    down_parts, normed_parts = [None] * count, [None] * count
    for at in order:
        down_parts[at], normed_parts[at], units = units_back_piece(
            at, count, core, pieces[at], others[at], gate_up_weight, down_weight, units
        )
    units = units.reshape(3, count * rows, total_hidden)

    grad_rows = jnp.concatenate(grad_own, axis=0)
    two_rows = jnp.concatenate(two_own, axis=0)
    down_grad = dot(units[0], grad_rows, TN).astype(bf16)
    split = half_hidden
    down_grad = jnp.concatenate(
        [sum_sequences(down_grad[:split]), sum_sequences(down_grad[split:])], axis=0
    )
    gate_up_grad = jnp.stack(
        [sum_sequences(dot(two_rows, units[kind], TN).astype(bf16)) for kind in (1, 2)]
    )

    normed_two_grad = scatter_rows(normed_parts)
    block_output = (after + scatter_rows(down_parts)).astype(bf16)
    gain_two_grad = jnp.sum(normed_two_grad * hat_two, axis=0)
    shift_two_grad = jnp.sum(normed_two_grad, axis=0)
    after_grad = output_grad.astype(f32) + norm_back(
        normed_two_grad * gain_two, hat_two, inverse_two
    )
    branch_own = gather_rows(after_grad.astype(bf16))
    branch_other = [sibling(branch_own[swap[at]]) for at in range(count)]
    mixed_grad = mixed_back(branch_own, branch_other, out_keep, out_taken)
    branch_rows = jnp.concatenate(branch_own, axis=0)
    out_grad = sum_sequences(
        dot(mixed_units.reshape(count * rows, -1), branch_rows, TN).astype(bf16)
    )
    project_grad = attend_backward(slot, qkv, mixed_grad, kept, logsum, cosine, sine)
    *normed_parts, project_units = project_back(
        core, swap, project_grad, sibling(project_grad), qkv_weight
    )
    bias_grad = jnp.sum(project_grad.astype(f32), axis=(1, 2))
    one_rows = jnp.concatenate(one_own, axis=0)
    project_units = project_units.reshape(3, count * rows, -1)
    qkv_grad = jnp.stack(
        [sum_sequences(dot(one_rows, project_units[kind], TN).astype(bf16)) for kind in range(3)]
    )
    normed_one_grad = scatter_rows(normed_parts)
    input_grad = after_grad + norm_back(normed_one_grad * gain_one, hat_one, inverse_one)
    gain_one_grad = jnp.sum(normed_one_grad * hat_one, axis=0)
    shift_one_grad = jnp.sum(normed_one_grad, axis=0)
    bias_grad = lax.psum(bias_grad, "dp")
    gain_one_grad, shift_one_grad, gain_two_grad, shift_two_grad = lax.psum(
        (gain_one_grad, shift_one_grad, gain_two_grad, shift_two_grad), ("dp", "row")
    )
    return (
        block_output,
        input_grad,
        gain_one_grad,
        shift_one_grad,
        qkv_grad,
        bias_grad,
        out_grad,
        gain_two_grad,
        shift_two_grad,
        gate_up_grad,
        down_grad,
    )


def inverse_places(place):
    spots = jnp.arange(place.shape[0])
    return jnp.sum(
        jnp.where(place[None, :] == spots[:, None], spots[None, :], 0), axis=1
    ).astype(jnp.int32)


def solution(mesh):
    placed = (
        P(("dp", "row"), "col"),
        P("col"),
        P("col"),
        P(None, "col", "row"),
        P(None, ("row", "col")),
        P("row", "col"),
        P("col"),
        P("col"),
        P(None, "col", "row"),
        P("row", "col"),
        P(("dp", "row"), "col"),
    )
    return jax.shard_map(
        shards,
        mesh=mesh,
        in_specs=placed,
        out_specs=(
            P(("dp", "row"), "col"),
            P(("dp", "row"), "col"),
            P("col"),
            P("col"),
            P(None, "col", "row"),
            P(None, ("row", "col")),
            P("row", "col"),
            P("col"),
            P("col"),
            P(None, "col", "row"),
            P("row", "col"),
        ),
        check_vma=False,
    )
```

```python
import functools

import jax
import jax.numpy as jnp
from jax import lax
from jax.experimental import pallas as pl
from jax.experimental.pallas import tpu as pltpu
from jax.sharding import PartitionSpec as P

HD = 64
ROT = 16
LANES = 128
MIB = 1 << 20

epsilon = 1e-05
base_rate = 10000.0
bf16 = jnp.bfloat16
f32 = jnp.float32

NN = (((1,), (0,)), ((), ()))
NT = (((1,), (1,)), ((), ()))
TN = (((0,), (0,)), ((), ()))


def dot(first, second, dims=NN):
    return lax.dot_general(first, second, dims, preferred_element_type=f32)


def row_permute(values, core_zero, core_one):
    pairs = [
        (row * 2 + core, (row ^ (core_one if core else core_zero)) * 2 + core)
        for row in range(4)
        for core in range(2)
    ]
    return lax.ppermute(values, ("row", "col"), pairs)


def first_way(values):
    return row_permute(values, 1, 2)


def second_way(values):
    return row_permute(values, 2, 1)


def sibling(values):
    return lax.ppermute(values, "col", [(0, 1), (1, 0)])


def grid_rows():
    return lax.axis_size("row") == 4


def places():
    row, core = lax.axis_index("row"), lax.axis_index("col")
    if grid_rows():
        one = jnp.where(core == 0, 1, 2)
        return jnp.stack([row, row ^ one, row ^ (3 - one), row ^ 3]), (0, 2, 1, 3)
    count = lax.axis_size("row")
    return jnp.arange(count), tuple(range(count))


def after(value, *earlier):
    return lax.optimization_barrier((value,) + earlier)[0]


def gather_rows(own):
    if grid_rows():
        near = first_way(own)
        side = second_way(own)
        return [own, near, side, second_way(near)]
    whole = lax.all_gather(own, "row", axis=0, tiled=True)
    return jnp.split(whole, lax.axis_size("row"), axis=0)


def scatter_rows(parts):
    if grid_rows():
        passing = first_way(parts[3])
        near = first_way(parts[1])
        side = second_way((parts[2].astype(f32) + passing.astype(f32)).astype(bf16))
        return parts[0].astype(f32) + near.astype(f32) + side.astype(f32)
    whole = jnp.concatenate(parts, axis=0)
    return lax.psum_scatter(whole, "row", scatter_dimension=0, tiled=True).astype(f32)


def line():
    return lax.axis_size("dp") == 4


def in_middle():
    place = lax.axis_index("dp")
    return (place == 1) | (place == 2)


def inward(part):
    return lax.ppermute(part, "dp", [(0, 1), (3, 2)])


def across(part):
    return lax.ppermute(part, "dp", [(1, 2), (2, 1)])


def outward(part):
    return lax.ppermute(part, "dp", [(1, 0), (2, 3)])


def plus(first, second):
    return (first.astype(f32) + second.astype(f32)).astype(first.dtype)


class Sum:
    def __init__(self, part):
        self.part = part
        self.moved = inward(part) if line() else None

    def middle(self, *earlier):
        if line():
            self.half = plus(self.part, after(self.moved, *earlier))
            self.moved = across(self.half)
        return self

    def out(self, *earlier):
        if line():
            self.total = plus(self.half, after(self.moved, *earlier))
            self.moved = outward(self.total)
        return self

    def value(self, *earlier):
        if line():
            return jnp.where(in_middle(), self.total, after(self.moved, *earlier)).astype(f32)
        return lax.psum(self.part, "dp").astype(f32)


def sum_rows(values):
    if grid_rows():
        values = values + first_way(values)
        return values + second_way(values)
    return lax.psum(values, "row")


def width_pair(first, second):
    return lax.psum((first, second), "col")


def normalize(values):
    width = values.shape[1] * lax.axis_size("col")
    totals, squares = width_pair(jnp.sum(values, axis=-1), jnp.sum(values * values, axis=-1))
    average = totals / width
    spread = squares / width - average * average
    inverse = lax.rsqrt(spread + epsilon)[:, None]
    return ((values - average[:, None]) * inverse, inverse)


def norm_back(scaled, normed_hat, inverse):
    width = normed_hat.shape[1] * lax.axis_size("col")
    first, second = width_pair(jnp.sum(scaled, axis=-1), jnp.sum(scaled * normed_hat, axis=-1))
    return inverse * (scaled - first[:, None] / width - normed_hat * second[:, None] / width)


def rotary_tables(place, rows):
    half_dims = ROT // 2
    lane = jnp.arange(LANES) % HD
    freqs = base_rate ** (-(2.0 * (lane % half_dims).astype(f32)) / ROT)
    where = (place[:, None] * rows + jnp.arange(rows)[None, :]).astype(f32)
    angles = where[:, :, None] * freqs
    turned = lane < ROT
    cosine = jnp.where(turned, jnp.cos(angles), 1.0)
    sine = jnp.where(turned, jnp.where(lane < half_dims, -1.0, 1.0) * jnp.sin(angles), 0.0)
    return cosine, sine


def turn(values, cosine, sine):
    half_dims = ROT // 2
    lane = lax.broadcasted_iota(jnp.int32, values.shape, 1) % HD
    partner = jnp.where(
        lane < half_dims,
        pltpu.roll(values, LANES - half_dims, 1),
        pltpu.roll(values, half_dims, 1),
    )
    return values * cosine + partner * sine


def params(mib, *order):
    return pltpu.CompilerParams(vmem_limit_bytes=mib * MIB)


def cost(flops, moved, hard=0):
    return pl.CostEstimate(flops=int(flops), bytes_accessed=int(moved), transcendentals=int(hard))


def project_kernel(own, other, keep, taken, bias, cosine, sine, *rest):
    out = rest[-1]
    kind = pl.program_id(0)
    result = dot(own[...], keep[0]) + dot(other[...], taken[0]) + bias[0].astype(f32)

    @pl.when(kind < 2)
    def _():
        for at in range(0, result.shape[1], LANES):
            part = slice(at, at + LANES)
            out[0, 0, :, part] = turn(result[:, part], cosine[0], sine[0]).astype(bf16)

    @pl.when(kind == 2)
    def _():
        out[0, 0] = result.astype(bf16)


def project_piece(index, count, own, other, keep, taken, bias, cosine, sine, before):
    rows, width = own.shape
    units = keep.shape[2]
    whole = lambda k: (0, 0)
    table = pl.BlockSpec((1, rows, LANES), lambda k: (index, 0, 0))
    weight = pl.BlockSpec((1, width, units), lambda k: (k, 0, 0))
    in_specs = [
        pl.BlockSpec((rows, width), whole),
        pl.BlockSpec((rows, width), whole),
        weight,
        weight,
        pl.BlockSpec((1, 1, units), lambda k: (k, 0, 0)),
        table,
        table,
    ]
    args = [own, other, keep, taken, bias, cosine, sine]
    aliases = {}
    if before is not None:
        in_specs.append(pl.BlockSpec(memory_space=pl.ANY))
        args.append(before)
        aliases = {7: 0}
    return pl.pallas_call(
        project_kernel,
        grid=(3,),
        in_specs=in_specs,
        out_specs=pl.BlockSpec((1, 1, rows, units), lambda k: (index, k, 0, 0)),
        out_shape=jax.ShapeDtypeStruct((count, 3, rows, units), bf16),
        input_output_aliases=aliases,
        compiler_params=params(24),
        cost_estimate=cost(12 * rows * width * units, 4 * rows * width + 12 * width * units),
        name="project_piece",
    )(*args)


def causal(rows):
    keys = lax.broadcasted_iota(jnp.int32, (rows, rows), 0)
    return keys <= lax.broadcasted_iota(jnp.int32, (rows, rows), 1)


def head_lanes(values, head):
    lane = lax.broadcasted_iota(jnp.int32, values.shape, 1)
    return jnp.where((lane >= head * HD) & (lane < (head + 1) * HD), values, jnp.zeros_like(values))


def walk(stop, body, carry):
    if isinstance(stop, int):
        for step in range(stop):
            carry = body(step, carry)
        return carry
    return lax.fori_loop(0, stop, body, carry)


def each(count, body):
    if count <= 4:
        for step in range(count):
            body(step)
    else:
        lax.fori_loop(0, count, lambda step, carry: (body(step), carry)[1], 0)


def row_range(step, rows):
    return pl.ds(step * rows if isinstance(step, int) else pl.multiple_of(step * rows, rows), rows)


def attend_kernel(slot, qkv, mixed, kept, logsum, scores):
    count, _, rows, _ = qkv.shape
    heads = LANES // HD
    scale = HD**-0.5

    def one(at):
        here = slot[at]
        query = qkv[here, 0] * jnp.asarray(scale, bf16)
        for head in range(heads):

            def look(past, highest):
                block = dot(head_lanes(qkv[slot[past], 1], head), query, NT)
                scores[row_range(past, rows), :] = block
                return jnp.maximum(highest, jnp.max(block, axis=0, keepdims=True))

            def add(past, carry):
                total, outs = carry
                weights = jnp.exp(scores[row_range(past, rows), :] - highest)
                total = total + jnp.sum(weights, axis=0, keepdims=True)
                value = jnp.transpose(qkv[slot[past], 2])[head * HD : (head + 1) * HD]
                return total, outs + dot(value, weights.astype(bf16))

            block = dot(head_lanes(qkv[here, 1], head), query, NT)
            block = jnp.where(causal(rows), block, -1e30)
            scores[row_range(at, rows), :] = block
            highest = walk(at, look, jnp.max(block, axis=0, keepdims=True))
            total, outs = walk(
                at + 1, add, (jnp.zeros((1, rows), f32), jnp.zeros((HD, rows), f32))
            )
            kept[0, here, pl.ds(head * HD, HD), :] = outs / total
            logsum[0, here, pl.ds(head, 1), :] = highest + jnp.log(total)
        mixed[here] = jnp.transpose(kept[0, here]).astype(bf16)

    each(count, one)


def attend_forward(slot, qkv):
    count, _, rows, units = qkv.shape
    pairs = units // LANES
    work = rows * rows * count * (count + 1) // 2 * units
    return pl.pallas_call(
        attend_kernel,
        grid_spec=pltpu.PrefetchScalarGridSpec(
            num_scalar_prefetch=1,
            grid=(pairs,),
            in_specs=[pl.BlockSpec((count, 3, rows, LANES), lambda p, s: (0, 0, 0, p))],
            out_specs=[
                pl.BlockSpec((count, rows, LANES), lambda p, s: (0, 0, p)),
                pl.BlockSpec((1, count, LANES, rows), lambda p, s: (p, 0, 0, 0)),
                pl.BlockSpec((1, count, 8, rows), lambda p, s: (p, 0, 0, 0)),
            ],
            scratch_shapes=[pltpu.VMEM((count * rows, rows), f32)],
        ),
        out_shape=[
            jax.ShapeDtypeStruct((count, rows, units), bf16),
            jax.ShapeDtypeStruct((pairs, count, LANES, rows), f32),
            jax.ShapeDtypeStruct((pairs, count, 8, rows), f32),
        ],
        compiler_params=params(40),
        cost_estimate=cost(16 * work, 16 * count * rows * units, work // HD),
        name="attend_forward",
    )(slot, qkv)


def attend_back_kernel(slot, qkv, grads, kept, logsum, cosine, sine, out, dq, dk, dv, inner):
    count, _, rows, _ = qkv.shape
    heads = LANES // HD
    scale = HD**-0.5
    dk[...] = jnp.zeros_like(dk)
    dv[...] = jnp.zeros_like(dv)

    def sums(at):
        product = jnp.transpose(grads[at].astype(f32)) * kept[0, at]
        for head in range(heads):
            part = product[head * HD : (head + 1) * HD]
            inner[at, pl.ds(head, 1), :] = jnp.sum(part, axis=0, keepdims=True)

    def one(at):
        here = slot[at]
        query = qkv[here, 0] * jnp.asarray(scale, bf16)
        grad = grads[here]
        for head in range(heads):
            query_head = head_lanes(query, head)
            grad_head = head_lanes(grad, head)

            def look(past, query_grad, last=False):
                there = slot[past]
                key = qkv[there, 1]
                block = dot(key, query_head, NT)
                weights = jnp.exp(block - logsum[0, here, pl.ds(head, 1), :])
                if last:
                    weights = jnp.where(causal(rows), weights, 0.0)
                moved = dot(qkv[there, 2], grad_head, NT)
                raw = (weights * (moved - inner[here, pl.ds(head, 1), :])).astype(bf16)
                dv[there] += dot(weights.astype(bf16), grad_head)
                dk[there] += dot(raw, query_head)
                turned = jnp.transpose(key)[head * HD : (head + 1) * HD]
                return query_grad + dot(turned, raw)

            query_grad = walk(at, look, jnp.zeros((HD, rows), f32))
            dq[pl.ds(head * HD, HD), :] = look(at, query_grad, True) * scale
        out[0, here] = turn(jnp.transpose(dq[...]), cosine[here], -sine[here]).astype(bf16)

    def finish(at):
        out[1, at] = turn(dk[at], cosine[at], -sine[at]).astype(bf16)
        out[2, at] = dv[at].astype(bf16)

    each(count, sums)
    each(count, one)
    each(count, finish)


def attend_backward(slot, qkv, grads, kept, logsum, cosine, sine):
    count, _, rows, units = qkv.shape
    pairs = units // LANES
    work = rows * rows * count * (count + 1) // 2 * units
    table = pl.BlockSpec((count, rows, LANES), lambda p, s: (0, 0, 0))
    return pl.pallas_call(
        attend_back_kernel,
        grid_spec=pltpu.PrefetchScalarGridSpec(
            num_scalar_prefetch=1,
            grid=(pairs,),
            in_specs=[
                pl.BlockSpec((count, 3, rows, LANES), lambda p, s: (0, 0, 0, p)),
                pl.BlockSpec((count, rows, LANES), lambda p, s: (0, 0, p)),
                pl.BlockSpec((1, count, LANES, rows), lambda p, s: (p, 0, 0, 0)),
                pl.BlockSpec((1, count, 8, rows), lambda p, s: (p, 0, 0, 0)),
                table,
                table,
            ],
            out_specs=pl.BlockSpec((3, count, rows, LANES), lambda p, s: (0, 0, 0, p)),
            scratch_shapes=[
                pltpu.VMEM((LANES, rows), f32),
                pltpu.VMEM((count, rows, LANES), f32),
                pltpu.VMEM((count, rows, LANES), f32),
                pltpu.VMEM((count, 8, rows), f32),
            ],
        ),
        out_shape=jax.ShapeDtypeStruct((3, count, rows, units), bf16),
        compiler_params=params(48),
        cost_estimate=cost(40 * work, 24 * count * rows * units, work // HD),
        name="attend_backward",
    )(slot, qkv, grads, kept, logsum, cosine, sine)


def ordered(core, own, other, out, width):
    rest = out.shape[-1] - width
    lead = core[0] == 0
    out[..., :width] = jnp.where(lead, own[...], other[...])
    out[..., width:] = jnp.where(lead, other[..., :rest], own[..., :rest])


def block_of(width):
    return 256 if width % 256 == 0 else LANES


def mixed_out_kernel(swap, core, own, other, weight, *outs):
    units = outs[-1]
    count = own.shape[0]

    @pl.when(pl.program_id(0) == 0)
    def _():
        for at in range(count):
            ordered(core, own.at[at], other.at[swap[at]], units.at[at], own.shape[2])

    for at in range(count):
        outs[at][...] = dot(units[at], weight[...]).astype(bf16)


def mixed_out(core, swap, own, other, weight):
    count, rows, units = own.shape
    width = weight.shape[1]
    block = block_of(width)
    whole = lambda k, s: (0, 0, 0)
    return pl.pallas_call(
        functools.partial(mixed_out_kernel, swap),
        grid_spec=pltpu.PrefetchScalarGridSpec(
            num_scalar_prefetch=1,
            grid=(width // block,),
            in_specs=[
                pl.BlockSpec((count, rows, units), whole),
                pl.BlockSpec((count, rows, units), whole),
                pl.BlockSpec((2 * units, block), lambda k, s: (0, k)),
            ],
            out_specs=[pl.BlockSpec((rows, block), lambda k, s: (0, k))] * count
            + [pl.BlockSpec((count, rows, 2 * units), whole)],
        ),
        out_shape=[jax.ShapeDtypeStruct((rows, width), bf16)] * count
        + [jax.ShapeDtypeStruct((count, rows, 2 * units), bf16)],
        compiler_params=params(24),
        cost_estimate=cost(4 * count * rows * units * width, 2 * count * rows * (width + 4 * units)),
        name="mixed_out",
    )(core, own, other, weight)


def hidden_kernel(members, *refs):
    own, other, grad_own, grad_other = (refs[k * members : (k + 1) * members] for k in range(4))
    gate_up, taken, down, down_taken = refs[4 * members : 4 * members + 4]
    outs = refs[4 * members + 4 :]
    for at in range(members):
        gate = dot(own[at][...], gate_up[0]) + dot(other[at][...], taken[0])
        up = dot(own[at][...], gate_up[1]) + dot(other[at][...], taken[1])
        grad = dot(grad_own[at][...], down[...], NT) + dot(grad_other[at][...], down_taken[...], NT)
        sigmoid = jax.nn.sigmoid(gate)
        silu = gate * sigmoid
        slope = sigmoid * (1.0 + gate * (1.0 - sigmoid))
        outs[at][0] = (grad * up * slope).astype(bf16)
        outs[at][1] = (grad * silu).astype(bf16)
        outs[at][2] = (silu * up).astype(bf16)


def hidden_pieces(own, other, grad_own, grad_other, gate_up, taken, down, down_taken):
    members = len(own)
    rows, width = own[0].shape
    units = gate_up.shape[2]
    block = block_of(units)
    rows_in = pl.BlockSpec((rows, width), lambda k: (0, 0))
    entry = pl.BlockSpec((2, width, block), lambda k: (0, 0, k))
    leave = pl.BlockSpec((block, width), lambda k: (k, 0))
    return pl.pallas_call(
        functools.partial(hidden_kernel, members),
        grid=(units // block,),
        in_specs=[rows_in] * (4 * members) + [entry, entry, leave, leave],
        out_specs=[pl.BlockSpec((3, rows, block), lambda k: (0, 0, k))] * members,
        out_shape=[jax.ShapeDtypeStruct((3, rows, units), bf16)] * members,
        compiler_params=params(40),
        cost_estimate=cost(
            12 * members * rows * width * units, 12 * width * units + 8 * members * rows * width
        ),
        name="hidden_pieces",
    )(*own, *other, *grad_own, *grad_other, gate_up, taken, down, down_taken)


def down_grad_kernel(count, second_steps, core, *refs):
    own, other, grads = refs[:count], refs[count : 2 * count], refs[2 * count]
    first, second, units = refs[-3:]
    rows = own[0].shape[1]
    lead = core[0] == 0

    def part(mine, out):
        for at in range(count):
            units[pl.ds(at * rows, rows), :] = jnp.where(mine, own[at][0], other[at][0])
        out[...] = dot(units[...], grads[...], TN).astype(bf16)

    part(lead, first)

    @pl.when(pl.program_id(0) < second_steps)
    def _():
        part(jnp.logical_not(lead), second)


def down_grad_parts(core, own, other, grads, total):
    count = len(own)
    _, rows, half = own[0].shape
    width = grads.shape[1]
    block = 384
    rest = total - half
    second_steps = -(-rest // block)
    piece = pl.BlockSpec((1, rows, block), lambda k, s: (2, 0, k))
    return pl.pallas_call(
        functools.partial(down_grad_kernel, count, second_steps),
        grid_spec=pltpu.PrefetchScalarGridSpec(
            num_scalar_prefetch=1,
            grid=(half // block,),
            in_specs=[piece] * (2 * count) + [pl.BlockSpec(grads.shape, lambda k, s: (0, 0))],
            out_specs=[
                pl.BlockSpec((block, width), lambda k, s: (k, 0)),
                pl.BlockSpec((block, width), lambda k, s: (jnp.minimum(k, second_steps - 1), 0)),
            ],
            scratch_shapes=[pltpu.VMEM((count * rows, block), bf16)],
        ),
        out_shape=[
            jax.ShapeDtypeStruct((half, width), bf16),
            jax.ShapeDtypeStruct((rest, width), bf16),
        ],
        compiler_params=params(40),
        cost_estimate=cost(
            2 * count * rows * total * width, 2 * count * rows * (width + 2 * half) + 2 * total * width
        ),
        name="down_grad_parts",
    )(core, *own, *other, grads)


def normed_back_kernel(members, core, *refs):
    own, other, gate_up = refs[:members], refs[members : 2 * members], refs[2 * members]
    outs = refs[-members - 2 : -2]
    gate, up = refs[-2:]
    rows = own[0].shape[1]

    @pl.when(pl.program_id(0) == 0)
    def _():
        for at in range(members):
            for kind, units in ((0, gate), (1, up)):
                ordered(
                    core,
                    own[at].at[kind],
                    other[at].at[kind],
                    units.at[pl.ds(at * rows, rows)],
                    own[0].shape[2],
                )

    for at in range(members):
        span = pl.ds(at * rows, rows)
        outs[at][...] = (
            dot(gate[span, :], gate_up[0], NT) + dot(up[span, :], gate_up[1], NT)
        ).astype(bf16)


def normed_back_pieces(index, count, core, own, other, gate_up, before):
    members = len(own)
    _, rows, half = own[0].shape
    _, width, total = gate_up.shape
    block = block_of(width)
    halves = pl.BlockSpec((2, rows, half), lambda k, s: (0, 0, 0))
    in_specs = [halves] * (2 * members) + [
        pl.BlockSpec((2, block, total), lambda k, s: (0, k, 0))
    ]
    args = [*own, *other, gate_up]
    aliases = {}
    if before is not None:
        aliases = {len(args) + 1: members, len(args) + 2: members + 1}
        in_specs += [pl.BlockSpec(memory_space=pl.ANY)] * 2
        args += before
    columns = pl.BlockSpec((rows, block), lambda k, s: (0, k))
    units = pl.BlockSpec((members * rows, total), lambda k, s: (index, 0))
    units_shape = jax.ShapeDtypeStruct((count * rows, total), bf16)
    result = pl.pallas_call(
        functools.partial(normed_back_kernel, members),
        grid_spec=pltpu.PrefetchScalarGridSpec(
            num_scalar_prefetch=1,
            grid=(width // block,),
            in_specs=in_specs,
            out_specs=[columns] * members + [units, units],
        ),
        out_shape=[jax.ShapeDtypeStruct((rows, width), bf16)] * members
        + [units_shape, units_shape],
        input_output_aliases=aliases,
        compiler_params=params(48),
        cost_estimate=cost(
            4 * members * rows * width * total, 4 * width * total + 8 * members * rows * total
        ),
        name="normed_back_pieces",
    )(core, *args)
    return result[:members], result[members:]


def down_out_kernel(count, core, *refs):
    own, other, down = refs[:count], refs[count : 2 * count], refs[2 * count]
    outs, units = refs[2 * count + 1 : -1], refs[-1]

    @pl.when(pl.program_id(0) == 0)
    def _():
        for at in range(count):
            ordered(core, own[at].at[0], other[at].at[0], units.at[at], own[at].shape[2])

    for at in range(count):
        outs[at][...] = dot(units[at], down[...]).astype(bf16)


def down_out(core, own, other, down):
    count = len(own)
    _, rows, half = own[0].shape
    total, width = down.shape
    block = block_of(width)
    piece = pl.BlockSpec((1, rows, half), lambda k, s: (2, 0, 0))
    return pl.pallas_call(
        functools.partial(down_out_kernel, count),
        grid_spec=pltpu.PrefetchScalarGridSpec(
            num_scalar_prefetch=1,
            grid=(width // block,),
            in_specs=[piece] * (2 * count) + [pl.BlockSpec((total, block), lambda k, s: (0, k))],
            out_specs=[pl.BlockSpec((rows, block), lambda k, s: (0, k))] * count,
            scratch_shapes=[pltpu.VMEM((count, rows, total), bf16)],
        ),
        out_shape=[jax.ShapeDtypeStruct((rows, width), bf16)] * count,
        compiler_params=params(48),
        cost_estimate=cost(
            2 * count * rows * total * width, 2 * total * width + 4 * count * rows * total
        ),
        name="down_out",
    )(core, *own, *other, down)


def mixed_grad_kernel(count, *refs):
    keep, taken, out = refs[-3:]
    for at in range(count):
        out[at] = (
            dot(refs[at][...], keep[...], NT) + dot(refs[count + at][...], taken[...], NT)
        ).astype(bf16)


def mixed_back(own, other, keep, taken):
    count = len(own)
    rows, width = own[0].shape
    units = keep.shape[0]
    return pl.pallas_call(
        functools.partial(mixed_grad_kernel, count),
        out_shape=jax.ShapeDtypeStruct((count, rows, units), bf16),
        compiler_params=params(24 if count == 4 else 40),
        cost_estimate=cost(4 * count * rows * width * units, 4 * count * rows * width),
        name="mixed_back",
    )(*own, *other, keep, taken)


def project_back_kernel(swap, core, own, other, weight, *outs):
    units = outs[-1]
    count = own.shape[1]

    @pl.when(pl.program_id(0) == 0)
    def _():
        for kind in range(3):
            for at in range(count):
                ordered(
                    core,
                    own.at[kind, at],
                    other.at[kind, swap[at]],
                    units.at[kind, at],
                    own.shape[3],
                )

    for at in range(count):
        outs[at][...] = sum(dot(units[kind, at], weight[kind], NT) for kind in range(3)).astype(bf16)


def project_back(core, swap, own, other, weight):
    _, count, rows, half = own.shape
    _, width, total = weight.shape
    block = block_of(width)
    whole = lambda k, s: (0, 0, 0, 0)
    return pl.pallas_call(
        functools.partial(project_back_kernel, swap),
        grid_spec=pltpu.PrefetchScalarGridSpec(
            num_scalar_prefetch=1,
            grid=(width // block,),
            in_specs=[
                pl.BlockSpec((3, count, rows, half), whole),
                pl.BlockSpec((3, count, rows, half), whole),
                pl.BlockSpec((3, block, total), lambda k, s: (0, k, 0)),
            ],
            out_specs=[pl.BlockSpec((rows, block), lambda k, s: (0, k))] * count
            + [pl.BlockSpec((3, count, rows, total), whole)],
        ),
        out_shape=[jax.ShapeDtypeStruct((rows, width), bf16)] * count
        + [jax.ShapeDtypeStruct((3, count, rows, total), bf16)],
        compiler_params=params(40),
        cost_estimate=cost(6 * count * rows * total * width, 2 * count * rows * (width + 6 * total)),
        name="project_back",
    )(core, own, other, weight)


def halves(weight, axis, width):
    lead = lax.slice_in_dim(weight, 0, width, axis=axis)
    rest = lax.slice_in_dim(weight, width, weight.shape[axis], axis=axis)
    pad = [(0, 0)] * weight.ndim
    pad[axis] = (0, width - rest.shape[axis])
    rest = jnp.pad(rest, pad)
    first = lax.axis_index("col") == 0
    return jnp.where(first, lead, rest), jnp.where(first, rest, lead)


def shards(
    block_input,
    norm1_gain,
    norm1_shift,
    qkv_weight,
    qkv_bias,
    out_weight,
    norm2_gain,
    norm2_shift,
    gate_up_weight,
    down_weight,
    output_grad,
):
    count = lax.axis_size("row")
    rows = block_input.shape[0]
    core = lax.axis_index("col").astype(jnp.int32)[None]
    place, swap = places()
    slot = inverse_places(place)
    cosine, sine = rotary_tables(place, rows)
    half_units = out_weight.shape[0] // 2
    total_hidden = down_weight.shape[0]
    half_hidden = -(-total_hidden // (2 * LANES)) * LANES

    inputs = block_input.astype(f32)
    gain_one = norm1_gain.astype(f32)
    gain_two = norm2_gain.astype(f32)
    hat_one, inverse_one = normalize(inputs)
    normed_one = (hat_one * gain_one + norm1_shift.astype(f32)).astype(bf16)

    qkv_keep, qkv_send = halves(qkv_weight, 2, half_units)
    gate_up_keep, gate_up_send = halves(gate_up_weight, 2, half_hidden)
    down_keep, down_send = halves(down_weight, 0, half_hidden)
    out_keep, out_send = halves(out_weight, 0, half_units)
    qkv_taken = sibling(qkv_send)
    gate_up_taken = sibling(gate_up_send)
    down_taken = sibling(down_send)
    out_taken = sibling(out_send)

    def project(at, own, other, before):
        return project_piece(
            at, count, own, other, qkv_keep, qkv_taken,
            qkv_bias[:, None, :], cosine, sine, before,
        )

    one_own = gather_rows(normed_one)
    qkv = None
    for at in range(count):
        ready = one_own if at == 0 else [after(piece, qkv) for piece in one_own]
        qkv = project(at, ready[at], sibling(ready[swap[at]]), qkv)
    grad_own = gather_rows(after(output_grad, one_own[-1]))
    grad_own[0] = output_grad
    mixed, kept, logsum = attend_forward(slot, qkv)
    grad_other = [sibling(after(grad_own[swap[at]], mixed)) for at in range(count)]
    *branch, mixed_units = mixed_out(core, swap, mixed, sibling(mixed), out_weight)
    after_rows = inputs + scatter_rows(branch)
    hat_two, inverse_two = normalize(after_rows)
    normed_two = (hat_two * gain_two + norm2_shift.astype(f32)).astype(bf16)

    two_own = gather_rows(normed_two)
    groups = [(0,), (1, 2), (3,)] if grid_rows() else [(at,) for at in range(count)]
    order = (1, 2, 0, 3) if grid_rows() else tuple(range(count))
    index = {(0,): 2, (1, 2): 0, (3,): 3}
    mine, theirs = [None] * count, [None] * count
    normed_parts = [None] * count
    units = None
    done = []

    def hidden(group, *earlier):
        ready = [after(two_own[at], *earlier) for at in range(count)]
        results = hidden_pieces(
            [ready[at] for at in group],
            [sibling(ready[swap[at]]) for at in group],
            [grad_own[at] for at in group],
            [grad_other[at] for at in group],
            gate_up_keep, gate_up_taken, down_keep, down_taken,
        )
        for at, result in zip(group, results):
            mine[at] = result
        for at in group:
            theirs[at] = sibling(mine[swap[at]])
        return results[0]

    def back(group, units, *earlier):
        parts, units = normed_back_pieces(
            index[group] if grid_rows() else group[0],
            count, core,
            [mine[at] for at in group],
            [after(theirs[at], *earlier) for at in group],
            gate_up_weight, units,
        )
        for at, part in zip(group, parts):
            normed_parts[at] = part
        return units

    last = hidden(groups[0])
    units = back(groups[0], None)
    for group in groups[1:]:
        last = hidden(group, last, units[0]) if group == groups[1] else hidden(group, last)
    grad_rows = jnp.concatenate([grad_own[at] for at in order], axis=0)
    two_rows = jnp.concatenate([two_own[at] for at in order], axis=0)
    down_sums = [
        Sum(part)
        for part in down_grad_parts(
            core,
            [mine[at] for at in order],
            [theirs[at] for at in order],
            grad_rows,
            total_hidden,
        )
    ]
    for group in groups[1:]:
        units = back(group, units, down_sums[0].part)
    normed_two_grad = scatter_rows(normed_parts)
    left = two_rows[:, : two_rows.shape[1] // 2]
    right = two_rows[:, two_rows.shape[1] // 2 :]
    gate_up_sums = [
        Sum(dot(rows_part, after(units[kind], normed_parts[0]), TN).astype(bf16))
        for kind in (0, 1)
        for rows_part in (left, right)
    ]
    down_sums[0].middle(units[0])

    after_grad = output_grad.astype(f32) + norm_back(
        normed_two_grad * gain_two, hat_two, inverse_two
    )
    branch_own = gather_rows(after_grad.astype(bf16))
    branch_other = [sibling(branch_own[swap[at]]) for at in range(count)]
    mixed_grad = mixed_back(branch_own, branch_other, out_keep, out_taken)
    down_parts = down_out(core, mine, [after(piece, after_grad) for piece in theirs], down_weight)
    gathered = branch_own[-1]
    down_parts = [after(part, gathered) for part in down_parts]
    down_sums[1].middle(normed_two_grad)
    down_sums[0].out(after_grad)

    branch_rows = jnp.concatenate(branch_own, axis=0)
    out_sum = Sum(dot(mixed_units.reshape(count * rows, -1), branch_rows, TN).astype(bf16))
    project_grad = attend_backward(slot, qkv, mixed_grad, kept, logsum, cosine, sine)
    gate_up_sums[0].middle(mixed_grad)
    down_sums[1].out(mixed_grad)
    down = scatter_rows(down_parts)
    block_output = (after_rows + down).astype(bf16)
    gate_up_sums[1].middle(project_grad)
    gate_up_sums[0].out(project_grad)

    *one_parts, project_units = project_back(
        core, swap, project_grad, sibling(project_grad), qkv_weight
    )
    one_rows = jnp.concatenate(one_own, axis=0)
    project_units = project_units.reshape(3, count * rows, -1)
    qkv_sums = [Sum(dot(one_rows, project_units[kind], TN).astype(bf16)) for kind in range(3)]
    normed_one_grad = scatter_rows(one_parts)
    sent = qkv_sums[2].part
    gate_up_sums[2].middle(sent)
    gate_up_sums[1].out(sent)
    input_grad = after_grad + norm_back(normed_one_grad * gain_one, hat_one, inverse_one)
    gate_up_sums[3].middle(input_grad)
    gate_up_sums[2].out(input_grad)

    gains = jnp.stack(
        [
            jnp.sum(normed_one_grad * hat_one, axis=0),
            jnp.sum(normed_one_grad, axis=0),
            jnp.sum(normed_two_grad * hat_two, axis=0),
            jnp.sum(normed_two_grad, axis=0),
        ]
    )
    bias_grad = jnp.sum(project_grad.astype(f32), axis=(1, 2))
    gains = sum_rows(after(gains, gate_up_sums[3].half if line() else input_grad))
    width = gains.shape[1]
    small = jnp.concatenate(
        [gains.reshape(-1, LANES), bias_grad.reshape(-1, LANES)], axis=0
    )
    small_sum = Sum(small)
    out_sum.middle(gate_up_sums[3].moved if line() else input_grad)
    gate_up_sums[3].out()
    rest = [out_sum, *qkv_sums, small_sum]
    for at, item in enumerate(rest):
        if at:
            item.middle()
            rest[at - 1].out()
    rest[-1].out()
    small = rest[-1].value()
    gains = small[: 4 * width // LANES].reshape(4, width)
    bias_grad = small[4 * width // LANES :].reshape(bias_grad.shape)

    down_grad = jnp.concatenate([item.value() for item in down_sums], axis=0)
    gate_up_grad = jnp.stack(
        [
            jnp.concatenate([gate_up_sums[2 * kind].value(), gate_up_sums[2 * kind + 1].value()], axis=0)
            for kind in (0, 1)
        ]
    )
    qkv_grad = jnp.stack([item.value() for item in qkv_sums])
    return (
        block_output,
        input_grad,
        gains[0],
        gains[1],
        qkv_grad,
        bias_grad,
        out_sum.value(),
        gains[2],
        gains[3],
        gate_up_grad,
        down_grad,
    )


def inverse_places(place):
    spots = jnp.arange(place.shape[0])
    return jnp.sum(
        jnp.where(place[None, :] == spots[:, None], spots[None, :], 0), axis=1
    ).astype(jnp.int32)


def solution(mesh):
    placed = (
        P(("dp", "row"), "col"),
        P("col"),
        P("col"),
        P(None, "col", "row"),
        P(None, ("row", "col")),
        P("row", "col"),
        P("col"),
        P("col"),
        P(None, "col", "row"),
        P("row", "col"),
        P(("dp", "row"), "col"),
    )
    return jax.shard_map(
        shards,
        mesh=mesh,
        in_specs=placed,
        out_specs=(
            P(("dp", "row"), "col"),
            P(("dp", "row"), "col"),
            P("col"),
            P("col"),
            P(None, "col", "row"),
            P(None, ("row", "col")),
            P("row", "col"),
            P("col"),
            P("col"),
            P(None, "col", "row"),
            P("row", "col"),
        ),
        check_vma=False,
    )
```

```python
import functools

import jax
import jax.numpy as jnp
from jax import lax
from jax.experimental import pallas as pl
from jax.experimental.pallas import tpu as pltpu
from jax.sharding import PartitionSpec as P

HD = 64
ROT = 16
LANES = 128
MIB = 1 << 20
COST = 1 << 16

epsilon = 1e-05
base_rate = 10000.0
bf16 = jnp.bfloat16
f32 = jnp.float32

NN = (((1,), (0,)), ((), ()))
NT = (((1,), (1,)), ((), ()))
TN = (((0,), (0,)), ((), ()))


def dot(first, second, dims=NN):
    return lax.dot_general(first, second, dims, preferred_element_type=f32)


def row_permute(values, core_zero, core_one):
    pairs = [
        (row * 2 + core, (row ^ (core_one if core else core_zero)) * 2 + core)
        for row in range(4)
        for core in range(2)
    ]
    return lax.ppermute(values, ("row", "col"), pairs)


def first_way(values):
    return row_permute(values, 1, 2)


def second_way(values):
    return row_permute(values, 2, 1)


def sibling(values):
    return lax.ppermute(values, "col", [(0, 1), (1, 0)])


def grid_rows():
    return lax.axis_size("row") == 4


def places():
    row, core = lax.axis_index("row"), lax.axis_index("col")
    if grid_rows():
        one = jnp.where(core == 0, 1, 2)
        return jnp.stack([row ^ one, row ^ (3 - one), row, row ^ 3]), (1, 0, 2, 3)
    count = lax.axis_size("row")
    return jnp.arange(count), tuple(range(count))


def after(value, *earlier):
    return lax.optimization_barrier((value,) + earlier)[0]


def gather_rows(own):
    if grid_rows():
        near = first_way(own)
        side = second_way(own)
        return [near, side, own], lambda *earlier: [second_way(after(near, side, *earlier))]
    whole = lax.all_gather(own, "row", axis=0, tiled=True)
    return jnp.split(whole, lax.axis_size("row"), axis=0), lambda *earlier: []


def scatter_rows(parts):
    if grid_rows():
        passing = first_way(parts[3])
        near = first_way(parts[0])
        side = second_way(plus(parts[1], passing))
        return parts[2].astype(f32) + near.astype(f32) + side.astype(f32)
    whole = jnp.concatenate(parts, axis=0)
    return lax.psum_scatter(whole, "row", scatter_dimension=0, tiled=True).astype(f32)


def line():
    return lax.axis_size("dp") == 4


def in_middle():
    place = lax.axis_index("dp")
    return (place == 1) | (place == 2)


def inward(part):
    return lax.ppermute(part, "dp", [(0, 1), (3, 2)])


def across(part):
    return lax.ppermute(part, "dp", [(1, 2), (2, 1)])


def outward(part):
    return lax.ppermute(part, "dp", [(1, 0), (2, 3)])


def plus(first, second):
    return (first.astype(f32) + second.astype(f32)).astype(first.dtype)


class Line:
    def __init__(self):
        self.parts, self.inner, self.half, self.other, self.total, self.outer = ([] for _ in range(6))

    def feed(self):
        at = len(self.inner)
        if at < len(self.parts) and at < len(self.half) + 2:
            part = self.parts[at]
            self.inner.append(inward(after(part, self.half[at - 2]) if at >= 2 else part))

    def add(self, *parts):
        self.parts += parts
        if line():
            for _ in parts:
                self.feed()

    def tick(self, *earlier):
        if not line():
            return earlier[0] if earlier else None
        at = len(self.half)
        if at < len(self.parts):
            self.half.append(plus(self.parts[at], after(self.inner[at], *earlier)))
            self.feed()
        back = len(self.total)
        if back < len(self.other):
            moved = after(self.other[back], self.half[at]) if at < len(self.half) else self.other[back]
            self.total.append(plus(self.half[back], after(moved, *earlier)))
            ready = self.total[-1]
            self.outer.append(outward(after(ready, self.outer[-1]) if self.outer else ready))
        if at < len(self.half):
            ready = self.half[-1]
            self.other.append(across(after(ready, self.total[-1]) if self.total else ready))
        return self.half[-1]

    def finish(self):
        while line() and len(self.total) < len(self.parts):
            self.tick()

    def value(self, at):
        if line():
            return jnp.where(in_middle(), self.total[at], self.outer[at]).astype(f32)
        return lax.psum(self.parts[at], "dp").astype(f32)


def gather_whole(own):
    return lax.all_gather(own, "row", axis=0, tiled=True)


def scatter_whole(parts):
    return lax.psum_scatter(parts, "row", scatter_dimension=0, tiled=True).astype(f32)


def sum_rows(values):
    if grid_rows():
        values = values + first_way(values)
        return values + second_way(values)
    return lax.psum(values, "row")


def width_pair(first, second):
    return lax.psum((first, second), "col")


def normalize(values):
    width = values.shape[1] * lax.axis_size("col")
    totals, squares = width_pair(jnp.sum(values, axis=-1), jnp.sum(values * values, axis=-1))
    average = totals / width
    spread = squares / width - average * average
    inverse = lax.rsqrt(spread + epsilon)[:, None]
    return ((values - average[:, None]) * inverse, inverse)


def norm_back(scaled, normed_hat, inverse):
    width = normed_hat.shape[1] * lax.axis_size("col")
    first, second = width_pair(jnp.sum(scaled, axis=-1), jnp.sum(scaled * normed_hat, axis=-1))
    return inverse * (scaled - first[:, None] / width - normed_hat * second[:, None] / width)


def rotary_tables(place, rows):
    half_dims = ROT // 2
    lane = jnp.arange(LANES) % HD
    freqs = base_rate ** (-(2.0 * (lane % half_dims).astype(f32)) / ROT)
    where = (place[:, None] * rows + jnp.arange(rows)[None, :]).astype(f32)
    angles = where[:, :, None] * freqs
    turned = lane < ROT
    cosine = jnp.where(turned, jnp.cos(angles), 1.0)
    sine = jnp.where(turned, jnp.where(lane < half_dims, -1.0, 1.0) * jnp.sin(angles), 0.0)
    return cosine, sine


def turn(values, cosine, sine):
    half_dims = ROT // 2
    lane = lax.broadcasted_iota(jnp.int32, values.shape, 1) % HD
    partner = jnp.where(
        lane < half_dims,
        pltpu.roll(values, LANES - half_dims, 1),
        pltpu.roll(values, half_dims, 1),
    )
    return values * cosine + partner * sine


def params(mib, *order):
    return pltpu.CompilerParams(vmem_limit_bytes=mib * MIB)


def cost(flops, moved, hard=0):
    return pl.CostEstimate(
        flops=int(flops) // COST, bytes_accessed=int(moved) // COST, transcendentals=int(hard) // COST
    )


def project_kernel(members, *refs):
    own, other = refs[:members], refs[members : 2 * members]
    keep, taken, bias = refs[2 * members : 2 * members + 3]
    cosine, sine = refs[2 * members + 3 : 3 * members + 3], refs[3 * members + 3 : 4 * members + 3]
    out = refs[-1]
    kind = pl.program_id(0)
    for at in range(members):
        result = dot(own[at][...], keep[0]) + dot(other[at][...], taken[0]) + bias[0].astype(f32)

        @pl.when(kind < 2)
        def _():
            for start in range(0, result.shape[1], LANES):
                part = slice(start, start + LANES)
                out[at, 0, :, part] = turn(result[:, part], cosine[at][0], sine[at][0]).astype(bf16)

        @pl.when(kind == 2)
        def _():
            out[at, 0] = result.astype(bf16)


def project_pieces(index, group, count, own, other, keep, taken, bias, cosine, sine, before):
    members = len(own)
    rows, width = own[0].shape
    units = keep.shape[2]
    piece = pl.BlockSpec((rows, width), lambda k: (0, 0))
    tables = [
        pl.BlockSpec((1, rows, LANES), functools.partial(lambda at, k: (at, 0, 0), at))
        for at in group
    ]
    weight = pl.BlockSpec((1, width, units), lambda k: (k, 0, 0))
    in_specs = [piece] * (2 * members) + [
        weight,
        weight,
        pl.BlockSpec((1, 1, units), lambda k: (k, 0, 0)),
        *tables,
        *tables,
    ]
    args = [*own, *other, keep, taken, bias] + [cosine] * members + [sine] * members
    aliases = {}
    if before is not None:
        aliases = {len(args): 0}
        in_specs.append(pl.BlockSpec(memory_space=pl.ANY))
        args.append(before)
    return pl.pallas_call(
        functools.partial(project_kernel, members),
        grid=(3,),
        in_specs=in_specs,
        out_specs=pl.BlockSpec((members, 1, rows, units), lambda k: (index, k, 0, 0)),
        out_shape=jax.ShapeDtypeStruct((count, 3, rows, units), bf16),
        input_output_aliases=aliases,
        compiler_params=params(32),
        cost_estimate=cost(
            12 * members * rows * width * units, 4 * members * rows * width + 12 * width * units
        ),
        name="project_pieces",
    )(*args)


def causal(rows):
    keys = lax.broadcasted_iota(jnp.int32, (rows, rows), 0)
    return keys <= lax.broadcasted_iota(jnp.int32, (rows, rows), 1)


def head_lanes(values, head):
    lane = lax.broadcasted_iota(jnp.int32, values.shape, 1)
    return jnp.where((lane >= head * HD) & (lane < (head + 1) * HD), values, jnp.zeros_like(values))


def walk(stop, body, carry):
    if isinstance(stop, int):
        for step in range(stop):
            carry = body(step, carry)
        return carry
    return lax.fori_loop(0, stop, body, carry)


def each(count, body):
    if count <= 4:
        for step in range(count):
            body(step)
    else:
        lax.fori_loop(0, count, lambda step, carry: (body(step), carry)[1], 0)


def row_range(step, rows):
    return pl.ds(step * rows if isinstance(step, int) else pl.multiple_of(step * rows, rows), rows)


def attend_kernel(slot, qkv, mixed, kept, logsum, scores):
    count, _, rows, _ = qkv.shape
    heads = LANES // HD
    scale = HD**-0.5

    def one(at):
        here = slot[at]
        query = qkv[here, 0] * jnp.asarray(scale, bf16)
        for head in range(heads):

            def look(past, highest):
                block = dot(head_lanes(qkv[slot[past], 1], head), query, NT)
                scores[row_range(past, rows), :] = block
                return jnp.maximum(highest, jnp.max(block, axis=0, keepdims=True))

            def add(past, carry):
                total, outs = carry
                weights = jnp.exp(scores[row_range(past, rows), :] - highest)
                total = total + jnp.sum(weights, axis=0, keepdims=True)
                value = jnp.transpose(qkv[slot[past], 2])[head * HD : (head + 1) * HD]
                return total, outs + dot(value, weights.astype(bf16))

            block = dot(head_lanes(qkv[here, 1], head), query, NT)
            block = jnp.where(causal(rows), block, -1e30)
            scores[row_range(at, rows), :] = block
            highest = walk(at, look, jnp.max(block, axis=0, keepdims=True))
            total, outs = walk(
                at + 1, add, (jnp.zeros((1, rows), f32), jnp.zeros((HD, rows), f32))
            )
            kept[0, here, pl.ds(head * HD, HD), :] = outs / total
            logsum[0, here, pl.ds(head, 1), :] = highest + jnp.log(total)
        mixed[here] = jnp.transpose(kept[0, here]).astype(bf16)

    each(count, one)


def attend_forward(slot, qkv):
    count, _, rows, units = qkv.shape
    pairs = units // LANES
    work = rows * rows * count * (count + 1) // 2 * units
    return pl.pallas_call(
        attend_kernel,
        grid_spec=pltpu.PrefetchScalarGridSpec(
            num_scalar_prefetch=1,
            grid=(pairs,),
            in_specs=[pl.BlockSpec((count, 3, rows, LANES), lambda p, s: (0, 0, 0, p))],
            out_specs=[
                pl.BlockSpec((count, rows, LANES), lambda p, s: (0, 0, p)),
                pl.BlockSpec((1, count, LANES, rows), lambda p, s: (p, 0, 0, 0)),
                pl.BlockSpec((1, count, 8, rows), lambda p, s: (p, 0, 0, 0)),
            ],
            scratch_shapes=[pltpu.VMEM((count * rows, rows), f32)],
        ),
        out_shape=[
            jax.ShapeDtypeStruct((count, rows, units), bf16),
            jax.ShapeDtypeStruct((pairs, count, LANES, rows), f32),
            jax.ShapeDtypeStruct((pairs, count, 8, rows), f32),
        ],
        compiler_params=params(40),
        cost_estimate=cost(16 * work, 16 * count * rows * units, work // HD),
        name="attend_forward",
    )(slot, qkv)


def attend_back_kernel(slot, qkv, grads, kept, logsum, cosine, sine, out, dq, dk, dv, inner):
    count, _, rows, _ = qkv.shape
    heads = LANES // HD
    scale = HD**-0.5
    dk[...] = jnp.zeros_like(dk)
    dv[...] = jnp.zeros_like(dv)

    def sums(at):
        product = jnp.transpose(grads[at].astype(f32)) * kept[0, at]
        for head in range(heads):
            part = product[head * HD : (head + 1) * HD]
            inner[at, pl.ds(head, 1), :] = jnp.sum(part, axis=0, keepdims=True)

    def one(at):
        here = slot[at]
        query = qkv[here, 0] * jnp.asarray(scale, bf16)
        grad = grads[here]
        for head in range(heads):
            query_head = head_lanes(query, head)
            grad_head = head_lanes(grad, head)

            def look(past, query_grad, last=False):
                there = slot[past]
                key = qkv[there, 1]
                block = dot(key, query_head, NT)
                weights = jnp.exp(block - logsum[0, here, pl.ds(head, 1), :])
                if last:
                    weights = jnp.where(causal(rows), weights, 0.0)
                moved = dot(qkv[there, 2], grad_head, NT)
                raw = (weights * (moved - inner[here, pl.ds(head, 1), :])).astype(bf16)
                dv[there] += dot(weights.astype(bf16), grad_head)
                dk[there] += dot(raw, query_head)
                turned = jnp.transpose(key)[head * HD : (head + 1) * HD]
                return query_grad + dot(turned, raw)

            query_grad = walk(at, look, jnp.zeros((HD, rows), f32))
            dq[pl.ds(head * HD, HD), :] = look(at, query_grad, True) * scale
        out[0, here] = turn(jnp.transpose(dq[...]), cosine[here], -sine[here]).astype(bf16)

    def finish(at):
        out[1, at] = turn(dk[at], cosine[at], -sine[at]).astype(bf16)
        out[2, at] = dv[at].astype(bf16)

    each(count, sums)
    each(count, one)
    each(count, finish)


def attend_backward(slot, qkv, grads, kept, logsum, cosine, sine):
    count, _, rows, units = qkv.shape
    pairs = units // LANES
    work = rows * rows * count * (count + 1) // 2 * units
    table = pl.BlockSpec((count, rows, LANES), lambda p, s: (0, 0, 0))
    return pl.pallas_call(
        attend_back_kernel,
        grid_spec=pltpu.PrefetchScalarGridSpec(
            num_scalar_prefetch=1,
            grid=(pairs,),
            in_specs=[
                pl.BlockSpec((count, 3, rows, LANES), lambda p, s: (0, 0, 0, p)),
                pl.BlockSpec((count, rows, LANES), lambda p, s: (0, 0, p)),
                pl.BlockSpec((1, count, LANES, rows), lambda p, s: (p, 0, 0, 0)),
                pl.BlockSpec((1, count, 8, rows), lambda p, s: (p, 0, 0, 0)),
                table,
                table,
            ],
            out_specs=pl.BlockSpec((3, count, rows, LANES), lambda p, s: (0, 0, 0, p)),
            scratch_shapes=[
                pltpu.VMEM((LANES, rows), f32),
                pltpu.VMEM((count, rows, LANES), f32),
                pltpu.VMEM((count, rows, LANES), f32),
                pltpu.VMEM((count, 8, rows), f32),
            ],
        ),
        out_shape=jax.ShapeDtypeStruct((3, count, rows, units), bf16),
        compiler_params=params(48),
        cost_estimate=cost(40 * work, 24 * count * rows * units, work // HD),
        name="attend_backward",
    )(slot, qkv, grads, kept, logsum, cosine, sine)


def ordered(core, own, other, out, width):
    rest = out.shape[-1] - width
    lead = core[0] == 0
    out[..., :width] = jnp.where(lead, own[...], other[...])
    out[..., width:] = jnp.where(lead, other[..., :rest], own[..., :rest])


def block_of(width):
    return 256 if width % 256 == 0 else LANES


def mixed_out_kernel(swap, core, place, own, other, weight, *outs):
    units = outs[-1]
    count = own.shape[0]

    @pl.when(pl.program_id(0) == 0)
    def _():
        for at in range(count):
            ordered(core, own.at[at], other.at[swap[at]], units.at[place[at]], own.shape[2])

    for at in range(count):
        outs[at][...] = dot(units[place[at]], weight[...]).astype(bf16)


def mixed_out(core, place, swap, own, other, weight):
    count, rows, units = own.shape
    width = weight.shape[1]
    block = block_of(width)
    whole = lambda k, *s: (0, 0, 0)
    return pl.pallas_call(
        functools.partial(mixed_out_kernel, swap),
        grid_spec=pltpu.PrefetchScalarGridSpec(
            num_scalar_prefetch=2,
            grid=(width // block,),
            in_specs=[
                pl.BlockSpec((count, rows, units), whole),
                pl.BlockSpec((count, rows, units), whole),
                pl.BlockSpec((2 * units, block), lambda k, *s: (0, k)),
            ],
            out_specs=[pl.BlockSpec((rows, block), lambda k, *s: (0, k))] * count
            + [pl.BlockSpec((count, rows, 2 * units), whole)],
        ),
        out_shape=[jax.ShapeDtypeStruct((rows, width), bf16)] * count
        + [jax.ShapeDtypeStruct((count, rows, 2 * units), bf16)],
        compiler_params=params(24),
        cost_estimate=cost(4 * count * rows * units * width, 2 * count * rows * (width + 4 * units)),
        name="mixed_out",
    )(core, place, own, other, weight)


def hidden_kernel(members, place, *refs):
    own, other, grad_own, grad_other = (refs[k * members : (k + 1) * members] for k in range(4))
    gate_up, taken, down, down_taken = refs[4 * members : 4 * members + 4]
    outs = refs[4 * members + 4 :]
    for at in range(members):
        gate = dot(own[at][...], gate_up[0]) + dot(other[at][...], taken[0])
        up = dot(own[at][...], gate_up[1]) + dot(other[at][...], taken[1])
        grad = dot(grad_own[at][...], down[...], NT) + dot(grad_other[at][...], down_taken[...], NT)
        sigmoid = jax.nn.sigmoid(gate)
        silu = gate * sigmoid
        slope = sigmoid * (1.0 + gate * (1.0 - sigmoid))
        outs[at][0] = (grad * up * slope).astype(bf16)
        outs[at][1] = (grad * silu).astype(bf16)
        outs[at][2] = (silu * up).astype(bf16)


def hidden_pieces(group, place, own, other, grad_own, grad_other, gate_up, taken, down, down_taken):
    members = len(own)
    rows, width = own[0].shape
    units = gate_up.shape[2]
    block = block_of(units)
    rows_in = pl.BlockSpec((rows, width), lambda k, s: (0, 0))
    grads = [
        pl.BlockSpec((rows, width), functools.partial(lambda at, k, s: (s[at], 0), at))
        for at in group
    ]
    entry = pl.BlockSpec((2, width, block), lambda k, s: (0, 0, k))
    leave = pl.BlockSpec((block, width), lambda k, s: (k, 0))
    return pl.pallas_call(
        functools.partial(hidden_kernel, members),
        grid_spec=pltpu.PrefetchScalarGridSpec(
            num_scalar_prefetch=1,
            grid=(units // block,),
            in_specs=[rows_in] * (2 * members) + grads + grads + [entry, entry, leave, leave],
            out_specs=[pl.BlockSpec((3, rows, block), lambda k, s: (0, 0, k))] * members,
        ),
        out_shape=[jax.ShapeDtypeStruct((3, rows, units), bf16)] * members,
        compiler_params=params(40),
        cost_estimate=cost(
            12 * members * rows * width * units, 12 * width * units + 8 * members * rows * width
        ),
        name="hidden_pieces",
    )(
        place, *own, *other, *([grad_own] * members), *([grad_other] * members),
        gate_up, taken, down, down_taken,
    )


def down_grad_kernel(count, second_steps, core, place, *refs):
    own, other, grads = refs[:count], refs[count : 2 * count], refs[2 * count]
    first, second, units = refs[-3:]
    rows = own[0].shape[1]
    lead = core[0] == 0

    def part(mine, out):
        for at in range(count):
            units[row_range(place[at], rows), :] = jnp.where(mine, own[at][0], other[at][0])
        out[...] = dot(units[...], grads[...], TN).astype(bf16)

    part(lead, first)

    @pl.when(pl.program_id(0) < second_steps)
    def _():
        part(jnp.logical_not(lead), second)


def down_grad_parts(core, place, own, other, grads, total):
    count = len(own)
    _, rows, half = own[0].shape
    width = grads.shape[1]
    block = 384
    rest = total - half
    second_steps = -(-rest // block)
    piece = pl.BlockSpec((1, rows, block), lambda k, *s: (2, 0, k))
    return pl.pallas_call(
        functools.partial(down_grad_kernel, count, second_steps),
        grid_spec=pltpu.PrefetchScalarGridSpec(
            num_scalar_prefetch=2,
            grid=(half // block,),
            in_specs=[piece] * (2 * count) + [pl.BlockSpec(grads.shape, lambda k, *s: (0, 0))],
            out_specs=[
                pl.BlockSpec((block, width), lambda k, *s: (k, 0)),
                pl.BlockSpec((block, width), lambda k, *s: (jnp.minimum(k, second_steps - 1), 0)),
            ],
            scratch_shapes=[pltpu.VMEM((count * rows, block), bf16)],
        ),
        out_shape=[
            jax.ShapeDtypeStruct((half, width), bf16),
            jax.ShapeDtypeStruct((rest, width), bf16),
        ],
        compiler_params=params(40),
        cost_estimate=cost(
            2 * count * rows * total * width, 2 * count * rows * (width + 2 * half) + 2 * total * width
        ),
        name="down_grad_parts",
    )(core, place, *own, *other, grads)


def normed_back_kernel(count, core, place, *refs):
    own, other, gate_up = refs[:count], refs[count : 2 * count], refs[2 * count]
    out, gate, up = refs[-3:]
    rows = own[0].shape[1]

    @pl.when(pl.program_id(0) == 0)
    def _():
        for at in range(count):
            span = pl.ds(at * rows, rows)
            for kind, units in ((0, gate), (1, up)):
                ordered(
                    core, own[at].at[kind], other[at].at[kind], units.at[span], own[0].shape[2]
                )

    for at in range(count):
        span = pl.ds(at * rows, rows)
        out[row_range(place[at], rows), :] = (
            dot(gate[span, :], gate_up[0], NT) + dot(up[span, :], gate_up[1], NT)
        ).astype(bf16)


def normed_back(core, place, own, other, gate_up):
    count = len(own)
    _, rows, half = own[0].shape
    _, width, total = gate_up.shape
    block = block_of(width)
    once = pl.Buffered(1)
    units = pl.BlockSpec((count * rows, total), lambda k, *s: (0, 0), pipeline_mode=once)
    units_shape = jax.ShapeDtypeStruct((count * rows, total), bf16)
    return pl.pallas_call(
        functools.partial(normed_back_kernel, count),
        grid_spec=pltpu.PrefetchScalarGridSpec(
            num_scalar_prefetch=2,
            grid=(width // block,),
            in_specs=[pl.BlockSpec((2, rows, half), lambda k, *s: (0, 0, 0), pipeline_mode=once)]
            * (2 * count)
            + [pl.BlockSpec((2, block, total), lambda k, *s: (0, k, 0))],
            out_specs=[
                pl.BlockSpec((count * rows, block), lambda k, *s: (0, k)),
                units,
                units,
            ],
        ),
        out_shape=[
            jax.ShapeDtypeStruct((count * rows, width), bf16),
            units_shape,
            units_shape,
        ],
        compiler_params=params(48),
        cost_estimate=cost(
            4 * count * rows * width * total, 4 * width * total + 8 * count * rows * total
        ),
        name="normed_back",
    )(core, place, *own, *other, gate_up)


def down_out_kernel(count, core, place, *refs):
    own, other, down = refs[:count], refs[count : 2 * count], refs[2 * count]
    out, units = refs[-2:]
    rows = own[0].shape[1]

    @pl.when(pl.program_id(0) == 0)
    def _():
        for at in range(count):
            ordered(core, own[at].at[0], other[at].at[0], units.at[at], own[at].shape[2])

    for at in range(count):
        out[row_range(place[at], rows), :] = dot(units[at], down[...]).astype(bf16)


def down_out(core, place, own, other, down):
    count = len(own)
    _, rows, half = own[0].shape
    total, width = down.shape
    block = block_of(width)
    piece = pl.BlockSpec((1, rows, half), lambda k, *s: (2, 0, 0))
    return pl.pallas_call(
        functools.partial(down_out_kernel, count),
        grid_spec=pltpu.PrefetchScalarGridSpec(
            num_scalar_prefetch=2,
            grid=(width // block,),
            in_specs=[piece] * (2 * count) + [pl.BlockSpec((total, block), lambda k, *s: (0, k))],
            out_specs=pl.BlockSpec((count * rows, block), lambda k, *s: (0, k)),
            scratch_shapes=[pltpu.VMEM((count, rows, total), bf16)],
        ),
        out_shape=jax.ShapeDtypeStruct((count * rows, width), bf16),
        compiler_params=params(48),
        cost_estimate=cost(
            2 * count * rows * total * width, 2 * total * width + 4 * count * rows * total
        ),
        name="down_out",
    )(core, place, *own, *other, down)


def weight_grad_kernel(pieces, parts, *refs):
    rows_in, units, outs, rows = refs[:pieces], refs[pieces], refs[pieces + 1 : -1], refs[-1]
    if pieces == 1:
        left = rows_in[0][...]
    else:
        size = rows_in[0].shape[0]
        for at in range(pieces):
            rows[pl.ds(at * size, size), :] = rows_in[at][...]
        left = rows[...]
    result = dot(left, units[...].reshape(units.shape[-2:]), TN).astype(bf16)
    if parts == 1:
        outs[0][...] = result
    else:
        steps = pl.num_programs(0) // parts
        for at in range(parts):

            @pl.when(pl.program_id(0) // steps == at)
            def _():
                outs[at][...] = result


def weight_grad(rows, units, kind=None, parts=1):
    pieces = len(rows)
    size, width = rows[0].shape
    total, columns = units.shape[-2:]
    block = 256 if width // parts % 256 == 0 else LANES
    steps = width // block // parts
    if kind is None:
        units_spec = pl.BlockSpec((total, columns), lambda k: (0, 0))
    else:
        units_spec = pl.BlockSpec((1, total, columns), lambda k: (kind, 0, 0))
    outs = [
        pl.BlockSpec(
            (block, columns),
            functools.partial(lambda at, k: (jnp.clip(k - at * steps, 0, steps - 1), 0), at),
        )
        for at in range(parts)
    ]
    return pl.pallas_call(
        functools.partial(weight_grad_kernel, pieces, parts),
        grid=(steps * parts,),
        in_specs=[pl.BlockSpec((size, block), lambda k: (0, k))] * pieces + [units_spec],
        out_specs=outs,
        out_shape=[jax.ShapeDtypeStruct((width // parts, columns), bf16)] * parts,
        scratch_shapes=[pltpu.VMEM((total, block), bf16)],
        compiler_params=params(32),
        cost_estimate=cost(
            2 * total * width * columns, 2 * (total * (width + columns) + width * columns)
        ),
        name="weight_grad",
    )(*rows, units)


def mixed_grad_kernel(place, own, other, keep, taken, out):
    out[0] = (dot(own[...], keep[...], NT) + dot(other[...], taken[...], NT)).astype(bf16)


def mixed_back(place, count, own, other, keep, taken):
    rows = own.shape[0] // count
    units, width = keep.shape
    piece = pl.BlockSpec((rows, width), lambda at, s: (s[at], 0))
    weight = pl.BlockSpec((units, width), lambda at, s: (0, 0))
    return pl.pallas_call(
        mixed_grad_kernel,
        grid_spec=pltpu.PrefetchScalarGridSpec(
            num_scalar_prefetch=1,
            grid=(count,),
            in_specs=[piece, piece, weight, weight],
            out_specs=pl.BlockSpec((1, rows, units), lambda at, s: (at, 0, 0)),
        ),
        out_shape=jax.ShapeDtypeStruct((count, rows, units), bf16),
        compiler_params=params(24),
        cost_estimate=cost(4 * count * rows * width * units, 4 * count * rows * width),
        name="mixed_back",
    )(place, own, other, keep, taken)


def project_back_kernel(swap, core, place, own, other, weight, out, units):
    count, rows = own.shape[1:3]

    @pl.when(pl.program_id(0) == 0)
    def _():
        for kind in range(3):
            for at in range(count):
                ordered(
                    core,
                    own.at[kind, at],
                    other.at[kind, swap[at]],
                    units.at[kind, at],
                    own.shape[3],
                )

    for at in range(count):
        out[row_range(place[at], rows), :] = sum(
            dot(units[kind, at], weight[kind], NT) for kind in range(3)
        ).astype(bf16)


def project_back(core, place, swap, own, other, weight):
    _, count, rows, half = own.shape
    _, width, total = weight.shape
    block = block_of(width)
    whole = lambda k, *s: (0, 0, 0, 0)
    return pl.pallas_call(
        functools.partial(project_back_kernel, swap),
        grid_spec=pltpu.PrefetchScalarGridSpec(
            num_scalar_prefetch=2,
            grid=(width // block,),
            in_specs=[
                pl.BlockSpec((3, count, rows, half), whole),
                pl.BlockSpec((3, count, rows, half), whole),
                pl.BlockSpec((3, block, total), lambda k, *s: (0, k, 0)),
            ],
            out_specs=[
                pl.BlockSpec((count * rows, block), lambda k, *s: (0, k)),
                pl.BlockSpec((3, count, rows, total), whole),
            ],
        ),
        out_shape=[
            jax.ShapeDtypeStruct((count * rows, width), bf16),
            jax.ShapeDtypeStruct((3, count, rows, total), bf16),
        ],
        compiler_params=params(40),
        cost_estimate=cost(6 * count * rows * total * width, 2 * count * rows * (width + 6 * total)),
        name="project_back",
    )(core, place, own, other, weight)


def halves(weight, axis, width):
    lead = lax.slice_in_dim(weight, 0, width, axis=axis)
    rest = lax.slice_in_dim(weight, width, weight.shape[axis], axis=axis)
    pad = [(0, 0)] * weight.ndim
    pad[axis] = (0, width - rest.shape[axis])
    rest = jnp.pad(rest, pad)
    first = lax.axis_index("col") == 0
    return jnp.where(first, lead, rest), jnp.where(first, rest, lead)


def shards(
    block_input,
    norm1_gain,
    norm1_shift,
    qkv_weight,
    qkv_bias,
    out_weight,
    norm2_gain,
    norm2_shift,
    gate_up_weight,
    down_weight,
    output_grad,
):
    count = lax.axis_size("row")
    rows = block_input.shape[0]
    core = lax.axis_index("col").astype(jnp.int32)[None]
    place, swap = places()
    place = place.astype(jnp.int32)
    slot = inverse_places(place)
    cosine, sine = rotary_tables(place, rows)
    half_units = out_weight.shape[0] // 2
    total_hidden = down_weight.shape[0]
    half_hidden = -(-total_hidden // (2 * LANES)) * LANES
    if grid_rows():
        groups = (((2,), 2), ((0, 1), 0), ((3,), 3))
    else:
        groups = tuple(((at,), at) for at in range(count))

    inputs = block_input.astype(f32)
    gain_one = norm1_gain.astype(f32)
    gain_two = norm2_gain.astype(f32)
    hat_one, inverse_one = normalize(inputs)
    normed_one = (hat_one * gain_one + norm1_shift.astype(f32)).astype(bf16)

    one_own, fetch = gather_rows(normed_one)
    qkv_keep, qkv_send = halves(after(qkv_weight, normed_one), 2, half_units)
    qkv_taken = sibling(qkv_send)
    qkv = None
    for group, index in groups:
        ready = one_own if qkv is None else [after(piece, qkv) for piece in one_own]
        qkv = project_pieces(
            index, group, count,
            [ready[at] for at in group],
            [sibling(ready[swap[at]]) for at in group],
            qkv_keep, qkv_taken, qkv_bias[:, None, :], cosine, sine, qkv,
        )
        if group == groups[0][0]:
            gate_up_keep, gate_up_send = halves(after(gate_up_weight, qkv), 2, half_hidden)
            down_keep, down_send = halves(after(down_weight, qkv), 0, half_hidden)
            out_keep, out_send = halves(after(out_weight, qkv), 0, half_units)
            one_own += fetch(qkv)
            one_own = [after(piece, gate_up_keep, down_keep, out_keep) for piece in one_own]
    near = one_own[-1]
    gate_up_taken = sibling(after(gate_up_send, near))
    down_taken = sibling(after(down_send, near))
    grad_own = gather_whole(after(output_grad, near))
    mixed, kept, logsum = attend_forward(slot, qkv)
    mixed = after(mixed, gate_up_taken, down_taken)
    *branch, mixed_units = mixed_out(core, place, swap, mixed, sibling(mixed), out_weight)
    after_rows = inputs + scatter_rows(branch)
    hat_two, inverse_two = normalize(after_rows)
    grad_other = sibling(after(grad_own, inverse_two))
    normed_two = (hat_two * gain_two + norm2_shift.astype(f32)).astype(bf16)

    two_own, fetch = gather_rows(normed_two)
    mine, theirs = [None] * count, [None] * count
    last = None
    for group, _ in groups:
        ready = two_own if last is None else [after(piece, last) for piece in two_own]
        results = hidden_pieces(
            group, place,
            [ready[at] for at in group],
            [sibling(ready[swap[at]]) for at in group],
            grad_own, grad_other, gate_up_keep, gate_up_taken, down_keep, down_taken,
        )
        for at, result in zip(group, results):
            mine[at] = result
        for at in group:
            theirs[at] = sibling(mine[swap[at]])
        if last is None:
            two_own += fetch(results[0])
        last = results[0]

    sums = Line()
    sums.add(*down_grad_parts(core, place, mine, theirs, grad_own, total_hidden))
    normed_part, gate_units, up_units = normed_back(
        after(core, sums.parts[1]), place, mine, theirs, gate_up_weight
    )
    normed_two_grad = scatter_whole(normed_part)
    sums.add(*weight_grad(two_own, after(gate_units, normed_part), parts=2))
    token = sums.tick(sums.parts[3])
    sums.add(*weight_grad(two_own, after(up_units, token), parts=2))
    down_part = down_out(after(core, sums.parts[5]), place, mine, theirs, down_weight)
    after_grad = output_grad.astype(f32) + norm_back(
        normed_two_grad * gain_two, hat_two, inverse_two
    )
    branch_grad = after_grad.astype(bf16)
    token = sums.tick(down_part)
    branch_own = gather_whole(branch_grad)
    token = sums.tick(branch_grad, token)
    token = sums.tick(token)
    down = scatter_whole(after(down_part, branch_own))
    branch_other = sibling(after(branch_own, token))
    mixed_grad = mixed_back(place, count, branch_own, branch_other, out_keep, sibling(out_send))
    project_grad = attend_backward(slot, qkv, mixed_grad, kept, logsum, cosine, sine)
    sums.add(
        *weight_grad([mixed_units.reshape(count * rows, -1)], after(branch_own, project_grad))
    )
    token = sums.tick(sums.parts[-1])
    one_part, project_units = project_back(
        after(core, token), place, swap, project_grad, sibling(project_grad), qkv_weight
    )
    normed_one_grad = scatter_whole(one_part)
    project_units = project_units.reshape(3, count * rows, -1)
    for kind in range(3):
        sums.add(*weight_grad(one_own, after(project_units, one_part), kind))
    token = sums.tick(sums.parts[-1])
    bias_grad = jnp.sum(project_grad.astype(f32), axis=(1, 2))
    block_output = (after_rows + down).astype(bf16)
    token = sums.tick(token)
    input_grad = after_grad + norm_back(normed_one_grad * gain_one, hat_one, inverse_one)
    gains = jnp.stack(
        [
            jnp.sum(normed_one_grad * hat_one, axis=0),
            jnp.sum(normed_one_grad, axis=0),
            jnp.sum(normed_two_grad * hat_two, axis=0),
            jnp.sum(normed_two_grad, axis=0),
        ]
    )
    width = gains.shape[1]
    gains = sum_rows(gains)
    sums.add(jnp.concatenate([gains.reshape(-1, LANES), bias_grad.reshape(-1, LANES)], axis=0))
    sums.finish()
    small = sums.value(10)
    gains = small[: 4 * width // LANES].reshape(4, width)
    bias_grad = small[4 * width // LANES :].reshape(bias_grad.shape)

    down_grad = jnp.concatenate([sums.value(0), sums.value(1)], axis=0)
    gate_up_grad = jnp.stack(
        [
            jnp.concatenate([sums.value(2), sums.value(3)], axis=0),
            jnp.concatenate([sums.value(4), sums.value(5)], axis=0),
        ]
    )
    qkv_grad = jnp.stack([sums.value(at) for at in (7, 8, 9)])
    return (
        block_output,
        input_grad,
        gains[0],
        gains[1],
        qkv_grad,
        bias_grad,
        sums.value(6),
        gains[2],
        gains[3],
        gate_up_grad,
        down_grad,
    )


def inverse_places(place):
    spots = jnp.arange(place.shape[0])
    return jnp.sum(
        jnp.where(place[None, :] == spots[:, None], spots[None, :], 0), axis=1
    ).astype(jnp.int32)


def solution(mesh):
    placed = (
        P(("dp", "row"), "col"),
        P("col"),
        P("col"),
        P(None, "col", "row"),
        P(None, ("row", "col")),
        P("row", "col"),
        P("col"),
        P("col"),
        P(None, "col", "row"),
        P("row", "col"),
        P(("dp", "row"), "col"),
    )
    return jax.shard_map(
        shards,
        mesh=mesh,
        in_specs=placed,
        out_specs=(
            P(("dp", "row"), "col"),
            P(("dp", "row"), "col"),
            P("col"),
            P("col"),
            P(None, "col", "row"),
            P(None, ("row", "col")),
            P("row", "col"),
            P("col"),
            P("col"),
            P(None, "col", "row"),
            P("row", "col"),
        ),
        check_vma=False,
    )
```

```python
import functools

import jax
import jax.numpy as jnp
import numpy as np
from jax import lax
from jax.experimental import pallas as pl
from jax.experimental.pallas import tpu as pltpu
from jax.sharding import PartitionSpec as P

HD = 64
ROT = 16
LANES = 128
MIB = 1 << 20
DOWN_BLOCK = 384

epsilon = 1e-05
base_rate = 10000.0
bf16 = jnp.bfloat16
f32 = jnp.float32

NN = (((1,), (0,)), ((), ()))
NT = (((1,), (1,)), ((), ()))
TN = (((0,), (0,)), ((), ()))


def dot(first, second, dims=NN):
    return lax.dot_general(first, second, dims, preferred_element_type=f32)


def row_permute(values, core_zero, core_one):
    pairs = [
        (row * 2 + core, (row ^ (core_one if core else core_zero)) * 2 + core)
        for row in range(4)
        for core in range(2)
    ]
    return lax.ppermute(values, ("row", "col"), pairs)


def first_way(values):
    return row_permute(values, 1, 2)


def second_way(values):
    return row_permute(values, 2, 1)


def sibling(values):
    return lax.ppermute(values, "col", [(0, 1), (1, 0)])


def grid_rows():
    return lax.axis_size("row") == 4


def places():
    row, core = lax.axis_index("row"), lax.axis_index("col")
    if grid_rows():
        one = jnp.where(core == 0, 1, 2)
        return jnp.stack([row ^ one, row ^ (3 - one), row, row ^ 3]), (1, 0, 2, 3)
    count = lax.axis_size("row")
    return jnp.arange(count), tuple(range(count))


def after(value, *earlier):
    return lax.optimization_barrier((value,) + earlier)[0]


def gather_rows(own):
    if grid_rows():
        near = first_way(own)
        side = second_way(own)
        return [near, side, own], lambda *earlier: [second_way(after(near, side, *earlier))]
    whole = lax.all_gather(own, "row", axis=0, tiled=True)
    return jnp.split(whole, lax.axis_size("row"), axis=0), lambda *earlier: []


def scatter_rows(parts, clock):
    if grid_rows():
        passing = first_way(parts[3])
        near = first_way(parts[0])
        side = second_way(clock.mark(plus(parts[1], clock(passing))))
        return parts[2].astype(f32) + near.astype(f32) + side.astype(f32)
    whole = jnp.concatenate(parts, axis=0)
    return lax.psum_scatter(whole, "row", scatter_dimension=0, tiled=True).astype(f32)


def line():
    return lax.axis_size("dp") == 4


def in_middle():
    place = lax.axis_index("dp")
    return (place == 1) | (place == 2)


def inward(part):
    return lax.ppermute(part, "dp", [(0, 1), (3, 2)])


def across(part):
    return lax.ppermute(part, "dp", [(1, 2), (2, 1)])


def outward(part):
    return lax.ppermute(part, "dp", [(1, 0), (2, 3)])


def plus(first, second):
    return (first.astype(f32) + second.astype(f32)).astype(first.dtype)


class Clock:
    def __init__(self):
        self.last = None

    def __call__(self, value):
        return value if self.last is None else after(value, self.last)

    def mark(self, value):
        self.last = value
        return value


class Line:
    def __init__(self, clock):
        self.clock = clock
        self.parts, self.inner, self.half, self.other, self.total, self.outer = ([] for _ in range(6))
        self.settled = 0

    def feed(self):
        at = len(self.inner)
        if at < len(self.parts) and at < len(self.half) + 2:
            part = self.parts[at]
            self.inner.append(inward(after(part, self.inner[at - 2]) if at >= 2 else part))

    def add(self, *parts):
        self.parts += parts
        if line():
            for _ in parts:
                self.feed()

    def join(self):
        if line():
            at = len(self.half)
            self.half.append(self.clock.mark(plus(self.parts[at], self.clock(self.inner[at]))))
            self.feed()
            ready = self.half[at]
            self.other.append(across(after(ready, self.other[-1]) if self.other else ready))

    def total_up(self):
        if line():
            at = len(self.total)
            self.total.append(self.clock.mark(plus(self.half[at], self.clock(self.other[at]))))
            ready = self.total[at]
            self.outer.append(outward(after(ready, self.outer[-1]) if self.outer else ready))

    def settle(self, shape, places, block, before=None):
        for index, start in places:
            at = self.settled
            self.settled += 1
            if line():
                before = self.clock.mark(
                    settle(shape, index, start, block, self.clock, self.total[at], self.outer[at], before)
                )
            else:
                value = lax.psum(self.parts[at], "dp").astype(f32)[None]
                before = jnp.zeros(shape, f32) if before is None else before
                before = lax.dynamic_update_slice(before, value, (index, start, 0))
        return before

    def small(self, at):
        if line():
            return jnp.where(in_middle(), self.total[at], self.outer[at])
        return lax.psum(self.parts[at], "dp")


def gather_whole(own):
    return lax.all_gather(own, "row", axis=0, tiled=True)


def scatter_whole(parts):
    return lax.psum_scatter(parts, "row", scatter_dimension=0, tiled=True).astype(f32)


def sum_rows(values):
    if grid_rows():
        values = values + first_way(values)
        return values + second_way(values)
    return lax.psum(values, "row")


def width_pair(first, second):
    both = jnp.stack([first, second])
    both = both + sibling(both)
    return both[0], both[1]


def normalize(values):
    width = values.shape[1] * lax.axis_size("col")
    totals, squares = width_pair(jnp.sum(values, axis=-1), jnp.sum(values * values, axis=-1))
    average = totals / width
    spread = squares / width - average * average
    inverse = lax.rsqrt(spread + epsilon)[:, None]
    return ((values - average[:, None]) * inverse, inverse)


def norm_back(scaled, normed_hat, inverse):
    width = normed_hat.shape[1] * lax.axis_size("col")
    first, second = width_pair(jnp.sum(scaled, axis=-1), jnp.sum(scaled * normed_hat, axis=-1))
    return inverse * (scaled - first[:, None] / width - normed_hat * second[:, None] / width)


def rotary_tables(count, rows):
    half_dims = ROT // 2
    lane = np.arange(LANES) % HD
    freqs = np.float32(base_rate) ** (-(2.0 * (lane % half_dims).astype(np.float32)) / np.float32(ROT))
    angles = np.arange(count * rows, dtype=np.float32)[:, None] * freqs.astype(np.float32)[None, :]
    turned = lane < ROT
    sign = np.where(lane < half_dims, -1.0, 1.0)
    cosine = np.where(turned, np.cos(angles.astype(np.float64)), 1.0)
    sine = np.where(turned, sign * np.sin(angles.astype(np.float64)), 0.0)
    shape = (count, rows, LANES)
    return jnp.asarray(cosine.reshape(shape), f32), jnp.asarray(sine.reshape(shape), f32)


def turn(values, cosine, sine):
    half_dims = ROT // 2
    lane = lax.broadcasted_iota(jnp.int32, values.shape, 1) % HD
    partner = jnp.where(
        lane < half_dims,
        pltpu.roll(values, LANES - half_dims, 1),
        pltpu.roll(values, half_dims, 1),
    )
    return values * cosine + partner * sine


def params(mib, *order):
    return pltpu.CompilerParams(vmem_limit_bytes=mib * MIB)


def cost(flops, moved, hard=0):
    return pl.CostEstimate(flops=int(flops), bytes_accessed=int(moved), transcendentals=int(hard))


def project_kernel(members, place, *refs):
    own, other = refs[:members], refs[members : 2 * members]
    keep, taken, bias = refs[2 * members : 2 * members + 3]
    cosine, sine = refs[2 * members + 3 : 3 * members + 3], refs[3 * members + 3 : 4 * members + 3]
    out = refs[-1]
    kind = pl.program_id(0)
    for at in range(members):
        result = dot(own[at][...], keep[0]) + dot(other[at][...], taken[0]) + bias[0].astype(f32)

        @pl.when(kind < 2)
        def _():
            for start in range(0, result.shape[1], LANES):
                part = slice(start, start + LANES)
                out[at, 0, :, part] = turn(result[:, part], cosine[at][0], sine[at][0]).astype(bf16)

        @pl.when(kind == 2)
        def _():
            out[at, 0] = result.astype(bf16)


def project_pieces(index, group, count, place, own, other, keep, taken, bias, cosine, sine, before):
    members = len(own)
    rows, width = own[0].shape
    units = keep.shape[2]
    piece = pl.BlockSpec((rows, width), lambda k, s: (0, 0))
    tables = [
        pl.BlockSpec((1, rows, LANES), functools.partial(lambda at, k, s: (s[at], 0, 0), at))
        for at in group
    ]
    weight = pl.BlockSpec((1, width, units), lambda k, s: (k, 0, 0))
    in_specs = [piece] * (2 * members) + [
        weight,
        weight,
        pl.BlockSpec((1, 1, units), lambda k, s: (k, 0, 0)),
        *tables,
        *tables,
    ]
    args = [*own, *other, keep, taken, bias] + [cosine] * members + [sine] * members
    aliases = {}
    if before is not None:
        aliases = {len(args) + 1: 0}
        in_specs.append(pl.BlockSpec(memory_space=pl.ANY))
        args.append(before)
    return pl.pallas_call(
        functools.partial(project_kernel, members),
        grid_spec=pltpu.PrefetchScalarGridSpec(
            num_scalar_prefetch=1,
            grid=(3,),
            in_specs=in_specs,
            out_specs=pl.BlockSpec((members, 1, rows, units), lambda k, s: (index, k, 0, 0)),
        ),
        out_shape=jax.ShapeDtypeStruct((count, 3, rows, units), bf16),
        input_output_aliases=aliases,
        compiler_params=params(32),
        cost_estimate=cost(
            12 * members * rows * width * units, 4 * members * rows * width + 12 * width * units
        ),
        name="project_pieces",
    )(place, *args)


def causal(rows):
    keys = lax.broadcasted_iota(jnp.int32, (rows, rows), 0)
    return keys <= lax.broadcasted_iota(jnp.int32, (rows, rows), 1)


def head_lanes(values, head):
    lane = lax.broadcasted_iota(jnp.int32, values.shape, 1)
    return jnp.where((lane >= head * HD) & (lane < (head + 1) * HD), values, jnp.zeros_like(values))


def walk(stop, body, carry):
    if isinstance(stop, int):
        for step in range(stop):
            carry = body(step, carry)
        return carry
    return lax.fori_loop(0, stop, body, carry)


def each(count, body):
    if count <= 4:
        for step in range(count):
            body(step)
    else:
        lax.fori_loop(0, count, lambda step, carry: (body(step), carry)[1], 0)


def row_range(step, rows):
    return pl.ds(step * rows if isinstance(step, int) else pl.multiple_of(step * rows, rows), rows)


def attend_kernel(slot, qkv, mixed, kept, logsum, scores):
    count, _, rows, _ = qkv.shape
    heads = LANES // HD
    scale = HD**-0.5

    def one(at):
        here = slot[at]
        query = qkv[here, 0] * jnp.asarray(scale, bf16)
        for head in range(heads):

            def look(past, highest):
                block = dot(head_lanes(qkv[slot[past], 1], head), query, NT)
                scores[row_range(past, rows), :] = block
                return jnp.maximum(highest, jnp.max(block, axis=0, keepdims=True))

            def add(past, carry):
                total, outs = carry
                weights = jnp.exp(scores[row_range(past, rows), :] - highest)
                total = total + jnp.sum(weights, axis=0, keepdims=True)
                value = jnp.transpose(qkv[slot[past], 2])[head * HD : (head + 1) * HD]
                return total, outs + dot(value, weights.astype(bf16))

            block = dot(head_lanes(qkv[here, 1], head), query, NT)
            block = jnp.where(causal(rows), block, -1e30)
            scores[row_range(at, rows), :] = block
            highest = walk(at, look, jnp.max(block, axis=0, keepdims=True))
            total, outs = walk(
                at + 1, add, (jnp.zeros((1, rows), f32), jnp.zeros((HD, rows), f32))
            )
            kept[0, here, pl.ds(head * HD, HD), :] = outs / total
            logsum[0, here, pl.ds(head, 1), :] = highest + jnp.log(total)
        mixed[here] = jnp.transpose(kept[0, here]).astype(bf16)

    each(count, one)


def attend_forward(slot, qkv):
    count, _, rows, units = qkv.shape
    pairs = units // LANES
    work = rows * rows * count * (count + 1) // 2 * units
    return pl.pallas_call(
        attend_kernel,
        grid_spec=pltpu.PrefetchScalarGridSpec(
            num_scalar_prefetch=1,
            grid=(pairs,),
            in_specs=[pl.BlockSpec((count, 3, rows, LANES), lambda p, s: (0, 0, 0, p))],
            out_specs=[
                pl.BlockSpec((count, rows, LANES), lambda p, s: (0, 0, p)),
                pl.BlockSpec((1, count, LANES, rows), lambda p, s: (p, 0, 0, 0)),
                pl.BlockSpec((1, count, 8, rows), lambda p, s: (p, 0, 0, 0)),
            ],
            scratch_shapes=[pltpu.VMEM((count * rows, rows), f32)],
        ),
        out_shape=[
            jax.ShapeDtypeStruct((count, rows, units), bf16),
            jax.ShapeDtypeStruct((pairs, count, LANES, rows), f32),
            jax.ShapeDtypeStruct((pairs, count, 8, rows), f32),
        ],
        compiler_params=params(40),
        cost_estimate=cost(16 * work, 16 * count * rows * units, work // HD),
        name="attend_forward",
    )(slot, qkv)


def attend_back_kernel(slot, place, qkv, grads, kept, logsum, cosine, sine, out, dq, dk, dv, inner):
    count, _, rows, _ = qkv.shape
    heads = LANES // HD
    scale = HD**-0.5
    dk[...] = jnp.zeros_like(dk)
    dv[...] = jnp.zeros_like(dv)

    def sums(at):
        product = jnp.transpose(grads[at].astype(f32)) * kept[0, at]
        for head in range(heads):
            part = product[head * HD : (head + 1) * HD]
            inner[at, pl.ds(head, 1), :] = jnp.sum(part, axis=0, keepdims=True)

    def one(at):
        here = slot[at]
        query = qkv[here, 0] * jnp.asarray(scale, bf16)
        grad = grads[here]
        for head in range(heads):
            query_head = head_lanes(query, head)
            grad_head = head_lanes(grad, head)

            def look(past, query_grad, last=False):
                there = slot[past]
                key = qkv[there, 1]
                block = dot(key, query_head, NT)
                weights = jnp.exp(block - logsum[0, here, pl.ds(head, 1), :])
                if last:
                    weights = jnp.where(causal(rows), weights, 0.0)
                moved = dot(qkv[there, 2], grad_head, NT)
                raw = (weights * (moved - inner[here, pl.ds(head, 1), :])).astype(bf16)
                dv[there] += dot(weights.astype(bf16), grad_head)
                dk[there] += dot(raw, query_head)
                turned = jnp.transpose(key)[head * HD : (head + 1) * HD]
                return query_grad + dot(turned, raw)

            query_grad = walk(at, look, jnp.zeros((HD, rows), f32))
            dq[pl.ds(head * HD, HD), :] = look(at, query_grad, True) * scale
        out[0, here] = turn(jnp.transpose(dq[...]), cosine[at], -sine[at]).astype(bf16)

    def finish(at):
        out[1, at] = turn(dk[at], cosine[place[at]], -sine[place[at]]).astype(bf16)
        out[2, at] = dv[at].astype(bf16)

    each(count, sums)
    each(count, one)
    each(count, finish)


def attend_backward(slot, place, qkv, grads, kept, logsum, cosine, sine):
    count, _, rows, units = qkv.shape
    pairs = units // LANES
    work = rows * rows * count * (count + 1) // 2 * units
    table = pl.BlockSpec((count, rows, LANES), lambda p, *s: (0, 0, 0))
    return pl.pallas_call(
        attend_back_kernel,
        grid_spec=pltpu.PrefetchScalarGridSpec(
            num_scalar_prefetch=2,
            grid=(pairs,),
            in_specs=[
                pl.BlockSpec((count, 3, rows, LANES), lambda p, *s: (0, 0, 0, p)),
                pl.BlockSpec((count, rows, LANES), lambda p, *s: (0, 0, p)),
                pl.BlockSpec((1, count, LANES, rows), lambda p, *s: (p, 0, 0, 0)),
                pl.BlockSpec((1, count, 8, rows), lambda p, *s: (p, 0, 0, 0)),
                table,
                table,
            ],
            out_specs=pl.BlockSpec((3, count, rows, LANES), lambda p, *s: (0, 0, 0, p)),
            scratch_shapes=[
                pltpu.VMEM((LANES, rows), f32),
                pltpu.VMEM((count, rows, LANES), f32),
                pltpu.VMEM((count, rows, LANES), f32),
                pltpu.VMEM((count, 8, rows), f32),
            ],
        ),
        out_shape=jax.ShapeDtypeStruct((3, count, rows, units), bf16),
        compiler_params=params(48),
        cost_estimate=cost(40 * work, 24 * count * rows * units, work // HD),
        name="attend_backward",
    )(slot, place, qkv, grads, kept, logsum, cosine, sine)


def ordered(core, own, other, out, width):
    rest = out.shape[-1] - width
    lead = core[0] == 0
    out[..., :width] = jnp.where(lead, own[...], other[...])
    out[..., width:] = jnp.where(lead, other[..., :rest], own[..., :rest])


def block_of(width):
    return 256 if width % 256 == 0 else LANES


def mixed_out_kernel(swap, core, place, own, other, weight, *outs):
    units = outs[-1]
    count = own.shape[0]

    @pl.when(pl.program_id(0) == 0)
    def _():
        for at in range(count):
            ordered(core, own.at[at], other.at[swap[at]], units.at[place[at]], own.shape[2])

    for at in range(count):
        outs[at][...] = dot(units[place[at]], weight[...]).astype(bf16)


def mixed_out(core, place, swap, own, other, weight):
    count, rows, units = own.shape
    width = weight.shape[1]
    block = block_of(width)
    whole = lambda k, *s: (0, 0, 0)
    return pl.pallas_call(
        functools.partial(mixed_out_kernel, swap),
        grid_spec=pltpu.PrefetchScalarGridSpec(
            num_scalar_prefetch=2,
            grid=(width // block,),
            in_specs=[
                pl.BlockSpec((count, rows, units), whole),
                pl.BlockSpec((count, rows, units), whole),
                pl.BlockSpec((2 * units, block), lambda k, *s: (0, k)),
            ],
            out_specs=[pl.BlockSpec((rows, block), lambda k, *s: (0, k))] * count
            + [pl.BlockSpec((count, rows, 2 * units), whole)],
        ),
        out_shape=[jax.ShapeDtypeStruct((rows, width), bf16)] * count
        + [jax.ShapeDtypeStruct((count, rows, 2 * units), bf16)],
        compiler_params=params(24),
        cost_estimate=cost(4 * count * rows * units * width, 2 * count * rows * (width + 4 * units)),
        name="mixed_out",
    )(core, place, own, other, weight)


def hidden_kernel(members, place, *refs):
    own, other, grad_own, grad_other = (refs[k * members : (k + 1) * members] for k in range(4))
    gate_up, taken, down, down_taken = refs[4 * members : 4 * members + 4]
    outs = refs[4 * members + 4 :]
    for at in range(members):
        gate = dot(own[at][...], gate_up[0]) + dot(other[at][...], taken[0])
        up = dot(own[at][...], gate_up[1]) + dot(other[at][...], taken[1])
        grad = dot(grad_own[at][...], down[...], NT) + dot(grad_other[at][...], down_taken[...], NT)
        sigmoid = jax.nn.sigmoid(gate)
        silu = gate * sigmoid
        slope = sigmoid * (1.0 + gate * (1.0 - sigmoid))
        outs[at][0] = (grad * up * slope).astype(bf16)
        outs[at][1] = (grad * silu).astype(bf16)
        outs[at][2] = (silu * up).astype(bf16)


def hidden_pieces(group, place, own, other, grad_own, grad_other, gate_up, taken, down, down_taken):
    members = len(own)
    rows, width = own[0].shape
    units = gate_up.shape[2]
    block = block_of(units)
    rows_in = pl.BlockSpec((rows, width), lambda k, s: (0, 0))
    grads = [
        pl.BlockSpec((rows, width), functools.partial(lambda at, k, s: (s[at], 0), at))
        for at in group
    ]
    entry = pl.BlockSpec((2, width, block), lambda k, s: (0, 0, k))
    leave = pl.BlockSpec((block, width), lambda k, s: (k, 0))
    return pl.pallas_call(
        functools.partial(hidden_kernel, members),
        grid_spec=pltpu.PrefetchScalarGridSpec(
            num_scalar_prefetch=1,
            grid=(units // block,),
            in_specs=[rows_in] * (2 * members) + grads + grads + [entry, entry, leave, leave],
            out_specs=[pl.BlockSpec((3, rows, block), lambda k, s: (0, 0, k))] * members,
        ),
        out_shape=[jax.ShapeDtypeStruct((3, rows, units), bf16)] * members,
        compiler_params=params(40),
        cost_estimate=cost(
            12 * members * rows * width * units, 12 * width * units + 8 * members * rows * width
        ),
        name="hidden_pieces",
    )(
        place, *own, *other, *([grad_own] * members), *([grad_other] * members),
        gate_up, taken, down, down_taken,
    )


def down_grad_kernel(count, steps, second_steps, core, place, *refs):
    own, other, grads = refs[:count], refs[count : 2 * count], refs[2 * count]
    firsts, second, units = refs[2 * count + 1 : -2], refs[-2], refs[-1]
    rows = own[0].shape[1]
    lead = core[0] == 0
    step = pl.program_id(0)

    def part(mine):
        for at in range(count):
            units[row_range(place[at], rows), :] = jnp.where(mine, own[at][0], other[at][0])
        return dot(units[...], grads[...], TN).astype(bf16)

    result = part(lead)
    for at in range(steps):

        @pl.when(step == at)
        def _():
            firsts[at][...] = result

    @pl.when(step < second_steps)
    def _():
        second[...] = part(jnp.logical_not(lead))


def down_grad_parts(core, place, own, other, grads, total):
    count = len(own)
    _, rows, half = own[0].shape
    width = grads.shape[1]
    block = DOWN_BLOCK
    rest = total - half
    steps = half // block
    second_steps = -(-rest // block)
    piece = pl.BlockSpec((1, rows, block), lambda k, *s: (2, 0, k))
    return pl.pallas_call(
        functools.partial(down_grad_kernel, count, steps, second_steps),
        grid_spec=pltpu.PrefetchScalarGridSpec(
            num_scalar_prefetch=2,
            grid=(steps,),
            in_specs=[piece] * (2 * count) + [pl.BlockSpec(grads.shape, lambda k, *s: (0, 0))],
            out_specs=[pl.BlockSpec((block, width), lambda k, *s: (0, 0))] * steps
            + [pl.BlockSpec((block, width), lambda k, *s: (jnp.minimum(k, second_steps - 1), 0))],
            scratch_shapes=[pltpu.VMEM((count * rows, block), bf16)],
        ),
        out_shape=[jax.ShapeDtypeStruct((block, width), bf16)] * steps
        + [jax.ShapeDtypeStruct((rest, width), bf16)],
        compiler_params=params(40),
        cost_estimate=cost(
            2 * count * rows * total * width, 2 * count * rows * (width + 2 * half) + 2 * total * width
        ),
        name="down_grad_parts",
    )(core, place, *own, *other, grads)


def normed_back_kernel(count, core, place, *refs):
    own, other, gate_up = refs[:count], refs[count : 2 * count], refs[2 * count]
    out, gate, up = refs[-3:]
    rows = own[0].shape[1]

    @pl.when(pl.program_id(0) == 0)
    def _():
        for at in range(count):
            span = pl.ds(at * rows, rows)
            for kind, units in ((0, gate), (1, up)):
                ordered(
                    core, own[at].at[kind], other[at].at[kind], units.at[span], own[0].shape[2]
                )

    for at in range(count):
        span = pl.ds(at * rows, rows)
        out[row_range(place[at], rows), :] = (
            dot(gate[span, :], gate_up[0], NT) + dot(up[span, :], gate_up[1], NT)
        ).astype(bf16)


def normed_back(core, place, own, other, gate_up):
    count = len(own)
    _, rows, half = own[0].shape
    _, width, total = gate_up.shape
    block = block_of(width)
    once = pl.Buffered(1)
    units = pl.BlockSpec((count * rows, total), lambda k, *s: (0, 0), pipeline_mode=once)
    units_shape = jax.ShapeDtypeStruct((count * rows, total), bf16)
    return pl.pallas_call(
        functools.partial(normed_back_kernel, count),
        grid_spec=pltpu.PrefetchScalarGridSpec(
            num_scalar_prefetch=2,
            grid=(width // block,),
            in_specs=[pl.BlockSpec((2, rows, half), lambda k, *s: (0, 0, 0), pipeline_mode=once)]
            * (2 * count)
            + [pl.BlockSpec((2, block, total), lambda k, *s: (0, k, 0))],
            out_specs=[
                pl.BlockSpec((count * rows, block), lambda k, *s: (0, k)),
                units,
                units,
            ],
        ),
        out_shape=[
            jax.ShapeDtypeStruct((count * rows, width), bf16),
            units_shape,
            units_shape,
        ],
        compiler_params=params(48),
        cost_estimate=cost(
            4 * count * rows * width * total, 4 * width * total + 8 * count * rows * total
        ),
        name="normed_back",
    )(core, place, *own, *other, gate_up)


def down_out_kernel(count, core, place, *refs):
    own, other, down = refs[:count], refs[count : 2 * count], refs[2 * count]
    out, units = refs[-2:]
    rows = own[0].shape[1]

    @pl.when(pl.program_id(0) == 0)
    def _():
        for at in range(count):
            ordered(core, own[at].at[0], other[at].at[0], units.at[at], own[at].shape[2])

    for at in range(count):
        out[row_range(place[at], rows), :] = dot(units[at], down[...]).astype(bf16)


def down_out(core, place, own, other, down):
    count = len(own)
    _, rows, half = own[0].shape
    total, width = down.shape
    block = block_of(width)
    piece = pl.BlockSpec((1, rows, half), lambda k, *s: (2, 0, 0))
    return pl.pallas_call(
        functools.partial(down_out_kernel, count),
        grid_spec=pltpu.PrefetchScalarGridSpec(
            num_scalar_prefetch=2,
            grid=(width // block,),
            in_specs=[piece] * (2 * count) + [pl.BlockSpec((total, block), lambda k, *s: (0, k))],
            out_specs=pl.BlockSpec((count * rows, block), lambda k, *s: (0, k)),
            scratch_shapes=[pltpu.VMEM((count, rows, total), bf16)],
        ),
        out_shape=jax.ShapeDtypeStruct((count * rows, width), bf16),
        compiler_params=params(48),
        cost_estimate=cost(
            2 * count * rows * total * width, 2 * total * width + 4 * count * rows * total
        ),
        name="down_out",
    )(core, place, *own, *other, down)


def settle_kernel(middle, total, moved, *rest):
    rest[-1][0] = jnp.where(middle[0] == 1, total[...], moved[...]).astype(f32)


def settle(shape, index, start, block, clock, total, moved, before):
    rows, width = total.shape
    middle = clock(in_middle().astype(jnp.int32)[None])
    piece = pl.BlockSpec((block, width), lambda k, s: (k, 0))
    in_specs, args, aliases = [piece, piece], [total, moved], {}
    if before is not None:
        in_specs.append(pl.BlockSpec(memory_space=pl.ANY))
        args.append(before)
        aliases = {3: 0}
    return pl.pallas_call(
        settle_kernel,
        grid_spec=pltpu.PrefetchScalarGridSpec(
            num_scalar_prefetch=1,
            grid=(rows // block,),
            in_specs=in_specs,
            out_specs=pl.BlockSpec((1, block, width), lambda k, s: (index, start // block + k, 0)),
        ),
        out_shape=jax.ShapeDtypeStruct(shape, f32),
        input_output_aliases=aliases,
        compiler_params=params(16),
        cost_estimate=cost(0, 8 * rows * width),
        name="settle",
    )(middle, *args)


def weight_grad_kernel(pieces, kinds, parts, *refs):
    rows_in, units = refs[:pieces], refs[pieces : pieces + kinds]
    outs, rows = refs[pieces + kinds : -1], refs[-1]
    size = rows_in[0].shape[0]
    for at in range(pieces):
        rows[:, pl.ds(at * size, size)] = jnp.transpose(rows_in[at][...])
    steps = pl.num_programs(0) // parts
    for kind in range(kinds):
        array = units[kind][...]
        result = dot(rows[...], array.reshape(array.shape[-2:])).astype(bf16)
        for at in range(parts):

            @pl.when(pl.program_id(0) // steps == at)
            def _():
                outs[kind * parts + at][...] = result


def weight_grads(rows, units, indices=(None,), parts=1):
    pieces, kinds = len(rows), len(units)
    size, width = rows[0].shape
    total, columns = units[0].shape[-2:]
    block = 256 if width // parts % 256 == 0 else LANES
    steps = width // block // parts
    specs = [
        pl.BlockSpec((total, columns), lambda k: (0, 0))
        if index is None
        else pl.BlockSpec((1, total, columns), functools.partial(lambda at, k: (at, 0, 0), index))
        for index in indices
    ]
    outs = [
        pl.BlockSpec(
            (block, columns),
            functools.partial(lambda at, k: (jnp.clip(k - at * steps, 0, steps - 1), 0), at),
        )
        for _ in range(kinds)
        for at in range(parts)
    ]
    return pl.pallas_call(
        functools.partial(weight_grad_kernel, pieces, kinds, parts),
        grid=(steps * parts,),
        in_specs=[pl.BlockSpec((size, block), lambda k: (0, k))] * pieces + specs,
        out_specs=outs,
        out_shape=[jax.ShapeDtypeStruct((width // parts, columns), bf16)] * (kinds * parts),
        scratch_shapes=[pltpu.VMEM((block, total), bf16)],
        compiler_params=params(48),
        cost_estimate=cost(
            2 * total * width * columns * kinds,
            2 * (total * (width + columns * kinds) + width * columns * kinds),
        ),
        name="weight_grads",
    )(*rows, *units)


def mixed_grad_kernel(place, own, other, keep, taken, out):
    out[0] = (dot(own[...], keep[...], NT) + dot(other[...], taken[...], NT)).astype(bf16)


def mixed_back(place, count, own, other, keep, taken):
    rows = own.shape[0] // count
    units, width = keep.shape
    piece = pl.BlockSpec((rows, width), lambda at, s: (s[at], 0))
    weight = pl.BlockSpec((units, width), lambda at, s: (0, 0))
    return pl.pallas_call(
        mixed_grad_kernel,
        grid_spec=pltpu.PrefetchScalarGridSpec(
            num_scalar_prefetch=1,
            grid=(count,),
            in_specs=[piece, piece, weight, weight],
            out_specs=pl.BlockSpec((1, rows, units), lambda at, s: (at, 0, 0)),
        ),
        out_shape=jax.ShapeDtypeStruct((count, rows, units), bf16),
        compiler_params=params(24),
        cost_estimate=cost(4 * count * rows * width * units, 4 * count * rows * width),
        name="mixed_back",
    )(place, own, other, keep, taken)


def project_back_kernel(swap, core, place, own, other, weight, out, units):
    count, rows = own.shape[1:3]

    @pl.when(pl.program_id(0) == 0)
    def _():
        for kind in range(3):
            for at in range(count):
                ordered(
                    core,
                    own.at[kind, at],
                    other.at[kind, swap[at]],
                    units.at[kind, at],
                    own.shape[3],
                )

    for at in range(count):
        out[row_range(place[at], rows), :] = sum(
            dot(units[kind, at], weight[kind], NT) for kind in range(3)
        ).astype(bf16)


def project_back(core, place, swap, own, other, weight):
    _, count, rows, half = own.shape
    _, width, total = weight.shape
    block = block_of(width)
    whole = lambda k, *s: (0, 0, 0, 0)
    return pl.pallas_call(
        functools.partial(project_back_kernel, swap),
        grid_spec=pltpu.PrefetchScalarGridSpec(
            num_scalar_prefetch=2,
            grid=(width // block,),
            in_specs=[
                pl.BlockSpec((3, count, rows, half), whole),
                pl.BlockSpec((3, count, rows, half), whole),
                pl.BlockSpec((3, block, total), lambda k, *s: (0, k, 0)),
            ],
            out_specs=[
                pl.BlockSpec((count * rows, block), lambda k, *s: (0, k)),
                pl.BlockSpec((3, count, rows, total), whole),
            ],
        ),
        out_shape=[
            jax.ShapeDtypeStruct((count * rows, width), bf16),
            jax.ShapeDtypeStruct((3, count, rows, total), bf16),
        ],
        compiler_params=params(40),
        cost_estimate=cost(6 * count * rows * total * width, 2 * count * rows * (width + 6 * total)),
        name="project_back",
    )(core, place, own, other, weight)


def halves(weight, axis, width):
    lead = lax.slice_in_dim(weight, 0, width, axis=axis)
    rest = lax.slice_in_dim(weight, width, weight.shape[axis], axis=axis)
    pad = [(0, 0)] * weight.ndim
    pad[axis] = (0, width - rest.shape[axis])
    rest = jnp.pad(rest, pad)
    first = lax.axis_index("col") == 0
    return jnp.where(first, lead, rest), jnp.where(first, rest, lead)


def shards(
    block_input,
    norm1_gain,
    norm1_shift,
    qkv_weight,
    qkv_bias,
    out_weight,
    norm2_gain,
    norm2_shift,
    gate_up_weight,
    down_weight,
    output_grad,
):
    count = lax.axis_size("row")
    rows = block_input.shape[0]
    core = lax.axis_index("col").astype(jnp.int32)[None]
    place, swap = places()
    place = place.astype(jnp.int32)
    slot = inverse_places(place)
    half_units = out_weight.shape[0] // 2
    total_hidden = down_weight.shape[0]
    half_hidden = -(-total_hidden // (2 * LANES)) * LANES
    if grid_rows():
        groups = (((2,), 2), ((0, 1), 0), ((3,), 3))
    else:
        groups = tuple(((at,), at) for at in range(count))

    clock = Clock()
    inputs = block_input.astype(f32)
    gain_one = norm1_gain.astype(f32)
    gain_two = norm2_gain.astype(f32)
    hat_one, inverse_one = normalize(inputs)
    normed_one = clock.mark((hat_one * gain_one + norm1_shift.astype(f32)).astype(bf16))

    one_own, fetch = gather_rows(normed_one)
    qkv_keep, qkv_send = halves(clock(qkv_weight), 2, half_units)
    clock.mark(qkv_keep)
    qkv_taken = sibling(qkv_send)
    cosine, sine = rotary_tables(count, rows)
    bias = qkv_bias[:, None, :]
    qkv = None
    for group, index in groups:
        if qkv is not None and len(one_own) < count:
            one_own += fetch(clock.last)
        others = [sibling(clock(one_own[swap[at]])) for at in group]
        qkv = clock.mark(
            project_pieces(
                index, group, count, place, [one_own[at] for at in group], others,
                qkv_keep, qkv_taken, clock(bias), cosine, sine, qkv,
            )
        )
        if group == groups[0][0]:
            gate_up_keep, gate_up_send = halves(clock(gate_up_weight), 2, half_hidden)
            clock.mark(gate_up_keep)
            down_keep, down_send = halves(clock(down_weight), 0, half_hidden)
            clock.mark(down_keep)
            out_keep, out_send = halves(clock(out_weight), 0, half_units)
            clock.mark(out_keep)
    gate_up_taken = sibling(clock(gate_up_send))
    down_taken = sibling(clock(down_send))
    out_taken = sibling(clock(out_send))
    grad_own = gather_whole(after(output_grad, others[-1]))
    mixed, kept, logsum = attend_forward(clock(slot), qkv)
    clock.mark(mixed)
    *branch, mixed_units = mixed_out(clock(core), place, swap, mixed, sibling(mixed), out_weight)
    clock.mark(branch[0])
    branch = scatter_rows(branch, clock)
    grad_other = sibling(clock(grad_own))
    after_rows = inputs + branch
    hat_two, inverse_two = normalize(after_rows)
    normed_two = clock.mark((hat_two * gain_two + norm2_shift.astype(f32)).astype(bf16))

    two_own, fetch = gather_rows(normed_two)
    mine, theirs = [None] * count, [None] * count
    for group, _ in groups:
        if group != groups[0][0] and len(two_own) < count:
            two_own += fetch(clock.last)
        results = hidden_pieces(
            group, clock(place),
            [two_own[at] for at in group],
            [sibling(clock(two_own[swap[at]])) for at in group],
            grad_own, grad_other, gate_up_keep, gate_up_taken, down_keep, down_taken,
        )
        clock.mark(results[0])
        for at, result in zip(group, results):
            mine[at] = result
        for at in group:
            theirs[at] = sibling(mine[swap[at]])

    sums = Line(clock)
    parts = down_grad_parts(clock(core), place, mine, theirs, grad_own, total_hidden)
    down_count = len(parts)
    clock.mark(parts[0])
    sums.add(*parts)
    normed_part, gate_units, up_units = normed_back(clock(core), place, mine, theirs, gate_up_weight)
    clock.mark(normed_part)
    normed_two_grad = scatter_whole(normed_part)
    sums.join()
    parts = weight_grads(two_own, [clock(gate_units), up_units], (None, None), 2)
    clock.mark(parts[0])
    sums.add(*parts)
    sums.join()
    sums.total_up()
    down_part = clock.mark(down_out(clock(core), place, mine, theirs, down_weight))
    sums.join()
    sums.total_up()
    normed_two_grad = clock(normed_two_grad)
    after_grad = output_grad.astype(f32) + norm_back(
        normed_two_grad * gain_two, hat_two, inverse_two
    )
    branch_grad = clock.mark(after_grad.astype(bf16))
    branch_own = gather_whole(branch_grad)
    sums.join()
    sums.total_up()
    sums.join()
    sums.total_up()
    down = scatter_whole(after(down_part, branch_own))
    branch_other = sibling(clock(branch_own))
    mixed_grad = clock.mark(
        mixed_back(clock(place), count, branch_own, branch_other, out_keep, out_taken)
    )
    parts = weight_grads([mixed_units.reshape(count * rows, -1)], [clock(branch_own)])
    clock.mark(parts[0])
    sums.add(*parts)
    project_grad = clock.mark(
        attend_backward(clock(slot), place, qkv, mixed_grad, kept, logsum, cosine, sine)
    )
    project_other = sibling(project_grad)
    sums.join()
    sums.total_up()
    one_part, project_units = project_back(
        clock(core), place, swap, project_grad, project_other, qkv_weight
    )
    clock.mark(one_part)
    normed_one_grad = scatter_whole(one_part)
    project_units = project_units.reshape(3, count * rows, -1)
    sums.join()
    parts = weight_grads(one_own, [clock(project_units)] * 3, (0, 1, 2))
    clock.mark(parts[0])
    sums.add(*parts)
    sums.total_up()
    spots = [(0, at * DOWN_BLOCK) for at in range(down_count)]
    down_grad = sums.settle((1,) + down_weight.shape, spots, LANES)
    block_output = clock.mark((after_rows + clock(down)).astype(bf16))
    bias_grad = jnp.sum(clock(project_grad).astype(f32), axis=(1, 2))
    clock.mark(bias_grad)
    sums.join()
    sums.total_up()
    normed_one_grad = clock(normed_one_grad)
    input_grad = clock.mark(
        after_grad + norm_back(normed_one_grad * gain_one, hat_one, inverse_one)
    )
    gains = jnp.stack(
        [
            jnp.sum(normed_one_grad * hat_one, axis=0),
            jnp.sum(normed_one_grad, axis=0),
            jnp.sum(normed_two_grad * hat_two, axis=0),
            jnp.sum(normed_two_grad, axis=0),
        ]
    )
    width = gains.shape[1]
    gains = sum_rows(clock.mark(gains))
    sums.add(jnp.concatenate([gains.reshape(-1, LANES), bias_grad.reshape(-1, LANES)], axis=0))
    last = len(sums.parts) - 1
    half_width = two_own[0].shape[1] // 2
    gate_up_block = block_of(half_width)
    qkv_block = block_of(qkv_weight.shape[1])
    sums.join()
    sums.total_up()
    gate_up_grad = sums.settle(
        gate_up_weight.shape, ((0, 0), (0, half_width), (1, 0)), gate_up_block
    )
    sums.join()
    sums.total_up()
    gate_up_grad = sums.settle(gate_up_weight.shape, ((1, half_width),), gate_up_block, gate_up_grad)
    sums.join()
    sums.total_up()
    out_grad = sums.settle((1,) + out_weight.shape, ((0, 0),), block_of(out_weight.shape[0]))
    sums.join()
    sums.total_up()
    qkv_grad = sums.settle(qkv_weight.shape, ((0, 0), (1, 0)), qkv_block)
    sums.total_up()
    qkv_grad = sums.settle(qkv_weight.shape, ((2, 0),), qkv_block, qkv_grad)
    small = sums.small(last)
    gains = small[: 4 * width // LANES].reshape(4, width)
    bias_grad = small[4 * width // LANES :].reshape(bias_grad.shape)
    return (
        block_output,
        input_grad,
        gains[0],
        gains[1],
        qkv_grad,
        bias_grad,
        out_grad[0],
        gains[2],
        gains[3],
        gate_up_grad,
        down_grad[0],
    )


def inverse_places(place):
    spots = jnp.arange(place.shape[0])
    return jnp.sum(
        jnp.where(place[None, :] == spots[:, None], spots[None, :], 0), axis=1
    ).astype(jnp.int32)


def solution(mesh):
    placed = (
        P(("dp", "row"), "col"),
        P("col"),
        P("col"),
        P(None, "col", "row"),
        P(None, ("row", "col")),
        P("row", "col"),
        P("col"),
        P("col"),
        P(None, "col", "row"),
        P("row", "col"),
        P(("dp", "row"), "col"),
    )
    return jax.shard_map(
        shards,
        mesh=mesh,
        in_specs=placed,
        out_specs=(
            P(("dp", "row"), "col"),
            P(("dp", "row"), "col"),
            P("col"),
            P("col"),
            P(None, "col", "row"),
            P(None, ("row", "col")),
            P("row", "col"),
            P("col"),
            P("col"),
            P(None, "col", "row"),
            P("row", "col"),
        ),
        check_vma=False,
    )
```

```python
import functools

import jax
import jax.numpy as jnp
import numpy as np
from jax import lax
from jax.experimental import pallas as pl
from jax.experimental.pallas import tpu as pltpu
from jax.sharding import PartitionSpec as P

HD = 64
ROT = 16
LANES = 128
MIB = 1 << 20
DOWN_BLOCK = 384

epsilon = 1e-05
base_rate = 10000.0
bf16 = jnp.bfloat16
f32 = jnp.float32

NN = (((1,), (0,)), ((), ()))
NT = (((1,), (1,)), ((), ()))
TN = (((0,), (0,)), ((), ()))


def dot(first, second, dims=NN):
    return lax.dot_general(first, second, dims, preferred_element_type=f32)


def row_permute(values, core_zero, core_one):
    pairs = [
        (row * 2 + core, (row ^ (core_one if core else core_zero)) * 2 + core)
        for row in range(4)
        for core in range(2)
    ]
    return lax.ppermute(values, ("row", "col"), pairs)


def first_way(values):
    return row_permute(values, 1, 2)


def second_way(values):
    return row_permute(values, 2, 1)


def sibling(values):
    return lax.ppermute(values, "col", [(0, 1), (1, 0)])


def grid_rows():
    return lax.axis_size("row") == 4


def places():
    row, core = lax.axis_index("row"), lax.axis_index("col")
    if grid_rows():
        one = jnp.where(core == 0, 1, 2)
        return jnp.stack([row ^ one, row ^ (3 - one), row, row ^ 3]), (1, 0, 2, 3)
    count = lax.axis_size("row")
    return jnp.arange(count), tuple(range(count))


def after(value, *earlier):
    return lax.optimization_barrier((value,) + earlier)[0]


def gather_rows(own):
    if grid_rows():
        near = first_way(own)
        side = second_way(own)
        return [near, side, own], lambda *earlier: [second_way(after(near, side, *earlier))]
    whole = lax.all_gather(own, "row", axis=0, tiled=True)
    return jnp.split(whole, lax.axis_size("row"), axis=0), lambda *earlier: []


def scatter_rows(parts, clock):
    if grid_rows():
        passing = first_way(parts[3])
        near = first_way(parts[0])
        side = second_way(clock.mark(plus(parts[1], after(clock(passing), near))))
        return parts[2].astype(f32) + near.astype(f32) + side.astype(f32)
    whole = jnp.concatenate(parts, axis=0)
    return lax.psum_scatter(whole, "row", scatter_dimension=0, tiled=True).astype(f32)


def line():
    return lax.axis_size("dp") == 4


def in_middle():
    place = lax.axis_index("dp")
    return (place == 1) | (place == 2)


def inward(part):
    return lax.ppermute(part, "dp", [(0, 1), (3, 2)])


def across(part):
    return lax.ppermute(part, "dp", [(1, 2), (2, 1)])


def outward(part):
    return lax.ppermute(part, "dp", [(1, 0), (2, 3)])


def plus(first, second):
    return (first.astype(f32) + second.astype(f32)).astype(first.dtype)


class Clock:
    def __init__(self):
        self.last = None

    def __call__(self, value):
        return value if self.last is None else after(value, self.last)

    def mark(self, value):
        self.last = value
        return value


class Line:
    def __init__(self, clock):
        self.clock = clock
        self.parts, self.inner, self.half, self.other, self.total, self.outer = ([] for _ in range(6))
        self.settled = 0

    def feed(self):
        at = len(self.inner)
        if at < len(self.parts) and at < len(self.half) + 2:
            part = self.parts[at]
            self.inner.append(inward(after(part, self.inner[at - 2]) if at >= 2 else part))

    def add(self, *parts):
        self.parts += parts
        if line():
            for _ in parts:
                self.feed()

    def join(self):
        if line():
            at = len(self.half)
            left = self.outer[at - 3 : at - 2] if at >= 3 else []
            came = after(self.clock(self.inner[at]), *left)
            self.half.append(self.clock.mark(plus(self.parts[at], came)))
            self.feed()
            ready = self.half[at]
            self.other.append(across(after(ready, self.other[-1]) if self.other else ready))

    def total_up(self):
        if line():
            at = len(self.total)
            self.total.append(self.clock.mark(plus(self.half[at], self.clock(self.other[at]))))
            ready = self.total[at]
            self.outer.append(outward(after(ready, self.outer[-1]) if self.outer else ready))

    def settle(self, shape, places, block, before=None):
        for index, start in places:
            at = self.settled
            self.settled += 1
            if line():
                before = self.clock.mark(
                    settle(shape, index, start, block, self.clock, self.total[at], self.outer[at], before)
                )
            else:
                value = lax.psum(self.parts[at], "dp").astype(f32)[None]
                before = jnp.zeros(shape, f32) if before is None else before
                before = lax.dynamic_update_slice(before, value, (index, start, 0))
        return before

    def small(self, at):
        if line():
            return jnp.where(in_middle(), self.total[at], self.outer[at])
        return lax.psum(self.parts[at], "dp")


def gather_whole(own):
    return lax.all_gather(own, "row", axis=0, tiled=True)


def scatter_whole(parts):
    return lax.psum_scatter(parts, "row", scatter_dimension=0, tiled=True).astype(f32)


def sum_rows(values, clock):
    if grid_rows():
        values = clock.mark(values + clock(first_way(values)))
        return clock.mark(values + clock(second_way(values)))
    return lax.psum(values, "row")


def width_pair(first, second):
    both = jnp.stack([first, second])
    both = both + sibling(both)
    return both[0], both[1]


def normalize(values):
    width = values.shape[1] * lax.axis_size("col")
    totals, squares = width_pair(jnp.sum(values, axis=-1), jnp.sum(values * values, axis=-1))
    average = totals / width
    spread = squares / width - average * average
    inverse = lax.rsqrt(spread + epsilon)[:, None]
    return ((values - average[:, None]) * inverse, inverse)


def norm_back(scaled, normed_hat, inverse):
    width = normed_hat.shape[1] * lax.axis_size("col")
    first, second = width_pair(jnp.sum(scaled, axis=-1), jnp.sum(scaled * normed_hat, axis=-1))
    return inverse * (scaled - first[:, None] / width - normed_hat * second[:, None] / width)


def rotary_tables(count, rows):
    half_dims = ROT // 2
    lane = np.arange(LANES) % HD
    freqs = np.float32(base_rate) ** (-(2.0 * (lane % half_dims).astype(np.float32)) / np.float32(ROT))
    angles = np.arange(count * rows, dtype=np.float32)[:, None] * freqs.astype(np.float32)[None, :]
    turned = lane < ROT
    sign = np.where(lane < half_dims, -1.0, 1.0)
    cosine = np.where(turned, np.cos(angles.astype(np.float64)), 1.0)
    sine = np.where(turned, sign * np.sin(angles.astype(np.float64)), 0.0)
    shape = (count, rows, LANES)
    return jnp.asarray(cosine.reshape(shape), f32), jnp.asarray(sine.reshape(shape), f32)


def turn(values, cosine, sine):
    half_dims = ROT // 2
    lane = lax.broadcasted_iota(jnp.int32, values.shape, 1) % HD
    partner = jnp.where(
        lane < half_dims,
        pltpu.roll(values, LANES - half_dims, 1),
        pltpu.roll(values, half_dims, 1),
    )
    return values * cosine + partner * sine


def params(mib, *order):
    return pltpu.CompilerParams(vmem_limit_bytes=mib * MIB)


def cost(flops, moved, hard=0):
    return pl.CostEstimate(flops=int(flops), bytes_accessed=int(moved), transcendentals=int(hard))


def project_kernel(members, place, *refs):
    own, other = refs[:members], refs[members : 2 * members]
    keep, taken, bias = refs[2 * members : 2 * members + 3]
    cosine, sine = refs[2 * members + 3 : 3 * members + 3], refs[3 * members + 3 : 4 * members + 3]
    out = refs[-1]
    kind = pl.program_id(0)
    for at in range(members):
        result = dot(own[at][...], keep[0]) + dot(other[at][...], taken[0]) + bias[0].astype(f32)

        @pl.when(kind < 2)
        def _():
            for start in range(0, result.shape[1], LANES):
                part = slice(start, start + LANES)
                out[at, 0, :, part] = turn(result[:, part], cosine[at][0], sine[at][0]).astype(bf16)

        @pl.when(kind == 2)
        def _():
            out[at, 0] = result.astype(bf16)


def project_pieces(index, group, count, place, own, other, keep, taken, bias, cosine, sine, before):
    members = len(own)
    rows, width = own[0].shape
    units = keep.shape[2]
    piece = pl.BlockSpec((rows, width), lambda k, s: (0, 0), pipeline_mode=pl.Buffered(1))
    tables = [
        pl.BlockSpec((1, rows, LANES), functools.partial(lambda at, k, s: (s[at], 0, 0), at))
        for at in group
    ]
    weight = pl.BlockSpec((1, width, units), lambda k, s: (k, 0, 0))
    in_specs = [piece] * (2 * members) + [
        weight,
        weight,
        pl.BlockSpec((1, 1, units), lambda k, s: (k, 0, 0)),
        *tables,
        *tables,
    ]
    args = [*own, *other, keep, taken, bias] + [cosine] * members + [sine] * members
    aliases = {}
    if before is not None:
        aliases = {len(args) + 1: 0}
        in_specs.append(pl.BlockSpec(memory_space=pl.ANY))
        args.append(before)
    return pl.pallas_call(
        functools.partial(project_kernel, members),
        grid_spec=pltpu.PrefetchScalarGridSpec(
            num_scalar_prefetch=1,
            grid=(3,),
            in_specs=in_specs,
            out_specs=pl.BlockSpec((members, 1, rows, units), lambda k, s: (index, k, 0, 0)),
        ),
        out_shape=jax.ShapeDtypeStruct((count, 3, rows, units), bf16),
        input_output_aliases=aliases,
        compiler_params=params(24),
        cost_estimate=cost(
            12 * members * rows * width * units, 4 * members * rows * width + 12 * width * units
        ),
        name="project_pieces",
    )(place, *args)


def causal(rows):
    keys = lax.broadcasted_iota(jnp.int32, (rows, rows), 0)
    return keys <= lax.broadcasted_iota(jnp.int32, (rows, rows), 1)


def head_lanes(values, head):
    lane = lax.broadcasted_iota(jnp.int32, values.shape, 1)
    return jnp.where((lane >= head * HD) & (lane < (head + 1) * HD), values, jnp.zeros_like(values))


def walk(stop, body, carry):
    if isinstance(stop, int):
        for step in range(stop):
            carry = body(step, carry)
        return carry
    return lax.fori_loop(0, stop, body, carry)


def each(count, body):
    if count <= 4:
        for step in range(count):
            body(step)
    else:
        lax.fori_loop(0, count, lambda step, carry: (body(step), carry)[1], 0)


def row_range(step, rows):
    return pl.ds(step * rows if isinstance(step, int) else pl.multiple_of(step * rows, rows), rows)


def attend_kernel(slot, qkv, mixed, kept, logsum, scores):
    count, _, rows, _ = qkv.shape
    heads = LANES // HD
    scale = HD**-0.5

    def one(at):
        here = slot[at]
        query = qkv[here, 0] * jnp.asarray(scale, bf16)
        for head in range(heads):

            def look(past, highest):
                block = dot(head_lanes(qkv[slot[past], 1], head), query, NT)
                scores[row_range(past, rows), :] = block
                return jnp.maximum(highest, jnp.max(block, axis=0, keepdims=True))

            def add(past, carry):
                total, outs = carry
                weights = jnp.exp(scores[row_range(past, rows), :] - highest)
                total = total + jnp.sum(weights, axis=0, keepdims=True)
                value = jnp.transpose(qkv[slot[past], 2])[head * HD : (head + 1) * HD]
                return total, outs + dot(value, weights.astype(bf16))

            block = dot(head_lanes(qkv[here, 1], head), query, NT)
            block = jnp.where(causal(rows), block, -1e30)
            scores[row_range(at, rows), :] = block
            highest = walk(at, look, jnp.max(block, axis=0, keepdims=True))
            total, outs = walk(
                at + 1, add, (jnp.zeros((1, rows), f32), jnp.zeros((HD, rows), f32))
            )
            kept[0, here, pl.ds(head * HD, HD), :] = outs / total
            logsum[0, here, pl.ds(head, 1), :] = highest + jnp.log(total)
        mixed[here] = jnp.transpose(kept[0, here]).astype(bf16)

    each(count, one)


def attend_forward(slot, qkv):
    count, _, rows, units = qkv.shape
    pairs = units // LANES
    work = rows * rows * count * (count + 1) // 2 * units
    return pl.pallas_call(
        attend_kernel,
        grid_spec=pltpu.PrefetchScalarGridSpec(
            num_scalar_prefetch=1,
            grid=(pairs,),
            in_specs=[pl.BlockSpec((count, 3, rows, LANES), lambda p, s: (0, 0, 0, p))],
            out_specs=[
                pl.BlockSpec((count, rows, LANES), lambda p, s: (0, 0, p)),
                pl.BlockSpec((1, count, LANES, rows), lambda p, s: (p, 0, 0, 0)),
                pl.BlockSpec((1, count, 8, rows), lambda p, s: (p, 0, 0, 0)),
            ],
            scratch_shapes=[pltpu.VMEM((count * rows, rows), f32)],
        ),
        out_shape=[
            jax.ShapeDtypeStruct((count, rows, units), bf16),
            jax.ShapeDtypeStruct((pairs, count, LANES, rows), f32),
            jax.ShapeDtypeStruct((pairs, count, 8, rows), f32),
        ],
        compiler_params=params(20),
        cost_estimate=cost(16 * work, 16 * count * rows * units, work // HD),
        name="attend_forward",
    )(slot, qkv)


def attend_back_kernel(slot, place, qkv, grads, kept, logsum, cosine, sine, out, dq, dk, dv, inner):
    count, _, rows, _ = qkv.shape
    heads = LANES // HD
    scale = HD**-0.5
    dk[...] = jnp.zeros_like(dk)
    dv[...] = jnp.zeros_like(dv)

    def sums(at):
        product = jnp.transpose(grads[at].astype(f32)) * kept[0, at]
        for head in range(heads):
            part = product[head * HD : (head + 1) * HD]
            inner[at, pl.ds(head, 1), :] = jnp.sum(part, axis=0, keepdims=True)

    def one(at):
        here = slot[at]
        query = qkv[here, 0] * jnp.asarray(scale, bf16)
        grad = grads[here]
        for head in range(heads):
            query_head = head_lanes(query, head)
            grad_head = head_lanes(grad, head)

            def look(past, query_grad, last=False):
                there = slot[past]
                key = qkv[there, 1]
                block = dot(key, query_head, NT)
                weights = jnp.exp(block - logsum[0, here, pl.ds(head, 1), :])
                if last:
                    weights = jnp.where(causal(rows), weights, 0.0)
                moved = dot(qkv[there, 2], grad_head, NT)
                raw = (weights * (moved - inner[here, pl.ds(head, 1), :])).astype(bf16)
                dv[there] += dot(weights.astype(bf16), grad_head)
                dk[there] += dot(raw, query_head)
                turned = jnp.transpose(key)[head * HD : (head + 1) * HD]
                return query_grad + dot(turned, raw)

            query_grad = walk(at, look, jnp.zeros((HD, rows), f32))
            dq[pl.ds(head * HD, HD), :] = look(at, query_grad, True) * scale
        out[0, here] = turn(jnp.transpose(dq[...]), cosine[at], -sine[at]).astype(bf16)

    def finish(at):
        out[1, at] = turn(dk[at], cosine[place[at]], -sine[place[at]]).astype(bf16)
        out[2, at] = dv[at].astype(bf16)

    each(count, sums)
    each(count, one)
    each(count, finish)


def attend_backward(slot, place, qkv, grads, kept, logsum, cosine, sine):
    count, _, rows, units = qkv.shape
    pairs = units // LANES
    work = rows * rows * count * (count + 1) // 2 * units
    table = pl.BlockSpec((count, rows, LANES), lambda p, *s: (0, 0, 0))
    return pl.pallas_call(
        attend_back_kernel,
        grid_spec=pltpu.PrefetchScalarGridSpec(
            num_scalar_prefetch=2,
            grid=(pairs,),
            in_specs=[
                pl.BlockSpec((count, 3, rows, LANES), lambda p, *s: (0, 0, 0, p)),
                pl.BlockSpec((count, rows, LANES), lambda p, *s: (0, 0, p)),
                pl.BlockSpec((1, count, LANES, rows), lambda p, *s: (p, 0, 0, 0)),
                pl.BlockSpec((1, count, 8, rows), lambda p, *s: (p, 0, 0, 0)),
                table,
                table,
            ],
            out_specs=pl.BlockSpec((3, count, rows, LANES), lambda p, *s: (0, 0, 0, p)),
            scratch_shapes=[
                pltpu.VMEM((LANES, rows), f32),
                pltpu.VMEM((count, rows, LANES), f32),
                pltpu.VMEM((count, rows, LANES), f32),
                pltpu.VMEM((count, 8, rows), f32),
            ],
        ),
        out_shape=jax.ShapeDtypeStruct((3, count, rows, units), bf16),
        compiler_params=params(24),
        cost_estimate=cost(40 * work, 24 * count * rows * units, work // HD),
        name="attend_backward",
    )(slot, place, qkv, grads, kept, logsum, cosine, sine)


def ordered(core, own, other, out, width):
    rest = out.shape[-1] - width
    lead = core[0] == 0
    out[..., :width] = jnp.where(lead, own[...], other[...])
    out[..., width:] = jnp.where(lead, other[..., :rest], own[..., :rest])


def block_of(width):
    return 256 if width % 256 == 0 else LANES


def mixed_out_kernel(swap, core, place, own, other, weight, *outs):
    units = outs[-1]
    count = own.shape[0]

    @pl.when(pl.program_id(0) == 0)
    def _():
        for at in range(count):
            ordered(core, own.at[at], other.at[swap[at]], units.at[place[at]], own.shape[2])

    for at in range(count):
        outs[at][...] = dot(units[place[at]], weight[...]).astype(bf16)


def mixed_out(core, place, swap, own, other, weight):
    count, rows, units = own.shape
    width = weight.shape[1]
    block = block_of(width)
    whole = lambda k, *s: (0, 0, 0)
    return pl.pallas_call(
        functools.partial(mixed_out_kernel, swap),
        grid_spec=pltpu.PrefetchScalarGridSpec(
            num_scalar_prefetch=2,
            grid=(width // block,),
            in_specs=[
                pl.BlockSpec((count, rows, units), whole),
                pl.BlockSpec((count, rows, units), whole),
                pl.BlockSpec((2 * units, block), lambda k, *s: (0, k)),
            ],
            out_specs=[pl.BlockSpec((rows, block), lambda k, *s: (0, k))] * count
            + [pl.BlockSpec((count, rows, 2 * units), whole)],
        ),
        out_shape=[jax.ShapeDtypeStruct((rows, width), bf16)] * count
        + [jax.ShapeDtypeStruct((count, rows, 2 * units), bf16)],
        compiler_params=params(16),
        cost_estimate=cost(4 * count * rows * units * width, 2 * count * rows * (width + 4 * units)),
        name="mixed_out",
    )(core, place, own, other, weight)


def hidden_kernel(members, place, *refs):
    own, other, grad_own, grad_other = (refs[k * members : (k + 1) * members] for k in range(4))
    gate_up, taken, down, down_taken = refs[4 * members : 4 * members + 4]
    outs = refs[4 * members + 4 :]
    for at in range(members):
        gate = dot(own[at][...], gate_up[0]) + dot(other[at][...], taken[0])
        up = dot(own[at][...], gate_up[1]) + dot(other[at][...], taken[1])
        grad = dot(grad_own[at][...], down[...], NT) + dot(grad_other[at][...], down_taken[...], NT)
        sigmoid = jax.nn.sigmoid(gate)
        silu = gate * sigmoid
        slope = sigmoid * (1.0 + gate * (1.0 - sigmoid))
        outs[at][0] = (grad * up * slope).astype(bf16)
        outs[at][1] = (grad * silu).astype(bf16)
        outs[at][2] = (silu * up).astype(bf16)


def hidden_pieces(group, place, own, other, grad_own, grad_other, gate_up, taken, down, down_taken):
    members = len(own)
    rows, width = own[0].shape
    units = gate_up.shape[2]
    block = block_of(units)
    rows_in = pl.BlockSpec((rows, width), lambda k, s: (0, 0), pipeline_mode=pl.Buffered(1))
    grads = [
        pl.BlockSpec(
            (rows, width),
            functools.partial(lambda at, k, s: (s[at], 0), at),
            pipeline_mode=pl.Buffered(1),
        )
        for at in group
    ]
    entry = pl.BlockSpec((2, width, block), lambda k, s: (0, 0, k))
    leave = pl.BlockSpec((block, width), lambda k, s: (k, 0))
    return pl.pallas_call(
        functools.partial(hidden_kernel, members),
        grid_spec=pltpu.PrefetchScalarGridSpec(
            num_scalar_prefetch=1,
            grid=(units // block,),
            in_specs=[rows_in] * (2 * members) + grads + grads + [entry, entry, leave, leave],
            out_specs=[pl.BlockSpec((3, rows, block), lambda k, s: (0, 0, k))] * members,
        ),
        out_shape=[jax.ShapeDtypeStruct((3, rows, units), bf16)] * members,
        compiler_params=params(28),
        cost_estimate=cost(
            12 * members * rows * width * units, 12 * width * units + 8 * members * rows * width
        ),
        name="hidden_pieces",
    )(
        place, *own, *other, *([grad_own] * members), *([grad_other] * members),
        gate_up, taken, down, down_taken,
    )


def down_grad_kernel(count, steps, second_steps, core, place, *refs):
    own, other, grads = refs[:count], refs[count : 2 * count], refs[2 * count]
    firsts, second, units = refs[2 * count + 1 : -2], refs[-2], refs[-1]
    rows = own[0].shape[1]
    lead = core[0] == 0
    step = pl.program_id(0)

    def part(mine):
        for at in range(count):
            units[row_range(place[at], rows), :] = jnp.where(mine, own[at][0], other[at][0])
        return dot(units[...], grads[...], TN).astype(bf16)

    result = part(lead)
    for at in range(steps):

        @pl.when(step == at)
        def _():
            firsts[at][...] = result

    @pl.when(step < second_steps)
    def _():
        second[...] = part(jnp.logical_not(lead))


def down_grad_parts(core, place, own, other, grads, total):
    count = len(own)
    _, rows, half = own[0].shape
    width = grads.shape[1]
    block = DOWN_BLOCK
    rest = total - half
    steps = half // block
    second_steps = -(-rest // block)
    piece = pl.BlockSpec((1, rows, block), lambda k, *s: (2, 0, k))
    return pl.pallas_call(
        functools.partial(down_grad_kernel, count, steps, second_steps),
        grid_spec=pltpu.PrefetchScalarGridSpec(
            num_scalar_prefetch=2,
            grid=(steps,),
            in_specs=[piece] * (2 * count) + [
                pl.BlockSpec(grads.shape, lambda k, *s: (0, 0), pipeline_mode=pl.Buffered(1))
            ],
            out_specs=[pl.BlockSpec((block, width), lambda k, *s: (0, 0))] * steps
            + [pl.BlockSpec((block, width), lambda k, *s: (jnp.minimum(k, second_steps - 1), 0))],
            scratch_shapes=[pltpu.VMEM((count * rows, block), bf16)],
        ),
        out_shape=[jax.ShapeDtypeStruct((block, width), bf16)] * steps
        + [jax.ShapeDtypeStruct((rest, width), bf16)],
        compiler_params=params(24),
        cost_estimate=cost(
            2 * count * rows * total * width, 2 * count * rows * (width + 2 * half) + 2 * total * width
        ),
        name="down_grad_parts",
    )(core, place, *own, *other, grads)


def normed_back_kernel(count, core, place, *refs):
    own, other, gate_up = refs[:count], refs[count : 2 * count], refs[2 * count]
    out, gate, up = refs[-3:]
    rows = own[0].shape[1]

    @pl.when(pl.program_id(0) == 0)
    def _():
        for at in range(count):
            span = pl.ds(at * rows, rows)
            for kind, units in ((0, gate), (1, up)):
                ordered(
                    core, own[at].at[kind], other[at].at[kind], units.at[span], own[0].shape[2]
                )

    for at in range(count):
        span = pl.ds(at * rows, rows)
        out[row_range(place[at], rows), :] = (
            dot(gate[span, :], gate_up[0], NT) + dot(up[span, :], gate_up[1], NT)
        ).astype(bf16)


def normed_back(core, place, own, other, gate_up):
    count = len(own)
    _, rows, half = own[0].shape
    _, width, total = gate_up.shape
    block = block_of(width)
    once = pl.Buffered(1)
    units = pl.BlockSpec((count * rows, total), lambda k, *s: (0, 0), pipeline_mode=once)
    units_shape = jax.ShapeDtypeStruct((count * rows, total), bf16)
    return pl.pallas_call(
        functools.partial(normed_back_kernel, count),
        grid_spec=pltpu.PrefetchScalarGridSpec(
            num_scalar_prefetch=2,
            grid=(width // block,),
            in_specs=[pl.BlockSpec((2, rows, half), lambda k, *s: (0, 0, 0), pipeline_mode=once)]
            * (2 * count)
            + [pl.BlockSpec((2, block, total), lambda k, *s: (0, k, 0))],
            out_specs=[
                pl.BlockSpec((count * rows, block), lambda k, *s: (0, k)),
                units,
                units,
            ],
        ),
        out_shape=[
            jax.ShapeDtypeStruct((count * rows, width), bf16),
            units_shape,
            units_shape,
        ],
        compiler_params=params(36),
        cost_estimate=cost(
            4 * count * rows * width * total, 4 * width * total + 8 * count * rows * total
        ),
        name="normed_back",
    )(core, place, *own, *other, gate_up)


def down_out_kernel(count, core, place, *refs):
    own, other, down = refs[:count], refs[count : 2 * count], refs[2 * count]
    out, units = refs[-2:]
    rows = own[0].shape[1]

    @pl.when(pl.program_id(0) == 0)
    def _():
        for at in range(count):
            ordered(core, own[at].at[0], other[at].at[0], units.at[at], own[at].shape[2])

    for at in range(count):
        out[row_range(place[at], rows), :] = dot(units[at], down[...]).astype(bf16)


def down_out(core, place, own, other, down):
    count = len(own)
    _, rows, half = own[0].shape
    total, width = down.shape
    block = block_of(width)
    piece = pl.BlockSpec((1, rows, half), lambda k, *s: (2, 0, 0), pipeline_mode=pl.Buffered(1))
    return pl.pallas_call(
        functools.partial(down_out_kernel, count),
        grid_spec=pltpu.PrefetchScalarGridSpec(
            num_scalar_prefetch=2,
            grid=(width // block,),
            in_specs=[piece] * (2 * count) + [pl.BlockSpec((total, block), lambda k, *s: (0, k))],
            out_specs=pl.BlockSpec((count * rows, block), lambda k, *s: (0, k)),
            scratch_shapes=[pltpu.VMEM((count, rows, total), bf16)],
        ),
        out_shape=jax.ShapeDtypeStruct((count * rows, width), bf16),
        compiler_params=params(28),
        cost_estimate=cost(
            2 * count * rows * total * width, 2 * total * width + 4 * count * rows * total
        ),
        name="down_out",
    )(core, place, *own, *other, down)


def settle_kernel(middle, total, moved, *rest):
    rest[-1][0] = jnp.where(middle[0] == 1, total[...], moved[...]).astype(f32)


def settle(shape, index, start, block, clock, total, moved, before):
    rows, width = total.shape
    middle = clock(in_middle().astype(jnp.int32)[None])
    piece = pl.BlockSpec((block, width), lambda k, s: (k, 0))
    in_specs, args, aliases = [piece, piece], [total, moved], {}
    if before is not None:
        in_specs.append(pl.BlockSpec(memory_space=pl.ANY))
        args.append(before)
        aliases = {3: 0}
    return pl.pallas_call(
        settle_kernel,
        grid_spec=pltpu.PrefetchScalarGridSpec(
            num_scalar_prefetch=1,
            grid=(rows // block,),
            in_specs=in_specs,
            out_specs=pl.BlockSpec((1, block, width), lambda k, s: (index, start // block + k, 0)),
        ),
        out_shape=jax.ShapeDtypeStruct(shape, f32),
        input_output_aliases=aliases,
        compiler_params=params(8),
        cost_estimate=cost(0, 8 * rows * width),
        name="settle",
    )(middle, *args)


def weight_grad_kernel(pieces, kinds, parts, *refs):
    rows_in, units = refs[:pieces], refs[pieces : pieces + kinds]
    outs, rows = refs[pieces + kinds : -1], refs[-1]
    size = rows_in[0].shape[0]
    for at in range(pieces):
        rows[:, pl.ds(at * size, size)] = jnp.transpose(rows_in[at][...])
    steps = pl.num_programs(0) // parts
    for kind in range(kinds):
        array = units[kind][...]
        result = dot(rows[...], array.reshape(array.shape[-2:])).astype(bf16)
        for at in range(parts):

            @pl.when(pl.program_id(0) // steps == at)
            def _():
                outs[kind * parts + at][...] = result


def weight_grads(rows, units, indices=(None,), parts=1):
    pieces, kinds = len(rows), len(units)
    size, width = rows[0].shape
    total, columns = units[0].shape[-2:]
    block = 256 if width // parts % 256 == 0 else LANES
    steps = width // block // parts
    specs = [
        pl.BlockSpec((total, columns), lambda k: (0, 0), pipeline_mode=pl.Buffered(1))
        if index is None
        else pl.BlockSpec(
            (1, total, columns),
            functools.partial(lambda at, k: (at, 0, 0), index),
            pipeline_mode=pl.Buffered(1),
        )
        for index in indices
    ]
    outs = [
        pl.BlockSpec(
            (block, columns),
            functools.partial(lambda at, k: (jnp.clip(k - at * steps, 0, steps - 1), 0), at),
        )
        for _ in range(kinds)
        for at in range(parts)
    ]
    return pl.pallas_call(
        functools.partial(weight_grad_kernel, pieces, kinds, parts),
        grid=(steps * parts,),
        in_specs=[pl.BlockSpec((size, block), lambda k: (0, k))] * pieces + specs,
        out_specs=outs,
        out_shape=[jax.ShapeDtypeStruct((width // parts, columns), bf16)] * (kinds * parts),
        scratch_shapes=[pltpu.VMEM((block, total), bf16)],
        compiler_params=params(28),
        cost_estimate=cost(
            2 * total * width * columns * kinds,
            2 * (total * (width + columns * kinds) + width * columns * kinds),
        ),
        name="weight_grads",
    )(*rows, *units)


def mixed_grad_kernel(place, own, other, keep, taken, out):
    out[0] = (dot(own[...], keep[...], NT) + dot(other[...], taken[...], NT)).astype(bf16)


def mixed_back(place, count, own, other, keep, taken):
    rows = own.shape[0] // count
    units, width = keep.shape
    piece = pl.BlockSpec((rows, width), lambda at, s: (s[at], 0))
    weight = pl.BlockSpec((units, width), lambda at, s: (0, 0))
    return pl.pallas_call(
        mixed_grad_kernel,
        grid_spec=pltpu.PrefetchScalarGridSpec(
            num_scalar_prefetch=1,
            grid=(count,),
            in_specs=[piece, piece, weight, weight],
            out_specs=pl.BlockSpec((1, rows, units), lambda at, s: (at, 0, 0)),
        ),
        out_shape=jax.ShapeDtypeStruct((count, rows, units), bf16),
        compiler_params=params(12),
        cost_estimate=cost(4 * count * rows * width * units, 4 * count * rows * width),
        name="mixed_back",
    )(place, own, other, keep, taken)


def project_back_kernel(swap, core, place, own, other, weight, out, units):
    count, rows = own.shape[1:3]

    @pl.when(pl.program_id(0) == 0)
    def _():
        for kind in range(3):
            for at in range(count):
                ordered(
                    core,
                    own.at[kind, at],
                    other.at[kind, swap[at]],
                    units.at[kind, at],
                    own.shape[3],
                )

    for at in range(count):
        out[row_range(place[at], rows), :] = sum(
            dot(units[kind, at], weight[kind], NT) for kind in range(3)
        ).astype(bf16)


def project_back(core, place, swap, own, other, weight):
    _, count, rows, half = own.shape
    _, width, total = weight.shape
    block = block_of(width)
    whole = lambda k, *s: (0, 0, 0, 0)
    return pl.pallas_call(
        functools.partial(project_back_kernel, swap),
        grid_spec=pltpu.PrefetchScalarGridSpec(
            num_scalar_prefetch=2,
            grid=(width // block,),
            in_specs=[
                pl.BlockSpec((3, count, rows, half), whole),
                pl.BlockSpec((3, count, rows, half), whole),
                pl.BlockSpec((3, block, total), lambda k, *s: (0, k, 0)),
            ],
            out_specs=[
                pl.BlockSpec((count * rows, block), lambda k, *s: (0, k)),
                pl.BlockSpec((3, count, rows, total), whole),
            ],
        ),
        out_shape=[
            jax.ShapeDtypeStruct((count * rows, width), bf16),
            jax.ShapeDtypeStruct((3, count, rows, total), bf16),
        ],
        compiler_params=params(28),
        cost_estimate=cost(6 * count * rows * total * width, 2 * count * rows * (width + 6 * total)),
        name="project_back",
    )(core, place, own, other, weight)


def halves(weight, axis, width):
    lead = lax.slice_in_dim(weight, 0, width, axis=axis)
    rest = lax.slice_in_dim(weight, width, weight.shape[axis], axis=axis)
    pad = [(0, 0)] * weight.ndim
    pad[axis] = (0, width - rest.shape[axis])
    rest = jnp.pad(rest, pad)
    first = lax.axis_index("col") == 0
    return jnp.where(first, lead, rest), jnp.where(first, rest, lead)


def shards(
    block_input,
    norm1_gain,
    norm1_shift,
    qkv_weight,
    qkv_bias,
    out_weight,
    norm2_gain,
    norm2_shift,
    gate_up_weight,
    down_weight,
    output_grad,
):
    count = lax.axis_size("row")
    rows = block_input.shape[0]
    core = lax.axis_index("col").astype(jnp.int32)[None]
    place, swap = places()
    place = place.astype(jnp.int32)
    slot = inverse_places(place)
    half_units = out_weight.shape[0] // 2
    total_hidden = down_weight.shape[0]
    half_hidden = -(-total_hidden // (2 * LANES)) * LANES
    if grid_rows():
        groups = (((2,), 2), ((0, 1), 0), ((3,), 3))
    else:
        groups = tuple(((at,), at) for at in range(count))

    clock = Clock()
    inputs = block_input.astype(f32)
    gain_one = norm1_gain.astype(f32)
    gain_two = norm2_gain.astype(f32)
    hat_one, inverse_one = normalize(inputs)
    normed_one = clock.mark((hat_one * gain_one + norm1_shift.astype(f32)).astype(bf16))

    one_own, fetch = gather_rows(normed_one)
    qkv_keep, qkv_send = halves(clock(qkv_weight), 2, half_units)
    clock.mark(qkv_keep)
    qkv_taken = sibling(qkv_send)
    cosine, sine = rotary_tables(count, rows)
    bias = qkv_bias[:, None, :]
    qkv = None
    for group, index in groups:
        if qkv is not None and len(one_own) < count:
            one_own += fetch(clock.last)
        others = [sibling(clock(one_own[swap[at]])) for at in group]
        qkv = clock.mark(
            project_pieces(
                index, group, count, place, [one_own[at] for at in group], others,
                qkv_keep, qkv_taken, clock(bias), cosine, sine, qkv,
            )
        )
        if group == groups[0][0]:
            gate_up_keep, gate_up_send = halves(clock(gate_up_weight), 2, half_hidden)
            clock.mark(gate_up_keep)
            down_keep, down_send = halves(clock(down_weight), 0, half_hidden)
            clock.mark(down_keep)
            out_keep, out_send = halves(clock(out_weight), 0, half_units)
            clock.mark(out_keep)
    gate_up_taken = sibling(clock(gate_up_send))
    down_taken = sibling(clock(down_send))
    out_taken = sibling(clock(out_send))
    grad_own = gather_whole(after(output_grad, others[-1]))
    mixed, kept, logsum = attend_forward(clock(slot), qkv)
    clock.mark(mixed)
    *branch, mixed_units = mixed_out(clock(core), place, swap, mixed, sibling(mixed), out_weight)
    clock.mark(branch[0])
    branch = scatter_rows(branch, clock)
    grad_other = sibling(clock(grad_own))
    after_rows = inputs + branch
    hat_two, inverse_two = normalize(after_rows)
    normed_two = clock.mark((hat_two * gain_two + norm2_shift.astype(f32)).astype(bf16))

    two_own, fetch = gather_rows(normed_two)
    mine, theirs = [None] * count, [None] * count
    for group, _ in groups:
        if group != groups[0][0] and len(two_own) < count:
            two_own += fetch(clock.last)
        results = hidden_pieces(
            group, clock(place),
            [two_own[at] for at in group],
            [sibling(clock(two_own[swap[at]])) for at in group],
            grad_own, grad_other, gate_up_keep, gate_up_taken, down_keep, down_taken,
        )
        clock.mark(results[0])
        for at, result in zip(group, results):
            mine[at] = result
        for at in group:
            theirs[at] = sibling(mine[swap[at]])

    normed_part, gate_units, up_units = normed_back(clock(core), place, mine, theirs, gate_up_weight)
    clock.mark(normed_part)
    normed_two_grad = scatter_whole(normed_part)
    sums = Line(clock)
    parts = down_grad_parts(clock(core), place, mine, theirs, grad_own, total_hidden)
    down_count = len(parts)
    clock.mark(parts[0])
    sums.add(*parts)
    parts = weight_grads(two_own, [clock(gate_units), up_units], (None, None), 2)
    clock.mark(parts[0])
    sums.add(*parts)
    sums.join()
    down_part = clock.mark(down_out(clock(core), place, mine, theirs, down_weight))
    sums.join()
    sums.total_up()
    normed_two_grad = clock(normed_two_grad)
    after_grad = output_grad.astype(f32) + norm_back(
        normed_two_grad * gain_two, hat_two, inverse_two
    )
    branch_grad = clock.mark(after_grad.astype(bf16))
    branch_own = gather_whole(branch_grad)
    sums.join()
    sums.total_up()
    sums.join()
    sums.total_up()
    down = scatter_whole(after(down_part, branch_own))
    branch_other = sibling(clock(branch_own))
    mixed_grad = clock.mark(
        mixed_back(clock(place), count, branch_own, branch_other, out_keep, out_taken)
    )
    parts = weight_grads([mixed_units.reshape(count * rows, -1)], [clock(branch_own)])
    clock.mark(parts[0])
    sums.add(*parts)
    sums.join()
    sums.total_up()
    project_grad = clock.mark(
        attend_backward(clock(slot), place, qkv, mixed_grad, kept, logsum, cosine, sine)
    )
    project_other = sibling(project_grad)
    sums.join()
    sums.total_up()
    one_part, project_units = project_back(
        clock(core), place, swap, project_grad, project_other, qkv_weight
    )
    clock.mark(one_part)
    normed_one_grad = scatter_whole(one_part)
    project_units = project_units.reshape(3, count * rows, -1)
    parts = weight_grads(one_own, [clock(project_units)] * 3, (0, 1, 2))
    clock.mark(parts[0])
    sums.add(*parts)
    sums.join()
    sums.total_up()
    spots = [(0, at * DOWN_BLOCK) for at in range(down_count)]
    down_grad = sums.settle((1,) + down_weight.shape, spots, LANES)
    block_output = clock.mark((after_rows + clock(down)).astype(bf16))
    bias_grad = jnp.sum(clock(project_grad).astype(f32), axis=(1, 2))
    clock.mark(bias_grad)
    sums.join()
    sums.total_up()
    normed_one_grad = clock(normed_one_grad)
    input_grad = after_grad + norm_back(normed_one_grad * gain_one, hat_one, inverse_one)
    gains = jnp.stack(
        [
            jnp.sum(normed_one_grad * hat_one, axis=0),
            jnp.sum(normed_one_grad, axis=0),
            jnp.sum(normed_two_grad * hat_two, axis=0),
            jnp.sum(normed_two_grad, axis=0),
        ]
    )
    width = gains.shape[1]
    gains = sum_rows(clock.mark(gains), clock)
    input_grad = clock.mark(clock(input_grad))
    half_width = two_own[0].shape[1] // 2
    gate_up_block = block_of(half_width)
    qkv_block = block_of(qkv_weight.shape[1])
    sums.join()
    sums.total_up()
    gate_up_grad = sums.settle(gate_up_weight.shape, ((0, 0), (0, half_width)), gate_up_block)
    sums.add(jnp.concatenate([gains.reshape(-1, LANES), bias_grad.reshape(-1, LANES)], axis=0))
    last = len(sums.parts) - 1
    sums.join()
    sums.total_up()
    gate_up_grad = sums.settle(
        gate_up_weight.shape, ((1, 0), (1, half_width)), gate_up_block, gate_up_grad
    )
    sums.join()
    sums.total_up()
    out_grad = sums.settle((1,) + out_weight.shape, ((0, 0),), block_of(out_weight.shape[0]))
    sums.join()
    sums.total_up()
    qkv_grad = sums.settle(qkv_weight.shape, ((0, 0), (1, 0)), qkv_block)
    sums.total_up()
    qkv_grad = sums.settle(qkv_weight.shape, ((2, 0),), qkv_block, qkv_grad)
    small = sums.small(last)
    gains = small[: 4 * width // LANES].reshape(4, width)
    bias_grad = small[4 * width // LANES :].reshape(bias_grad.shape)
    return (
        block_output,
        input_grad,
        gains[0],
        gains[1],
        qkv_grad,
        bias_grad,
        out_grad[0],
        gains[2],
        gains[3],
        gate_up_grad,
        down_grad[0],
    )


def inverse_places(place):
    spots = jnp.arange(place.shape[0])
    return jnp.sum(
        jnp.where(place[None, :] == spots[:, None], spots[None, :], 0), axis=1
    ).astype(jnp.int32)


def solution(mesh):
    placed = (
        P(("dp", "row"), "col"),
        P("col"),
        P("col"),
        P(None, "col", "row"),
        P(None, ("row", "col")),
        P("row", "col"),
        P("col"),
        P("col"),
        P(None, "col", "row"),
        P("row", "col"),
        P(("dp", "row"), "col"),
    )
    return jax.shard_map(
        shards,
        mesh=mesh,
        in_specs=placed,
        out_specs=(
            P(("dp", "row"), "col"),
            P(("dp", "row"), "col"),
            P("col"),
            P("col"),
            P(None, "col", "row"),
            P(None, ("row", "col")),
            P("row", "col"),
            P("col"),
            P("col"),
            P(None, "col", "row"),
            P("row", "col"),
        ),
        check_vma=False,
    )
```

```python
import functools

import jax
import jax.numpy as jnp
import numpy as np
from jax import lax
from jax.experimental import pallas as pl
from jax.experimental.pallas import tpu as pltpu
from jax.sharding import PartitionSpec as P

HD = 64
ROT = 16
LANES = 128
VMEM = 60 << 20

epsilon = 1e-05
base_rate = 10000.0
bf16 = jnp.bfloat16
f32 = jnp.float32

NN = (((1,), (0,)), ((), ()))
NT = (((1,), (1,)), ((), ()))
TN = (((0,), (0,)), ((), ()))


def dot(first, second, dims=NN):
    return lax.dot_general(first, second, dims, preferred_element_type=f32)


def row_permute(values, core_zero, core_one):
    pairs = [
        (row * 2 + core, (row ^ (core_one if core else core_zero)) * 2 + core)
        for row in range(4)
        for core in range(2)
    ]
    return lax.ppermute(values, ("row", "col"), pairs)


def first_way(values):
    return row_permute(values, 1, 2)


def second_way(values):
    return row_permute(values, 2, 1)


def sibling(values):
    return lax.ppermute(values, "col", [(0, 1), (1, 0)])


def grid_rows():
    return lax.axis_size("row") == 4


def places():
    row, core = lax.axis_index("row"), lax.axis_index("col")
    if grid_rows():
        one = jnp.where(core == 0, 1, 2)
        return jnp.stack([row ^ one, row ^ (3 - one), row, row ^ 3]), (1, 0, 2, 3)
    count = lax.axis_size("row")
    return jnp.arange(count), tuple(range(count))


def after(value, *earlier):
    return lax.optimization_barrier((value,) + earlier)[0]


def gather_rows(own):
    if grid_rows():
        near = first_way(own)
        side = second_way(own)
        return [near, side, own], lambda *earlier: [second_way(after(near, side, *earlier))]
    whole = lax.all_gather(own, "row", axis=0, tiled=True)
    return jnp.split(whole, lax.axis_size("row"), axis=0), lambda *earlier: []


def scatter_rows(parts, clock):
    if grid_rows():
        passing = first_way(parts[3])
        near = first_way(parts[0])
        side = second_way(clock.mark(plus(parts[1], after(clock(passing), near))))
        return parts[2].astype(f32) + near.astype(f32) + side.astype(f32)
    whole = jnp.concatenate(parts, axis=0)
    return lax.psum_scatter(whole, "row", scatter_dimension=0, tiled=True).astype(f32)


def line():
    return lax.axis_size("dp") == 4


def in_middle():
    place = lax.axis_index("dp")
    return (place == 1) | (place == 2)


def inward(part):
    return lax.ppermute(part, "dp", [(0, 1), (3, 2)])


def across(part):
    return lax.ppermute(part, "dp", [(1, 2), (2, 1)])


def outward(part):
    return lax.ppermute(part, "dp", [(1, 0), (2, 3)])


def plus(first, second):
    return (first.astype(f32) + second.astype(f32)).astype(first.dtype)


class Clock:
    def __init__(self):
        self.last = None

    def __call__(self, value):
        return value if self.last is None else after(value, self.last)

    def mark(self, value):
        self.last = value
        return value


class Line:
    def __init__(self, clock):
        self.clock = clock
        self.parts, self.inner, self.half, self.other, self.total, self.outer = ([] for _ in range(6))
        self.settled = 0

    def feed(self):
        at = len(self.inner)
        if at < len(self.parts) and at < len(self.half) + 2:
            part = self.parts[at]
            self.inner.append(inward(after(part, self.inner[at - 2]) if at >= 2 else part))

    def add(self, *parts):
        self.parts += parts
        if line():
            for _ in parts:
                self.feed()

    def join(self):
        if line():
            at = len(self.half)
            left = self.outer[at - 3 : at - 2] if at >= 3 else []
            came = after(self.clock(self.inner[at]), *left)
            self.half.append(self.clock.mark(plus(self.parts[at], came)))
            self.feed()
            ready = self.half[at]
            self.other.append(across(after(ready, self.other[-1]) if self.other else ready))

    def total_up(self):
        if line():
            at = len(self.total)
            self.total.append(self.clock.mark(plus(self.half[at], self.clock(self.other[at]))))
            ready = self.total[at]
            self.outer.append(outward(after(ready, self.outer[-1]) if self.outer else ready))

    def settle(self, shape, places, block, before=None):
        for index, start in places:
            at = self.settled
            self.settled += 1
            if line():
                before = self.clock.mark(
                    settle(shape, index, start, block, self.clock, self.total[at], self.outer[at], before)
                )
            else:
                value = lax.psum(self.parts[at], "dp").astype(f32)[None]
                before = jnp.zeros(shape, f32) if before is None else before
                before = lax.dynamic_update_slice(before, value, (index, start, 0))
        return before

    def small(self, at):
        if line():
            return jnp.where(in_middle(), self.total[at], self.outer[at])
        return lax.psum(self.parts[at], "dp")


def gather_whole(own):
    return lax.all_gather(own, "row", axis=0, tiled=True)


def scatter_whole(parts):
    return lax.psum_scatter(parts, "row", scatter_dimension=0, tiled=True).astype(f32)


def sum_rows(values, clock):
    if grid_rows():
        values = clock.mark(values + clock(first_way(values)))
        return clock.mark(values + clock(second_way(values)))
    return lax.psum(values, "row")


def width_pair(first, second):
    both = jnp.stack([first, second])
    both = both + sibling(both)
    return both[0], both[1]


def normalize(values):
    width = values.shape[1] * lax.axis_size("col")
    totals, squares = width_pair(jnp.sum(values, axis=-1), jnp.sum(values * values, axis=-1))
    average = totals / width
    spread = squares / width - average * average
    inverse = lax.rsqrt(spread + epsilon)[:, None]
    return ((values - average[:, None]) * inverse, inverse)


def norm_back(scaled, normed_hat, inverse):
    width = normed_hat.shape[1] * lax.axis_size("col")
    first, second = width_pair(jnp.sum(scaled, axis=-1), jnp.sum(scaled * normed_hat, axis=-1))
    return inverse * (scaled - first[:, None] / width - normed_hat * second[:, None] / width)


def rotary_tables(count, rows):
    half_dims = ROT // 2
    lane = np.arange(LANES) % HD
    freqs = np.float32(base_rate) ** (-(2.0 * (lane % half_dims).astype(np.float32)) / np.float32(ROT))
    angles = np.arange(count * rows, dtype=np.float32)[:, None] * freqs.astype(np.float32)[None, :]
    turned = lane < ROT
    sign = np.where(lane < half_dims, -1.0, 1.0)
    cosine = np.where(turned, np.cos(angles.astype(np.float64)), 1.0)
    sine = np.where(turned, sign * np.sin(angles.astype(np.float64)), 0.0)
    shape = (count, rows, LANES)
    return jnp.asarray(cosine.reshape(shape), f32), jnp.asarray(sine.reshape(shape), f32)


def turn(values, cosine, sine):
    half_dims = ROT // 2
    lane = lax.broadcasted_iota(jnp.int32, values.shape, 1) % HD
    partner = jnp.where(
        lane < half_dims,
        pltpu.roll(values, LANES - half_dims, 1),
        pltpu.roll(values, half_dims, 1),
    )
    return values * cosine + partner * sine


def params():
    return pltpu.CompilerParams(vmem_limit_bytes=VMEM)


def cost(flops, moved, hard=0):
    return pl.CostEstimate(flops=int(flops), bytes_accessed=int(moved), transcendentals=int(hard))


def project_kernel(members, place, *refs):
    own, other = refs[:members], refs[members : 2 * members]
    keep, taken, bias = refs[2 * members : 2 * members + 3]
    cosine, sine = refs[2 * members + 3 : 3 * members + 3], refs[3 * members + 3 : 4 * members + 3]
    out = refs[-1]
    kind = pl.program_id(0)
    for at in range(members):
        result = dot(own[at][...], keep[0]) + dot(other[at][...], taken[0]) + bias[0].astype(f32)

        @pl.when(kind < 2)
        def _():
            for start in range(0, result.shape[1], LANES):
                part = slice(start, start + LANES)
                out[at, 0, :, part] = turn(result[:, part], cosine[at][0], sine[at][0]).astype(bf16)

        @pl.when(kind == 2)
        def _():
            out[at, 0] = result.astype(bf16)


def project_pieces(index, group, count, place, own, other, keep, taken, bias, cosine, sine, before):
    members = len(own)
    rows, width = own[0].shape
    units = keep.shape[2]
    piece = pl.BlockSpec((rows, width), lambda k, s: (0, 0), pipeline_mode=pl.Buffered(1))
    tables = [
        pl.BlockSpec((1, rows, LANES), functools.partial(lambda at, k, s: (s[at], 0, 0), at))
        for at in group
    ]
    weight = pl.BlockSpec((1, width, units), lambda k, s: (k, 0, 0))
    in_specs = [piece] * (2 * members) + [
        weight,
        weight,
        pl.BlockSpec((1, 1, units), lambda k, s: (k, 0, 0)),
        *tables,
        *tables,
    ]
    args = [*own, *other, keep, taken, bias] + [cosine] * members + [sine] * members
    aliases = {}
    if before is not None:
        aliases = {len(args) + 1: 0}
        in_specs.append(pl.BlockSpec(memory_space=pl.ANY))
        args.append(before)
    return pl.pallas_call(
        functools.partial(project_kernel, members),
        grid_spec=pltpu.PrefetchScalarGridSpec(
            num_scalar_prefetch=1,
            grid=(3,),
            in_specs=in_specs,
            out_specs=pl.BlockSpec((members, 1, rows, units), lambda k, s: (index, k, 0, 0)),
        ),
        out_shape=jax.ShapeDtypeStruct((count, 3, rows, units), bf16),
        input_output_aliases=aliases,
        compiler_params=params(),
        cost_estimate=cost(
            12 * members * rows * width * units, 4 * members * rows * width + 12 * width * units
        ),
        name="project_pieces",
    )(place, *args)


def causal(rows):
    keys = lax.broadcasted_iota(jnp.int32, (rows, rows), 0)
    return keys <= lax.broadcasted_iota(jnp.int32, (rows, rows), 1)


def head_lanes(values, head):
    lane = lax.broadcasted_iota(jnp.int32, values.shape, 1)
    return jnp.where((lane >= head * HD) & (lane < (head + 1) * HD), values, jnp.zeros_like(values))


def walk(stop, body, carry):
    if isinstance(stop, int):
        for step in range(stop):
            carry = body(step, carry)
        return carry
    return lax.fori_loop(0, stop, body, carry)


def each(count, body):
    if count <= 4:
        for step in range(count):
            body(step)
    else:
        lax.fori_loop(0, count, lambda step, carry: (body(step), carry)[1], 0)


def row_range(step, rows):
    return pl.ds(step * rows if isinstance(step, int) else pl.multiple_of(step * rows, rows), rows)


def attend_kernel(slot, qkv, mixed, kept, logsum, scores):
    count, _, rows, _ = qkv.shape
    heads = LANES // HD
    scale = HD**-0.5

    def one(at):
        here = slot[at]
        query = qkv[here, 0] * jnp.asarray(scale, bf16)
        for head in range(heads):

            def look(past, highest):
                block = dot(head_lanes(qkv[slot[past], 1], head), query, NT)
                scores[row_range(past, rows), :] = block
                return jnp.maximum(highest, jnp.max(block, axis=0, keepdims=True))

            def add(past, carry):
                total, outs = carry
                weights = jnp.exp(scores[row_range(past, rows), :] - highest)
                total = total + jnp.sum(weights, axis=0, keepdims=True)
                value = jnp.transpose(qkv[slot[past], 2])[head * HD : (head + 1) * HD]
                return total, outs + dot(value, weights.astype(bf16))

            block = dot(head_lanes(qkv[here, 1], head), query, NT)
            block = jnp.where(causal(rows), block, -1e30)
            scores[row_range(at, rows), :] = block
            highest = walk(at, look, jnp.max(block, axis=0, keepdims=True))
            total, outs = walk(
                at + 1, add, (jnp.zeros((1, rows), f32), jnp.zeros((HD, rows), f32))
            )
            kept[0, here, pl.ds(head * HD, HD), :] = outs / total
            logsum[0, here, pl.ds(head, 1), :] = highest + jnp.log(total)
        mixed[here] = jnp.transpose(kept[0, here]).astype(bf16)

    each(count, one)


def attend_forward(slot, qkv):
    count, _, rows, units = qkv.shape
    pairs = units // LANES
    work = rows * rows * count * (count + 1) // 2 * units
    return pl.pallas_call(
        attend_kernel,
        grid_spec=pltpu.PrefetchScalarGridSpec(
            num_scalar_prefetch=1,
            grid=(pairs,),
            in_specs=[pl.BlockSpec((count, 3, rows, LANES), lambda p, s: (0, 0, 0, p))],
            out_specs=[
                pl.BlockSpec((count, rows, LANES), lambda p, s: (0, 0, p)),
                pl.BlockSpec((1, count, LANES, rows), lambda p, s: (p, 0, 0, 0)),
                pl.BlockSpec((1, count, 8, rows), lambda p, s: (p, 0, 0, 0)),
            ],
            scratch_shapes=[pltpu.VMEM((count * rows, rows), f32)],
        ),
        out_shape=[
            jax.ShapeDtypeStruct((count, rows, units), bf16),
            jax.ShapeDtypeStruct((pairs, count, LANES, rows), f32),
            jax.ShapeDtypeStruct((pairs, count, 8, rows), f32),
        ],
        compiler_params=params(),
        cost_estimate=cost(16 * work, 16 * count * rows * units, work // HD),
        name="attend_forward",
    )(slot, qkv)


def attend_back_kernel(slot, place, qkv, grads, kept, logsum, cosine, sine, out, dq, dk, dv, inner):
    count, _, rows, _ = qkv.shape
    heads = LANES // HD
    scale = HD**-0.5
    dk[...] = jnp.zeros_like(dk)
    dv[...] = jnp.zeros_like(dv)

    def sums(at):
        product = jnp.transpose(grads[at].astype(f32)) * kept[0, at]
        for head in range(heads):
            part = product[head * HD : (head + 1) * HD]
            inner[at, pl.ds(head, 1), :] = jnp.sum(part, axis=0, keepdims=True)

    def one(at):
        here = slot[at]
        query = qkv[here, 0] * jnp.asarray(scale, bf16)
        grad = grads[here]
        for head in range(heads):
            query_head = head_lanes(query, head)
            grad_head = head_lanes(grad, head)

            def look(past, query_grad, last=False):
                there = slot[past]
                key = qkv[there, 1]
                block = dot(key, query_head, NT)
                weights = jnp.exp(block - logsum[0, here, pl.ds(head, 1), :])
                if last:
                    weights = jnp.where(causal(rows), weights, 0.0)
                moved = dot(qkv[there, 2], grad_head, NT)
                raw = (weights * (moved - inner[here, pl.ds(head, 1), :])).astype(bf16)
                dv[there] += dot(weights.astype(bf16), grad_head)
                dk[there] += dot(raw, query_head)
                turned = jnp.transpose(key)[head * HD : (head + 1) * HD]
                return query_grad + dot(turned, raw)

            query_grad = walk(at, look, jnp.zeros((HD, rows), f32))
            dq[pl.ds(head * HD, HD), :] = look(at, query_grad, True) * scale
        out[0, here] = turn(jnp.transpose(dq[...]), cosine[at], -sine[at]).astype(bf16)

    def finish(at):
        out[1, at] = turn(dk[at], cosine[place[at]], -sine[place[at]]).astype(bf16)
        out[2, at] = dv[at].astype(bf16)

    each(count, sums)
    each(count, one)
    each(count, finish)


def attend_backward(slot, place, qkv, grads, kept, logsum, cosine, sine):
    count, _, rows, units = qkv.shape
    pairs = units // LANES
    work = rows * rows * count * (count + 1) // 2 * units
    table = pl.BlockSpec((count, rows, LANES), lambda p, *s: (0, 0, 0))
    return pl.pallas_call(
        attend_back_kernel,
        grid_spec=pltpu.PrefetchScalarGridSpec(
            num_scalar_prefetch=2,
            grid=(pairs,),
            in_specs=[
                pl.BlockSpec((count, 3, rows, LANES), lambda p, *s: (0, 0, 0, p)),
                pl.BlockSpec((count, rows, LANES), lambda p, *s: (0, 0, p)),
                pl.BlockSpec((1, count, LANES, rows), lambda p, *s: (p, 0, 0, 0)),
                pl.BlockSpec((1, count, 8, rows), lambda p, *s: (p, 0, 0, 0)),
                table,
                table,
            ],
            out_specs=pl.BlockSpec((3, count, rows, LANES), lambda p, *s: (0, 0, 0, p)),
            scratch_shapes=[
                pltpu.VMEM((LANES, rows), f32),
                pltpu.VMEM((count, rows, LANES), f32),
                pltpu.VMEM((count, rows, LANES), f32),
                pltpu.VMEM((count, 8, rows), f32),
            ],
        ),
        out_shape=jax.ShapeDtypeStruct((3, count, rows, units), bf16),
        compiler_params=params(),
        cost_estimate=cost(40 * work, 24 * count * rows * units, work // HD),
        name="attend_backward",
    )(slot, place, qkv, grads, kept, logsum, cosine, sine)


def ordered(core, own, other, out, width):
    rest = out.shape[-1] - width
    lead = core[0] == 0
    out[..., :width] = jnp.where(lead, own[...], other[...])
    out[..., width:] = jnp.where(lead, other[..., :rest], own[..., :rest])


def block_of(width):
    return 256 if width % 256 == 0 else LANES


def mixed_out_kernel(swap, core, place, own, other, weight, *outs):
    units = outs[-1]
    count = own.shape[0]

    @pl.when(pl.program_id(0) == 0)
    def _():
        for at in range(count):
            ordered(core, own.at[at], other.at[swap[at]], units.at[place[at]], own.shape[2])

    for at in range(count):
        outs[at][...] = dot(units[place[at]], weight[...]).astype(bf16)


def mixed_out(core, place, swap, own, other, weight):
    count, rows, units = own.shape
    width = weight.shape[1]
    block = block_of(width)
    whole = lambda k, *s: (0, 0, 0)
    return pl.pallas_call(
        functools.partial(mixed_out_kernel, swap),
        grid_spec=pltpu.PrefetchScalarGridSpec(
            num_scalar_prefetch=2,
            grid=(width // block,),
            in_specs=[
                pl.BlockSpec((count, rows, units), whole),
                pl.BlockSpec((count, rows, units), whole),
                pl.BlockSpec((2 * units, block), lambda k, *s: (0, k)),
            ],
            out_specs=[pl.BlockSpec((rows, block), lambda k, *s: (0, k))] * count
            + [pl.BlockSpec((count, rows, 2 * units), whole)],
        ),
        out_shape=[jax.ShapeDtypeStruct((rows, width), bf16)] * count
        + [jax.ShapeDtypeStruct((count, rows, 2 * units), bf16)],
        compiler_params=params(),
        cost_estimate=cost(4 * count * rows * units * width, 2 * count * rows * (width + 4 * units)),
        name="mixed_out",
    )(core, place, own, other, weight)


def hidden_kernel(members, place, *refs):
    own, other, grad_own, grad_other = (refs[k * members : (k + 1) * members] for k in range(4))
    gate_up, taken, down, down_taken = refs[4 * members : 4 * members + 4]
    outs = refs[4 * members + 4 :]
    for at in range(members):
        gate = dot(own[at][...], gate_up[0]) + dot(other[at][...], taken[0])
        up = dot(own[at][...], gate_up[1]) + dot(other[at][...], taken[1])
        grad = dot(grad_own[at][...], down[...], NT) + dot(grad_other[at][...], down_taken[...], NT)
        sigmoid = jax.nn.sigmoid(gate)
        silu = gate * sigmoid
        slope = sigmoid * (1.0 + gate * (1.0 - sigmoid))
        outs[at][0] = (grad * up * slope).astype(bf16)
        outs[at][1] = (grad * silu).astype(bf16)
        outs[at][2] = (silu * up).astype(bf16)


def hidden_pieces(group, place, own, other, grad_own, grad_other, gate_up, taken, down, down_taken):
    members = len(own)
    rows, width = own[0].shape
    units = gate_up.shape[2]
    block = block_of(units)
    rows_in = pl.BlockSpec((rows, width), lambda k, s: (0, 0), pipeline_mode=pl.Buffered(1))
    grads = [
        pl.BlockSpec(
            (rows, width),
            functools.partial(lambda at, k, s: (s[at], 0), at),
            pipeline_mode=pl.Buffered(1),
        )
        for at in group
    ]
    entry = pl.BlockSpec((2, width, block), lambda k, s: (0, 0, k))
    leave = pl.BlockSpec((block, width), lambda k, s: (k, 0))
    return pl.pallas_call(
        functools.partial(hidden_kernel, members),
        grid_spec=pltpu.PrefetchScalarGridSpec(
            num_scalar_prefetch=1,
            grid=(units // block,),
            in_specs=[rows_in] * (2 * members) + grads + grads + [entry, entry, leave, leave],
            out_specs=[pl.BlockSpec((3, rows, block), lambda k, s: (0, 0, k))] * members,
        ),
        out_shape=[jax.ShapeDtypeStruct((3, rows, units), bf16)] * members,
        compiler_params=params(),
        cost_estimate=cost(
            12 * members * rows * width * units, 12 * width * units + 8 * members * rows * width
        ),
        name="hidden_pieces",
    )(
        place, *own, *other, *([grad_own] * members), *([grad_other] * members),
        gate_up, taken, down, down_taken,
    )


def down_grad_kernel(count, second_steps, core, place, *refs):
    own, other, grads = refs[:count], refs[count : 2 * count], refs[2 * count]
    first, second, units = refs[-3:]
    rows = own[0].shape[1]
    lead = core[0] == 0

    def part(mine, out):
        for at in range(count):
            units[row_range(place[at], rows), :] = jnp.where(mine, own[at][0], other[at][0])
        out[...] = dot(units[...], grads[...], TN).astype(bf16)

    part(lead, first)

    @pl.when(pl.program_id(0) < second_steps)
    def _():
        part(jnp.logical_not(lead), second)


def down_grad_parts(core, place, own, other, grads, total):
    count = len(own)
    _, rows, half = own[0].shape
    width = grads.shape[1]
    block = 384
    rest = total - half
    second_steps = -(-rest // block)
    piece = pl.BlockSpec((1, rows, block), lambda k, *s: (2, 0, k))
    return pl.pallas_call(
        functools.partial(down_grad_kernel, count, second_steps),
        grid_spec=pltpu.PrefetchScalarGridSpec(
            num_scalar_prefetch=2,
            grid=(half // block,),
            in_specs=[piece] * (2 * count)
            + [pl.BlockSpec(grads.shape, lambda k, *s: (0, 0), pipeline_mode=pl.Buffered(1))],
            out_specs=[
                pl.BlockSpec((block, width), lambda k, *s: (k, 0)),
                pl.BlockSpec((block, width), lambda k, *s: (jnp.minimum(k, second_steps - 1), 0)),
            ],
            scratch_shapes=[pltpu.VMEM((count * rows, block), bf16)],
        ),
        out_shape=[
            jax.ShapeDtypeStruct((half, width), bf16),
            jax.ShapeDtypeStruct((rest, width), bf16),
        ],
        compiler_params=params(),
        cost_estimate=cost(
            2 * count * rows * total * width, 2 * count * rows * (width + 2 * half) + 2 * total * width
        ),
        name="down_grad_parts",
    )(core, place, *own, *other, grads)


def normed_back_kernel(count, core, place, *refs):
    own, other, gate_up = refs[:count], refs[count : 2 * count], refs[2 * count]
    out, gate, up = refs[-3:]
    rows = own[0].shape[1]

    @pl.when(pl.program_id(0) == 0)
    def _():
        for at in range(count):
            span = pl.ds(at * rows, rows)
            for kind, units in ((0, gate), (1, up)):
                ordered(
                    core, own[at].at[kind], other[at].at[kind], units.at[span], own[0].shape[2]
                )

    for at in range(count):
        span = pl.ds(at * rows, rows)
        out[row_range(place[at], rows), :] = (
            dot(gate[span, :], gate_up[0], NT) + dot(up[span, :], gate_up[1], NT)
        ).astype(bf16)


def normed_back(core, place, own, other, gate_up):
    count = len(own)
    _, rows, half = own[0].shape
    _, width, total = gate_up.shape
    block = block_of(width)
    once = pl.Buffered(1)
    units = pl.BlockSpec((count * rows, total), lambda k, *s: (0, 0), pipeline_mode=once)
    units_shape = jax.ShapeDtypeStruct((count * rows, total), bf16)
    return pl.pallas_call(
        functools.partial(normed_back_kernel, count),
        grid_spec=pltpu.PrefetchScalarGridSpec(
            num_scalar_prefetch=2,
            grid=(width // block,),
            in_specs=[pl.BlockSpec((2, rows, half), lambda k, *s: (0, 0, 0), pipeline_mode=once)]
            * (2 * count)
            + [pl.BlockSpec((2, block, total), lambda k, *s: (0, k, 0))],
            out_specs=[
                pl.BlockSpec((count * rows, block), lambda k, *s: (0, k)),
                units,
                units,
            ],
        ),
        out_shape=[
            jax.ShapeDtypeStruct((count * rows, width), bf16),
            units_shape,
            units_shape,
        ],
        compiler_params=params(),
        cost_estimate=cost(
            4 * count * rows * width * total, 4 * width * total + 8 * count * rows * total
        ),
        name="normed_back",
    )(core, place, *own, *other, gate_up)


def down_out_kernel(count, core, place, *refs):
    own, other, down = refs[:count], refs[count : 2 * count], refs[2 * count]
    out, units = refs[-2:]
    rows = own[0].shape[1]

    @pl.when(pl.program_id(0) == 0)
    def _():
        for at in range(count):
            ordered(core, own[at].at[0], other[at].at[0], units.at[at], own[at].shape[2])

    for at in range(count):
        out[row_range(place[at], rows), :] = dot(units[at], down[...]).astype(bf16)


def down_out(core, place, own, other, down):
    count = len(own)
    _, rows, half = own[0].shape
    total, width = down.shape
    block = block_of(width)
    piece = pl.BlockSpec((1, rows, half), lambda k, *s: (2, 0, 0), pipeline_mode=pl.Buffered(1))
    return pl.pallas_call(
        functools.partial(down_out_kernel, count),
        grid_spec=pltpu.PrefetchScalarGridSpec(
            num_scalar_prefetch=2,
            grid=(width // block,),
            in_specs=[piece] * (2 * count) + [pl.BlockSpec((total, block), lambda k, *s: (0, k))],
            out_specs=pl.BlockSpec((count * rows, block), lambda k, *s: (0, k)),
            scratch_shapes=[pltpu.VMEM((count, rows, total), bf16)],
        ),
        out_shape=jax.ShapeDtypeStruct((count * rows, width), bf16),
        compiler_params=params(),
        cost_estimate=cost(
            2 * count * rows * total * width, 2 * total * width + 4 * count * rows * total
        ),
        name="down_out",
    )(core, place, *own, *other, down)


def settle_kernel(middle, total, moved, *rest):
    rest[-1][0] = jnp.where(middle[0] == 1, total[...], moved[...]).astype(f32)


def settle(shape, index, start, block, clock, total, moved, before):
    rows, width = total.shape
    middle = clock(in_middle().astype(jnp.int32)[None])
    piece = pl.BlockSpec((block, width), lambda k, s: (k, 0))
    in_specs, args, aliases = [piece, piece], [total, moved], {}
    if before is not None:
        in_specs.append(pl.BlockSpec(memory_space=pl.ANY))
        args.append(before)
        aliases = {3: 0}
    return pl.pallas_call(
        settle_kernel,
        grid_spec=pltpu.PrefetchScalarGridSpec(
            num_scalar_prefetch=1,
            grid=(rows // block,),
            in_specs=in_specs,
            out_specs=pl.BlockSpec((1, block, width), lambda k, s: (index, start // block + k, 0)),
        ),
        out_shape=jax.ShapeDtypeStruct(shape, f32),
        input_output_aliases=aliases,
        compiler_params=params(),
        cost_estimate=cost(0, 8 * rows * width),
        name="settle",
    )(middle, *args)


def weight_grad_kernel(pieces, kinds, parts, stacked, *refs):
    rows_in, units = refs[:pieces], refs[pieces : pieces + kinds]
    outs, rows = refs[pieces + kinds : -1], refs[-1]
    size = rows_in[0].shape[0]
    for at in range(pieces):
        rows[:, pl.ds(at * size, size)] = jnp.transpose(rows_in[at][...])
    steps = pl.num_programs(0) // parts
    for kind in range(kinds):
        array = units[kind][...]
        result = dot(rows[...], array.reshape(array.shape[-2:])).astype(bf16)
        if stacked:
            outs[0][kind] = result
            continue
        for at in range(parts):

            @pl.when(pl.program_id(0) // steps == at)
            def _():
                outs[kind * parts + at][...] = result


def weight_grads(rows, units, indices=(None,), parts=1, stacked=False):
    pieces, kinds = len(rows), len(units)
    size, width = rows[0].shape
    total, columns = units[0].shape[-2:]
    block = 256 if width // parts % 256 == 0 else LANES
    steps = width // block // parts
    specs = [
        pl.BlockSpec((total, columns), lambda k: (0, 0), pipeline_mode=pl.Buffered(1))
        if index is None
        else pl.BlockSpec(
            (1, total, columns),
            functools.partial(lambda at, k: (at, 0, 0), index),
            pipeline_mode=pl.Buffered(1),
        )
        for index in indices
    ]
    outs = [
        pl.BlockSpec(
            (block, columns),
            functools.partial(lambda at, k: (jnp.clip(k - at * steps, 0, steps - 1), 0), at),
        )
        for _ in range(kinds)
        for at in range(parts)
    ]
    shapes = [jax.ShapeDtypeStruct((width // parts, columns), bf16)] * (kinds * parts)
    if stacked:
        outs = [pl.BlockSpec((kinds, block, columns), lambda k: (0, k, 0))]
        shapes = [jax.ShapeDtypeStruct((kinds, width, columns), bf16)]
    return pl.pallas_call(
        functools.partial(weight_grad_kernel, pieces, kinds, parts, stacked),
        grid=(steps * parts,),
        in_specs=[pl.BlockSpec((size, block), lambda k: (0, k))] * pieces + specs,
        out_specs=outs,
        out_shape=shapes,
        scratch_shapes=[pltpu.VMEM((block, total), bf16)],
        compiler_params=params(),
        cost_estimate=cost(
            2 * total * width * columns * kinds,
            2 * (total * (width + columns * kinds) + width * columns * kinds),
        ),
        name="weight_grads",
    )(*rows, *units)


def mixed_grad_kernel(place, own, other, keep, taken, out):
    out[0] = (dot(own[...], keep[...], NT) + dot(other[...], taken[...], NT)).astype(bf16)


def mixed_back(place, count, own, other, keep, taken):
    rows = own.shape[0] // count
    units, width = keep.shape
    piece = pl.BlockSpec((rows, width), lambda at, s: (s[at], 0))
    weight = pl.BlockSpec((units, width), lambda at, s: (0, 0))
    return pl.pallas_call(
        mixed_grad_kernel,
        grid_spec=pltpu.PrefetchScalarGridSpec(
            num_scalar_prefetch=1,
            grid=(count,),
            in_specs=[piece, piece, weight, weight],
            out_specs=pl.BlockSpec((1, rows, units), lambda at, s: (at, 0, 0)),
        ),
        out_shape=jax.ShapeDtypeStruct((count, rows, units), bf16),
        compiler_params=params(),
        cost_estimate=cost(4 * count * rows * width * units, 4 * count * rows * width),
        name="mixed_back",
    )(place, own, other, keep, taken)


def project_back_kernel(swap, core, own, other, weight, *outs):
    units = outs[-1]
    count = own.shape[1]

    @pl.when(pl.program_id(0) == 0)
    def _():
        for kind in range(3):
            for at in range(count):
                ordered(
                    core,
                    own.at[kind, at],
                    other.at[kind, swap[at]],
                    units.at[kind, at],
                    own.shape[3],
                )

    for at in range(count):
        outs[at][...] = sum(
            dot(units[kind, at], weight[kind], NT) for kind in range(3)
        ).astype(bf16)


def project_back(core, swap, own, other, weight):
    _, count, rows, half = own.shape
    _, width, total = weight.shape
    block = block_of(width)
    whole = lambda k, *s: (0, 0, 0, 0)
    return pl.pallas_call(
        functools.partial(project_back_kernel, swap),
        grid_spec=pltpu.PrefetchScalarGridSpec(
            num_scalar_prefetch=1,
            grid=(width // block,),
            in_specs=[
                pl.BlockSpec((3, count, rows, half), whole),
                pl.BlockSpec((3, count, rows, half), whole),
                pl.BlockSpec((3, block, total), lambda k, *s: (0, k, 0)),
            ],
            out_specs=[pl.BlockSpec((rows, block), lambda k, *s: (0, k))] * count
            + [pl.BlockSpec((3, count, rows, total), whole)],
        ),
        out_shape=[jax.ShapeDtypeStruct((rows, width), bf16)] * count
        + [jax.ShapeDtypeStruct((3, count, rows, total), bf16)],
        compiler_params=params(),
        cost_estimate=cost(6 * count * rows * total * width, 2 * count * rows * (width + 6 * total)),
        name="project_back",
    )(core, own, other, weight)


def halves(weight, axis, width):
    lead = lax.slice_in_dim(weight, 0, width, axis=axis)
    rest = lax.slice_in_dim(weight, width, weight.shape[axis], axis=axis)
    pad = [(0, 0)] * weight.ndim
    pad[axis] = (0, width - rest.shape[axis])
    rest = jnp.pad(rest, pad)
    first = lax.axis_index("col") == 0
    return jnp.where(first, lead, rest), jnp.where(first, rest, lead)


def shards(
    block_input,
    norm1_gain,
    norm1_shift,
    qkv_weight,
    qkv_bias,
    out_weight,
    norm2_gain,
    norm2_shift,
    gate_up_weight,
    down_weight,
    output_grad,
):
    count = lax.axis_size("row")
    rows = block_input.shape[0]
    core = lax.axis_index("col").astype(jnp.int32)[None]
    place, swap = places()
    place = place.astype(jnp.int32)
    slot = inverse_places(place)
    half_units = out_weight.shape[0] // 2
    total_hidden = down_weight.shape[0]
    half_hidden = -(-total_hidden // (2 * LANES)) * LANES
    if grid_rows():
        groups = (((2,), 2), ((0, 1), 0), ((3,), 3))
    else:
        groups = tuple(((at,), at) for at in range(count))

    clock = Clock()
    inputs = block_input.astype(f32)
    gain_one = norm1_gain.astype(f32)
    gain_two = norm2_gain.astype(f32)
    hat_one, inverse_one = normalize(inputs)
    normed_one = clock.mark((hat_one * gain_one + norm1_shift.astype(f32)).astype(bf16))

    one_own, fetch = gather_rows(normed_one)
    grad_own = None if grid_rows() else gather_whole(output_grad)
    qkv_keep, qkv_send = halves(clock(qkv_weight), 2, half_units)
    clock.mark(qkv_keep)
    qkv_taken = sibling(qkv_send)
    cosine, sine = rotary_tables(count, rows)
    bias = qkv_bias[:, None, :]
    qkv = None
    for group, index in groups:
        if qkv is not None and len(one_own) < count:
            grad_own = gather_whole(after(output_grad, one_own[0], one_own[1], clock.last))
            one_own += fetch(clock.last)
        others = [sibling(clock(one_own[swap[at]])) for at in group]
        qkv = clock.mark(
            project_pieces(
                index, group, count, place, [one_own[at] for at in group], others,
                qkv_keep, qkv_taken, clock(bias), cosine, sine, qkv,
            )
        )
        if group == groups[0][0]:
            gate_up_keep, gate_up_send = halves(clock(gate_up_weight), 2, half_hidden)
            clock.mark(gate_up_keep)
            down_keep, down_send = halves(clock(down_weight), 0, half_hidden)
            clock.mark(down_keep)
            out_keep, out_send = halves(clock(out_weight), 0, half_units)
            clock.mark(out_keep)
    gate_up_taken = sibling(clock(gate_up_send))
    down_taken = sibling(clock(down_send))
    out_taken = sibling(clock(out_send))
    mixed, kept, logsum = attend_forward(clock(slot), qkv)
    clock.mark(mixed)
    *branch, mixed_units = mixed_out(clock(core), place, swap, mixed, sibling(mixed), out_weight)
    clock.mark(branch[0])
    branch = scatter_rows(branch, clock)
    grad_other = sibling(clock(grad_own))
    after_rows = inputs + branch
    hat_two, inverse_two = normalize(after_rows)
    normed_two = clock.mark((hat_two * gain_two + norm2_shift.astype(f32)).astype(bf16))

    two_own, fetch = gather_rows(normed_two)
    mine, theirs = [None] * count, [None] * count
    for group, _ in groups:
        if group != groups[0][0] and len(two_own) < count:
            two_own += fetch(clock.last)
        results = hidden_pieces(
            group, clock(place),
            [two_own[at] for at in group],
            [sibling(clock(two_own[swap[at]])) for at in group],
            grad_own, grad_other, gate_up_keep, gate_up_taken, down_keep, down_taken,
        )
        clock.mark(results[0])
        for at, result in zip(group, results):
            mine[at] = result
        for at in group:
            theirs[at] = sibling(mine[swap[at]])

    normed_part, gate_units, up_units = normed_back(clock(core), place, mine, theirs, gate_up_weight)
    clock.mark(normed_part)
    normed_two_grad = scatter_whole(normed_part)
    sums = Line(clock)
    parts = down_grad_parts(clock(core), place, mine, theirs, grad_own, total_hidden)
    clock.mark(parts[0])
    sums.add(*parts)
    parts = weight_grads(two_own, [clock(gate_units), up_units], (None, None), 2)
    clock.mark(parts[0])
    sums.add(*parts)
    sums.join()
    down_part = clock.mark(down_out(clock(core), place, mine, theirs, down_weight))
    normed_two_grad = clock(normed_two_grad)
    after_grad = output_grad.astype(f32) + norm_back(
        normed_two_grad * gain_two, hat_two, inverse_two
    )
    branch_grad = clock.mark(after_grad.astype(bf16))
    branch_own = gather_whole(branch_grad)
    sums.join()
    sums.total_up()
    sums.join()
    sums.total_up()
    down = scatter_whole(after(down_part, branch_own))
    branch_other = sibling(clock(branch_own))
    mixed_grad = clock.mark(
        mixed_back(clock(place), count, branch_own, branch_other, out_keep, out_taken)
    )
    parts = weight_grads([mixed_units.reshape(count * rows, -1)], [clock(branch_own)])
    clock.mark(parts[0])
    sums.add(*parts)
    project_grad = clock.mark(
        attend_backward(clock(slot), place, qkv, mixed_grad, kept, logsum, cosine, sine)
    )
    project_other = sibling(project_grad)
    sums.join()
    sums.total_up()
    *one_parts, project_units = project_back(
        clock(core), swap, project_grad, project_other, qkv_weight
    )
    clock.mark(one_parts[0])
    block_output = clock.mark((after_rows + clock(down)).astype(bf16))
    project_units = project_units.reshape(3, count * rows, -1)
    parts = weight_grads(one_own, [clock(project_units)] * 3, (0, 1, 2), stacked=True)
    qkv_grad = lax.psum(clock.mark(parts[0]), "dp")
    normed_one_grad = clock.mark(scatter_rows(one_parts, clock))
    sums.join()
    sums.total_up()
    input_grad = after_grad + norm_back(normed_one_grad * gain_one, hat_one, inverse_one)
    gains = jnp.stack(
        [
            jnp.sum(normed_one_grad * hat_one, axis=0),
            jnp.sum(normed_one_grad, axis=0),
            jnp.sum(normed_two_grad * hat_two, axis=0),
            jnp.sum(normed_two_grad, axis=0),
        ]
    )
    width = gains.shape[1]
    gains = sum_rows(clock.mark(gains), clock)
    input_grad = clock.mark(clock(input_grad))
    bias_grad = jnp.sum(clock(project_grad).astype(f32), axis=(1, 2))
    clock.mark(bias_grad)
    sums.join()
    sums.total_up()
    sums.add(jnp.concatenate([gains.reshape(-1, LANES), bias_grad.reshape(-1, LANES)], axis=0))
    last = len(sums.parts) - 1
    half_width = two_own[0].shape[1] // 2
    gate_up_block = block_of(half_width)
    sums.join()
    sums.total_up()
    down_grad = sums.settle((1,) + down_weight.shape, ((0, 0), (0, half_hidden)), LANES)
    sums.join()
    sums.total_up()
    gate_up_grad = sums.settle(
        gate_up_weight.shape, ((0, 0), (0, half_width), (1, 0)), gate_up_block
    )
    sums.total_up()
    gate_up_grad = sums.settle(gate_up_weight.shape, ((1, half_width),), gate_up_block, gate_up_grad)
    out_grad = sums.settle((1,) + out_weight.shape, ((0, 0),), block_of(out_weight.shape[0]))
    qkv_grad = clock(qkv_grad).astype(f32)
    small = sums.small(last)
    gains = small[: 4 * width // LANES].reshape(4, width)
    bias_grad = small[4 * width // LANES :].reshape(bias_grad.shape)
    return (
        block_output,
        input_grad,
        gains[0],
        gains[1],
        qkv_grad,
        bias_grad,
        out_grad[0],
        gains[2],
        gains[3],
        gate_up_grad,
        down_grad[0],
    )


def inverse_places(place):
    spots = jnp.arange(place.shape[0])
    return jnp.sum(
        jnp.where(place[None, :] == spots[:, None], spots[None, :], 0), axis=1
    ).astype(jnp.int32)


def solution(mesh):
    placed = (
        P(("dp", "row"), "col"),
        P("col"),
        P("col"),
        P(None, "col", "row"),
        P(None, ("row", "col")),
        P("row", "col"),
        P("col"),
        P("col"),
        P(None, "col", "row"),
        P("row", "col"),
        P(("dp", "row"), "col"),
    )
    return jax.shard_map(
        shards,
        mesh=mesh,
        in_specs=placed,
        out_specs=(
            P(("dp", "row"), "col"),
            P(("dp", "row"), "col"),
            P("col"),
            P("col"),
            P(None, "col", "row"),
            P(None, ("row", "col")),
            P("row", "col"),
            P("col"),
            P("col"),
            P(None, "col", "row"),
            P("row", "col"),
        ),
        check_vma=False,
    )
```

```python
import functools

import jax
import jax.numpy as jnp
import numpy as np
from jax import lax
from jax.experimental import pallas as pl
from jax.experimental.pallas import tpu as pltpu
from jax.sharding import PartitionSpec as P

HD = 64
ROT = 16
LANES = 128

epsilon = 1e-05
base_rate = 10000.0
bf16 = jnp.bfloat16
f32 = jnp.float32

NN = (((1,), (0,)), ((), ()))
NT = (((1,), (1,)), ((), ()))
TN = (((0,), (0,)), ((), ()))


def dot(first, second, dims=NN):
    return lax.dot_general(first, second, dims, preferred_element_type=f32)


def row_permute(values, core_zero, core_one):
    pairs = [
        (row * 2 + core, (row ^ (core_one if core else core_zero)) * 2 + core)
        for row in range(4)
        for core in range(2)
    ]
    return lax.ppermute(values, ("row", "col"), pairs)


def first_way(values):
    return row_permute(values, 1, 2)


def second_way(values):
    return row_permute(values, 2, 1)


def sibling(values):
    return lax.ppermute(values, "col", [(0, 1), (1, 0)])


def grid_rows():
    return lax.axis_size("row") == 4


def places():
    row, core = lax.axis_index("row"), lax.axis_index("col")
    if grid_rows():
        one = jnp.where(core == 0, 1, 2)
        return jnp.stack([row ^ one, row ^ (3 - one), row, row ^ 3]), (1, 0, 2, 3)
    count = lax.axis_size("row")
    return jnp.arange(count), tuple(range(count))


def after(value, *earlier):
    return lax.optimization_barrier((value,) + earlier)[0]


def gather_rows(own):
    if grid_rows():
        near = first_way(own)
        side = second_way(own)
        return [near, side, own], lambda *earlier: [second_way(after(near, side, *earlier))]
    whole = lax.all_gather(own, "row", axis=0, tiled=True)
    return jnp.split(whole, lax.axis_size("row"), axis=0), lambda *earlier: []


def scatter_rows(parts, clock):
    if grid_rows():
        passing = first_way(parts[3])
        near = first_way(parts[0])
        side = second_way(clock.mark(plus(parts[1], clock(passing))))
        return parts[2].astype(f32) + near.astype(f32) + side.astype(f32)
    whole = jnp.concatenate(parts, axis=0)
    return lax.psum_scatter(whole, "row", scatter_dimension=0, tiled=True).astype(f32)


def line():
    return lax.axis_size("dp") == 4


def in_middle():
    place = lax.axis_index("dp")
    return (place == 1) | (place == 2)


def inward(part):
    return lax.ppermute(part, "dp", [(0, 1), (3, 2)])


def across(part):
    return lax.ppermute(part, "dp", [(1, 2), (2, 1)])


def outward(part):
    return lax.ppermute(part, "dp", [(1, 0), (2, 3)])


def plus(first, second):
    return (first.astype(f32) + second.astype(f32)).astype(first.dtype)


class Clock:
    def __init__(self):
        self.last = None

    def __call__(self, value):
        return value if self.last is None else after(value, self.last)

    def mark(self, value):
        self.last = value
        return value


class Line:
    def __init__(self, clock):
        self.clock = clock
        self.parts, self.inner, self.half, self.other, self.total, self.outer = ([] for _ in range(6))
        self.settled = 0

    def feed(self):
        at = len(self.inner)
        if at < len(self.parts) and at < len(self.half) + 2:
            part = self.parts[at]
            self.inner.append(inward(after(part, self.inner[at - 2]) if at >= 2 else part))

    def add(self, *parts):
        self.parts += parts
        if line():
            for _ in parts:
                self.feed()

    def join(self):
        if line():
            at = len(self.half)
            self.half.append(self.clock.mark(plus(self.parts[at], self.clock(self.inner[at]))))
            self.feed()
            ready = self.half[at]
            self.other.append(across(after(ready, self.other[-1]) if self.other else ready))

    def total_up(self):
        if line():
            at = len(self.total)
            self.total.append(self.clock.mark(plus(self.half[at], self.clock(self.other[at]))))
            ready = self.total[at]
            self.outer.append(outward(after(ready, self.outer[-1]) if self.outer else ready))

    def settle(self, shape, places, block, before=None):
        for index, start in places:
            at = self.settled
            self.settled += 1
            if line():
                before = self.clock.mark(
                    settle(shape, index, start, block, self.clock, self.total[at], self.outer[at], before)
                )
            else:
                value = lax.psum(self.parts[at], "dp").astype(f32)[None]
                before = jnp.zeros(shape, f32) if before is None else before
                before = lax.dynamic_update_slice(before, value, (index, start, 0))
        return before

    def small(self, at):
        if line():
            return jnp.where(in_middle(), self.total[at], self.outer[at])
        return lax.psum(self.parts[at], "dp")


def gather_whole(own):
    return lax.all_gather(own, "row", axis=0, tiled=True)


def scatter_whole(parts):
    return lax.psum_scatter(parts, "row", scatter_dimension=0, tiled=True).astype(f32)


def sum_rows(values, clock):
    if grid_rows():
        values = clock.mark(values + clock(first_way(values)))
        return clock.mark(values + clock(second_way(values)))
    return lax.psum(values, "row")


def width_pair(first, second, between=None):
    both = jnp.stack([first, second])
    moved = sibling(both)
    if between is not None:
        moved = after(moved, between(both))
    both = both + moved
    return both[0], both[1]


def normalize(values, between=None):
    width = values.shape[1] * lax.axis_size("col")
    totals, squares = width_pair(
        jnp.sum(values, axis=-1), jnp.sum(values * values, axis=-1), between
    )
    average = totals / width
    spread = squares / width - average * average
    inverse = lax.rsqrt(spread + epsilon)[:, None]
    return ((values - average[:, None]) * inverse, inverse)


def norm_back(scaled, normed_hat, inverse):
    width = normed_hat.shape[1] * lax.axis_size("col")
    first, second = width_pair(jnp.sum(scaled, axis=-1), jnp.sum(scaled * normed_hat, axis=-1))
    return inverse * (scaled - first[:, None] / width - normed_hat * second[:, None] / width)


def rotary_tables(count, rows):
    half_dims = ROT // 2
    lane = np.arange(LANES) % HD
    freqs = np.float32(base_rate) ** (-(2.0 * (lane % half_dims).astype(np.float32)) / np.float32(ROT))
    angles = np.arange(count * rows, dtype=np.float32)[:, None] * freqs.astype(np.float32)[None, :]
    turned = lane < ROT
    sign = np.where(lane < half_dims, -1.0, 1.0)
    cosine = np.where(turned, np.cos(angles.astype(np.float64)), 1.0)
    sine = np.where(turned, sign * np.sin(angles.astype(np.float64)), 0.0)
    shape = (count, rows, LANES)
    return jnp.asarray(cosine.reshape(shape), f32), jnp.asarray(sine.reshape(shape), f32)


def turn(values, cosine, sine):
    half_dims = ROT // 2
    lane = lax.broadcasted_iota(jnp.int32, values.shape, 1) % HD
    partner = jnp.where(
        lane < half_dims,
        pltpu.roll(values, LANES - half_dims, 1),
        pltpu.roll(values, half_dims, 1),
    )
    return values * cosine + partner * sine


def params(mib=60):
    return pltpu.CompilerParams(vmem_limit_bytes=mib << 20)


def cost(flops, moved, hard=0):
    return pl.CostEstimate(flops=int(flops), bytes_accessed=int(moved), transcendentals=int(hard))


def project_kernel(members, place, *refs):
    own, other = refs[:members], refs[members : 2 * members]
    keep, taken, bias = refs[2 * members : 2 * members + 3]
    cosine, sine = refs[2 * members + 3 : 3 * members + 3], refs[3 * members + 3 : 4 * members + 3]
    out = refs[-1]
    kind = pl.program_id(0)
    for at in range(members):
        result = dot(own[at][...], keep[0]) + dot(other[at][...], taken[0]) + bias[0].astype(f32)

        @pl.when(kind < 2)
        def _():
            for start in range(0, result.shape[1], LANES):
                part = slice(start, start + LANES)
                out[at, 0, :, part] = turn(result[:, part], cosine[at][0], sine[at][0]).astype(bf16)

        @pl.when(kind == 2)
        def _():
            out[at, 0] = result.astype(bf16)


def project_pieces(index, group, count, place, own, other, keep, taken, bias, cosine, sine, before):
    members = len(own)
    rows, width = own[0].shape
    units = keep.shape[2]
    piece = pl.BlockSpec((rows, width), lambda k, s: (0, 0), pipeline_mode=pl.Buffered(1))
    tables = [
        pl.BlockSpec((1, rows, LANES), functools.partial(lambda at, k, s: (s[at], 0, 0), at))
        for at in group
    ]
    weight = pl.BlockSpec((1, width, units), lambda k, s: (k, 0, 0))
    in_specs = [piece] * (2 * members) + [
        weight,
        weight,
        pl.BlockSpec((1, 1, units), lambda k, s: (k, 0, 0)),
        *tables,
        *tables,
    ]
    args = [*own, *other, keep, taken, bias] + [cosine] * members + [sine] * members
    aliases = {}
    if before is not None:
        aliases = {len(args) + 1: 0}
        in_specs.append(pl.BlockSpec(memory_space=pl.ANY))
        args.append(before)
    return pl.pallas_call(
        functools.partial(project_kernel, members),
        grid_spec=pltpu.PrefetchScalarGridSpec(
            num_scalar_prefetch=1,
            grid=(3,),
            in_specs=in_specs,
            out_specs=pl.BlockSpec((members, 1, rows, units), lambda k, s: (index, k, 0, 0)),
        ),
        out_shape=jax.ShapeDtypeStruct((count, 3, rows, units), bf16),
        input_output_aliases=aliases,
        compiler_params=params(24),
        cost_estimate=cost(
            12 * members * rows * width * units, 4 * members * rows * width + 12 * width * units
        ),
        name="project_pieces",
    )(place, *args)


def causal(rows):
    keys = lax.broadcasted_iota(jnp.int32, (rows, rows), 0)
    return keys <= lax.broadcasted_iota(jnp.int32, (rows, rows), 1)


def head_lanes(values, head):
    lane = lax.broadcasted_iota(jnp.int32, values.shape, 1)
    return jnp.where((lane >= head * HD) & (lane < (head + 1) * HD), values, jnp.zeros_like(values))


def walk(stop, body, carry):
    if isinstance(stop, int):
        for step in range(stop):
            carry = body(step, carry)
        return carry
    return lax.fori_loop(0, stop, body, carry)


def each(count, body):
    if count <= 4:
        for step in range(count):
            body(step)
    else:
        lax.fori_loop(0, count, lambda step, carry: (body(step), carry)[1], 0)


def row_range(step, rows):
    return pl.ds(step * rows if isinstance(step, int) else pl.multiple_of(step * rows, rows), rows)


def attend_kernel(slot, qkv, mixed, kept, logsum, scores):
    count, _, rows, _ = qkv.shape
    heads = LANES // HD
    scale = HD**-0.5

    def one(at):
        here = slot[at]
        query = qkv[here, 0] * jnp.asarray(scale, bf16)
        for head in range(heads):

            def look(past, highest):
                block = dot(head_lanes(qkv[slot[past], 1], head), query, NT)
                scores[row_range(past, rows), :] = block
                return jnp.maximum(highest, jnp.max(block, axis=0, keepdims=True))

            def add(past, carry):
                total, outs = carry
                weights = jnp.exp(scores[row_range(past, rows), :] - highest)
                total = total + jnp.sum(weights, axis=0, keepdims=True)
                value = jnp.transpose(qkv[slot[past], 2])[head * HD : (head + 1) * HD]
                return total, outs + dot(value, weights.astype(bf16))

            block = dot(head_lanes(qkv[here, 1], head), query, NT)
            block = jnp.where(causal(rows), block, -1e30)
            scores[row_range(at, rows), :] = block
            highest = walk(at, look, jnp.max(block, axis=0, keepdims=True))
            total, outs = walk(
                at + 1, add, (jnp.zeros((1, rows), f32), jnp.zeros((HD, rows), f32))
            )
            kept[0, here, pl.ds(head * HD, HD), :] = outs / total
            logsum[0, here, pl.ds(head, 1), :] = highest + jnp.log(total)
        mixed[here] = jnp.transpose(kept[0, here]).astype(bf16)

    each(count, one)


def attend_forward(slot, qkv):
    count, _, rows, units = qkv.shape
    pairs = units // LANES
    work = rows * rows * count * (count + 1) // 2 * units
    return pl.pallas_call(
        attend_kernel,
        grid_spec=pltpu.PrefetchScalarGridSpec(
            num_scalar_prefetch=1,
            grid=(pairs,),
            in_specs=[pl.BlockSpec((count, 3, rows, LANES), lambda p, s: (0, 0, 0, p))],
            out_specs=[
                pl.BlockSpec((count, rows, LANES), lambda p, s: (0, 0, p)),
                pl.BlockSpec((1, count, LANES, rows), lambda p, s: (p, 0, 0, 0)),
                pl.BlockSpec((1, count, 8, rows), lambda p, s: (p, 0, 0, 0)),
            ],
            scratch_shapes=[pltpu.VMEM((count * rows, rows), f32)],
        ),
        out_shape=[
            jax.ShapeDtypeStruct((count, rows, units), bf16),
            jax.ShapeDtypeStruct((pairs, count, LANES, rows), f32),
            jax.ShapeDtypeStruct((pairs, count, 8, rows), f32),
        ],
        compiler_params=params(40),
        cost_estimate=cost(16 * work, 16 * count * rows * units, work // HD),
        name="attend_forward",
    )(slot, qkv)


def attend_back_kernel(slot, place, qkv, grads, kept, logsum, cosine, sine, out, dq, dk, dv, inner):
    count, _, rows, _ = qkv.shape
    heads = LANES // HD
    scale = HD**-0.5
    dk[...] = jnp.zeros_like(dk)
    dv[...] = jnp.zeros_like(dv)

    def sums(at):
        product = jnp.transpose(grads[at].astype(f32)) * kept[0, at]
        for head in range(heads):
            part = product[head * HD : (head + 1) * HD]
            inner[at, pl.ds(head, 1), :] = jnp.sum(part, axis=0, keepdims=True)

    def one(at):
        here = slot[at]
        query = qkv[here, 0] * jnp.asarray(scale, bf16)
        grad = grads[here]
        for head in range(heads):
            query_head = head_lanes(query, head)
            grad_head = head_lanes(grad, head)

            def look(past, query_grad, last=False):
                there = slot[past]
                key = qkv[there, 1]
                block = dot(key, query_head, NT)
                weights = jnp.exp(block - logsum[0, here, pl.ds(head, 1), :])
                if last:
                    weights = jnp.where(causal(rows), weights, 0.0)
                moved = dot(qkv[there, 2], grad_head, NT)
                raw = (weights * (moved - inner[here, pl.ds(head, 1), :])).astype(bf16)
                dv[there] += dot(weights.astype(bf16), grad_head)
                dk[there] += dot(raw, query_head)
                turned = jnp.transpose(key)[head * HD : (head + 1) * HD]
                return query_grad + dot(turned, raw)

            query_grad = walk(at, look, jnp.zeros((HD, rows), f32))
            dq[pl.ds(head * HD, HD), :] = look(at, query_grad, True) * scale
        out[0, here] = turn(jnp.transpose(dq[...]), cosine[at], -sine[at]).astype(bf16)

    def finish(at):
        out[1, at] = turn(dk[at], cosine[place[at]], -sine[place[at]]).astype(bf16)
        out[2, at] = dv[at].astype(bf16)

    each(count, sums)
    each(count, one)
    each(count, finish)


def attend_backward(slot, place, qkv, grads, kept, logsum, cosine, sine):
    count, _, rows, units = qkv.shape
    pairs = units // LANES
    work = rows * rows * count * (count + 1) // 2 * units
    table = pl.BlockSpec((count, rows, LANES), lambda p, *s: (0, 0, 0))
    return pl.pallas_call(
        attend_back_kernel,
        grid_spec=pltpu.PrefetchScalarGridSpec(
            num_scalar_prefetch=2,
            grid=(pairs,),
            in_specs=[
                pl.BlockSpec((count, 3, rows, LANES), lambda p, *s: (0, 0, 0, p)),
                pl.BlockSpec((count, rows, LANES), lambda p, *s: (0, 0, p)),
                pl.BlockSpec((1, count, LANES, rows), lambda p, *s: (p, 0, 0, 0)),
                pl.BlockSpec((1, count, 8, rows), lambda p, *s: (p, 0, 0, 0)),
                table,
                table,
            ],
            out_specs=pl.BlockSpec((3, count, rows, LANES), lambda p, *s: (0, 0, 0, p)),
            scratch_shapes=[
                pltpu.VMEM((LANES, rows), f32),
                pltpu.VMEM((count, rows, LANES), f32),
                pltpu.VMEM((count, rows, LANES), f32),
                pltpu.VMEM((count, 8, rows), f32),
            ],
        ),
        out_shape=jax.ShapeDtypeStruct((3, count, rows, units), bf16),
        compiler_params=params(),
        cost_estimate=cost(40 * work, 24 * count * rows * units, work // HD),
        name="attend_backward",
    )(slot, place, qkv, grads, kept, logsum, cosine, sine)


def ordered(core, own, other, out, width):
    rest = out.shape[-1] - width
    lead = core[0] == 0
    out[..., :width] = jnp.where(lead, own[...], other[...])
    out[..., width:] = jnp.where(lead, other[..., :rest], own[..., :rest])


def block_of(width):
    return 256 if width % 256 == 0 else LANES


def mixed_out_kernel(swap, core, own, other, weight, *outs):
    units = outs[-1]
    count = own.shape[0]

    @pl.when(pl.program_id(0) == 0)
    def _():
        for at in range(count):
            ordered(core, own.at[at], other.at[swap[at]], units.at[at], own.shape[2])

    for at in range(count):
        outs[at][...] = dot(units[at], weight[...]).astype(bf16)


def mixed_out(core, swap, own, other, weight):
    count, rows, units = own.shape
    width = weight.shape[1]
    block = block_of(width)
    whole = lambda k, *s: (0, 0, 0)
    return pl.pallas_call(
        functools.partial(mixed_out_kernel, swap),
        grid_spec=pltpu.PrefetchScalarGridSpec(
            num_scalar_prefetch=1,
            grid=(width // block,),
            in_specs=[
                pl.BlockSpec((count, rows, units), whole),
                pl.BlockSpec((count, rows, units), whole),
                pl.BlockSpec((2 * units, block), lambda k, *s: (0, k)),
            ],
            out_specs=[pl.BlockSpec((rows, block), lambda k, *s: (0, k))] * count
            + [pl.BlockSpec((count, rows, 2 * units), whole)],
        ),
        out_shape=[jax.ShapeDtypeStruct((rows, width), bf16)] * count
        + [jax.ShapeDtypeStruct((count, rows, 2 * units), bf16)],
        compiler_params=params(24),
        cost_estimate=cost(4 * count * rows * units * width, 2 * count * rows * (width + 4 * units)),
        name="mixed_out",
    )(core, own, other, weight)


def hidden_kernel(members, place, *refs):
    own, other, grad_own, grad_other = (refs[k * members : (k + 1) * members] for k in range(4))
    gate_up, taken, down, down_taken = refs[4 * members : 4 * members + 4]
    outs = refs[4 * members + 4 :]
    for at in range(members):
        gate = dot(own[at][...], gate_up[0]) + dot(other[at][...], taken[0])
        up = dot(own[at][...], gate_up[1]) + dot(other[at][...], taken[1])
        grad = dot(grad_own[at][...], down[...], NT) + dot(grad_other[at][...], down_taken[...], NT)
        sigmoid = jax.nn.sigmoid(gate)
        silu = gate * sigmoid
        slope = sigmoid * (1.0 + gate * (1.0 - sigmoid))
        outs[at][0] = (grad * up * slope).astype(bf16)
        outs[at][1] = (grad * silu).astype(bf16)
        outs[at][2] = (silu * up).astype(bf16)


def hidden_pieces(group, place, own, other, grad_own, grad_other, gate_up, taken, down, down_taken):
    members = len(own)
    rows, width = own[0].shape
    units = gate_up.shape[2]
    block = block_of(units)
    rows_in = pl.BlockSpec((rows, width), lambda k, s: (0, 0), pipeline_mode=pl.Buffered(1))
    grads = [
        pl.BlockSpec(
            (rows, width),
            functools.partial(lambda at, k, s: (s[at], 0), at),
            pipeline_mode=pl.Buffered(1),
        )
        for at in group
    ]
    entry = pl.BlockSpec((2, width, block), lambda k, s: (0, 0, k))
    leave = pl.BlockSpec((block, width), lambda k, s: (k, 0))
    return pl.pallas_call(
        functools.partial(hidden_kernel, members),
        grid_spec=pltpu.PrefetchScalarGridSpec(
            num_scalar_prefetch=1,
            grid=(units // block,),
            in_specs=[rows_in] * (2 * members) + grads + grads + [entry, entry, leave, leave],
            out_specs=[pl.BlockSpec((3, rows, block), lambda k, s: (0, 0, k))] * members,
        ),
        out_shape=[jax.ShapeDtypeStruct((3, rows, units), bf16)] * members,
        compiler_params=params(40),
        cost_estimate=cost(
            12 * members * rows * width * units, 12 * width * units + 8 * members * rows * width
        ),
        name="hidden_pieces",
    )(
        place, *own, *other, *([grad_own] * members), *([grad_other] * members),
        gate_up, taken, down, down_taken,
    )


def down_grad_kernel(count, steps, core, place, *refs):
    own, other, grads = refs[:count], refs[count : 2 * count], refs[2 * count]
    out, units = refs[-2:]
    rows = own[0].shape[1]
    mine = (core[0] == 0) == (pl.program_id(0) < steps)
    for at in range(count):
        units[row_range(place[at], rows), :] = jnp.where(mine, own[at][0], other[at][0])
    out[...] = dot(units[...], grads[...], TN).astype(bf16)


def down_weight_grad(core, place, own, other, grads, total):
    count = len(own)
    _, rows, half = own[0].shape
    width = grads.shape[1]
    block = 384
    steps = half // block
    every = steps + -(-(total - half) // block)
    piece = pl.BlockSpec(
        (1, rows, block), lambda k, *s: (2, 0, jnp.where(k < steps, k, k - steps))
    )
    return pl.pallas_call(
        functools.partial(down_grad_kernel, count, steps),
        grid_spec=pltpu.PrefetchScalarGridSpec(
            num_scalar_prefetch=2,
            grid=(every,),
            in_specs=[piece] * (2 * count)
            + [pl.BlockSpec(grads.shape, lambda k, *s: (0, 0), pipeline_mode=pl.Buffered(1))],
            out_specs=pl.BlockSpec((block, width), lambda k, *s: (k, 0)),
            scratch_shapes=[pltpu.VMEM((count * rows, block), bf16)],
        ),
        out_shape=jax.ShapeDtypeStruct((total, width), bf16),
        compiler_params=params(),
        cost_estimate=cost(
            2 * count * rows * total * width, 2 * count * rows * (width + 2 * half) + 2 * total * width
        ),
        name="down_weight_grad",
    )(core, place, *own, *other, grads)


def normed_back_kernel(count, core, *refs):
    own, other, gate_up = refs[:count], refs[count : 2 * count], refs[2 * count]
    outs, gate, up = refs[2 * count + 1 : -2], refs[-2], refs[-1]
    rows = own[0].shape[1]

    @pl.when(pl.program_id(0) == 0)
    def _():
        for at in range(count):
            span = pl.ds(at * rows, rows)
            for kind, units in ((0, gate), (1, up)):
                ordered(
                    core, own[at].at[kind], other[at].at[kind], units.at[span], own[0].shape[2]
                )

    for at in range(count):
        span = pl.ds(at * rows, rows)
        outs[at][...] = (
            dot(gate[span, :], gate_up[0], NT) + dot(up[span, :], gate_up[1], NT)
        ).astype(bf16)


def normed_back(core, own, other, gate_up):
    count = len(own)
    _, rows, half = own[0].shape
    _, width, total = gate_up.shape
    block = block_of(width)
    once = pl.Buffered(1)
    units = pl.BlockSpec((count * rows, total), lambda k, s: (0, 0), pipeline_mode=once)
    units_shape = jax.ShapeDtypeStruct((count * rows, total), bf16)
    return pl.pallas_call(
        functools.partial(normed_back_kernel, count),
        grid_spec=pltpu.PrefetchScalarGridSpec(
            num_scalar_prefetch=1,
            grid=(width // block,),
            in_specs=[pl.BlockSpec((2, rows, half), lambda k, s: (0, 0, 0), pipeline_mode=once)]
            * (2 * count)
            + [pl.BlockSpec((2, block, total), lambda k, s: (0, k, 0))],
            out_specs=[pl.BlockSpec((rows, block), lambda k, s: (0, k))] * count + [units, units],
        ),
        out_shape=[jax.ShapeDtypeStruct((rows, width), bf16)] * count + [units_shape, units_shape],
        compiler_params=params(),
        cost_estimate=cost(
            4 * count * rows * width * total, 4 * width * total + 8 * count * rows * total
        ),
        name="normed_back",
    )(core, *own, *other, gate_up)


def down_out_kernel(count, core, *refs):
    own, other, down = refs[:count], refs[count : 2 * count], refs[2 * count]
    outs, units = refs[2 * count + 1 : -1], refs[-1]

    @pl.when(pl.program_id(0) == 0)
    def _():
        for at in range(count):
            ordered(core, own[at].at[0], other[at].at[0], units.at[at], own[at].shape[2])

    for at in range(count):
        outs[at][...] = dot(units[at], down[...]).astype(bf16)


def down_out(core, own, other, down):
    count = len(own)
    _, rows, half = own[0].shape
    total, width = down.shape
    block = block_of(width)
    piece = pl.BlockSpec((1, rows, half), lambda k, s: (2, 0, 0), pipeline_mode=pl.Buffered(1))
    return pl.pallas_call(
        functools.partial(down_out_kernel, count),
        grid_spec=pltpu.PrefetchScalarGridSpec(
            num_scalar_prefetch=1,
            grid=(width // block,),
            in_specs=[piece] * (2 * count) + [pl.BlockSpec((total, block), lambda k, s: (0, k))],
            out_specs=[pl.BlockSpec((rows, block), lambda k, s: (0, k))] * count,
            scratch_shapes=[pltpu.VMEM((count, rows, total), bf16)],
        ),
        out_shape=[jax.ShapeDtypeStruct((rows, width), bf16)] * count,
        compiler_params=params(),
        cost_estimate=cost(
            2 * count * rows * total * width, 2 * total * width + 4 * count * rows * total
        ),
        name="down_out",
    )(core, *own, *other, down)


def settle_kernel(middle, total, moved, *rest):
    rest[-1][0] = jnp.where(middle[0] == 1, total[...], moved[...]).astype(f32)


def settle(shape, index, start, block, clock, total, moved, before):
    rows, width = total.shape
    middle = clock(in_middle().astype(jnp.int32)[None])
    piece = pl.BlockSpec((block, width), lambda k, s: (k, 0))
    in_specs, args, aliases = [piece, piece], [total, moved], {}
    if before is not None:
        in_specs.append(pl.BlockSpec(memory_space=pl.ANY))
        args.append(before)
        aliases = {3: 0}
    return pl.pallas_call(
        settle_kernel,
        grid_spec=pltpu.PrefetchScalarGridSpec(
            num_scalar_prefetch=1,
            grid=(rows // block,),
            in_specs=in_specs,
            out_specs=pl.BlockSpec((1, block, width), lambda k, s: (index, start // block + k, 0)),
        ),
        out_shape=jax.ShapeDtypeStruct(shape, f32),
        input_output_aliases=aliases,
        compiler_params=params(16),
        cost_estimate=cost(0, 8 * rows * width),
        name="settle",
    )(middle, *args)


def widen_kernel(value, *rest):
    rest[-1][0] = value[...].astype(f32)


def widen(shape, index, value, before):
    block = block_of(shape[1])
    width = shape[2]
    in_specs, args, aliases = [pl.BlockSpec((block, width), lambda k: (k, 0))], [value], {}
    if before is not None:
        in_specs.append(pl.BlockSpec(memory_space=pl.ANY))
        args.append(before)
        aliases = {1: 0}
    return pl.pallas_call(
        widen_kernel,
        grid=(shape[1] // block,),
        in_specs=in_specs,
        out_specs=pl.BlockSpec((1, block, width), lambda k: (index, k, 0)),
        out_shape=jax.ShapeDtypeStruct(shape, f32),
        input_output_aliases=aliases,
        compiler_params=params(16),
        cost_estimate=cost(0, 6 * shape[1] * width),
        name="widen",
    )(*args)


def weight_grad_kernel(pieces, kinds, parts, stacked, *refs):
    rows_in, units = refs[:pieces], refs[pieces : pieces + kinds]
    outs, rows = refs[pieces + kinds : -1], refs[-1]
    size = rows_in[0].shape[0]
    for at in range(pieces):
        rows[:, pl.ds(at * size, size)] = jnp.transpose(rows_in[at][...])
    steps = pl.num_programs(0) // parts
    for kind in range(kinds):
        array = units[kind][...]
        result = dot(rows[...], array.reshape(array.shape[-2:])).astype(bf16)
        if stacked:
            outs[0][kind] = result
            continue
        for at in range(parts):

            @pl.when(pl.program_id(0) // steps == at)
            def _():
                outs[kind * parts + at][...] = result


def weight_grads(rows, units, indices=(None,), parts=1, stacked=False):
    pieces, kinds = len(rows), len(units)
    size, width = rows[0].shape
    total, columns = units[0].shape[-2:]
    block = 256 if width // parts % 256 == 0 else LANES
    steps = width // block // parts
    specs = [
        pl.BlockSpec((total, columns), lambda k: (0, 0), pipeline_mode=pl.Buffered(1))
        if index is None
        else pl.BlockSpec(
            (1, total, columns),
            functools.partial(lambda at, k: (at, 0, 0), index),
            pipeline_mode=pl.Buffered(1),
        )
        for index in indices
    ]
    outs = [
        pl.BlockSpec(
            (block, columns),
            functools.partial(lambda at, k: (jnp.clip(k - at * steps, 0, steps - 1), 0), at),
        )
        for _ in range(kinds)
        for at in range(parts)
    ]
    shapes = [jax.ShapeDtypeStruct((width // parts, columns), bf16)] * (kinds * parts)
    if stacked:
        outs = [pl.BlockSpec((kinds, block, columns), lambda k: (0, k, 0))]
        shapes = [jax.ShapeDtypeStruct((kinds, width, columns), bf16)]
    return pl.pallas_call(
        functools.partial(weight_grad_kernel, pieces, kinds, parts, stacked),
        grid=(steps * parts,),
        in_specs=[pl.BlockSpec((size, block), lambda k: (0, k))] * pieces + specs,
        out_specs=outs,
        out_shape=shapes,
        scratch_shapes=[pltpu.VMEM((block, total), bf16)],
        compiler_params=params(),
        cost_estimate=cost(
            2 * total * width * columns * kinds,
            2 * (total * (width + columns * kinds) + width * columns * kinds),
        ),
        name="weight_grads",
    )(*rows, *units)


def mixed_grad_kernel(count, *refs):
    keep, taken, out = refs[-3:]
    for at in range(count):
        out[at] = (
            dot(refs[at][...], keep[...], NT) + dot(refs[count + at][...], taken[...], NT)
        ).astype(bf16)


def mixed_back(own, other, keep, taken):
    count = len(own)
    rows, width = own[0].shape
    units = keep.shape[0]
    return pl.pallas_call(
        functools.partial(mixed_grad_kernel, count),
        out_shape=jax.ShapeDtypeStruct((count, rows, units), bf16),
        compiler_params=params(),
        cost_estimate=cost(4 * count * rows * width * units, 4 * count * rows * width),
        name="mixed_back",
    )(*own, *other, keep, taken)


def project_back_kernel(swap, core, own, other, weight, *outs):
    units = outs[-1]
    count = own.shape[1]

    @pl.when(pl.program_id(0) == 0)
    def _():
        for kind in range(3):
            for at in range(count):
                ordered(
                    core,
                    own.at[kind, at],
                    other.at[kind, swap[at]],
                    units.at[kind, at],
                    own.shape[3],
                )

    for at in range(count):
        outs[at][...] = sum(
            dot(units[kind, at], weight[kind], NT) for kind in range(3)
        ).astype(bf16)


def project_back(core, swap, own, other, weight):
    _, count, rows, half = own.shape
    _, width, total = weight.shape
    block = block_of(width)
    whole = lambda k, *s: (0, 0, 0, 0)
    return pl.pallas_call(
        functools.partial(project_back_kernel, swap),
        grid_spec=pltpu.PrefetchScalarGridSpec(
            num_scalar_prefetch=1,
            grid=(width // block,),
            in_specs=[
                pl.BlockSpec((3, count, rows, half), whole),
                pl.BlockSpec((3, count, rows, half), whole),
                pl.BlockSpec((3, block, total), lambda k, *s: (0, k, 0)),
            ],
            out_specs=[pl.BlockSpec((rows, block), lambda k, *s: (0, k))] * count
            + [pl.BlockSpec((3, count, rows, total), whole)],
        ),
        out_shape=[jax.ShapeDtypeStruct((rows, width), bf16)] * count
        + [jax.ShapeDtypeStruct((3, count, rows, total), bf16)],
        compiler_params=params(),
        cost_estimate=cost(6 * count * rows * total * width, 2 * count * rows * (width + 6 * total)),
        name="project_back",
    )(core, own, other, weight)


def halves(weight, axis, width):
    lead = lax.slice_in_dim(weight, 0, width, axis=axis)
    rest = lax.slice_in_dim(weight, width, weight.shape[axis], axis=axis)
    pad = [(0, 0)] * weight.ndim
    pad[axis] = (0, width - rest.shape[axis])
    rest = jnp.pad(rest, pad)
    first = lax.axis_index("col") == 0
    return jnp.where(first, lead, rest), jnp.where(first, rest, lead)


def shards(
    block_input,
    norm1_gain,
    norm1_shift,
    qkv_weight,
    qkv_bias,
    out_weight,
    norm2_gain,
    norm2_shift,
    gate_up_weight,
    down_weight,
    output_grad,
):
    count = lax.axis_size("row")
    rows = block_input.shape[0]
    core = lax.axis_index("col").astype(jnp.int32)[None]
    place, swap = places()
    place = place.astype(jnp.int32)
    slot = inverse_places(place)
    half_units = out_weight.shape[0] // 2
    total_hidden = down_weight.shape[0]
    half_hidden = -(-total_hidden // (2 * LANES)) * LANES
    if grid_rows():
        groups = (((2,), 2), ((0, 1), 0), ((3,), 3))
    else:
        groups = tuple(((at,), at) for at in range(count))

    clock = Clock()
    inputs = block_input.astype(f32)
    gain_one = norm1_gain.astype(f32)
    gain_two = norm2_gain.astype(f32)
    split = {}

    def between(stats):
        split["keep"], split["send"] = halves(after(qkv_weight, stats), 2, half_units)
        return split["keep"]

    hat_one, inverse_one = normalize(inputs, between)
    normed_one = clock.mark((hat_one * gain_one + norm1_shift.astype(f32)).astype(bf16))

    one_own, fetch = gather_rows(normed_one)
    grad_own = None if grid_rows() else gather_whole(output_grad)
    qkv_keep = split["keep"]
    qkv_taken = sibling(split["send"])
    cosine, sine = rotary_tables(count, rows)
    bias = qkv_bias[:, None, :]
    qkv = None
    for group, index in groups:
        if qkv is not None and len(one_own) < count:
            grad_own = gather_whole(after(output_grad, one_own[0], one_own[1], clock.last))
            one_own += fetch(clock.last)
        others = [sibling(clock(one_own[swap[at]])) for at in group]
        qkv = clock.mark(
            project_pieces(
                index, group, count, place, [one_own[at] for at in group], others,
                qkv_keep, qkv_taken, clock(bias), cosine, sine, qkv,
            )
        )
        if group == groups[0][0]:
            gate_up_keep, gate_up_send = halves(clock(gate_up_weight), 2, half_hidden)
            clock.mark(gate_up_keep)
            down_keep, down_send = halves(clock(down_weight), 0, half_hidden)
            clock.mark(down_keep)
            out_keep, out_send = halves(clock(out_weight), 0, half_units)
            clock.mark(out_keep)
    gate_up_taken = sibling(clock(gate_up_send))
    down_taken = sibling(clock(down_send))
    out_taken = sibling(clock(out_send))
    mixed, kept, logsum = attend_forward(clock(slot), qkv)
    clock.mark(mixed)
    *branch, mixed_units = mixed_out(clock(core), swap, mixed, sibling(mixed), out_weight)
    clock.mark(branch[0])
    branch = scatter_rows(branch, clock)
    grad_other = sibling(clock(grad_own))
    after_rows = inputs + branch
    hat_two, inverse_two = normalize(after_rows)
    normed_two = clock.mark((hat_two * gain_two + norm2_shift.astype(f32)).astype(bf16))

    two_own, fetch = gather_rows(normed_two)
    mine, theirs = [None] * count, [None] * count
    for group, _ in groups:
        if group != groups[0][0] and len(two_own) < count:
            two_own += fetch(clock.last)
        results = hidden_pieces(
            group, clock(place),
            [two_own[at] for at in group],
            [sibling(clock(two_own[swap[at]])) for at in group],
            grad_own, grad_other, gate_up_keep, gate_up_taken, down_keep, down_taken,
        )
        clock.mark(results[0])
        for at, result in zip(group, results):
            mine[at] = result
        for at in group:
            theirs[at] = sibling(mine[swap[at]])

    *normed_parts, gate_units, up_units = normed_back(clock(core), mine, theirs, gate_up_weight)
    clock.mark(normed_parts[0])
    down_grad = clock.mark(
        down_weight_grad(clock(core), place, mine, theirs, grad_own, total_hidden)
    )
    down_grad = lax.psum(down_grad, "dp")
    parts = weight_grads(two_own, [clock(gate_units), up_units], (None, None), 2)
    clock.mark(parts[0])
    sums = Line(clock)
    sums.add(*parts)
    normed_two_grad = clock.mark(scatter_rows(normed_parts, clock))
    after_grad = output_grad.astype(f32) + norm_back(
        normed_two_grad * gain_two, hat_two, inverse_two
    )
    branch_grad = clock.mark(after_grad.astype(bf16))
    branch_own, fetch = gather_rows(branch_grad)
    down_parts = down_out(clock(core), mine, theirs, down_weight)
    clock.mark(down_parts[0])
    if len(branch_own) < count:
        branch_own += fetch(clock.last)
    branch_other = [sibling(branch_own[swap[at]]) for at in range(count)]
    sums.join()
    mixed_grad = clock.mark(mixed_back(branch_own, branch_other, clock(out_keep), out_taken))
    branch_rows = clock.mark(jnp.concatenate(branch_own, axis=0))
    parts = weight_grads([mixed_units.reshape(count * rows, -1)], [branch_rows])
    clock.mark(parts[0])
    sums.add(*parts)
    project_grad = clock.mark(
        attend_backward(clock(slot), place, qkv, mixed_grad, kept, logsum, cosine, sine)
    )
    project_other = sibling(project_grad)
    down_grad = clock.mark(clock(down_grad))
    sums.join()
    sums.total_up()
    if grid_rows():
        far = first_way(down_parts[3])
        near = first_way(down_parts[0])
        side = second_way(clock.mark(plus(down_parts[1], clock(far))))
    *one_parts, project_units = project_back(
        clock(core), swap, project_grad, project_other, qkv_weight
    )
    clock.mark(one_parts[0])
    if grid_rows():
        down = down_parts[2].astype(f32) + near.astype(f32) + clock(side).astype(f32)
    else:
        down = scatter_rows(down_parts, clock)
    block_output = clock.mark((after_rows + down).astype(bf16))
    project_units = project_units.reshape(3, count * rows, -1)
    query_grad, key_grad, value_grad = weight_grads(
        one_own, [clock(project_units)] * 3, (0, 1, 2)
    )
    clock.mark(query_grad)
    query_grad = lax.psum(query_grad, "dp")
    sums.join()
    sums.total_up()
    normed_one_grad = clock.mark(scatter_rows(one_parts, clock))
    input_grad = after_grad + norm_back(normed_one_grad * gain_one, hat_one, inverse_one)
    gains = jnp.stack(
        [
            jnp.sum(normed_one_grad * hat_one, axis=0),
            jnp.sum(normed_one_grad, axis=0),
            jnp.sum(normed_two_grad * hat_two, axis=0),
            jnp.sum(normed_two_grad, axis=0),
        ]
    )
    width = gains.shape[1]
    gains = clock.mark(gains)
    sums.join()
    sums.total_up()
    query_grad = clock.mark(clock(query_grad))
    key_grad = lax.psum(clock(key_grad), "dp")
    gains = sum_rows(gains, clock)
    bias_grad = jnp.sum(clock(project_grad).astype(f32), axis=(1, 2))
    clock.mark(bias_grad)
    sums.add(jnp.concatenate([gains.reshape(-1, LANES), bias_grad.reshape(-1, LANES)], axis=0))
    input_grad = clock.mark(clock(input_grad))
    half_width = two_own[0].shape[1] // 2
    block = block_of(half_width)
    shape = gate_up_weight.shape
    sums.join()
    sums.total_up()
    gate_up_grad = sums.settle(shape, ((0, 0), (0, half_width), (1, 0)), block)
    down_grad = clock.mark(clock(down_grad).astype(f32))
    sums.join()
    sums.total_up()
    key_grad = clock.mark(clock(key_grad))
    value_grad = lax.psum(clock(value_grad), "dp")
    gate_up_grad = sums.settle(shape, ((1, half_width),), block, gate_up_grad)
    sums.total_up()
    out_grad = sums.settle((1,) + out_weight.shape, ((0, 0),), block_of(out_weight.shape[0]))
    small = sums.small(5)
    gains = small[: 4 * width // LANES].reshape(4, width)
    bias_grad = small[4 * width // LANES :].reshape(bias_grad.shape)
    qkv_grad = None
    for kind, grad in enumerate((query_grad, key_grad, clock(value_grad))):
        qkv_grad = widen(qkv_weight.shape, kind, grad, qkv_grad)
    return (
        block_output,
        input_grad,
        gains[0],
        gains[1],
        qkv_grad,
        bias_grad,
        out_grad[0],
        gains[2],
        gains[3],
        gate_up_grad,
        down_grad,
    )


def inverse_places(place):
    spots = jnp.arange(place.shape[0])
    return jnp.sum(
        jnp.where(place[None, :] == spots[:, None], spots[None, :], 0), axis=1
    ).astype(jnp.int32)


def solution(mesh):
    placed = (
        P(("dp", "row"), "col"),
        P("col"),
        P("col"),
        P(None, "col", "row"),
        P(None, ("row", "col")),
        P("row", "col"),
        P("col"),
        P("col"),
        P(None, "col", "row"),
        P("row", "col"),
        P(("dp", "row"), "col"),
    )
    return jax.shard_map(
        shards,
        mesh=mesh,
        in_specs=placed,
        out_specs=(
            P(("dp", "row"), "col"),
            P(("dp", "row"), "col"),
            P("col"),
            P("col"),
            P(None, "col", "row"),
            P(None, ("row", "col")),
            P("row", "col"),
            P("col"),
            P("col"),
            P(None, "col", "row"),
            P("row", "col"),
        ),
        check_vma=False,
    )
```

```python
import functools

import jax
import jax.numpy as jnp
import numpy as np
from jax import lax
from jax.experimental import pallas as pl
from jax.experimental.pallas import tpu as pltpu
from jax.sharding import PartitionSpec as P

HD = 64
ROT = 16
LANES = 128

epsilon = 1e-05
base_rate = 10000.0
bf16 = jnp.bfloat16
f32 = jnp.float32

NN = (((1,), (0,)), ((), ()))
NT = (((1,), (1,)), ((), ()))
TN = (((0,), (0,)), ((), ()))


def dot(first, second, dims=NN):
    return lax.dot_general(first, second, dims, preferred_element_type=f32)


def row_permute(values, core_zero, core_one):
    pairs = [
        (row * 2 + core, (row ^ (core_one if core else core_zero)) * 2 + core)
        for row in range(4)
        for core in range(2)
    ]
    return lax.ppermute(values, ("row", "col"), pairs)


def first_way(values):
    return row_permute(values, 1, 2)


def second_way(values):
    return row_permute(values, 2, 1)


def sibling(values):
    return lax.ppermute(values, "col", [(0, 1), (1, 0)])


def grid_rows():
    return lax.axis_size("row") == 4


def places():
    row, core = lax.axis_index("row"), lax.axis_index("col")
    if grid_rows():
        one = jnp.where(core == 0, 1, 2)
        return jnp.stack([row ^ one, row ^ (3 - one), row, row ^ 3]), (1, 0, 2, 3)
    count = lax.axis_size("row")
    return jnp.arange(count), tuple(range(count))


def after(value, *earlier):
    return lax.optimization_barrier((value,) + earlier)[0]


def gather_rows(own):
    if grid_rows():
        near = first_way(own)
        side = second_way(own)
        return [near, side, own], lambda *earlier: [second_way(after(near, side, *earlier))]
    whole = lax.all_gather(own, "row", axis=0, tiled=True)
    return jnp.split(whole, lax.axis_size("row"), axis=0), lambda *earlier: []


def scatter_rows(parts, clock):
    if grid_rows():
        passing = first_way(parts[3])
        near = first_way(parts[0])
        side = second_way(clock.mark(plus(parts[1], clock(passing))))
        return parts[2].astype(f32) + near.astype(f32) + side.astype(f32)
    whole = jnp.concatenate(parts, axis=0)
    return lax.psum_scatter(whole, "row", scatter_dimension=0, tiled=True).astype(f32)


def line():
    return lax.axis_size("dp") == 4


def in_middle():
    place = lax.axis_index("dp")
    return (place == 1) | (place == 2)


def inward(part):
    return lax.ppermute(part, "dp", [(0, 1), (3, 2)])


def across(part):
    return lax.ppermute(part, "dp", [(1, 2), (2, 1)])


def outward(part):
    return lax.ppermute(part, "dp", [(1, 0), (2, 3)])


def plus(first, second):
    return (first.astype(f32) + second.astype(f32)).astype(first.dtype)


class Clock:
    def __init__(self):
        self.last = None

    def __call__(self, value):
        return value if self.last is None else after(value, self.last)

    def mark(self, value):
        self.last = value
        return value


class Line:
    def __init__(self, clock):
        self.clock = clock
        self.parts, self.inner, self.half, self.other, self.total, self.outer = ([] for _ in range(6))
        self.settled = 0

    def feed(self):
        at = len(self.inner)
        if at < len(self.parts) and at < len(self.half) + 2:
            part = self.parts[at]
            self.inner.append(inward(after(part, self.inner[at - 2]) if at >= 2 else part))

    def add(self, *parts):
        self.parts += parts
        if line():
            for _ in parts:
                self.feed()

    def join(self):
        if line():
            at = len(self.half)
            self.half.append(self.clock.mark(plus(self.parts[at], self.clock(self.inner[at]))))
            self.feed()
            ready = self.half[at]
            self.other.append(across(after(ready, self.other[-1]) if self.other else ready))

    def total_up(self):
        if line():
            at = len(self.total)
            self.total.append(self.clock.mark(plus(self.half[at], self.clock(self.other[at]))))
            ready = self.total[at]
            self.outer.append(outward(after(ready, self.outer[-1]) if self.outer else ready))

    def settle(self, shape, places, block, before=None):
        for index, start in places:
            at = self.settled
            self.settled += 1
            if line():
                before = self.clock.mark(
                    settle(shape, index, start, block, self.clock, self.total[at], self.outer[at], before)
                )
            else:
                value = lax.psum(self.parts[at], "dp").astype(f32)[None]
                before = jnp.zeros(shape, f32) if before is None else before
                before = lax.dynamic_update_slice(before, value, (index, start, 0))
        return before

    def small(self, at):
        if line():
            return jnp.where(in_middle(), self.total[at], self.outer[at])
        return lax.psum(self.parts[at], "dp")


def gather_whole(own):
    return lax.all_gather(own, "row", axis=0, tiled=True)


def scatter_whole(parts):
    return lax.psum_scatter(parts, "row", scatter_dimension=0, tiled=True).astype(f32)


def sum_rows(values, clock):
    if grid_rows():
        values = clock.mark(values + clock(first_way(values)))
        return clock.mark(values + clock(second_way(values)))
    return lax.psum(values, "row")


def width_pair(first, second, between=None):
    both = jnp.stack([first, second])
    moved = sibling(both)
    if between is not None:
        moved = after(moved, between(both))
    both = both + moved
    return both[0], both[1]


def normalize(values, between=None):
    width = values.shape[1] * lax.axis_size("col")
    totals, squares = width_pair(
        jnp.sum(values, axis=-1), jnp.sum(values * values, axis=-1), between
    )
    average = totals / width
    spread = squares / width - average * average
    inverse = lax.rsqrt(spread + epsilon)[:, None]
    return ((values - average[:, None]) * inverse, inverse)


def norm_back(scaled, normed_hat, inverse):
    width = normed_hat.shape[1] * lax.axis_size("col")
    first, second = width_pair(jnp.sum(scaled, axis=-1), jnp.sum(scaled * normed_hat, axis=-1))
    return inverse * (scaled - first[:, None] / width - normed_hat * second[:, None] / width)


def rotary_tables(count, rows):
    half_dims = ROT // 2
    lane = np.arange(LANES) % HD
    freqs = np.float32(base_rate) ** (-(2.0 * (lane % half_dims).astype(np.float32)) / np.float32(ROT))
    angles = np.arange(count * rows, dtype=np.float32)[:, None] * freqs.astype(np.float32)[None, :]
    turned = lane < ROT
    sign = np.where(lane < half_dims, -1.0, 1.0)
    cosine = np.where(turned, np.cos(angles.astype(np.float64)), 1.0)
    sine = np.where(turned, sign * np.sin(angles.astype(np.float64)), 0.0)
    shape = (count, rows, LANES)
    return jnp.asarray(cosine.reshape(shape), f32), jnp.asarray(sine.reshape(shape), f32)


def turn(values, cosine, sine):
    half_dims = ROT // 2
    lane = lax.broadcasted_iota(jnp.int32, values.shape, 1) % HD
    partner = jnp.where(
        lane < half_dims,
        pltpu.roll(values, LANES - half_dims, 1),
        pltpu.roll(values, half_dims, 1),
    )
    return values * cosine + partner * sine


def params(mib=60):
    return pltpu.CompilerParams(vmem_limit_bytes=mib << 20)


def cost(flops, moved, hard=0):
    return pl.CostEstimate(flops=int(flops), bytes_accessed=int(moved), transcendentals=int(hard))


def project_kernel(members, place, *refs):
    own, other = refs[:members], refs[members : 2 * members]
    keep, taken, bias = refs[2 * members : 2 * members + 3]
    cosine, sine = refs[2 * members + 3 : 3 * members + 3], refs[3 * members + 3 : 4 * members + 3]
    out = refs[-1]
    kind = pl.program_id(0)
    for at in range(members):
        result = dot(own[at][...], keep[0]) + dot(other[at][...], taken[0]) + bias[0].astype(f32)

        @pl.when(kind < 2)
        def _():
            for start in range(0, result.shape[1], LANES):
                part = slice(start, start + LANES)
                out[at, 0, :, part] = turn(result[:, part], cosine[at][0], sine[at][0]).astype(bf16)

        @pl.when(kind == 2)
        def _():
            out[at, 0] = result.astype(bf16)


def project_pieces(index, group, count, place, own, other, keep, taken, bias, cosine, sine, before):
    members = len(own)
    rows, width = own[0].shape
    units = keep.shape[2]
    piece = pl.BlockSpec((rows, width), lambda k, s: (0, 0), pipeline_mode=pl.Buffered(1))
    tables = [
        pl.BlockSpec((1, rows, LANES), functools.partial(lambda at, k, s: (s[at], 0, 0), at))
        for at in group
    ]
    weight = pl.BlockSpec((1, width, units), lambda k, s: (k, 0, 0))
    in_specs = [piece] * (2 * members) + [
        weight,
        weight,
        pl.BlockSpec((1, 1, units), lambda k, s: (k, 0, 0)),
        *tables,
        *tables,
    ]
    args = [*own, *other, keep, taken, bias] + [cosine] * members + [sine] * members
    aliases = {}
    if before is not None:
        aliases = {len(args) + 1: 0}
        in_specs.append(pl.BlockSpec(memory_space=pl.ANY))
        args.append(before)
    return pl.pallas_call(
        functools.partial(project_kernel, members),
        grid_spec=pltpu.PrefetchScalarGridSpec(
            num_scalar_prefetch=1,
            grid=(3,),
            in_specs=in_specs,
            out_specs=pl.BlockSpec((members, 1, rows, units), lambda k, s: (index, k, 0, 0)),
        ),
        out_shape=jax.ShapeDtypeStruct((count, 3, rows, units), bf16),
        input_output_aliases=aliases,
        compiler_params=params(24),
        cost_estimate=cost(
            12 * members * rows * width * units, 4 * members * rows * width + 12 * width * units
        ),
        name="project_pieces",
    )(place, *args)


def causal(rows):
    keys = lax.broadcasted_iota(jnp.int32, (rows, rows), 0)
    return keys <= lax.broadcasted_iota(jnp.int32, (rows, rows), 1)


def head_lanes(values, head):
    lane = lax.broadcasted_iota(jnp.int32, values.shape, 1)
    return jnp.where((lane >= head * HD) & (lane < (head + 1) * HD), values, jnp.zeros_like(values))


def walk(stop, body, carry):
    if isinstance(stop, int):
        for step in range(stop):
            carry = body(step, carry)
        return carry
    return lax.fori_loop(0, stop, body, carry)


def each(count, body):
    if count <= 4:
        for step in range(count):
            body(step)
    else:
        lax.fori_loop(0, count, lambda step, carry: (body(step), carry)[1], 0)


def row_range(step, rows):
    return pl.ds(step * rows if isinstance(step, int) else pl.multiple_of(step * rows, rows), rows)


def attend_kernel(slot, qkv, mixed, kept, logsum, scores):
    count, _, rows, _ = qkv.shape
    heads = LANES // HD
    scale = HD**-0.5

    def one(at):
        here = slot[at]
        query = qkv[here, 0] * jnp.asarray(scale, bf16)
        for head in range(heads):

            def look(past, highest):
                block = dot(head_lanes(qkv[slot[past], 1], head), query, NT)
                scores[row_range(past, rows), :] = block
                return jnp.maximum(highest, jnp.max(block, axis=0, keepdims=True))

            def add(past, carry):
                total, outs = carry
                weights = jnp.exp(scores[row_range(past, rows), :] - highest)
                total = total + jnp.sum(weights, axis=0, keepdims=True)
                value = jnp.transpose(qkv[slot[past], 2])[head * HD : (head + 1) * HD]
                return total, outs + dot(value, weights.astype(bf16))

            block = dot(head_lanes(qkv[here, 1], head), query, NT)
            block = jnp.where(causal(rows), block, -1e30)
            scores[row_range(at, rows), :] = block
            highest = walk(at, look, jnp.max(block, axis=0, keepdims=True))
            total, outs = walk(
                at + 1, add, (jnp.zeros((1, rows), f32), jnp.zeros((HD, rows), f32))
            )
            kept[0, here, pl.ds(head * HD, HD), :] = outs / total
            logsum[0, here, pl.ds(head, 1), :] = highest + jnp.log(total)
        mixed[here] = jnp.transpose(kept[0, here]).astype(bf16)

    each(count, one)


def attend_forward(slot, qkv):
    count, _, rows, units = qkv.shape
    pairs = units // LANES
    work = rows * rows * count * (count + 1) // 2 * units
    return pl.pallas_call(
        attend_kernel,
        grid_spec=pltpu.PrefetchScalarGridSpec(
            num_scalar_prefetch=1,
            grid=(pairs,),
            in_specs=[pl.BlockSpec((count, 3, rows, LANES), lambda p, s: (0, 0, 0, p))],
            out_specs=[
                pl.BlockSpec((count, rows, LANES), lambda p, s: (0, 0, p)),
                pl.BlockSpec((1, count, LANES, rows), lambda p, s: (p, 0, 0, 0)),
                pl.BlockSpec((1, count, 8, rows), lambda p, s: (p, 0, 0, 0)),
            ],
            scratch_shapes=[pltpu.VMEM((count * rows, rows), f32)],
        ),
        out_shape=[
            jax.ShapeDtypeStruct((count, rows, units), bf16),
            jax.ShapeDtypeStruct((pairs, count, LANES, rows), f32),
            jax.ShapeDtypeStruct((pairs, count, 8, rows), f32),
        ],
        compiler_params=params(40),
        cost_estimate=cost(16 * work, 16 * count * rows * units, work // HD),
        name="attend_forward",
    )(slot, qkv)


def attend_back_kernel(slot, place, qkv, grads, kept, logsum, cosine, sine, out, dq, dk, dv, inner):
    count, _, rows, _ = qkv.shape
    heads = LANES // HD
    scale = HD**-0.5
    dk[...] = jnp.zeros_like(dk)
    dv[...] = jnp.zeros_like(dv)

    def sums(at):
        product = jnp.transpose(grads[at].astype(f32)) * kept[0, at]
        for head in range(heads):
            part = product[head * HD : (head + 1) * HD]
            inner[at, pl.ds(head, 1), :] = jnp.sum(part, axis=0, keepdims=True)

    def one(at):
        here = slot[at]
        query = qkv[here, 0] * jnp.asarray(scale, bf16)
        grad = grads[here]
        for head in range(heads):
            query_head = head_lanes(query, head)
            grad_head = head_lanes(grad, head)

            def look(past, query_grad, last=False):
                there = slot[past]
                key = qkv[there, 1]
                block = dot(key, query_head, NT)
                weights = jnp.exp(block - logsum[0, here, pl.ds(head, 1), :])
                if last:
                    weights = jnp.where(causal(rows), weights, 0.0)
                moved = dot(qkv[there, 2], grad_head, NT)
                raw = (weights * (moved - inner[here, pl.ds(head, 1), :])).astype(bf16)
                dv[there] += dot(weights.astype(bf16), grad_head)
                dk[there] += dot(raw, query_head)
                turned = jnp.transpose(key)[head * HD : (head + 1) * HD]
                return query_grad + dot(turned, raw)

            query_grad = walk(at, look, jnp.zeros((HD, rows), f32))
            dq[pl.ds(head * HD, HD), :] = look(at, query_grad, True) * scale
        out[0, here] = turn(jnp.transpose(dq[...]), cosine[at], -sine[at]).astype(bf16)

    def finish(at):
        out[1, at] = turn(dk[at], cosine[place[at]], -sine[place[at]]).astype(bf16)
        out[2, at] = dv[at].astype(bf16)

    each(count, sums)
    each(count, one)
    each(count, finish)


def attend_backward(slot, place, qkv, grads, kept, logsum, cosine, sine):
    count, _, rows, units = qkv.shape
    pairs = units // LANES
    work = rows * rows * count * (count + 1) // 2 * units
    table = pl.BlockSpec((count, rows, LANES), lambda p, *s: (0, 0, 0))
    return pl.pallas_call(
        attend_back_kernel,
        grid_spec=pltpu.PrefetchScalarGridSpec(
            num_scalar_prefetch=2,
            grid=(pairs,),
            in_specs=[
                pl.BlockSpec((count, 3, rows, LANES), lambda p, *s: (0, 0, 0, p)),
                pl.BlockSpec((count, rows, LANES), lambda p, *s: (0, 0, p)),
                pl.BlockSpec((1, count, LANES, rows), lambda p, *s: (p, 0, 0, 0)),
                pl.BlockSpec((1, count, 8, rows), lambda p, *s: (p, 0, 0, 0)),
                table,
                table,
            ],
            out_specs=pl.BlockSpec((3, count, rows, LANES), lambda p, *s: (0, 0, 0, p)),
            scratch_shapes=[
                pltpu.VMEM((LANES, rows), f32),
                pltpu.VMEM((count, rows, LANES), f32),
                pltpu.VMEM((count, rows, LANES), f32),
                pltpu.VMEM((count, 8, rows), f32),
            ],
        ),
        out_shape=jax.ShapeDtypeStruct((3, count, rows, units), bf16),
        compiler_params=params(),
        cost_estimate=cost(40 * work, 24 * count * rows * units, work // HD),
        name="attend_backward",
    )(slot, place, qkv, grads, kept, logsum, cosine, sine)


def ordered(core, own, other, out, width):
    rest = out.shape[-1] - width
    lead = core[0] == 0
    out[..., :width] = jnp.where(lead, own[...], other[...])
    out[..., width:] = jnp.where(lead, other[..., :rest], own[..., :rest])


def block_of(width):
    return 256 if width % 256 == 0 else LANES


def mixed_out_kernel(swap, core, own, other, weight, *outs):
    units = outs[-1]
    count = own.shape[0]

    @pl.when(pl.program_id(0) == 0)
    def _():
        for at in range(count):
            ordered(core, own.at[at], other.at[swap[at]], units.at[at], own.shape[2])

    for at in range(count):
        outs[at][...] = dot(units[at], weight[...]).astype(bf16)


def mixed_out(core, swap, own, other, weight):
    count, rows, units = own.shape
    width = weight.shape[1]
    block = block_of(width)
    whole = lambda k, *s: (0, 0, 0)
    return pl.pallas_call(
        functools.partial(mixed_out_kernel, swap),
        grid_spec=pltpu.PrefetchScalarGridSpec(
            num_scalar_prefetch=1,
            grid=(width // block,),
            in_specs=[
                pl.BlockSpec((count, rows, units), whole),
                pl.BlockSpec((count, rows, units), whole),
                pl.BlockSpec((2 * units, block), lambda k, *s: (0, k)),
            ],
            out_specs=[pl.BlockSpec((rows, block), lambda k, *s: (0, k))] * count
            + [pl.BlockSpec((count, rows, 2 * units), whole)],
        ),
        out_shape=[jax.ShapeDtypeStruct((rows, width), bf16)] * count
        + [jax.ShapeDtypeStruct((count, rows, 2 * units), bf16)],
        compiler_params=params(24),
        cost_estimate=cost(4 * count * rows * units * width, 2 * count * rows * (width + 4 * units)),
        name="mixed_out",
    )(core, own, other, weight)


def hidden_kernel(members, place, *refs):
    own, other, grad_own, grad_other = (refs[k * members : (k + 1) * members] for k in range(4))
    gate_up, taken, down, down_taken = refs[4 * members : 4 * members + 4]
    outs = refs[4 * members + 4 :]
    for at in range(members):
        gate = dot(own[at][...], gate_up[0]) + dot(other[at][...], taken[0])
        up = dot(own[at][...], gate_up[1]) + dot(other[at][...], taken[1])
        grad = dot(grad_own[at][...], down[...], NT) + dot(grad_other[at][...], down_taken[...], NT)
        sigmoid = jax.nn.sigmoid(gate)
        silu = gate * sigmoid
        slope = sigmoid * (1.0 + gate * (1.0 - sigmoid))
        outs[at][0] = (grad * up * slope).astype(bf16)
        outs[at][1] = (grad * silu).astype(bf16)
        outs[at][2] = (silu * up).astype(bf16)


def hidden_pieces(group, place, own, other, grad_own, grad_other, gate_up, taken, down, down_taken):
    members = len(own)
    rows, width = own[0].shape
    units = gate_up.shape[2]
    block = block_of(units)
    rows_in = pl.BlockSpec((rows, width), lambda k, s: (0, 0), pipeline_mode=pl.Buffered(1))
    grads = [
        pl.BlockSpec(
            (rows, width),
            functools.partial(lambda at, k, s: (s[at], 0), at),
            pipeline_mode=pl.Buffered(1),
        )
        for at in group
    ]
    entry = pl.BlockSpec((2, width, block), lambda k, s: (0, 0, k))
    leave = pl.BlockSpec((block, width), lambda k, s: (k, 0))
    return pl.pallas_call(
        functools.partial(hidden_kernel, members),
        grid_spec=pltpu.PrefetchScalarGridSpec(
            num_scalar_prefetch=1,
            grid=(units // block,),
            in_specs=[rows_in] * (2 * members) + grads + grads + [entry, entry, leave, leave],
            out_specs=[pl.BlockSpec((3, rows, block), lambda k, s: (0, 0, k))] * members,
        ),
        out_shape=[jax.ShapeDtypeStruct((3, rows, units), bf16)] * members,
        compiler_params=params(40),
        cost_estimate=cost(
            12 * members * rows * width * units, 12 * width * units + 8 * members * rows * width
        ),
        name="hidden_pieces",
    )(
        place, *own, *other, *([grad_own] * members), *([grad_other] * members),
        gate_up, taken, down, down_taken,
    )


def units_back_kernel(count, blocks, core, place, *refs):
    own, other, normed = refs[:count], refs[count : 2 * count], refs[2 * count : 3 * count]
    grads, gate_up = refs[3 * count : 3 * count + 2]
    parts = refs[3 * count + 2 : 4 * count + 2]
    sides = refs[4 * count + 2 : 4 * count + 6]
    first, second, gate, up, chosen, turned = refs[4 * count + 6 :]
    rows, half = own[0].shape[1:]
    step = pl.program_id(0)

    @pl.when(step == 0)
    def _():
        for at in range(count):
            span = pl.ds(at * rows, rows)
            for kind, units in ((0, gate), (1, up)):
                ordered(core, own[at].at[kind], other[at].at[kind], units.at[span], half)

    @pl.when(step < blocks)
    def _():
        for at in range(count):
            span = pl.ds(at * rows, rows)
            parts[at][...] = (
                dot(gate[span, :], gate_up[0], NT) + dot(up[span, :], gate_up[1], NT)
            ).astype(bf16)

    @pl.when((step >= blocks) & (step < 2 * blocks))
    def _():
        for at in range(count):
            turned[:, pl.ds(at * rows, rows)] = jnp.transpose(normed[at][...])
        for kind, units in ((0, gate), (1, up)):
            result = dot(turned[...], units[...]).astype(bf16)
            for side in range(2):

                @pl.when((step - blocks) // (blocks // 2) == side)
                def _():
                    sides[2 * kind + side][...] = result

    size = chosen.shape[1]
    starts = [(first, start) for start in range(0, half, size)]
    starts += [(second, start) for start in range(0, gate.shape[1] - half, size)]
    for at_step, (out, start) in enumerate(starts):

        @pl.when(step == 2 * blocks + at_step)
        def _():
            mine = (core[0] == 0) == (out is first)
            lanes = slice(start, start + size)
            for at in range(count):
                chosen[row_range(place[at], rows), :] = jnp.where(
                    mine, own[at][2, :, lanes], other[at][2, :, lanes]
                )
            out[...] = dot(chosen[...], grads[...], TN).astype(bf16)


def units_back(core, place, own, other, normed, grads, gate_up):
    count = len(own)
    _, rows, half = own[0].shape
    _, width, total = gate_up.shape
    block = block_of(width)
    blocks = width // block
    size = 384
    rest = total - half
    first_steps, second_steps = -(-half // size), -(-rest // size)
    once = pl.Buffered(1)

    def stage(start, stop):
        return lambda k: jnp.clip(k - start, 0, stop - start - 1)

    normed_at, side_at = stage(0, blocks), stage(blocks, 2 * blocks)
    first_at = stage(2 * blocks, 2 * blocks + first_steps)
    second_at = stage(2 * blocks + first_steps, 2 * blocks + first_steps + second_steps)
    sides = [
        pl.BlockSpec(
            (block, total),
            functools.partial(
                lambda side, k, *s: (
                    jnp.clip(side_at(k) - side * (blocks // 2), 0, blocks // 2 - 1),
                    0,
                ),
                side,
            ),
        )
        for _ in range(2)
        for side in range(2)
    ]
    result = pl.pallas_call(
        functools.partial(units_back_kernel, count, blocks),
        grid_spec=pltpu.PrefetchScalarGridSpec(
            num_scalar_prefetch=2,
            grid=(2 * blocks + first_steps + second_steps,),
            in_specs=[pl.BlockSpec((3, rows, half), lambda k, *s: (0, 0, 0), pipeline_mode=once)]
            * (2 * count)
            + [pl.BlockSpec((rows, block), lambda k, *s: (0, side_at(k)))] * count
            + [
                pl.BlockSpec(grads.shape, lambda k, *s: (0, 0), pipeline_mode=once),
                pl.BlockSpec((2, block, total), lambda k, *s: (0, normed_at(k), 0)),
            ],
            out_specs=[pl.BlockSpec((rows, block), lambda k, *s: (0, normed_at(k)))] * count
            + sides
            + [
                pl.BlockSpec((size, width), lambda k, *s: (first_at(k), 0)),
                pl.BlockSpec((size, width), lambda k, *s: (second_at(k), 0)),
            ],
            scratch_shapes=[
                pltpu.VMEM((count * rows, total), bf16),
                pltpu.VMEM((count * rows, total), bf16),
                pltpu.VMEM((count * rows, size), bf16),
                pltpu.VMEM((block, count * rows), bf16),
            ],
        ),
        out_shape=[jax.ShapeDtypeStruct((rows, width), bf16)] * count
        + [jax.ShapeDtypeStruct((width // 2, total), bf16)] * 4
        + [jax.ShapeDtypeStruct((half, width), bf16), jax.ShapeDtypeStruct((rest, width), bf16)],
        compiler_params=params(),
        cost_estimate=cost(
            10 * count * rows * width * total, 10 * width * total + 16 * count * rows * total
        ),
        name="units_back",
    )(core, place, *own, *other, *normed, grads, gate_up)
    return result[:count], result[count : count + 4], result[count + 4 :]


def down_out_kernel(count, core, *refs):
    own, other, down = refs[:count], refs[count : 2 * count], refs[2 * count]
    outs, units = refs[2 * count + 1 : -1], refs[-1]

    @pl.when(pl.program_id(0) == 0)
    def _():
        for at in range(count):
            ordered(core, own[at].at[0], other[at].at[0], units.at[at], own[at].shape[2])

    for at in range(count):
        outs[at][...] = dot(units[at], down[...]).astype(bf16)


def down_out(core, own, other, down):
    count = len(own)
    _, rows, half = own[0].shape
    total, width = down.shape
    block = block_of(width)
    piece = pl.BlockSpec((1, rows, half), lambda k, s: (2, 0, 0), pipeline_mode=pl.Buffered(1))
    return pl.pallas_call(
        functools.partial(down_out_kernel, count),
        grid_spec=pltpu.PrefetchScalarGridSpec(
            num_scalar_prefetch=1,
            grid=(width // block,),
            in_specs=[piece] * (2 * count) + [pl.BlockSpec((total, block), lambda k, s: (0, k))],
            out_specs=[pl.BlockSpec((rows, block), lambda k, s: (0, k))] * count,
            scratch_shapes=[pltpu.VMEM((count, rows, total), bf16)],
        ),
        out_shape=[jax.ShapeDtypeStruct((rows, width), bf16)] * count,
        compiler_params=params(),
        cost_estimate=cost(
            2 * count * rows * total * width, 2 * total * width + 4 * count * rows * total
        ),
        name="down_out",
    )(core, *own, *other, down)


def settle_kernel(middle, total, moved, *rest):
    rest[-1][0] = jnp.where(middle[0] == 1, total[...], moved[...]).astype(f32)


def settle(shape, index, start, block, clock, total, moved, before):
    rows, width = total.shape
    middle = clock(in_middle().astype(jnp.int32)[None])
    piece = pl.BlockSpec((block, width), lambda k, s: (k, 0))
    in_specs, args, aliases = [piece, piece], [total, moved], {}
    if before is not None:
        in_specs.append(pl.BlockSpec(memory_space=pl.ANY))
        args.append(before)
        aliases = {3: 0}
    return pl.pallas_call(
        settle_kernel,
        grid_spec=pltpu.PrefetchScalarGridSpec(
            num_scalar_prefetch=1,
            grid=(rows // block,),
            in_specs=in_specs,
            out_specs=pl.BlockSpec((1, block, width), lambda k, s: (index, start // block + k, 0)),
        ),
        out_shape=jax.ShapeDtypeStruct(shape, f32),
        input_output_aliases=aliases,
        compiler_params=params(16),
        cost_estimate=cost(0, 8 * rows * width),
        name="settle",
    )(middle, *args)


def weight_grad_kernel(pieces, kinds, parts, stacked, *refs):
    rows_in, units = refs[:pieces], refs[pieces : pieces + kinds]
    outs, rows = refs[pieces + kinds : -1], refs[-1]
    size = rows_in[0].shape[0]
    for at in range(pieces):
        rows[:, pl.ds(at * size, size)] = jnp.transpose(rows_in[at][...])
    steps = pl.num_programs(0) // parts
    for kind in range(kinds):
        array = units[kind][...]
        result = dot(rows[...], array.reshape(array.shape[-2:])).astype(bf16)
        if stacked:
            outs[0][kind] = result
            continue
        for at in range(parts):

            @pl.when(pl.program_id(0) // steps == at)
            def _():
                outs[kind * parts + at][...] = result


def weight_grads(rows, units, indices=(None,), parts=1, stacked=False):
    pieces, kinds = len(rows), len(units)
    size, width = rows[0].shape
    total, columns = units[0].shape[-2:]
    block = 256 if width // parts % 256 == 0 else LANES
    steps = width // block // parts
    specs = [
        pl.BlockSpec((total, columns), lambda k: (0, 0), pipeline_mode=pl.Buffered(1))
        if index is None
        else pl.BlockSpec(
            (1, total, columns),
            functools.partial(lambda at, k: (at, 0, 0), index),
            pipeline_mode=pl.Buffered(1),
        )
        for index in indices
    ]
    outs = [
        pl.BlockSpec(
            (block, columns),
            functools.partial(lambda at, k: (jnp.clip(k - at * steps, 0, steps - 1), 0), at),
        )
        for _ in range(kinds)
        for at in range(parts)
    ]
    shapes = [jax.ShapeDtypeStruct((width // parts, columns), bf16)] * (kinds * parts)
    if stacked:
        outs = [pl.BlockSpec((kinds, block, columns), lambda k: (0, k, 0))]
        shapes = [jax.ShapeDtypeStruct((kinds, width, columns), bf16)]
    return pl.pallas_call(
        functools.partial(weight_grad_kernel, pieces, kinds, parts, stacked),
        grid=(steps * parts,),
        in_specs=[pl.BlockSpec((size, block), lambda k: (0, k))] * pieces + specs,
        out_specs=outs,
        out_shape=shapes,
        scratch_shapes=[pltpu.VMEM((block, total), bf16)],
        compiler_params=params(),
        cost_estimate=cost(
            2 * total * width * columns * kinds,
            2 * (total * (width + columns * kinds) + width * columns * kinds),
        ),
        name="weight_grads",
    )(*rows, *units)


def mixed_grad_kernel(count, *refs):
    keep, taken, out = refs[-3:]
    for at in range(count):
        out[at] = (
            dot(refs[at][...], keep[...], NT) + dot(refs[count + at][...], taken[...], NT)
        ).astype(bf16)


def mixed_back(own, other, keep, taken):
    count = len(own)
    rows, width = own[0].shape
    units = keep.shape[0]
    return pl.pallas_call(
        functools.partial(mixed_grad_kernel, count),
        out_shape=jax.ShapeDtypeStruct((count, rows, units), bf16),
        compiler_params=params(),
        cost_estimate=cost(4 * count * rows * width * units, 4 * count * rows * width),
        name="mixed_back",
    )(*own, *other, keep, taken)


def project_back_kernel(swap, core, own, other, weight, *outs):
    units = outs[-1]
    count = own.shape[1]

    @pl.when(pl.program_id(0) == 0)
    def _():
        for kind in range(3):
            for at in range(count):
                ordered(
                    core,
                    own.at[kind, at],
                    other.at[kind, swap[at]],
                    units.at[kind, at],
                    own.shape[3],
                )

    for at in range(count):
        outs[at][...] = sum(
            dot(units[kind, at], weight[kind], NT) for kind in range(3)
        ).astype(bf16)


def project_back(core, swap, own, other, weight):
    _, count, rows, half = own.shape
    _, width, total = weight.shape
    block = block_of(width)
    whole = lambda k, *s: (0, 0, 0, 0)
    return pl.pallas_call(
        functools.partial(project_back_kernel, swap),
        grid_spec=pltpu.PrefetchScalarGridSpec(
            num_scalar_prefetch=1,
            grid=(width // block,),
            in_specs=[
                pl.BlockSpec((3, count, rows, half), whole),
                pl.BlockSpec((3, count, rows, half), whole),
                pl.BlockSpec((3, block, total), lambda k, *s: (0, k, 0)),
            ],
            out_specs=[pl.BlockSpec((rows, block), lambda k, *s: (0, k))] * count
            + [pl.BlockSpec((3, count, rows, total), whole)],
        ),
        out_shape=[jax.ShapeDtypeStruct((rows, width), bf16)] * count
        + [jax.ShapeDtypeStruct((3, count, rows, total), bf16)],
        compiler_params=params(),
        cost_estimate=cost(6 * count * rows * total * width, 2 * count * rows * (width + 6 * total)),
        name="project_back",
    )(core, own, other, weight)


def halves(weight, axis, width):
    lead = lax.slice_in_dim(weight, 0, width, axis=axis)
    rest = lax.slice_in_dim(weight, width, weight.shape[axis], axis=axis)
    pad = [(0, 0)] * weight.ndim
    pad[axis] = (0, width - rest.shape[axis])
    rest = jnp.pad(rest, pad)
    first = lax.axis_index("col") == 0
    return jnp.where(first, lead, rest), jnp.where(first, rest, lead)


def shards(
    block_input,
    norm1_gain,
    norm1_shift,
    qkv_weight,
    qkv_bias,
    out_weight,
    norm2_gain,
    norm2_shift,
    gate_up_weight,
    down_weight,
    output_grad,
):
    count = lax.axis_size("row")
    rows = block_input.shape[0]
    core = lax.axis_index("col").astype(jnp.int32)[None]
    place, swap = places()
    place = place.astype(jnp.int32)
    slot = inverse_places(place)
    half_units = out_weight.shape[0] // 2
    total_hidden = down_weight.shape[0]
    half_hidden = -(-total_hidden // (2 * LANES)) * LANES
    if grid_rows():
        groups = (((2,), 2), ((0, 1), 0), ((3,), 3))
    else:
        groups = tuple(((at,), at) for at in range(count))

    clock = Clock()
    inputs = block_input.astype(f32)
    gain_one = norm1_gain.astype(f32)
    gain_two = norm2_gain.astype(f32)
    split = {}

    def between(stats):
        split["keep"], split["send"] = halves(after(qkv_weight, stats), 2, half_units)
        return split["keep"]

    hat_one, inverse_one = normalize(inputs, between)
    normed_one = clock.mark((hat_one * gain_one + norm1_shift.astype(f32)).astype(bf16))

    one_own, fetch = gather_rows(normed_one)
    grad_own = None if grid_rows() else gather_whole(output_grad)
    qkv_keep = split["keep"]
    qkv_taken = sibling(split["send"])
    cosine, sine = rotary_tables(count, rows)
    bias = qkv_bias[:, None, :]
    qkv = None
    for group, index in groups:
        if qkv is not None and len(one_own) < count:
            grad_own = gather_whole(after(output_grad, one_own[0], one_own[1], clock.last))
            one_own += fetch(clock.last)
        others = [sibling(clock(one_own[swap[at]])) for at in group]
        qkv = clock.mark(
            project_pieces(
                index, group, count, place, [one_own[at] for at in group], others,
                qkv_keep, qkv_taken, clock(bias), cosine, sine, qkv,
            )
        )
        if group == groups[0][0]:
            gate_up_keep, gate_up_send = halves(clock(gate_up_weight), 2, half_hidden)
            clock.mark(gate_up_keep)
            down_keep, down_send = halves(clock(down_weight), 0, half_hidden)
            clock.mark(down_keep)
            out_keep, out_send = halves(clock(out_weight), 0, half_units)
            clock.mark(out_keep)
    gate_up_taken = sibling(clock(gate_up_send))
    down_taken = sibling(clock(down_send))
    out_taken = sibling(clock(out_send))
    mixed, kept, logsum = attend_forward(clock(slot), qkv)
    clock.mark(mixed)
    *branch, mixed_units = mixed_out(clock(core), swap, mixed, sibling(mixed), out_weight)
    clock.mark(branch[0])
    branch = scatter_rows(branch, clock)
    grad_other = sibling(clock(grad_own))
    after_rows = inputs + branch
    hat_two, inverse_two = normalize(after_rows)
    normed_two = clock.mark((hat_two * gain_two + norm2_shift.astype(f32)).astype(bf16))

    two_own, fetch = gather_rows(normed_two)
    mine, theirs = [None] * count, [None] * count
    for group, _ in groups:
        if group != groups[0][0] and len(two_own) < count:
            two_own += fetch(clock.last)
        results = hidden_pieces(
            group, clock(place),
            [two_own[at] for at in group],
            [sibling(clock(two_own[swap[at]])) for at in group],
            grad_own, grad_other, gate_up_keep, gate_up_taken, down_keep, down_taken,
        )
        clock.mark(results[0])
        for at, result in zip(group, results):
            mine[at] = result
        for at in group:
            theirs[at] = sibling(mine[swap[at]])

    normed_parts, gate_up_parts, down_grads = units_back(
        clock(core), place, mine, theirs, two_own, grad_own, gate_up_weight
    )
    clock.mark(normed_parts[0])
    sums = Line(clock)
    sums.add(*down_grads, *gate_up_parts)
    normed_two_grad = clock.mark(scatter_rows(normed_parts, clock))
    after_grad = output_grad.astype(f32) + norm_back(
        normed_two_grad * gain_two, hat_two, inverse_two
    )
    branch_grad = clock.mark(after_grad.astype(bf16))
    branch_own, fetch = gather_rows(branch_grad)
    sums.join()
    down_parts = down_out(clock(core), mine, theirs, down_weight)
    clock.mark(down_parts[0])
    if len(branch_own) < count:
        branch_own += fetch(clock.last)
    branch_other = [sibling(branch_own[swap[at]]) for at in range(count)]
    sums.join()
    branch_rows = clock.mark(jnp.concatenate(branch_own, axis=0))
    mixed_grad = clock.mark(mixed_back(branch_own, branch_other, clock(out_keep), out_taken))
    sums.total_up()
    project_grad = clock.mark(
        attend_backward(clock(slot), place, qkv, mixed_grad, kept, logsum, cosine, sine)
    )
    project_other = sibling(project_grad)
    parts = weight_grads([mixed_units.reshape(count * rows, -1)], [clock(branch_rows)])
    clock.mark(parts[0])
    sums.add(*parts)
    sums.join()
    sums.total_up()
    if grid_rows():
        far = first_way(down_parts[3])
        near = first_way(down_parts[0])
        side = second_way(clock.mark(plus(down_parts[1], clock(far))))
    *one_parts, project_units = project_back(
        clock(core), swap, project_grad, project_other, qkv_weight
    )
    clock.mark(one_parts[0])
    if grid_rows():
        down = down_parts[2].astype(f32) + near.astype(f32) + clock(side).astype(f32)
    else:
        down = scatter_rows(down_parts, clock)
    block_output = clock.mark((after_rows + down).astype(bf16))
    project_units = project_units.reshape(3, count * rows, -1)
    qkv_parts = weight_grads(one_own, [clock(project_units)] * 3, (0, 1, 2))
    clock.mark(qkv_parts[0])
    sums.join()
    sums.total_up()
    normed_one_grad = clock.mark(scatter_rows(one_parts, clock))
    input_grad = after_grad + norm_back(normed_one_grad * gain_one, hat_one, inverse_one)
    gains = jnp.stack(
        [
            jnp.sum(normed_one_grad * hat_one, axis=0),
            jnp.sum(normed_one_grad, axis=0),
            jnp.sum(normed_two_grad * hat_two, axis=0),
            jnp.sum(normed_two_grad, axis=0),
        ]
    )
    width = gains.shape[1]
    gains = clock.mark(gains)
    sums.join()
    sums.total_up()
    gains = sum_rows(gains, clock)
    bias_grad = jnp.sum(clock(project_grad).astype(f32), axis=(1, 2))
    clock.mark(bias_grad)
    small = jnp.concatenate([gains.reshape(-1, LANES), bias_grad.reshape(-1, LANES)], axis=0)
    sums.add(small, *qkv_parts)
    input_grad = clock.mark(clock(input_grad))
    half_width = two_own[0].shape[1] // 2
    block = block_of(half_width)
    shape = gate_up_weight.shape
    qkv_block = block_of(qkv_weight.shape[1])
    sums.join()
    sums.total_up()
    down_grad = sums.settle((1,) + down_weight.shape, ((0, 0), (0, half_hidden)), LANES)
    sums.join()
    sums.total_up()
    gate_up_grad = sums.settle(shape, ((0, 0), (0, half_width)), block)
    sums.join()
    sums.total_up()
    gate_up_grad = sums.settle(shape, ((1, 0),), block, gate_up_grad)
    sums.join()
    sums.total_up()
    gate_up_grad = sums.settle(shape, ((1, half_width),), block, gate_up_grad)
    sums.join()
    sums.total_up()
    out_grad = sums.settle((1,) + out_weight.shape, ((0, 0),), block_of(out_weight.shape[0]))
    sums.join()
    sums.total_up()
    small = sums.small(7)
    sums.settled = 8
    qkv_grad = sums.settle(qkv_weight.shape, ((0, 0),), qkv_block)
    sums.total_up()
    qkv_grad = sums.settle(qkv_weight.shape, ((1, 0), (2, 0)), qkv_block, qkv_grad)
    gains = small[: 4 * width // LANES].reshape(4, width)
    bias_grad = small[4 * width // LANES :].reshape(bias_grad.shape)
    return (
        block_output,
        input_grad,
        gains[0],
        gains[1],
        qkv_grad,
        bias_grad,
        out_grad[0],
        gains[2],
        gains[3],
        gate_up_grad,
        down_grad[0],
    )


def inverse_places(place):
    spots = jnp.arange(place.shape[0])
    return jnp.sum(
        jnp.where(place[None, :] == spots[:, None], spots[None, :], 0), axis=1
    ).astype(jnp.int32)


def solution(mesh):
    placed = (
        P(("dp", "row"), "col"),
        P("col"),
        P("col"),
        P(None, "col", "row"),
        P(None, ("row", "col")),
        P("row", "col"),
        P("col"),
        P("col"),
        P(None, "col", "row"),
        P("row", "col"),
        P(("dp", "row"), "col"),
    )
    return jax.shard_map(
        shards,
        mesh=mesh,
        in_specs=placed,
        out_specs=(
            P(("dp", "row"), "col"),
            P(("dp", "row"), "col"),
            P("col"),
            P("col"),
            P(None, "col", "row"),
            P(None, ("row", "col")),
            P("row", "col"),
            P("col"),
            P("col"),
            P(None, "col", "row"),
            P("row", "col"),
        ),
        check_vma=False,
    )
```

```python
import functools

import jax
import jax.numpy as jnp
import numpy as np
from jax import lax
from jax.experimental import pallas as pl
from jax.experimental.pallas import tpu as pltpu
from jax.sharding import PartitionSpec as P

HD = 64
ROT = 16
LANES = 128

epsilon = 1e-05
base_rate = 10000.0
bf16 = jnp.bfloat16
f32 = jnp.float32

NN = (((1,), (0,)), ((), ()))
NT = (((1,), (1,)), ((), ()))
TN = (((0,), (0,)), ((), ()))


def dot(first, second, dims=NN):
    return lax.dot_general(first, second, dims, preferred_element_type=f32)


def row_permute(values, core_zero, core_one):
    pairs = [
        (row * 2 + core, (row ^ (core_one if core else core_zero)) * 2 + core)
        for row in range(4)
        for core in range(2)
    ]
    return lax.ppermute(values, ("row", "col"), pairs)


def first_way(values):
    return row_permute(values, 1, 2)


def second_way(values):
    return row_permute(values, 2, 1)


def sibling(values):
    return lax.ppermute(values, "col", [(0, 1), (1, 0)])


def grid_rows():
    return lax.axis_size("row") == 4


def places():
    row, core = lax.axis_index("row"), lax.axis_index("col")
    if grid_rows():
        one = jnp.where(core == 0, 1, 2)
        return jnp.stack([row ^ one, row ^ (3 - one), row, row ^ 3]), (1, 0, 2, 3)
    count = lax.axis_size("row")
    return jnp.arange(count), tuple(range(count))


def after(value, *earlier):
    return lax.optimization_barrier((value,) + earlier)[0]


def gather_rows(own):
    if grid_rows():
        near = first_way(own)
        side = second_way(own)
        return [near, side, own], lambda *earlier: [second_way(after(near, side, *earlier))]
    whole = lax.all_gather(own, "row", axis=0, tiled=True)
    return jnp.split(whole, lax.axis_size("row"), axis=0), lambda *earlier: []


def scatter_rows(parts, clock):
    if grid_rows():
        passing = first_way(parts[3])
        near = first_way(parts[0])
        side = second_way(clock.mark(plus(parts[1], clock(passing))))
        return parts[2].astype(f32) + near.astype(f32) + side.astype(f32)
    whole = jnp.concatenate(parts, axis=0)
    return lax.psum_scatter(whole, "row", scatter_dimension=0, tiled=True).astype(f32)


def line():
    return lax.axis_size("dp") == 4


def in_middle():
    place = lax.axis_index("dp")
    return (place == 1) | (place == 2)


def inward(part):
    return lax.ppermute(part, "dp", [(0, 1), (3, 2)])


def across(part):
    return lax.ppermute(part, "dp", [(1, 2), (2, 1)])


def outward(part):
    return lax.ppermute(part, "dp", [(1, 0), (2, 3)])


def plus(first, second):
    return (first.astype(f32) + second.astype(f32)).astype(first.dtype)


class Clock:
    def __init__(self):
        self.last = None

    def __call__(self, value):
        return value if self.last is None else after(value, self.last)

    def mark(self, value):
        self.last = value
        return value


class Line:
    def __init__(self, clock):
        self.clock = clock
        self.parts, self.inner, self.half, self.other, self.total, self.outer = ([] for _ in range(6))
        self.settled = 0

    def feed(self):
        at = len(self.inner)
        if at < len(self.parts) and at < len(self.half) + 2:
            part = self.parts[at]
            self.inner.append(inward(after(part, self.inner[at - 2]) if at >= 2 else part))

    def add(self, *parts):
        self.parts += parts
        if line():
            for _ in parts:
                self.feed()

    def join(self):
        if line():
            at = len(self.half)
            self.half.append(self.clock.mark(plus(self.parts[at], self.clock(self.inner[at]))))
            self.feed()
            self.other.append(across(self.half[at]))

    def total_up(self):
        if line():
            at = len(self.total)
            self.total.append(self.clock.mark(plus(self.half[at], self.clock(self.other[at]))))
            self.outer.append(outward(self.total[at]))

    def settle(self, shape, places, block, before=None):
        for index, start in places:
            at = self.settled
            self.settled += 1
            if line():
                before = self.clock.mark(
                    settle(shape, index, start, block, self.clock, self.total[at], self.outer[at], before)
                )
            else:
                value = lax.psum(self.parts[at], "dp").astype(f32)[None]
                before = jnp.zeros(shape, f32) if before is None else before
                before = lax.dynamic_update_slice(before, value, (index, start, 0))
        return before

    def small(self, at):
        if line():
            return jnp.where(in_middle(), self.total[at], self.outer[at])
        return lax.psum(self.parts[at], "dp")


def gather_whole(own):
    return lax.all_gather(own, "row", axis=0, tiled=True)


def scatter_whole(parts):
    return lax.psum_scatter(parts, "row", scatter_dimension=0, tiled=True).astype(f32)


def sum_rows(values, clock):
    if grid_rows():
        values = clock.mark(values + clock(first_way(values)))
        return clock.mark(values + clock(second_way(values)))
    return lax.psum(values, "row")


def width_pair(first, second, between=None):
    both = jnp.stack([first, second])
    moved = sibling(both)
    if between is not None:
        moved = after(moved, between(both))
    both = both + moved
    return both[0], both[1]


def normalize(values, between=None):
    width = values.shape[1] * lax.axis_size("col")
    totals, squares = width_pair(
        jnp.sum(values, axis=-1), jnp.sum(values * values, axis=-1), between
    )
    average = totals / width
    spread = squares / width - average * average
    inverse = lax.rsqrt(spread + epsilon)[:, None]
    return ((values - average[:, None]) * inverse, inverse)


def norm_back(scaled, normed_hat, inverse):
    width = normed_hat.shape[1] * lax.axis_size("col")
    first, second = width_pair(jnp.sum(scaled, axis=-1), jnp.sum(scaled * normed_hat, axis=-1))
    return inverse * (scaled - first[:, None] / width - normed_hat * second[:, None] / width)


def rotary_tables(count, rows):
    half_dims = ROT // 2
    lane = np.arange(LANES) % HD
    freqs = np.float32(base_rate) ** (-(2.0 * (lane % half_dims).astype(np.float32)) / np.float32(ROT))
    angles = np.arange(count * rows, dtype=np.float32)[:, None] * freqs.astype(np.float32)[None, :]
    turned = lane < ROT
    sign = np.where(lane < half_dims, -1.0, 1.0)
    cosine = np.where(turned, np.cos(angles.astype(np.float64)), 1.0)
    sine = np.where(turned, sign * np.sin(angles.astype(np.float64)), 0.0)
    shape = (count, rows, LANES)
    return jnp.asarray(cosine.reshape(shape), f32), jnp.asarray(sine.reshape(shape), f32)


def turn(values, cosine, sine):
    half_dims = ROT // 2
    lane = lax.broadcasted_iota(jnp.int32, values.shape, 1) % HD
    partner = jnp.where(
        lane < half_dims,
        pltpu.roll(values, LANES - half_dims, 1),
        pltpu.roll(values, half_dims, 1),
    )
    return values * cosine + partner * sine


def params(mib=60):
    return pltpu.CompilerParams(vmem_limit_bytes=mib << 20)


def cost(flops, moved, hard=0):
    return pl.CostEstimate(flops=int(flops), bytes_accessed=int(moved), transcendentals=int(hard))


def project_kernel(members, place, *refs):
    own, other = refs[:members], refs[members : 2 * members]
    keep, taken, bias = refs[2 * members : 2 * members + 3]
    cosine, sine = refs[2 * members + 3 : 3 * members + 3], refs[3 * members + 3 : 4 * members + 3]
    out = refs[-1]
    kind = pl.program_id(0)
    for at in range(members):
        result = dot(own[at][...], keep[0]) + dot(other[at][...], taken[0]) + bias[0].astype(f32)

        @pl.when(kind < 2)
        def _():
            for start in range(0, result.shape[1], LANES):
                part = slice(start, start + LANES)
                out[at, 0, :, part] = turn(result[:, part], cosine[at][0], sine[at][0]).astype(bf16)

        @pl.when(kind == 2)
        def _():
            out[at, 0] = result.astype(bf16)


def project_pieces(index, group, count, place, own, other, keep, taken, bias, cosine, sine, before):
    members = len(own)
    rows, width = own[0].shape
    units = keep.shape[2]
    piece = pl.BlockSpec((rows, width), lambda k, s: (0, 0), pipeline_mode=pl.Buffered(1))
    tables = [
        pl.BlockSpec((1, rows, LANES), functools.partial(lambda at, k, s: (s[at], 0, 0), at))
        for at in group
    ]
    weight = pl.BlockSpec((1, width, units), lambda k, s: (k, 0, 0))
    in_specs = [piece] * (2 * members) + [
        weight,
        weight,
        pl.BlockSpec((1, 1, units), lambda k, s: (k, 0, 0)),
        *tables,
        *tables,
    ]
    args = [*own, *other, keep, taken, bias] + [cosine] * members + [sine] * members
    aliases = {}
    if before is not None:
        aliases = {len(args) + 1: 0}
        in_specs.append(pl.BlockSpec(memory_space=pl.ANY))
        args.append(before)
    return pl.pallas_call(
        functools.partial(project_kernel, members),
        grid_spec=pltpu.PrefetchScalarGridSpec(
            num_scalar_prefetch=1,
            grid=(3,),
            in_specs=in_specs,
            out_specs=pl.BlockSpec((members, 1, rows, units), lambda k, s: (index, k, 0, 0)),
        ),
        out_shape=jax.ShapeDtypeStruct((count, 3, rows, units), bf16),
        input_output_aliases=aliases,
        compiler_params=params(24),
        cost_estimate=cost(
            12 * members * rows * width * units, 4 * members * rows * width + 12 * width * units
        ),
        name="project_pieces",
    )(place, *args)


def causal(rows):
    keys = lax.broadcasted_iota(jnp.int32, (rows, rows), 0)
    return keys <= lax.broadcasted_iota(jnp.int32, (rows, rows), 1)


def head_lanes(values, head):
    lane = lax.broadcasted_iota(jnp.int32, values.shape, 1)
    return jnp.where((lane >= head * HD) & (lane < (head + 1) * HD), values, jnp.zeros_like(values))


def walk(stop, body, carry):
    if isinstance(stop, int):
        for step in range(stop):
            carry = body(step, carry)
        return carry
    return lax.fori_loop(0, stop, body, carry)


def each(count, body):
    if count <= 4:
        for step in range(count):
            body(step)
    else:
        lax.fori_loop(0, count, lambda step, carry: (body(step), carry)[1], 0)


def row_range(step, rows):
    return pl.ds(step * rows if isinstance(step, int) else pl.multiple_of(step * rows, rows), rows)


def attend_kernel(slot, qkv, mixed, kept, logsum, scores):
    count, _, rows, _ = qkv.shape
    heads = LANES // HD
    scale = HD**-0.5

    def one(at):
        here = slot[at]
        query = qkv[here, 0] * jnp.asarray(scale, bf16)
        for head in range(heads):

            def look(past, highest):
                block = dot(head_lanes(qkv[slot[past], 1], head), query, NT)
                scores[row_range(past, rows), :] = block
                return jnp.maximum(highest, jnp.max(block, axis=0, keepdims=True))

            def add(past, carry):
                total, outs = carry
                weights = jnp.exp(scores[row_range(past, rows), :] - highest)
                total = total + jnp.sum(weights, axis=0, keepdims=True)
                value = jnp.transpose(qkv[slot[past], 2])[head * HD : (head + 1) * HD]
                return total, outs + dot(value, weights.astype(bf16))

            block = dot(head_lanes(qkv[here, 1], head), query, NT)
            block = jnp.where(causal(rows), block, -1e30)
            scores[row_range(at, rows), :] = block
            highest = walk(at, look, jnp.max(block, axis=0, keepdims=True))
            total, outs = walk(
                at + 1, add, (jnp.zeros((1, rows), f32), jnp.zeros((HD, rows), f32))
            )
            kept[0, here, pl.ds(head * HD, HD), :] = outs / total
            logsum[0, here, pl.ds(head, 1), :] = highest + jnp.log(total)
        mixed[here] = jnp.transpose(kept[0, here]).astype(bf16)

    each(count, one)


def attend_forward(slot, qkv):
    count, _, rows, units = qkv.shape
    pairs = units // LANES
    work = rows * rows * count * (count + 1) // 2 * units
    return pl.pallas_call(
        attend_kernel,
        grid_spec=pltpu.PrefetchScalarGridSpec(
            num_scalar_prefetch=1,
            grid=(pairs,),
            in_specs=[pl.BlockSpec((count, 3, rows, LANES), lambda p, s: (0, 0, 0, p))],
            out_specs=[
                pl.BlockSpec((count, rows, LANES), lambda p, s: (0, 0, p)),
                pl.BlockSpec((1, count, LANES, rows), lambda p, s: (p, 0, 0, 0)),
                pl.BlockSpec((1, count, 8, rows), lambda p, s: (p, 0, 0, 0)),
            ],
            scratch_shapes=[pltpu.VMEM((count * rows, rows), f32)],
        ),
        out_shape=[
            jax.ShapeDtypeStruct((count, rows, units), bf16),
            jax.ShapeDtypeStruct((pairs, count, LANES, rows), f32),
            jax.ShapeDtypeStruct((pairs, count, 8, rows), f32),
        ],
        compiler_params=params(40),
        cost_estimate=cost(16 * work, 16 * count * rows * units, work // HD),
        name="attend_forward",
    )(slot, qkv)


def attend_back_kernel(slot, place, qkv, grads, kept, logsum, cosine, sine, out, dq, dk, dv, inner):
    count, _, rows, _ = qkv.shape
    heads = LANES // HD
    scale = HD**-0.5
    dk[...] = jnp.zeros_like(dk)
    dv[...] = jnp.zeros_like(dv)

    def sums(at):
        product = jnp.transpose(grads[at].astype(f32)) * kept[0, at]
        for head in range(heads):
            part = product[head * HD : (head + 1) * HD]
            inner[at, pl.ds(head, 1), :] = jnp.sum(part, axis=0, keepdims=True)

    def one(at):
        here = slot[at]
        query = qkv[here, 0] * jnp.asarray(scale, bf16)
        grad = grads[here]
        for head in range(heads):
            query_head = head_lanes(query, head)
            grad_head = head_lanes(grad, head)

            def look(past, query_grad, last=False):
                there = slot[past]
                key = qkv[there, 1]
                block = dot(key, query_head, NT)
                weights = jnp.exp(block - logsum[0, here, pl.ds(head, 1), :])
                if last:
                    weights = jnp.where(causal(rows), weights, 0.0)
                moved = dot(qkv[there, 2], grad_head, NT)
                raw = (weights * (moved - inner[here, pl.ds(head, 1), :])).astype(bf16)
                dv[there] += dot(weights.astype(bf16), grad_head)
                dk[there] += dot(raw, query_head)
                turned = jnp.transpose(key)[head * HD : (head + 1) * HD]
                return query_grad + dot(turned, raw)

            query_grad = walk(at, look, jnp.zeros((HD, rows), f32))
            dq[pl.ds(head * HD, HD), :] = look(at, query_grad, True) * scale
        out[0, here] = turn(jnp.transpose(dq[...]), cosine[at], -sine[at]).astype(bf16)

    def finish(at):
        out[1, at] = turn(dk[at], cosine[place[at]], -sine[place[at]]).astype(bf16)
        out[2, at] = dv[at].astype(bf16)

    each(count, sums)
    each(count, one)
    each(count, finish)


def attend_backward(slot, place, qkv, grads, kept, logsum, cosine, sine):
    count, _, rows, units = qkv.shape
    pairs = units // LANES
    work = rows * rows * count * (count + 1) // 2 * units
    table = pl.BlockSpec((count, rows, LANES), lambda p, *s: (0, 0, 0))
    return pl.pallas_call(
        attend_back_kernel,
        grid_spec=pltpu.PrefetchScalarGridSpec(
            num_scalar_prefetch=2,
            grid=(pairs,),
            in_specs=[
                pl.BlockSpec((count, 3, rows, LANES), lambda p, *s: (0, 0, 0, p)),
                pl.BlockSpec((count, rows, LANES), lambda p, *s: (0, 0, p)),
                pl.BlockSpec((1, count, LANES, rows), lambda p, *s: (p, 0, 0, 0)),
                pl.BlockSpec((1, count, 8, rows), lambda p, *s: (p, 0, 0, 0)),
                table,
                table,
            ],
            out_specs=pl.BlockSpec((3, count, rows, LANES), lambda p, *s: (0, 0, 0, p)),
            scratch_shapes=[
                pltpu.VMEM((LANES, rows), f32),
                pltpu.VMEM((count, rows, LANES), f32),
                pltpu.VMEM((count, rows, LANES), f32),
                pltpu.VMEM((count, 8, rows), f32),
            ],
        ),
        out_shape=jax.ShapeDtypeStruct((3, count, rows, units), bf16),
        compiler_params=params(),
        cost_estimate=cost(40 * work, 24 * count * rows * units, work // HD),
        name="attend_backward",
    )(slot, place, qkv, grads, kept, logsum, cosine, sine)


def ordered(core, own, other, out, width):
    rest = out.shape[-1] - width
    lead = core[0] == 0
    out[..., :width] = jnp.where(lead, own[...], other[...])
    out[..., width:] = jnp.where(lead, other[..., :rest], own[..., :rest])


def block_of(width):
    return 256 if width % 256 == 0 else LANES


def mixed_out_kernel(swap, core, own, other, weight, *outs):
    units = outs[-1]
    count = own.shape[0]

    @pl.when(pl.program_id(0) == 0)
    def _():
        for at in range(count):
            ordered(core, own.at[at], other.at[swap[at]], units.at[at], own.shape[2])

    for at in range(count):
        outs[at][...] = dot(units[at], weight[...]).astype(bf16)


def mixed_out(core, swap, own, other, weight):
    count, rows, units = own.shape
    width = weight.shape[1]
    block = block_of(width)
    whole = lambda k, *s: (0, 0, 0)
    return pl.pallas_call(
        functools.partial(mixed_out_kernel, swap),
        grid_spec=pltpu.PrefetchScalarGridSpec(
            num_scalar_prefetch=1,
            grid=(width // block,),
            in_specs=[
                pl.BlockSpec((count, rows, units), whole),
                pl.BlockSpec((count, rows, units), whole),
                pl.BlockSpec((2 * units, block), lambda k, *s: (0, k)),
            ],
            out_specs=[pl.BlockSpec((rows, block), lambda k, *s: (0, k))] * count
            + [pl.BlockSpec((count, rows, 2 * units), whole)],
        ),
        out_shape=[jax.ShapeDtypeStruct((rows, width), bf16)] * count
        + [jax.ShapeDtypeStruct((count, rows, 2 * units), bf16)],
        compiler_params=params(24),
        cost_estimate=cost(4 * count * rows * units * width, 2 * count * rows * (width + 4 * units)),
        name="mixed_out",
    )(core, own, other, weight)


def hidden_kernel(members, place, *refs):
    own, other, grad_own, grad_other = (refs[k * members : (k + 1) * members] for k in range(4))
    gate_up, taken, down, down_taken = refs[4 * members : 4 * members + 4]
    outs = refs[4 * members + 4 :]
    for at in range(members):
        gate = dot(own[at][...], gate_up[0]) + dot(other[at][...], taken[0])
        up = dot(own[at][...], gate_up[1]) + dot(other[at][...], taken[1])
        grad = dot(grad_own[at][...], down[...], NT) + dot(grad_other[at][...], down_taken[...], NT)
        sigmoid = jax.nn.sigmoid(gate)
        silu = gate * sigmoid
        slope = sigmoid * (1.0 + gate * (1.0 - sigmoid))
        outs[at][0] = (grad * up * slope).astype(bf16)
        outs[at][1] = (grad * silu).astype(bf16)
        outs[at][2] = (silu * up).astype(bf16)


def hidden_pieces(group, place, own, other, grad_own, grad_other, gate_up, taken, down, down_taken):
    members = len(own)
    rows, width = own[0].shape
    units = gate_up.shape[2]
    block = block_of(units)
    rows_in = pl.BlockSpec((rows, width), lambda k, s: (0, 0), pipeline_mode=pl.Buffered(1))
    grads = [
        pl.BlockSpec(
            (rows, width),
            functools.partial(lambda at, k, s: (s[at], 0), at),
            pipeline_mode=pl.Buffered(1),
        )
        for at in group
    ]
    entry = pl.BlockSpec((2, width, block), lambda k, s: (0, 0, k))
    leave = pl.BlockSpec((block, width), lambda k, s: (k, 0))
    return pl.pallas_call(
        functools.partial(hidden_kernel, members),
        grid_spec=pltpu.PrefetchScalarGridSpec(
            num_scalar_prefetch=1,
            grid=(units // block,),
            in_specs=[rows_in] * (2 * members) + grads + grads + [entry, entry, leave, leave],
            out_specs=[pl.BlockSpec((3, rows, block), lambda k, s: (0, 0, k))] * members,
        ),
        out_shape=[jax.ShapeDtypeStruct((3, rows, units), bf16)] * members,
        compiler_params=params(40),
        cost_estimate=cost(
            12 * members * rows * width * units, 12 * width * units + 8 * members * rows * width
        ),
        name="hidden_pieces",
    )(
        place, *own, *other, *([grad_own] * members), *([grad_other] * members),
        gate_up, taken, down, down_taken,
    )


def units_back_kernel(count, blocks, core, place, *refs):
    own, other, normed = refs[:count], refs[count : 2 * count], refs[2 * count : 3 * count]
    grads, gate_up = refs[3 * count : 3 * count + 2]
    parts = refs[3 * count + 2 : 4 * count + 2]
    sides = refs[4 * count + 2 : 4 * count + 6]
    first, second, gate, up, chosen, turned = refs[4 * count + 6 :]
    rows, half = own[0].shape[1:]
    step = pl.program_id(0)

    @pl.when(step == 0)
    def _():
        for at in range(count):
            span = pl.ds(at * rows, rows)
            for kind, units in ((0, gate), (1, up)):
                ordered(core, own[at].at[kind], other[at].at[kind], units.at[span], half)

    @pl.when(step < blocks)
    def _():
        result = (dot(gate[...], gate_up[0], NT) + dot(up[...], gate_up[1], NT)).astype(bf16)
        for at in range(count):
            parts[at][...] = result[at * rows : (at + 1) * rows]

    @pl.when((step >= blocks) & (step < 2 * blocks))
    def _():
        for at in range(count):
            turned[:, pl.ds(at * rows, rows)] = jnp.transpose(normed[at][...])
        for kind, units in ((0, gate), (1, up)):
            result = dot(turned[...], units[...]).astype(bf16)
            for side in range(2):

                @pl.when((step - blocks) // (blocks // 2) == side)
                def _():
                    sides[2 * kind + side][...] = result

    size = chosen.shape[1]
    starts = [(first, start) for start in range(0, half, size)]
    starts += [(second, start) for start in range(0, gate.shape[1] - half, size)]
    for at_step, (out, start) in enumerate(starts):

        @pl.when(step == 2 * blocks + at_step)
        def _():
            mine = (core[0] == 0) == (out is first)
            lanes = slice(start, start + size)
            for at in range(count):
                chosen[row_range(place[at], rows), :] = jnp.where(
                    mine, own[at][2, :, lanes], other[at][2, :, lanes]
                )
            out[...] = dot(chosen[...], grads[...], TN).astype(bf16)


def units_back(core, place, own, other, normed, grads, gate_up):
    count = len(own)
    _, rows, half = own[0].shape
    _, width, total = gate_up.shape
    block = block_of(width)
    blocks = width // block
    size = 384
    rest = total - half
    first_steps, second_steps = -(-half // size), -(-rest // size)
    once = pl.Buffered(1)

    def stage(start, stop):
        return lambda k: jnp.clip(k - start, 0, stop - start - 1)

    normed_at, side_at = stage(0, blocks), stage(blocks, 2 * blocks)
    first_at = stage(2 * blocks, 2 * blocks + first_steps)
    second_at = stage(2 * blocks + first_steps, 2 * blocks + first_steps + second_steps)
    sides = [
        pl.BlockSpec(
            (block, total),
            functools.partial(
                lambda side, k, *s: (
                    jnp.clip(side_at(k) - side * (blocks // 2), 0, blocks // 2 - 1),
                    0,
                ),
                side,
            ),
        )
        for _ in range(2)
        for side in range(2)
    ]
    result = pl.pallas_call(
        functools.partial(units_back_kernel, count, blocks),
        grid_spec=pltpu.PrefetchScalarGridSpec(
            num_scalar_prefetch=2,
            grid=(2 * blocks + first_steps + second_steps,),
            in_specs=[pl.BlockSpec((3, rows, half), lambda k, *s: (0, 0, 0), pipeline_mode=once)]
            * (2 * count)
            + [pl.BlockSpec((rows, block), lambda k, *s: (0, side_at(k)))] * count
            + [
                pl.BlockSpec(grads.shape, lambda k, *s: (0, 0), pipeline_mode=once),
                pl.BlockSpec((2, block, total), lambda k, *s: (0, normed_at(k), 0)),
            ],
            out_specs=[pl.BlockSpec((rows, block), lambda k, *s: (0, normed_at(k)))] * count
            + sides
            + [
                pl.BlockSpec((size, width), lambda k, *s: (first_at(k), 0)),
                pl.BlockSpec((size, width), lambda k, *s: (second_at(k), 0)),
            ],
            scratch_shapes=[
                pltpu.VMEM((count * rows, total), bf16),
                pltpu.VMEM((count * rows, total), bf16),
                pltpu.VMEM((count * rows, size), bf16),
                pltpu.VMEM((block, count * rows), bf16),
            ],
        ),
        out_shape=[jax.ShapeDtypeStruct((rows, width), bf16)] * count
        + [jax.ShapeDtypeStruct((width // 2, total), bf16)] * 4
        + [jax.ShapeDtypeStruct((half, width), bf16), jax.ShapeDtypeStruct((rest, width), bf16)],
        compiler_params=params(),
        cost_estimate=cost(
            10 * count * rows * width * total, 10 * width * total + 16 * count * rows * total
        ),
        name="units_back",
    )(core, place, *own, *other, *normed, grads, gate_up)
    return result[:count], result[count : count + 4], result[count + 4 :]


def down_out_kernel(count, core, *refs):
    own, other, down = refs[:count], refs[count : 2 * count], refs[2 * count]
    outs, units = refs[2 * count + 1 : -1], refs[-1]

    @pl.when(pl.program_id(0) == 0)
    def _():
        for at in range(count):
            ordered(core, own[at].at[0], other[at].at[0], units.at[at], own[at].shape[2])

    for at in range(count):
        outs[at][...] = dot(units[at], down[...]).astype(bf16)


def down_out(core, own, other, down):
    count = len(own)
    _, rows, half = own[0].shape
    total, width = down.shape
    block = block_of(width)
    piece = pl.BlockSpec((1, rows, half), lambda k, s: (2, 0, 0), pipeline_mode=pl.Buffered(1))
    return pl.pallas_call(
        functools.partial(down_out_kernel, count),
        grid_spec=pltpu.PrefetchScalarGridSpec(
            num_scalar_prefetch=1,
            grid=(width // block,),
            in_specs=[piece] * (2 * count) + [pl.BlockSpec((total, block), lambda k, s: (0, k))],
            out_specs=[pl.BlockSpec((rows, block), lambda k, s: (0, k))] * count,
            scratch_shapes=[pltpu.VMEM((count, rows, total), bf16)],
        ),
        out_shape=[jax.ShapeDtypeStruct((rows, width), bf16)] * count,
        compiler_params=params(),
        cost_estimate=cost(
            2 * count * rows * total * width, 2 * total * width + 4 * count * rows * total
        ),
        name="down_out",
    )(core, *own, *other, down)


def settle_kernel(middle, total, moved, *rest):
    rest[-1][0] = jnp.where(middle[0] == 1, total[...], moved[...]).astype(f32)


def settle(shape, index, start, block, clock, total, moved, before):
    rows, width = total.shape
    middle = clock(in_middle().astype(jnp.int32)[None])
    piece = pl.BlockSpec((block, width), lambda k, s: (k, 0))
    in_specs, args, aliases = [piece, piece], [total, moved], {}
    if before is not None:
        in_specs.append(pl.BlockSpec(memory_space=pl.ANY))
        args.append(before)
        aliases = {3: 0}
    return pl.pallas_call(
        settle_kernel,
        grid_spec=pltpu.PrefetchScalarGridSpec(
            num_scalar_prefetch=1,
            grid=(rows // block,),
            in_specs=in_specs,
            out_specs=pl.BlockSpec((1, block, width), lambda k, s: (index, start // block + k, 0)),
        ),
        out_shape=jax.ShapeDtypeStruct(shape, f32),
        input_output_aliases=aliases,
        compiler_params=params(16),
        cost_estimate=cost(0, 8 * rows * width),
        name="settle",
    )(middle, *args)


def weight_grad_kernel(pieces, kinds, parts, stacked, *refs):
    rows_in, units = refs[:pieces], refs[pieces : pieces + kinds]
    outs, rows = refs[pieces + kinds : -1], refs[-1]
    size = rows_in[0].shape[0]
    for at in range(pieces):
        rows[:, pl.ds(at * size, size)] = jnp.transpose(rows_in[at][...])
    steps = pl.num_programs(0) // parts
    for kind in range(kinds):
        array = units[kind][...]
        result = dot(rows[...], array.reshape(array.shape[-2:])).astype(bf16)
        if stacked:
            outs[0][kind] = result
            continue
        for at in range(parts):

            @pl.when(pl.program_id(0) // steps == at)
            def _():
                outs[kind * parts + at][...] = result


def weight_grads(rows, units, indices=(None,), parts=1, stacked=False):
    pieces, kinds = len(rows), len(units)
    size, width = rows[0].shape
    total, columns = units[0].shape[-2:]
    block = 256 if width // parts % 256 == 0 else LANES
    steps = width // block // parts
    specs = [
        pl.BlockSpec((total, columns), lambda k: (0, 0), pipeline_mode=pl.Buffered(1))
        if index is None
        else pl.BlockSpec(
            (1, total, columns),
            functools.partial(lambda at, k: (at, 0, 0), index),
            pipeline_mode=pl.Buffered(1),
        )
        for index in indices
    ]
    outs = [
        pl.BlockSpec(
            (block, columns),
            functools.partial(lambda at, k: (jnp.clip(k - at * steps, 0, steps - 1), 0), at),
        )
        for _ in range(kinds)
        for at in range(parts)
    ]
    shapes = [jax.ShapeDtypeStruct((width // parts, columns), bf16)] * (kinds * parts)
    if stacked:
        outs = [pl.BlockSpec((kinds, block, columns), lambda k: (0, k, 0))]
        shapes = [jax.ShapeDtypeStruct((kinds, width, columns), bf16)]
    return pl.pallas_call(
        functools.partial(weight_grad_kernel, pieces, kinds, parts, stacked),
        grid=(steps * parts,),
        in_specs=[pl.BlockSpec((size, block), lambda k: (0, k))] * pieces + specs,
        out_specs=outs,
        out_shape=shapes,
        scratch_shapes=[pltpu.VMEM((block, total), bf16)],
        compiler_params=params(),
        cost_estimate=cost(
            2 * total * width * columns * kinds,
            2 * (total * (width + columns * kinds) + width * columns * kinds),
        ),
        name="weight_grads",
    )(*rows, *units)


def mixed_grad_kernel(count, *refs):
    keep, taken, out = refs[-3:]
    for at in range(count):
        out[at] = (
            dot(refs[at][...], keep[...], NT) + dot(refs[count + at][...], taken[...], NT)
        ).astype(bf16)


def mixed_back(own, other, keep, taken):
    count = len(own)
    rows, width = own[0].shape
    units = keep.shape[0]
    return pl.pallas_call(
        functools.partial(mixed_grad_kernel, count),
        out_shape=jax.ShapeDtypeStruct((count, rows, units), bf16),
        compiler_params=params(),
        cost_estimate=cost(4 * count * rows * width * units, 4 * count * rows * width),
        name="mixed_back",
    )(*own, *other, keep, taken)


def project_back_kernel(swap, core, own, other, weight, *outs):
    units = outs[-1]
    count = own.shape[1]

    @pl.when(pl.program_id(0) == 0)
    def _():
        for kind in range(3):
            for at in range(count):
                ordered(
                    core,
                    own.at[kind, at],
                    other.at[kind, swap[at]],
                    units.at[kind, at],
                    own.shape[3],
                )

    for at in range(count):
        outs[at][...] = sum(
            dot(units[kind, at], weight[kind], NT) for kind in range(3)
        ).astype(bf16)


def project_back(core, swap, own, other, weight):
    _, count, rows, half = own.shape
    _, width, total = weight.shape
    block = block_of(width)
    whole = lambda k, *s: (0, 0, 0, 0)
    return pl.pallas_call(
        functools.partial(project_back_kernel, swap),
        grid_spec=pltpu.PrefetchScalarGridSpec(
            num_scalar_prefetch=1,
            grid=(width // block,),
            in_specs=[
                pl.BlockSpec((3, count, rows, half), whole),
                pl.BlockSpec((3, count, rows, half), whole),
                pl.BlockSpec((3, block, total), lambda k, *s: (0, k, 0)),
            ],
            out_specs=[pl.BlockSpec((rows, block), lambda k, *s: (0, k))] * count
            + [pl.BlockSpec((3, count, rows, total), whole)],
        ),
        out_shape=[jax.ShapeDtypeStruct((rows, width), bf16)] * count
        + [jax.ShapeDtypeStruct((3, count, rows, total), bf16)],
        compiler_params=params(),
        cost_estimate=cost(6 * count * rows * total * width, 2 * count * rows * (width + 6 * total)),
        name="project_back",
    )(core, own, other, weight)


def halves(weight, axis, width):
    lead = lax.slice_in_dim(weight, 0, width, axis=axis)
    rest = lax.slice_in_dim(weight, width, weight.shape[axis], axis=axis)
    pad = [(0, 0)] * weight.ndim
    pad[axis] = (0, width - rest.shape[axis])
    rest = jnp.pad(rest, pad)
    first = lax.axis_index("col") == 0
    return jnp.where(first, lead, rest), jnp.where(first, rest, lead)


def shards(
    block_input,
    norm1_gain,
    norm1_shift,
    qkv_weight,
    qkv_bias,
    out_weight,
    norm2_gain,
    norm2_shift,
    gate_up_weight,
    down_weight,
    output_grad,
):
    count = lax.axis_size("row")
    rows = block_input.shape[0]
    core = lax.axis_index("col").astype(jnp.int32)[None]
    place, swap = places()
    place = place.astype(jnp.int32)
    slot = inverse_places(place)
    half_units = out_weight.shape[0] // 2
    total_hidden = down_weight.shape[0]
    half_hidden = -(-total_hidden // (2 * LANES)) * LANES
    if grid_rows():
        groups = (((2,), 2), ((0, 1), 0), ((3,), 3))
    else:
        groups = tuple(((at,), at) for at in range(count))

    clock = Clock()
    inputs = block_input.astype(f32)
    gain_one = norm1_gain.astype(f32)
    gain_two = norm2_gain.astype(f32)
    split = {}

    def between(stats):
        split["keep"], split["send"] = halves(after(qkv_weight, stats), 2, half_units)
        return split["keep"]

    hat_one, inverse_one = normalize(inputs, between)
    normed_one = clock.mark((hat_one * gain_one + norm1_shift.astype(f32)).astype(bf16))

    one_own, fetch = gather_rows(normed_one)
    grad_own = None if grid_rows() else gather_whole(output_grad)
    qkv_keep = split["keep"]
    qkv_taken = sibling(split["send"])
    cosine, sine = rotary_tables(count, rows)
    bias = qkv_bias[:, None, :]
    qkv = None
    for group, index in groups:
        if qkv is not None and len(one_own) < count:
            grad_own = gather_whole(after(output_grad, one_own[0], one_own[1], clock.last))
            one_own += fetch(clock.last)
        others = [sibling(clock(one_own[swap[at]])) for at in group]
        qkv = clock.mark(
            project_pieces(
                index, group, count, place, [one_own[at] for at in group], others,
                qkv_keep, qkv_taken, clock(bias), cosine, sine, qkv,
            )
        )
        if group == groups[0][0]:
            gate_up_keep, gate_up_send = halves(clock(gate_up_weight), 2, half_hidden)
            clock.mark(gate_up_keep)
            down_keep, down_send = halves(clock(down_weight), 0, half_hidden)
            clock.mark(down_keep)
            out_keep, out_send = halves(clock(out_weight), 0, half_units)
            clock.mark(out_keep)
    gate_up_taken = sibling(clock(gate_up_send))
    down_taken = sibling(clock(down_send))
    out_taken = sibling(clock(out_send))
    mixed, kept, logsum = attend_forward(clock(slot), qkv)
    clock.mark(mixed)
    *branch, mixed_units = mixed_out(clock(core), swap, mixed, sibling(mixed), out_weight)
    clock.mark(branch[0])
    branch = scatter_rows(branch, clock)
    grad_other = sibling(clock(grad_own))
    after_rows = inputs + branch
    hat_two, inverse_two = normalize(after_rows)
    normed_two = clock.mark((hat_two * gain_two + norm2_shift.astype(f32)).astype(bf16))

    two_own, fetch = gather_rows(normed_two)
    mine, theirs = [None] * count, [None] * count
    for group, _ in groups:
        if group != groups[0][0] and len(two_own) < count:
            two_own += fetch(clock.last)
        results = hidden_pieces(
            group, clock(place),
            [two_own[at] for at in group],
            [sibling(clock(two_own[swap[at]])) for at in group],
            grad_own, grad_other, gate_up_keep, gate_up_taken, down_keep, down_taken,
        )
        clock.mark(results[0])
        for at, result in zip(group, results):
            mine[at] = result
        for at in group:
            theirs[at] = sibling(mine[swap[at]])

    normed_parts, gate_up_parts, down_grads = units_back(
        clock(core), place, mine, theirs, two_own, grad_own, gate_up_weight
    )
    clock.mark(normed_parts[0])
    sums = Line(clock)
    sums.add(*down_grads, *gate_up_parts)
    half_width = two_own[0].shape[1] // 2
    forms = {
        "down": ((1,) + down_weight.shape, LANES),
        "gate_up": (gate_up_weight.shape, block_of(half_width)),
        "out": ((1,) + out_weight.shape, block_of(out_weight.shape[0])),
        "qkv": (qkv_weight.shape, block_of(qkv_weight.shape[1])),
    }
    targets = [("down", 0, 0), ("down", 0, half_hidden)]
    targets += [("gate_up", kind, start) for kind in (0, 1) for start in (0, half_width)]
    targets += [("out", 0, 0), ("small", 0, 0)] + [("qkv", kind, 0) for kind in range(3)]
    settled = {}

    def settle_next():
        at = sums.settled
        name, part, start = targets[at]
        if name == "small":
            settled[name] = clock.mark(sums.small(at))
            sums.settled += 1
        else:
            shape, block = forms[name]
            settled[name] = sums.settle(shape, ((part, start),), block, settled.get(name))

    def tick():
        sums.join()
        sums.total_up()
        settle_next()

    normed_two_grad = clock.mark(scatter_rows(normed_parts, clock))
    after_grad = output_grad.astype(f32) + norm_back(
        normed_two_grad * gain_two, hat_two, inverse_two
    )
    branch_grad = clock.mark(after_grad.astype(bf16))
    branch_own, fetch = gather_rows(branch_grad)
    sums.join()
    down_parts = down_out(clock(core), mine, theirs, down_weight)
    clock.mark(down_parts[0])
    if len(branch_own) < count:
        branch_own += fetch(clock.last)
    branch_other = [sibling(branch_own[swap[at]]) for at in range(count)]
    sums.join()
    branch_rows = clock.mark(jnp.concatenate(branch_own, axis=0))
    mixed_grad = clock.mark(mixed_back(branch_own, branch_other, clock(out_keep), out_taken))
    sums.total_up()
    project_grad = clock.mark(
        attend_backward(clock(slot), place, qkv, mixed_grad, kept, logsum, cosine, sine)
    )
    project_other = sibling(project_grad)
    parts = weight_grads([mixed_units.reshape(count * rows, -1)], [clock(branch_rows)])
    clock.mark(parts[0])
    sums.add(*parts)
    sums.join()
    sums.total_up()
    if grid_rows():
        far = first_way(down_parts[3])
        near = first_way(down_parts[0])
        side = second_way(clock.mark(plus(down_parts[1], clock(far))))
    *one_parts, project_units = project_back(
        clock(core), swap, project_grad, project_other, qkv_weight
    )
    clock.mark(one_parts[0])
    if grid_rows():
        down = down_parts[2].astype(f32) + near.astype(f32) + clock(side).astype(f32)
    else:
        down = scatter_rows(down_parts, clock)
    block_output = clock.mark((after_rows + down).astype(bf16))
    settle_next()
    project_units = project_units.reshape(3, count * rows, -1)
    qkv_parts = weight_grads(one_own, [clock(project_units)] * 3, (0, 1, 2))
    clock.mark(qkv_parts[0])
    tick()
    normed_one_grad = clock.mark(scatter_rows(one_parts, clock))
    input_grad = after_grad + norm_back(normed_one_grad * gain_one, hat_one, inverse_one)
    gains = jnp.stack(
        [
            jnp.sum(normed_one_grad * hat_one, axis=0),
            jnp.sum(normed_one_grad, axis=0),
            jnp.sum(normed_two_grad * hat_two, axis=0),
            jnp.sum(normed_two_grad, axis=0),
        ]
    )
    width = gains.shape[1]
    gains = clock.mark(gains)
    tick()
    gains = sum_rows(gains, clock)
    bias_grad = jnp.sum(clock(project_grad).astype(f32), axis=(1, 2))
    clock.mark(bias_grad)
    small = jnp.concatenate([gains.reshape(-1, LANES), bias_grad.reshape(-1, LANES)], axis=0)
    sums.add(small, *qkv_parts)
    input_grad = clock.mark(clock(input_grad))
    while len(sums.half) < len(targets) if line() else sums.settled < len(targets) - 2:
        tick()
    sums.total_up()
    settle_next()
    settle_next()
    small = settled["small"]
    gains = small[: 4 * width // LANES].reshape(4, width)
    bias_grad = small[4 * width // LANES :].reshape(bias_grad.shape)
    return (
        block_output,
        input_grad,
        gains[0],
        gains[1],
        settled["qkv"],
        bias_grad,
        settled["out"][0],
        gains[2],
        gains[3],
        settled["gate_up"],
        settled["down"][0],
    )


def inverse_places(place):
    spots = jnp.arange(place.shape[0])
    return jnp.sum(
        jnp.where(place[None, :] == spots[:, None], spots[None, :], 0), axis=1
    ).astype(jnp.int32)


def solution(mesh):
    placed = (
        P(("dp", "row"), "col"),
        P("col"),
        P("col"),
        P(None, "col", "row"),
        P(None, ("row", "col")),
        P("row", "col"),
        P("col"),
        P("col"),
        P(None, "col", "row"),
        P("row", "col"),
        P(("dp", "row"), "col"),
    )
    return jax.shard_map(
        shards,
        mesh=mesh,
        in_specs=placed,
        out_specs=(
            P(("dp", "row"), "col"),
            P(("dp", "row"), "col"),
            P("col"),
            P("col"),
            P(None, "col", "row"),
            P(None, ("row", "col")),
            P("row", "col"),
            P("col"),
            P("col"),
            P(None, "col", "row"),
            P("row", "col"),
        ),
        check_vma=False,
    )
```

```python
import functools

import jax
import jax.numpy as jnp
import numpy as np
from jax import lax
from jax.experimental import pallas as pl
from jax.experimental.pallas import tpu as pltpu
from jax.sharding import PartitionSpec as P

HD = 64
ROT = 16
LANES = 128

epsilon = 1e-05
base_rate = 10000.0
bf16 = jnp.bfloat16
f32 = jnp.float32

NN = (((1,), (0,)), ((), ()))
NT = (((1,), (1,)), ((), ()))
TN = (((0,), (0,)), ((), ()))


def dot(first, second, dims=NN):
    return lax.dot_general(first, second, dims, preferred_element_type=f32)


def row_permute(values, core_zero, core_one):
    pairs = [
        (row * 2 + core, (row ^ (core_one if core else core_zero)) * 2 + core)
        for row in range(4)
        for core in range(2)
    ]
    return lax.ppermute(values, ("row", "col"), pairs)


def first_way(values):
    return row_permute(values, 1, 2)


def second_way(values):
    return row_permute(values, 2, 1)


def sibling(values):
    return lax.ppermute(values, "col", [(0, 1), (1, 0)])


def grid_rows():
    return lax.axis_size("row") == 4


def places():
    row, core = lax.axis_index("row"), lax.axis_index("col")
    if grid_rows():
        one = jnp.where(core == 0, 1, 2)
        return jnp.stack([row ^ one, row ^ (3 - one), row, row ^ 3]), (1, 0, 2, 3)
    count = lax.axis_size("row")
    return jnp.arange(count), tuple(range(count))


def after(value, *earlier):
    return lax.optimization_barrier((value,) + earlier)[0]


def gather_rows(own):
    if grid_rows():
        near = first_way(own)
        side = second_way(own)
        return [near, side, own], lambda *earlier: [second_way(after(near, side, *earlier))]
    whole = lax.all_gather(own, "row", axis=0, tiled=True)
    return jnp.split(whole, lax.axis_size("row"), axis=0), lambda *earlier: []


def scatter_rows(parts, clock):
    if grid_rows():
        passing = first_way(parts[3])
        near = first_way(parts[0])
        side = second_way(clock.mark(plus(parts[1], clock(passing))))
        return parts[2].astype(f32) + near.astype(f32) + side.astype(f32)
    whole = jnp.concatenate(parts, axis=0)
    return lax.psum_scatter(whole, "row", scatter_dimension=0, tiled=True).astype(f32)


def line():
    return lax.axis_size("dp") == 4


def in_middle():
    place = lax.axis_index("dp")
    return (place == 1) | (place == 2)


def inward(part):
    return lax.ppermute(part, "dp", [(0, 1), (3, 2)])


def across(part):
    return lax.ppermute(part, "dp", [(1, 2), (2, 1)])


def outward(part):
    return lax.ppermute(part, "dp", [(1, 0), (2, 3)])


def plus(first, second):
    return (first.astype(f32) + second.astype(f32)).astype(first.dtype)


class Clock:
    def __init__(self):
        self.last = None

    def __call__(self, value):
        return value if self.last is None else after(value, self.last)

    def mark(self, value):
        self.last = value
        return value


class Line:
    def __init__(self, clock):
        self.clock = clock
        self.parts, self.inner, self.half, self.other, self.total, self.outer = ([] for _ in range(6))
        self.settled = 0

    def feed(self):
        at = len(self.inner)
        if at < len(self.parts) and at < len(self.half) + 2:
            part = self.parts[at]
            self.inner.append(inward(after(part, self.inner[at - 2]) if at >= 2 else part))

    def add(self, *parts):
        self.parts += parts
        if line():
            for _ in parts:
                self.feed()

    def join(self):
        if line():
            at = len(self.half)
            self.half.append(self.clock.mark(plus(self.parts[at], self.clock(self.inner[at]))))
            self.feed()
            self.other.append(across(self.half[at]))

    def total_up(self):
        if line():
            at = len(self.total)
            self.total.append(self.clock.mark(plus(self.half[at], self.clock(self.other[at]))))
            self.outer.append(outward(self.total[at]))

    def settle(self, shape, places, block, before=None):
        for index, start in places:
            at = self.settled
            self.settled += 1
            if line():
                before = self.clock.mark(
                    settle(shape, index, start, block, self.clock, self.total[at], self.outer[at], before)
                )
            else:
                value = lax.psum(self.parts[at], "dp").astype(f32)[None]
                before = jnp.zeros(shape, f32) if before is None else before
                before = lax.dynamic_update_slice(before, value, (index, start, 0))
        return before

    def small(self, at):
        if line():
            return jnp.where(in_middle(), self.total[at], self.outer[at])
        return lax.psum(self.parts[at], "dp")


def gather_whole(own):
    return lax.all_gather(own, "row", axis=0, tiled=True)


def scatter_whole(parts):
    return lax.psum_scatter(parts, "row", scatter_dimension=0, tiled=True).astype(f32)


def sum_rows(values, clock):
    if grid_rows():
        values = clock.mark(values + clock(first_way(values)))
        return clock.mark(values + clock(second_way(values)))
    return lax.psum(values, "row")


def width_pair(first, second, between=None):
    both = jnp.stack([first, second])
    moved = sibling(both)
    if between is not None:
        moved = after(moved, between(both))
    both = both + moved
    return both[0], both[1]


def normalize(values, between=None):
    width = values.shape[1] * lax.axis_size("col")
    totals, squares = width_pair(
        jnp.sum(values, axis=-1), jnp.sum(values * values, axis=-1), between
    )
    average = totals / width
    spread = squares / width - average * average
    inverse = lax.rsqrt(spread + epsilon)[:, None]
    return ((values - average[:, None]) * inverse, inverse)


def norm_back(scaled, normed_hat, inverse):
    width = normed_hat.shape[1] * lax.axis_size("col")
    first, second = width_pair(jnp.sum(scaled, axis=-1), jnp.sum(scaled * normed_hat, axis=-1))
    return inverse * (scaled - first[:, None] / width - normed_hat * second[:, None] / width)


def rotary_tables(count, rows):
    half_dims = ROT // 2
    lane = np.arange(LANES) % HD
    freqs = np.float32(base_rate) ** (-(2.0 * (lane % half_dims).astype(np.float32)) / np.float32(ROT))
    angles = np.arange(count * rows, dtype=np.float32)[:, None] * freqs.astype(np.float32)[None, :]
    turned = lane < ROT
    sign = np.where(lane < half_dims, -1.0, 1.0)
    cosine = np.where(turned, np.cos(angles.astype(np.float64)), 1.0)
    sine = np.where(turned, sign * np.sin(angles.astype(np.float64)), 0.0)
    shape = (count, rows, LANES)
    return jnp.asarray(cosine.reshape(shape), f32), jnp.asarray(sine.reshape(shape), f32)


def turn(values, cosine, sine):
    half_dims = ROT // 2
    lane = lax.broadcasted_iota(jnp.int32, values.shape, 1) % HD
    partner = jnp.where(
        lane < half_dims,
        pltpu.roll(values, LANES - half_dims, 1),
        pltpu.roll(values, half_dims, 1),
    )
    return values * cosine + partner * sine


def params(mib=60):
    return pltpu.CompilerParams(vmem_limit_bytes=mib << 20)


def cost(flops, moved, hard=0):
    return pl.CostEstimate(flops=int(flops), bytes_accessed=int(moved), transcendentals=int(hard))


def project_kernel(members, place, *refs):
    own, other = refs[:members], refs[members : 2 * members]
    keep, taken, bias = refs[2 * members : 2 * members + 3]
    cosine, sine = refs[2 * members + 3 : 3 * members + 3], refs[3 * members + 3 : 4 * members + 3]
    out = refs[-1]
    kind = pl.program_id(0)
    for at in range(members):
        result = dot(own[at][...], keep[0]) + dot(other[at][...], taken[0]) + bias[0].astype(f32)

        @pl.when(kind < 2)
        def _():
            for start in range(0, result.shape[1], LANES):
                part = slice(start, start + LANES)
                out[at, 0, :, part] = turn(result[:, part], cosine[at][0], sine[at][0]).astype(bf16)

        @pl.when(kind == 2)
        def _():
            out[at, 0] = result.astype(bf16)


def project_pieces(index, group, count, place, own, other, keep, taken, bias, cosine, sine, before):
    members = len(own)
    rows, width = own[0].shape
    units = keep.shape[2]
    piece = pl.BlockSpec((rows, width), lambda k, s: (0, 0), pipeline_mode=pl.Buffered(1))
    tables = [
        pl.BlockSpec((1, rows, LANES), functools.partial(lambda at, k, s: (s[at], 0, 0), at))
        for at in group
    ]
    weight = pl.BlockSpec((1, width, units), lambda k, s: (k, 0, 0))
    in_specs = [piece] * (2 * members) + [
        weight,
        weight,
        pl.BlockSpec((1, 1, units), lambda k, s: (k, 0, 0)),
        *tables,
        *tables,
    ]
    args = [*own, *other, keep, taken, bias] + [cosine] * members + [sine] * members
    aliases = {}
    if before is not None:
        aliases = {len(args) + 1: 0}
        in_specs.append(pl.BlockSpec(memory_space=pl.ANY))
        args.append(before)
    return pl.pallas_call(
        functools.partial(project_kernel, members),
        grid_spec=pltpu.PrefetchScalarGridSpec(
            num_scalar_prefetch=1,
            grid=(3,),
            in_specs=in_specs,
            out_specs=pl.BlockSpec((members, 1, rows, units), lambda k, s: (index, k, 0, 0)),
        ),
        out_shape=jax.ShapeDtypeStruct((count, 3, rows, units), bf16),
        input_output_aliases=aliases,
        compiler_params=params(24),
        cost_estimate=cost(
            12 * members * rows * width * units, 4 * members * rows * width + 12 * width * units
        ),
        name="project_pieces",
    )(place, *args)


def causal(rows):
    keys = lax.broadcasted_iota(jnp.int32, (rows, rows), 0)
    return keys <= lax.broadcasted_iota(jnp.int32, (rows, rows), 1)


def head_lanes(values, head):
    lane = lax.broadcasted_iota(jnp.int32, values.shape, 1)
    return jnp.where((lane >= head * HD) & (lane < (head + 1) * HD), values, jnp.zeros_like(values))


def walk(stop, body, carry):
    if isinstance(stop, int):
        for step in range(stop):
            carry = body(step, carry)
        return carry
    return lax.fori_loop(0, stop, body, carry)


def each(count, body):
    if count <= 4:
        for step in range(count):
            body(step)
    else:
        lax.fori_loop(0, count, lambda step, carry: (body(step), carry)[1], 0)


def row_range(step, rows):
    return pl.ds(step * rows if isinstance(step, int) else pl.multiple_of(step * rows, rows), rows)


def attend_kernel(slot, qkv, mixed, kept, logsum, scores):
    count, _, rows, _ = qkv.shape
    heads = LANES // HD
    scale = HD**-0.5

    def one(at):
        here = slot[at]
        query = qkv[here, 0] * jnp.asarray(scale, bf16)
        for head in range(heads):

            def look(past, highest):
                block = dot(head_lanes(qkv[slot[past], 1], head), query, NT)
                scores[row_range(past, rows), :] = block
                return jnp.maximum(highest, jnp.max(block, axis=0, keepdims=True))

            def add(past, carry):
                total, outs = carry
                weights = jnp.exp(scores[row_range(past, rows), :] - highest)
                total = total + jnp.sum(weights, axis=0, keepdims=True)
                value = jnp.transpose(qkv[slot[past], 2])[head * HD : (head + 1) * HD]
                return total, outs + dot(value, weights.astype(bf16))

            block = dot(head_lanes(qkv[here, 1], head), query, NT)
            block = jnp.where(causal(rows), block, -1e30)
            scores[row_range(at, rows), :] = block
            highest = walk(at, look, jnp.max(block, axis=0, keepdims=True))
            total, outs = walk(
                at + 1, add, (jnp.zeros((1, rows), f32), jnp.zeros((HD, rows), f32))
            )
            kept[0, here, pl.ds(head * HD, HD), :] = outs / total
            logsum[0, here, pl.ds(head, 1), :] = highest + jnp.log(total)
        mixed[here] = jnp.transpose(kept[0, here]).astype(bf16)

    each(count, one)


def attend_forward(slot, qkv):
    count, _, rows, units = qkv.shape
    pairs = units // LANES
    work = rows * rows * count * (count + 1) // 2 * units
    return pl.pallas_call(
        attend_kernel,
        grid_spec=pltpu.PrefetchScalarGridSpec(
            num_scalar_prefetch=1,
            grid=(pairs,),
            in_specs=[pl.BlockSpec((count, 3, rows, LANES), lambda p, s: (0, 0, 0, p))],
            out_specs=[
                pl.BlockSpec((count, rows, LANES), lambda p, s: (0, 0, p)),
                pl.BlockSpec((1, count, LANES, rows), lambda p, s: (p, 0, 0, 0)),
                pl.BlockSpec((1, count, 8, rows), lambda p, s: (p, 0, 0, 0)),
            ],
            scratch_shapes=[pltpu.VMEM((count * rows, rows), f32)],
        ),
        out_shape=[
            jax.ShapeDtypeStruct((count, rows, units), bf16),
            jax.ShapeDtypeStruct((pairs, count, LANES, rows), f32),
            jax.ShapeDtypeStruct((pairs, count, 8, rows), f32),
        ],
        compiler_params=params(40),
        cost_estimate=cost(16 * work, 16 * count * rows * units, work // HD),
        name="attend_forward",
    )(slot, qkv)


def attend_back_kernel(slot, place, qkv, grads, kept, logsum, cosine, sine, out, dq, dk, dv, inner):
    count, _, rows, _ = qkv.shape
    heads = LANES // HD
    scale = HD**-0.5
    dk[...] = jnp.zeros_like(dk)
    dv[...] = jnp.zeros_like(dv)

    def sums(at):
        product = jnp.transpose(grads[at].astype(f32)) * kept[0, at]
        for head in range(heads):
            part = product[head * HD : (head + 1) * HD]
            inner[at, pl.ds(head, 1), :] = jnp.sum(part, axis=0, keepdims=True)

    def one(at):
        here = slot[at]
        query = qkv[here, 0] * jnp.asarray(scale, bf16)
        grad = grads[here]
        for head in range(heads):
            query_head = head_lanes(query, head)
            grad_head = head_lanes(grad, head)

            def look(past, query_grad, last=False):
                there = slot[past]
                key = qkv[there, 1]
                block = dot(key, query_head, NT)
                weights = jnp.exp(block - logsum[0, here, pl.ds(head, 1), :])
                if last:
                    weights = jnp.where(causal(rows), weights, 0.0)
                moved = dot(qkv[there, 2], grad_head, NT)
                raw = (weights * (moved - inner[here, pl.ds(head, 1), :])).astype(bf16)
                dv[there] += dot(weights.astype(bf16), grad_head)
                dk[there] += dot(raw, query_head)
                turned = jnp.transpose(key)[head * HD : (head + 1) * HD]
                return query_grad + dot(turned, raw)

            query_grad = walk(at, look, jnp.zeros((HD, rows), f32))
            dq[pl.ds(head * HD, HD), :] = look(at, query_grad, True) * scale
        out[0, here] = turn(jnp.transpose(dq[...]), cosine[at], -sine[at]).astype(bf16)

    def finish(at):
        out[1, at] = turn(dk[at], cosine[place[at]], -sine[place[at]]).astype(bf16)
        out[2, at] = dv[at].astype(bf16)

    each(count, sums)
    each(count, one)
    each(count, finish)


def attend_backward(slot, place, qkv, grads, kept, logsum, cosine, sine):
    count, _, rows, units = qkv.shape
    pairs = units // LANES
    work = rows * rows * count * (count + 1) // 2 * units
    table = pl.BlockSpec((count, rows, LANES), lambda p, *s: (0, 0, 0))
    return pl.pallas_call(
        attend_back_kernel,
        grid_spec=pltpu.PrefetchScalarGridSpec(
            num_scalar_prefetch=2,
            grid=(pairs,),
            in_specs=[
                pl.BlockSpec((count, 3, rows, LANES), lambda p, *s: (0, 0, 0, p)),
                pl.BlockSpec((count, rows, LANES), lambda p, *s: (0, 0, p)),
                pl.BlockSpec((1, count, LANES, rows), lambda p, *s: (p, 0, 0, 0)),
                pl.BlockSpec((1, count, 8, rows), lambda p, *s: (p, 0, 0, 0)),
                table,
                table,
            ],
            out_specs=pl.BlockSpec((3, count, rows, LANES), lambda p, *s: (0, 0, 0, p)),
            scratch_shapes=[
                pltpu.VMEM((LANES, rows), f32),
                pltpu.VMEM((count, rows, LANES), f32),
                pltpu.VMEM((count, rows, LANES), f32),
                pltpu.VMEM((count, 8, rows), f32),
            ],
        ),
        out_shape=jax.ShapeDtypeStruct((3, count, rows, units), bf16),
        compiler_params=params(),
        cost_estimate=cost(40 * work, 24 * count * rows * units, work // HD),
        name="attend_backward",
    )(slot, place, qkv, grads, kept, logsum, cosine, sine)


def ordered(core, own, other, out, width):
    rest = out.shape[-1] - width
    lead = core[0] == 0
    out[..., :width] = jnp.where(lead, own[...], other[...])
    out[..., width:] = jnp.where(lead, other[..., :rest], own[..., :rest])


def block_of(width):
    return 256 if width % 256 == 0 else LANES


def mixed_out_kernel(swap, core, own, other, weight, *outs):
    units = outs[-1]
    count = own.shape[0]

    @pl.when(pl.program_id(0) == 0)
    def _():
        for at in range(count):
            ordered(core, own.at[at], other.at[swap[at]], units.at[at], own.shape[2])

    for at in range(count):
        outs[at][...] = dot(units[at], weight[...]).astype(bf16)


def mixed_out(core, swap, own, other, weight):
    count, rows, units = own.shape
    width = weight.shape[1]
    block = block_of(width)
    whole = lambda k, *s: (0, 0, 0)
    return pl.pallas_call(
        functools.partial(mixed_out_kernel, swap),
        grid_spec=pltpu.PrefetchScalarGridSpec(
            num_scalar_prefetch=1,
            grid=(width // block,),
            in_specs=[
                pl.BlockSpec((count, rows, units), whole),
                pl.BlockSpec((count, rows, units), whole),
                pl.BlockSpec((2 * units, block), lambda k, *s: (0, k)),
            ],
            out_specs=[pl.BlockSpec((rows, block), lambda k, *s: (0, k))] * count
            + [pl.BlockSpec((count, rows, 2 * units), whole)],
        ),
        out_shape=[jax.ShapeDtypeStruct((rows, width), bf16)] * count
        + [jax.ShapeDtypeStruct((count, rows, 2 * units), bf16)],
        compiler_params=params(24),
        cost_estimate=cost(4 * count * rows * units * width, 2 * count * rows * (width + 4 * units)),
        name="mixed_out",
    )(core, own, other, weight)


def hidden_kernel(members, place, *refs):
    own, other, grad_own, grad_other = (refs[k * members : (k + 1) * members] for k in range(4))
    gate_up, taken, down, down_taken = refs[4 * members : 4 * members + 4]
    outs = refs[4 * members + 4 :]
    for at in range(members):
        gate = dot(own[at][...], gate_up[0]) + dot(other[at][...], taken[0])
        up = dot(own[at][...], gate_up[1]) + dot(other[at][...], taken[1])
        grad = dot(grad_own[at][...], down[...], NT) + dot(grad_other[at][...], down_taken[...], NT)
        sigmoid = jax.nn.sigmoid(gate)
        silu = gate * sigmoid
        slope = sigmoid * (1.0 + gate * (1.0 - sigmoid))
        outs[at][0] = (grad * up * slope).astype(bf16)
        outs[at][1] = (grad * silu).astype(bf16)
        outs[at][2] = (silu * up).astype(bf16)


def hidden_pieces(group, place, own, other, grad_own, grad_other, gate_up, taken, down, down_taken):
    members = len(own)
    rows, width = own[0].shape
    units = gate_up.shape[2]
    block = block_of(units)
    rows_in = pl.BlockSpec((rows, width), lambda k, s: (0, 0), pipeline_mode=pl.Buffered(1))
    grads = [
        pl.BlockSpec(
            (rows, width),
            functools.partial(lambda at, k, s: (s[at], 0), at),
            pipeline_mode=pl.Buffered(1),
        )
        for at in group
    ]
    entry = pl.BlockSpec((2, width, block), lambda k, s: (0, 0, k))
    leave = pl.BlockSpec((block, width), lambda k, s: (k, 0))
    return pl.pallas_call(
        functools.partial(hidden_kernel, members),
        grid_spec=pltpu.PrefetchScalarGridSpec(
            num_scalar_prefetch=1,
            grid=(units // block,),
            in_specs=[rows_in] * (2 * members) + grads + grads + [entry, entry, leave, leave],
            out_specs=[pl.BlockSpec((3, rows, block), lambda k, s: (0, 0, k))] * members,
        ),
        out_shape=[jax.ShapeDtypeStruct((3, rows, units), bf16)] * members,
        compiler_params=params(40),
        cost_estimate=cost(
            12 * members * rows * width * units, 12 * width * units + 8 * members * rows * width
        ),
        name="hidden_pieces",
    )(
        place, *own, *other, *([grad_own] * members), *([grad_other] * members),
        gate_up, taken, down, down_taken,
    )


def down_grad_kernel(count, steps, core, place, *refs):
    own, other, grads = refs[:count], refs[count : 2 * count], refs[2 * count]
    first, second, units = refs[-3:]
    rows = own[0].shape[1]
    leading = pl.program_id(0) < steps
    mine = (core[0] == 0) == leading
    for at in range(count):
        units[row_range(place[at], rows), :] = jnp.where(mine, own[at][0], other[at][0])
    result = dot(units[...], grads[...], TN).astype(bf16)

    @pl.when(leading)
    def _():
        first[...] = result

    @pl.when(jnp.logical_not(leading))
    def _():
        second[...] = result


def down_grad_parts(core, place, own, other, grads, total):
    count = len(own)
    _, rows, half = own[0].shape
    width = grads.shape[1]
    block = 384
    steps = half // block
    rest = total - half
    piece = pl.BlockSpec(
        (1, rows, block), lambda k, *s: (2, 0, jnp.where(k < steps, k, k - steps))
    )
    return pl.pallas_call(
        functools.partial(down_grad_kernel, count, steps),
        grid_spec=pltpu.PrefetchScalarGridSpec(
            num_scalar_prefetch=2,
            grid=(steps + -(-rest // block),),
            in_specs=[piece] * (2 * count)
            + [pl.BlockSpec(grads.shape, lambda k, *s: (0, 0), pipeline_mode=pl.Buffered(1))],
            out_specs=[
                pl.BlockSpec((block, width), lambda k, *s: (jnp.minimum(k, steps - 1), 0)),
                pl.BlockSpec((block, width), lambda k, *s: (jnp.maximum(k - steps, 0), 0)),
            ],
            scratch_shapes=[pltpu.VMEM((count * rows, block), bf16)],
        ),
        out_shape=[
            jax.ShapeDtypeStruct((half, width), bf16),
            jax.ShapeDtypeStruct((rest, width), bf16),
        ],
        compiler_params=params(),
        cost_estimate=cost(
            2 * count * rows * total * width, 2 * count * rows * (width + 2 * half) + 2 * total * width
        ),
        name="down_grad_parts",
    )(core, place, *own, *other, grads)


def units_back_kernel(count, blocks, core, *refs):
    own, other, normed = refs[:count], refs[count : 2 * count], refs[2 * count : 3 * count]
    gate_up = refs[3 * count]
    parts = refs[3 * count + 1 : 4 * count + 1]
    gate_grad, up_grad, gate, up, turned = refs[4 * count + 1 :]
    rows, half = own[0].shape[1:]
    step = pl.program_id(0)

    @pl.when(step == 0)
    def _():
        for at in range(count):
            span = pl.ds(at * rows, rows)
            for kind, units in ((0, gate), (1, up)):
                ordered(core, own[at].at[kind], other[at].at[kind], units.at[span], half)

    @pl.when(step < blocks)
    def _():
        result = (dot(gate[...], gate_up[0], NT) + dot(up[...], gate_up[1], NT)).astype(bf16)
        for at in range(count):
            parts[at][...] = result[at * rows : (at + 1) * rows]

    @pl.when(step >= blocks)
    def _():
        for at in range(count):
            turned[:, pl.ds(at * rows, rows)] = jnp.transpose(normed[at][...])
        gate_grad[...] = dot(turned[...], gate[...]).astype(bf16)
        up_grad[...] = dot(turned[...], up[...]).astype(bf16)


def units_back(core, own, other, normed, gate_up):
    count = len(own)
    _, rows, half = own[0].shape
    _, width, total = gate_up.shape
    block = block_of(width)
    blocks = width // block
    once = pl.Buffered(1)

    def normed_at(k):
        return jnp.minimum(k, blocks - 1)

    def grad_at(k):
        return jnp.maximum(k - blocks, 0)

    grad = pl.BlockSpec((block, total), lambda k, s: (grad_at(k), 0))
    result = pl.pallas_call(
        functools.partial(units_back_kernel, count, blocks),
        grid_spec=pltpu.PrefetchScalarGridSpec(
            num_scalar_prefetch=1,
            grid=(2 * blocks,),
            in_specs=[pl.BlockSpec((2, rows, half), lambda k, s: (0, 0, 0), pipeline_mode=once)]
            * (2 * count)
            + [pl.BlockSpec((rows, block), lambda k, s: (0, grad_at(k)))] * count
            + [pl.BlockSpec((2, block, total), lambda k, s: (0, normed_at(k), 0))],
            out_specs=[pl.BlockSpec((rows, block), lambda k, s: (0, normed_at(k)))] * count
            + [grad, grad],
            scratch_shapes=[
                pltpu.VMEM((count * rows, total), bf16),
                pltpu.VMEM((count * rows, total), bf16),
                pltpu.VMEM((block, count * rows), bf16),
            ],
        ),
        out_shape=[jax.ShapeDtypeStruct((rows, width), bf16)] * count
        + [jax.ShapeDtypeStruct((width, total), bf16)] * 2,
        compiler_params=params(),
        cost_estimate=cost(
            8 * count * rows * width * total, 8 * width * total + 12 * count * rows * total
        ),
        name="units_back",
    )(core, *own, *other, *normed, gate_up)
    return result[:count], result[count:]


def down_out_kernel(count, core, *refs):
    own, other, down = refs[:count], refs[count : 2 * count], refs[2 * count]
    outs, units = refs[2 * count + 1 : -1], refs[-1]

    @pl.when(pl.program_id(0) == 0)
    def _():
        for at in range(count):
            ordered(core, own[at].at[0], other[at].at[0], units.at[at], own[at].shape[2])

    for at in range(count):
        outs[at][...] = dot(units[at], down[...]).astype(bf16)


def down_out(core, own, other, down):
    count = len(own)
    _, rows, half = own[0].shape
    total, width = down.shape
    block = block_of(width)
    piece = pl.BlockSpec((1, rows, half), lambda k, s: (2, 0, 0), pipeline_mode=pl.Buffered(1))
    return pl.pallas_call(
        functools.partial(down_out_kernel, count),
        grid_spec=pltpu.PrefetchScalarGridSpec(
            num_scalar_prefetch=1,
            grid=(width // block,),
            in_specs=[piece] * (2 * count) + [pl.BlockSpec((total, block), lambda k, s: (0, k))],
            out_specs=[pl.BlockSpec((rows, block), lambda k, s: (0, k))] * count,
            scratch_shapes=[pltpu.VMEM((count, rows, total), bf16)],
        ),
        out_shape=[jax.ShapeDtypeStruct((rows, width), bf16)] * count,
        compiler_params=params(),
        cost_estimate=cost(
            2 * count * rows * total * width, 2 * total * width + 4 * count * rows * total
        ),
        name="down_out",
    )(core, *own, *other, down)


def settle_kernel(middle, total, moved, *rest):
    rest[-1][0] = jnp.where(middle[0] == 1, total[...], moved[...]).astype(f32)


def settle(shape, index, start, block, clock, total, moved, before):
    rows, width = total.shape
    middle = clock(in_middle().astype(jnp.int32)[None])
    piece = pl.BlockSpec((block, width), lambda k, s: (k, 0))
    in_specs, args, aliases = [piece, piece], [total, moved], {}
    if before is not None:
        in_specs.append(pl.BlockSpec(memory_space=pl.ANY))
        args.append(before)
        aliases = {3: 0}
    return pl.pallas_call(
        settle_kernel,
        grid_spec=pltpu.PrefetchScalarGridSpec(
            num_scalar_prefetch=1,
            grid=(rows // block,),
            in_specs=in_specs,
            out_specs=pl.BlockSpec((1, block, width), lambda k, s: (index, start // block + k, 0)),
        ),
        out_shape=jax.ShapeDtypeStruct(shape, f32),
        input_output_aliases=aliases,
        compiler_params=params(16),
        cost_estimate=cost(0, 8 * rows * width),
        name="settle",
    )(middle, *args)


def weight_grad_kernel(pieces, kinds, parts, stacked, *refs):
    rows_in, units = refs[:pieces], refs[pieces : pieces + kinds]
    outs, rows = refs[pieces + kinds : -1], refs[-1]
    size = rows_in[0].shape[0]
    for at in range(pieces):
        rows[:, pl.ds(at * size, size)] = jnp.transpose(rows_in[at][...])
    steps = pl.num_programs(0) // parts
    for kind in range(kinds):
        array = units[kind][...]
        result = dot(rows[...], array.reshape(array.shape[-2:])).astype(bf16)
        if stacked:
            outs[0][kind] = result
            continue
        for at in range(parts):

            @pl.when(pl.program_id(0) // steps == at)
            def _():
                outs[kind * parts + at][...] = result


def weight_grads(rows, units, indices=(None,), parts=1, stacked=False):
    pieces, kinds = len(rows), len(units)
    size, width = rows[0].shape
    total, columns = units[0].shape[-2:]
    block = 256 if width // parts % 256 == 0 else LANES
    steps = width // block // parts
    specs = [
        pl.BlockSpec((total, columns), lambda k: (0, 0), pipeline_mode=pl.Buffered(1))
        if index is None
        else pl.BlockSpec(
            (1, total, columns),
            functools.partial(lambda at, k: (at, 0, 0), index),
            pipeline_mode=pl.Buffered(1),
        )
        for index in indices
    ]
    outs = [
        pl.BlockSpec(
            (block, columns),
            functools.partial(lambda at, k: (jnp.clip(k - at * steps, 0, steps - 1), 0), at),
        )
        for _ in range(kinds)
        for at in range(parts)
    ]
    shapes = [jax.ShapeDtypeStruct((width // parts, columns), bf16)] * (kinds * parts)
    if stacked:
        outs = [pl.BlockSpec((kinds, block, columns), lambda k: (0, k, 0))]
        shapes = [jax.ShapeDtypeStruct((kinds, width, columns), bf16)]
    return pl.pallas_call(
        functools.partial(weight_grad_kernel, pieces, kinds, parts, stacked),
        grid=(steps * parts,),
        in_specs=[pl.BlockSpec((size, block), lambda k: (0, k))] * pieces + specs,
        out_specs=outs,
        out_shape=shapes,
        scratch_shapes=[pltpu.VMEM((block, total), bf16)],
        compiler_params=params(),
        cost_estimate=cost(
            2 * total * width * columns * kinds,
            2 * (total * (width + columns * kinds) + width * columns * kinds),
        ),
        name="weight_grads",
    )(*rows, *units)


def mixed_grad_kernel(count, *refs):
    keep, taken, out = refs[-3:]
    for at in range(count):
        out[at] = (
            dot(refs[at][...], keep[...], NT) + dot(refs[count + at][...], taken[...], NT)
        ).astype(bf16)


def mixed_back(own, other, keep, taken):
    count = len(own)
    rows, width = own[0].shape
    units = keep.shape[0]
    return pl.pallas_call(
        functools.partial(mixed_grad_kernel, count),
        out_shape=jax.ShapeDtypeStruct((count, rows, units), bf16),
        compiler_params=params(),
        cost_estimate=cost(4 * count * rows * width * units, 4 * count * rows * width),
        name="mixed_back",
    )(*own, *other, keep, taken)


def project_back_kernel(swap, core, own, other, weight, *outs):
    units = outs[-1]
    count = own.shape[1]

    @pl.when(pl.program_id(0) == 0)
    def _():
        for kind in range(3):
            for at in range(count):
                ordered(
                    core,
                    own.at[kind, at],
                    other.at[kind, swap[at]],
                    units.at[kind, at],
                    own.shape[3],
                )

    for at in range(count):
        outs[at][...] = sum(
            dot(units[kind, at], weight[kind], NT) for kind in range(3)
        ).astype(bf16)


def project_back(core, swap, own, other, weight):
    _, count, rows, half = own.shape
    _, width, total = weight.shape
    block = block_of(width)
    whole = lambda k, *s: (0, 0, 0, 0)
    return pl.pallas_call(
        functools.partial(project_back_kernel, swap),
        grid_spec=pltpu.PrefetchScalarGridSpec(
            num_scalar_prefetch=1,
            grid=(width // block,),
            in_specs=[
                pl.BlockSpec((3, count, rows, half), whole),
                pl.BlockSpec((3, count, rows, half), whole),
                pl.BlockSpec((3, block, total), lambda k, *s: (0, k, 0)),
            ],
            out_specs=[pl.BlockSpec((rows, block), lambda k, *s: (0, k))] * count
            + [pl.BlockSpec((3, count, rows, total), whole)],
        ),
        out_shape=[jax.ShapeDtypeStruct((rows, width), bf16)] * count
        + [jax.ShapeDtypeStruct((3, count, rows, total), bf16)],
        compiler_params=params(),
        cost_estimate=cost(6 * count * rows * total * width, 2 * count * rows * (width + 6 * total)),
        name="project_back",
    )(core, own, other, weight)


def halves(weight, axis, width):
    lead = lax.slice_in_dim(weight, 0, width, axis=axis)
    rest = lax.slice_in_dim(weight, width, weight.shape[axis], axis=axis)
    pad = [(0, 0)] * weight.ndim
    pad[axis] = (0, width - rest.shape[axis])
    rest = jnp.pad(rest, pad)
    first = lax.axis_index("col") == 0
    return jnp.where(first, lead, rest), jnp.where(first, rest, lead)


def shards(
    block_input,
    norm1_gain,
    norm1_shift,
    qkv_weight,
    qkv_bias,
    out_weight,
    norm2_gain,
    norm2_shift,
    gate_up_weight,
    down_weight,
    output_grad,
):
    count = lax.axis_size("row")
    rows = block_input.shape[0]
    core = lax.axis_index("col").astype(jnp.int32)[None]
    place, swap = places()
    place = place.astype(jnp.int32)
    slot = inverse_places(place)
    half_units = out_weight.shape[0] // 2
    total_hidden = down_weight.shape[0]
    half_hidden = -(-total_hidden // (2 * LANES)) * LANES
    if grid_rows():
        groups = (((2,), 2), ((0, 1), 0), ((3,), 3))
    else:
        groups = tuple(((at,), at) for at in range(count))

    clock = Clock()
    inputs = block_input.astype(f32)
    gain_one = norm1_gain.astype(f32)
    gain_two = norm2_gain.astype(f32)
    split = {}

    def between(stats):
        split["keep"], split["send"] = halves(after(qkv_weight, stats), 2, half_units)
        return split["keep"]

    hat_one, inverse_one = normalize(inputs, between)
    normed_one = clock.mark((hat_one * gain_one + norm1_shift.astype(f32)).astype(bf16))

    one_own, fetch = gather_rows(normed_one)
    grad_own = None if grid_rows() else gather_whole(output_grad)
    qkv_keep = split["keep"]
    qkv_taken = sibling(split["send"])
    cosine, sine = rotary_tables(count, rows)
    bias = qkv_bias[:, None, :]
    qkv = None
    for group, index in groups:
        if qkv is not None and len(one_own) < count:
            grad_own = gather_whole(after(output_grad, one_own[0], one_own[1], clock.last))
            one_own += fetch(clock.last)
        others = [sibling(clock(one_own[swap[at]])) for at in group]
        qkv = clock.mark(
            project_pieces(
                index, group, count, place, [one_own[at] for at in group], others,
                qkv_keep, qkv_taken, clock(bias), cosine, sine, qkv,
            )
        )
        if group == groups[0][0]:
            gate_up_keep, gate_up_send = halves(clock(gate_up_weight), 2, half_hidden)
            clock.mark(gate_up_keep)
            down_keep, down_send = halves(clock(down_weight), 0, half_hidden)
            clock.mark(down_keep)
            out_keep, out_send = halves(clock(out_weight), 0, half_units)
            clock.mark(out_keep)
    gate_up_taken = sibling(clock(gate_up_send))
    down_taken = sibling(clock(down_send))
    out_taken = sibling(clock(out_send))
    mixed, kept, logsum = attend_forward(clock(slot), qkv)
    clock.mark(mixed)
    *branch, mixed_units = mixed_out(clock(core), swap, mixed, sibling(mixed), out_weight)
    clock.mark(branch[0])
    branch = scatter_rows(branch, clock)
    grad_other = sibling(clock(grad_own))
    after_rows = inputs + branch
    hat_two, inverse_two = normalize(after_rows)
    normed_two = clock.mark((hat_two * gain_two + norm2_shift.astype(f32)).astype(bf16))

    two_own, fetch = gather_rows(normed_two)
    mine, theirs = [None] * count, [None] * count
    for group, _ in groups:
        if group != groups[0][0] and len(two_own) < count:
            two_own += fetch(clock.last)
        results = hidden_pieces(
            group, clock(place),
            [two_own[at] for at in group],
            [sibling(clock(two_own[swap[at]])) for at in group],
            grad_own, grad_other, gate_up_keep, gate_up_taken, down_keep, down_taken,
        )
        clock.mark(results[0])
        for at, result in zip(group, results):
            mine[at] = result
        for at in group:
            theirs[at] = sibling(mine[swap[at]])

    sums = Line(clock)
    parts = down_grad_parts(clock(core), place, mine, theirs, grad_own, total_hidden)
    clock.mark(parts[0])
    sums.add(*parts)
    normed_parts, parts = units_back(clock(core), mine, theirs, two_own, gate_up_weight)
    clock.mark(normed_parts[0])
    sums.add(*parts)
    sums.join()
    forms = {
        "down": ((1,) + down_weight.shape, LANES),
        "gate_up": (gate_up_weight.shape, block_of(gate_up_weight.shape[1])),
        "out": ((1,) + out_weight.shape, block_of(out_weight.shape[0])),
        "qkv": (qkv_weight.shape, block_of(qkv_weight.shape[1])),
    }
    targets = [("down", 0, 0), ("down", 0, half_hidden)]
    targets += [("gate_up", kind, 0) for kind in (0, 1)]
    targets += [("out", 0, 0), ("small", 0, 0)] + [("qkv", kind, 0) for kind in range(3)]
    settled = {}

    def settle_next():
        at = sums.settled
        name, part, start = targets[at]
        if name == "small":
            settled[name] = sums.small(at)
            sums.settled += 1
        else:
            shape, block = forms[name]
            settled[name] = sums.settle(shape, ((part, start),), block, settled.get(name))

    def tick():
        sums.join()
        sums.total_up()
        settle_next()

    normed_two_grad = clock.mark(scatter_rows(normed_parts, clock))
    after_grad = output_grad.astype(f32) + norm_back(
        normed_two_grad * gain_two, hat_two, inverse_two
    )
    branch_grad = clock.mark(after_grad.astype(bf16))
    branch_own, fetch = gather_rows(branch_grad)
    sums.join()
    down_parts = down_out(clock(core), mine, theirs, down_weight)
    clock.mark(down_parts[0])
    if len(branch_own) < count:
        branch_own += fetch(clock.last)
    branch_other = [sibling(branch_own[swap[at]]) for at in range(count)]
    sums.total_up()
    branch_rows = clock.mark(jnp.concatenate([clock(branch_own[0]), *branch_own[1:]], axis=0))
    mixed_grad = clock.mark(mixed_back(branch_own, branch_other, clock(out_keep), out_taken))
    project_grad = clock.mark(
        attend_backward(clock(slot), place, qkv, mixed_grad, kept, logsum, cosine, sine)
    )
    project_other = sibling(project_grad)
    parts = weight_grads([mixed_units.reshape(count * rows, -1)], [clock(branch_rows)])
    clock.mark(parts[0])
    sums.add(*parts)
    sums.total_up()
    if grid_rows():
        far = first_way(down_parts[3])
        near = first_way(down_parts[0])
        side = second_way(clock.mark(plus(down_parts[1], clock(far))))
    *one_parts, project_units = project_back(
        clock(core), swap, project_grad, project_other, qkv_weight
    )
    clock.mark(one_parts[0])
    if grid_rows():
        down = down_parts[2].astype(f32) + near.astype(f32) + clock(side).astype(f32)
    else:
        down = scatter_rows(down_parts, clock)
    block_output = clock.mark((after_rows + down).astype(bf16))
    sums.join()
    settle_next()
    project_units = project_units.reshape(3, count * rows, -1)
    qkv_parts = weight_grads(one_own, [clock(project_units)] * 3, (0, 1, 2))
    clock.mark(qkv_parts[0])
    settle_next()
    normed_one_grad = clock.mark(scatter_rows(one_parts, clock))
    input_grad = after_grad + norm_back(normed_one_grad * gain_one, hat_one, inverse_one)
    gains = jnp.stack(
        [
            jnp.sum(normed_one_grad * hat_one, axis=0),
            jnp.sum(normed_one_grad, axis=0),
            jnp.sum(normed_two_grad * hat_two, axis=0),
            jnp.sum(normed_two_grad, axis=0),
        ]
    )
    width = gains.shape[1]
    gains = clock.mark(gains)
    sums.join()
    sums.total_up()
    gains = sum_rows(gains, clock)
    bias_grad = jnp.sum(clock(project_grad).astype(f32), axis=(1, 2))
    clock.mark(bias_grad)
    small = jnp.concatenate([gains.reshape(-1, LANES), bias_grad.reshape(-1, LANES)], axis=0)
    sums.add(small, *qkv_parts)
    input_grad = clock.mark(clock(input_grad))
    while len(sums.half) < len(targets) if line() else sums.settled < len(targets) - 2:
        tick()
    sums.total_up()
    settle_next()
    settle_next()
    small = settled["small"]
    gains = small[: 4 * width // LANES].reshape(4, width)
    bias_grad = small[4 * width // LANES :].reshape(bias_grad.shape)
    return (
        block_output,
        input_grad,
        gains[0],
        gains[1],
        settled["qkv"],
        bias_grad,
        settled["out"][0],
        gains[2],
        gains[3],
        settled["gate_up"],
        settled["down"][0],
    )


def inverse_places(place):
    spots = jnp.arange(place.shape[0])
    return jnp.sum(
        jnp.where(place[None, :] == spots[:, None], spots[None, :], 0), axis=1
    ).astype(jnp.int32)


def solution(mesh):
    placed = (
        P(("dp", "row"), "col"),
        P("col"),
        P("col"),
        P(None, "col", "row"),
        P(None, ("row", "col")),
        P("row", "col"),
        P("col"),
        P("col"),
        P(None, "col", "row"),
        P("row", "col"),
        P(("dp", "row"), "col"),
    )
    return jax.shard_map(
        shards,
        mesh=mesh,
        in_specs=placed,
        out_specs=(
            P(("dp", "row"), "col"),
            P(("dp", "row"), "col"),
            P("col"),
            P("col"),
            P(None, "col", "row"),
            P(None, ("row", "col")),
            P("row", "col"),
            P("col"),
            P("col"),
            P(None, "col", "row"),
            P("row", "col"),
        ),
        check_vma=False,
    )
```

```python
import functools

import jax
import jax.numpy as jnp
import numpy as np
from jax import lax
from jax.experimental import pallas as pl
from jax.experimental.pallas import tpu as pltpu
from jax.sharding import PartitionSpec as P

HD = 64
ROT = 16
LANES = 128

epsilon = 1e-05
base_rate = 10000.0
bf16 = jnp.bfloat16
f32 = jnp.float32

NN = (((1,), (0,)), ((), ()))
NT = (((1,), (1,)), ((), ()))
TN = (((0,), (0,)), ((), ()))


def dot(first, second, dims=NN):
    return lax.dot_general(first, second, dims, preferred_element_type=f32)


def row_permute(values, core_zero, core_one):
    pairs = [
        (row * 2 + core, (row ^ (core_one if core else core_zero)) * 2 + core)
        for row in range(4)
        for core in range(2)
    ]
    return lax.ppermute(values, ("row", "col"), pairs)


def first_way(values):
    return row_permute(values, 1, 2)


def second_way(values):
    return row_permute(values, 2, 1)


def sibling(values):
    return lax.ppermute(values, "col", [(0, 1), (1, 0)])


def grid_rows():
    return lax.axis_size("row") == 4


def places():
    row, core = lax.axis_index("row"), lax.axis_index("col")
    if grid_rows():
        one = jnp.where(core == 0, 1, 2)
        return jnp.stack([row ^ one, row ^ (3 - one), row, row ^ 3]), (1, 0, 2, 3)
    count = lax.axis_size("row")
    return jnp.arange(count), tuple(range(count))


def after(value, *earlier):
    return lax.optimization_barrier((value,) + earlier)[0]


def gather_rows(own):
    if grid_rows():
        near = first_way(own)
        side = second_way(own)
        return [near, side, own], lambda *earlier: [second_way(after(near, side, *earlier))]
    whole = lax.all_gather(own, "row", axis=0, tiled=True)
    return jnp.split(whole, lax.axis_size("row"), axis=0), lambda *earlier: []


def scatter_rows(parts, clock):
    if grid_rows():
        passing = first_way(parts[3])
        near = first_way(parts[0])
        side = second_way(clock.mark(plus(parts[1], clock(passing))))
        return parts[2].astype(f32) + near.astype(f32) + side.astype(f32)
    whole = jnp.concatenate(parts, axis=0)
    return lax.psum_scatter(whole, "row", scatter_dimension=0, tiled=True).astype(f32)


def line():
    return lax.axis_size("dp") == 4


def in_middle():
    place = lax.axis_index("dp")
    return (place == 1) | (place == 2)


def inward(part):
    return lax.ppermute(part, "dp", [(0, 1), (3, 2)])


def across(part):
    return lax.ppermute(part, "dp", [(1, 2), (2, 1)])


def outward(part):
    return lax.ppermute(part, "dp", [(1, 0), (2, 3)])


def plus(first, second):
    return (first.astype(f32) + second.astype(f32)).astype(first.dtype)


class Clock:
    def __init__(self):
        self.last = None

    def __call__(self, value):
        return value if self.last is None else after(value, self.last)

    def mark(self, value):
        self.last = value
        return value


class Line:
    def __init__(self, clock):
        self.clock = clock
        self.parts, self.inner, self.half, self.other, self.total, self.outer = ([] for _ in range(6))
        self.settled = 0

    def feed(self):
        at = len(self.inner)
        if at < len(self.parts) and at < len(self.half) + 2:
            part = self.parts[at]
            self.inner.append(inward(after(part, self.inner[at - 2]) if at >= 2 else part))

    def add(self, *parts):
        self.parts += parts
        if line():
            for _ in parts:
                self.feed()

    def join(self):
        if line():
            at = len(self.half)
            self.half.append(self.clock.mark(plus(self.parts[at], self.clock(self.inner[at]))))
            self.feed()
            self.other.append(across(self.half[at]))

    def total_up(self):
        if line():
            at = len(self.total)
            self.total.append(self.clock.mark(plus(self.half[at], self.clock(self.other[at]))))
            self.outer.append(outward(self.total[at]))

    def settle(self, shape, places, block, before=None):
        for index, start in places:
            at = self.settled
            self.settled += 1
            if line():
                before = self.clock.mark(
                    settle(shape, index, start, block, self.clock, self.total[at], self.outer[at], before)
                )
            else:
                value = lax.psum(self.parts[at], "dp").astype(f32)[None]
                before = jnp.zeros(shape, f32) if before is None else before
                before = lax.dynamic_update_slice(before, value, (index, start, 0))
        return before

    def small(self, at):
        if line():
            return jnp.where(in_middle(), self.total[at], self.outer[at])
        return lax.psum(self.parts[at], "dp")


def gather_whole(own):
    return lax.all_gather(own, "row", axis=0, tiled=True)


def scatter_whole(parts):
    return lax.psum_scatter(parts, "row", scatter_dimension=0, tiled=True).astype(f32)


def sum_rows(values, clock):
    if grid_rows():
        values = clock.mark(values + clock(first_way(values)))
        return clock.mark(values + clock(second_way(values)))
    return lax.psum(values, "row")


def width_pair(first, second, between=None):
    both = jnp.stack([first, second])
    moved = sibling(both)
    if between is not None:
        moved = after(moved, between(both))
    both = both + moved
    return both[0], both[1]


def normalize(values, between=None):
    width = values.shape[1] * lax.axis_size("col")
    totals, squares = width_pair(
        jnp.sum(values, axis=-1), jnp.sum(values * values, axis=-1), between
    )
    average = totals / width
    spread = squares / width - average * average
    inverse = lax.rsqrt(spread + epsilon)[:, None]
    return ((values - average[:, None]) * inverse, inverse)


def norm_back(scaled, normed_hat, inverse):
    width = normed_hat.shape[1] * lax.axis_size("col")
    first, second = width_pair(jnp.sum(scaled, axis=-1), jnp.sum(scaled * normed_hat, axis=-1))
    return inverse * (scaled - first[:, None] / width - normed_hat * second[:, None] / width)


def rotary_tables(count, rows):
    half_dims = ROT // 2
    lane = np.arange(LANES) % HD
    freqs = np.float32(base_rate) ** (-(2.0 * (lane % half_dims).astype(np.float32)) / np.float32(ROT))
    angles = np.arange(count * rows, dtype=np.float32)[:, None] * freqs.astype(np.float32)[None, :]
    turned = lane < ROT
    sign = np.where(lane < half_dims, -1.0, 1.0)
    cosine = np.where(turned, np.cos(angles.astype(np.float64)), 1.0)
    sine = np.where(turned, sign * np.sin(angles.astype(np.float64)), 0.0)
    shape = (count, rows, LANES)
    return jnp.asarray(cosine.reshape(shape), f32), jnp.asarray(sine.reshape(shape), f32)


def turn(values, cosine, sine):
    half_dims = ROT // 2
    lane = lax.broadcasted_iota(jnp.int32, values.shape, 1) % HD
    partner = jnp.where(
        lane < half_dims,
        pltpu.roll(values, LANES - half_dims, 1),
        pltpu.roll(values, half_dims, 1),
    )
    return values * cosine + partner * sine


def params(mib=60):
    return pltpu.CompilerParams(vmem_limit_bytes=mib << 20)


def cost(flops, moved, hard=0):
    return pl.CostEstimate(flops=int(flops), bytes_accessed=int(moved), transcendentals=int(hard))


def project_kernel(members, place, *refs):
    own, other = refs[:members], refs[members : 2 * members]
    keep, taken, bias = refs[2 * members : 2 * members + 3]
    cosine, sine = refs[2 * members + 3 : 3 * members + 3], refs[3 * members + 3 : 4 * members + 3]
    out = refs[-1]
    kind = pl.program_id(0)
    for at in range(members):
        result = dot(own[at][...], keep[0]) + dot(other[at][...], taken[0]) + bias[0].astype(f32)

        @pl.when(kind < 2)
        def _():
            for start in range(0, result.shape[1], LANES):
                part = slice(start, start + LANES)
                out[at, 0, :, part] = turn(result[:, part], cosine[at][0], sine[at][0]).astype(bf16)

        @pl.when(kind == 2)
        def _():
            out[at, 0] = result.astype(bf16)


def project_pieces(index, group, count, place, own, other, keep, taken, bias, cosine, sine, before):
    members = len(own)
    rows, width = own[0].shape
    units = keep.shape[2]
    piece = pl.BlockSpec((rows, width), lambda k, s: (0, 0), pipeline_mode=pl.Buffered(1))
    tables = [
        pl.BlockSpec((1, rows, LANES), functools.partial(lambda at, k, s: (s[at], 0, 0), at))
        for at in group
    ]
    weight = pl.BlockSpec((1, width, units), lambda k, s: (k, 0, 0))
    in_specs = [piece] * (2 * members) + [
        weight,
        weight,
        pl.BlockSpec((1, 1, units), lambda k, s: (k, 0, 0)),
        *tables,
        *tables,
    ]
    args = [*own, *other, keep, taken, bias] + [cosine] * members + [sine] * members
    aliases = {}
    if before is not None:
        aliases = {len(args) + 1: 0}
        in_specs.append(pl.BlockSpec(memory_space=pl.ANY))
        args.append(before)
    return pl.pallas_call(
        functools.partial(project_kernel, members),
        grid_spec=pltpu.PrefetchScalarGridSpec(
            num_scalar_prefetch=1,
            grid=(3,),
            in_specs=in_specs,
            out_specs=pl.BlockSpec((members, 1, rows, units), lambda k, s: (index, k, 0, 0)),
        ),
        out_shape=jax.ShapeDtypeStruct((count, 3, rows, units), bf16),
        input_output_aliases=aliases,
        compiler_params=params(24),
        cost_estimate=cost(
            12 * members * rows * width * units, 4 * members * rows * width + 12 * width * units
        ),
        name="project_pieces",
    )(place, *args)


def causal(rows):
    keys = lax.broadcasted_iota(jnp.int32, (rows, rows), 0)
    return keys <= lax.broadcasted_iota(jnp.int32, (rows, rows), 1)


def head_lanes(values, head):
    lane = lax.broadcasted_iota(jnp.int32, values.shape, 1)
    return jnp.where((lane >= head * HD) & (lane < (head + 1) * HD), values, jnp.zeros_like(values))


def walk(stop, body, carry):
    if isinstance(stop, int):
        for step in range(stop):
            carry = body(step, carry)
        return carry
    return lax.fori_loop(0, stop, body, carry)


def each(count, body):
    if count <= 4:
        for step in range(count):
            body(step)
    else:
        lax.fori_loop(0, count, lambda step, carry: (body(step), carry)[1], 0)


def row_range(step, rows):
    return pl.ds(step * rows if isinstance(step, int) else pl.multiple_of(step * rows, rows), rows)


def attend_kernel(slot, qkv, mixed, kept, logsum, scores):
    count, _, rows, _ = qkv.shape
    heads = LANES // HD
    scale = HD**-0.5

    def one(at):
        here = slot[at]
        query = qkv[here, 0] * jnp.asarray(scale, bf16)
        for head in range(heads):

            def look(past, highest):
                block = dot(head_lanes(qkv[slot[past], 1], head), query, NT)
                scores[row_range(past, rows), :] = block
                return jnp.maximum(highest, jnp.max(block, axis=0, keepdims=True))

            def add(past, carry):
                total, outs = carry
                weights = jnp.exp(scores[row_range(past, rows), :] - highest)
                total = total + jnp.sum(weights, axis=0, keepdims=True)
                value = jnp.transpose(qkv[slot[past], 2])[head * HD : (head + 1) * HD]
                return total, outs + dot(value, weights.astype(bf16))

            block = dot(head_lanes(qkv[here, 1], head), query, NT)
            block = jnp.where(causal(rows), block, -1e30)
            scores[row_range(at, rows), :] = block
            highest = walk(at, look, jnp.max(block, axis=0, keepdims=True))
            total, outs = walk(
                at + 1, add, (jnp.zeros((1, rows), f32), jnp.zeros((HD, rows), f32))
            )
            kept[0, here, pl.ds(head * HD, HD), :] = outs / total
            logsum[0, here, pl.ds(head, 1), :] = highest + jnp.log(total)
        mixed[here] = jnp.transpose(kept[0, here]).astype(bf16)

    each(count, one)


def attend_forward(slot, qkv):
    count, _, rows, units = qkv.shape
    pairs = units // LANES
    work = rows * rows * count * (count + 1) // 2 * units
    return pl.pallas_call(
        attend_kernel,
        grid_spec=pltpu.PrefetchScalarGridSpec(
            num_scalar_prefetch=1,
            grid=(pairs,),
            in_specs=[pl.BlockSpec((count, 3, rows, LANES), lambda p, s: (0, 0, 0, p))],
            out_specs=[
                pl.BlockSpec((count, rows, LANES), lambda p, s: (0, 0, p)),
                pl.BlockSpec((1, count, LANES, rows), lambda p, s: (p, 0, 0, 0)),
                pl.BlockSpec((1, count, 8, rows), lambda p, s: (p, 0, 0, 0)),
            ],
            scratch_shapes=[pltpu.VMEM((count * rows, rows), f32)],
        ),
        out_shape=[
            jax.ShapeDtypeStruct((count, rows, units), bf16),
            jax.ShapeDtypeStruct((pairs, count, LANES, rows), f32),
            jax.ShapeDtypeStruct((pairs, count, 8, rows), f32),
        ],
        compiler_params=params(40),
        cost_estimate=cost(16 * work, 16 * count * rows * units, work // HD),
        name="attend_forward",
    )(slot, qkv)


def attend_back_kernel(slot, place, qkv, grads, kept, logsum, cosine, sine, out, dq, dk, dv, inner):
    count, _, rows, _ = qkv.shape
    heads = LANES // HD
    scale = HD**-0.5
    dk[...] = jnp.zeros_like(dk)
    dv[...] = jnp.zeros_like(dv)

    def sums(at):
        product = jnp.transpose(grads[at].astype(f32)) * kept[0, at]
        for head in range(heads):
            part = product[head * HD : (head + 1) * HD]
            inner[at, pl.ds(head, 1), :] = jnp.sum(part, axis=0, keepdims=True)

    def one(at):
        here = slot[at]
        query = qkv[here, 0] * jnp.asarray(scale, bf16)
        grad = grads[here]
        for head in range(heads):
            query_head = head_lanes(query, head)
            grad_head = head_lanes(grad, head)

            def look(past, query_grad, last=False):
                there = slot[past]
                key = qkv[there, 1]
                block = dot(key, query_head, NT)
                weights = jnp.exp(block - logsum[0, here, pl.ds(head, 1), :])
                if last:
                    weights = jnp.where(causal(rows), weights, 0.0)
                moved = dot(qkv[there, 2], grad_head, NT)
                raw = (weights * (moved - inner[here, pl.ds(head, 1), :])).astype(bf16)
                dv[there] += dot(weights.astype(bf16), grad_head)
                dk[there] += dot(raw, query_head)
                turned = jnp.transpose(key)[head * HD : (head + 1) * HD]
                return query_grad + dot(turned, raw)

            query_grad = walk(at, look, jnp.zeros((HD, rows), f32))
            dq[pl.ds(head * HD, HD), :] = look(at, query_grad, True) * scale
        out[0, here] = turn(jnp.transpose(dq[...]), cosine[at], -sine[at]).astype(bf16)

    def finish(at):
        out[1, at] = turn(dk[at], cosine[place[at]], -sine[place[at]]).astype(bf16)
        out[2, at] = dv[at].astype(bf16)

    each(count, sums)
    each(count, one)
    each(count, finish)


def attend_backward(slot, place, qkv, grads, kept, logsum, cosine, sine):
    count, _, rows, units = qkv.shape
    pairs = units // LANES
    work = rows * rows * count * (count + 1) // 2 * units
    table = pl.BlockSpec((count, rows, LANES), lambda p, *s: (0, 0, 0))
    return pl.pallas_call(
        attend_back_kernel,
        grid_spec=pltpu.PrefetchScalarGridSpec(
            num_scalar_prefetch=2,
            grid=(pairs,),
            in_specs=[
                pl.BlockSpec((count, 3, rows, LANES), lambda p, *s: (0, 0, 0, p)),
                pl.BlockSpec((count, rows, LANES), lambda p, *s: (0, 0, p)),
                pl.BlockSpec((1, count, LANES, rows), lambda p, *s: (p, 0, 0, 0)),
                pl.BlockSpec((1, count, 8, rows), lambda p, *s: (p, 0, 0, 0)),
                table,
                table,
            ],
            out_specs=pl.BlockSpec((3, count, rows, LANES), lambda p, *s: (0, 0, 0, p)),
            scratch_shapes=[
                pltpu.VMEM((LANES, rows), f32),
                pltpu.VMEM((count, rows, LANES), f32),
                pltpu.VMEM((count, rows, LANES), f32),
                pltpu.VMEM((count, 8, rows), f32),
            ],
        ),
        out_shape=jax.ShapeDtypeStruct((3, count, rows, units), bf16),
        compiler_params=params(),
        cost_estimate=cost(40 * work, 24 * count * rows * units, work // HD),
        name="attend_backward",
    )(slot, place, qkv, grads, kept, logsum, cosine, sine)


def ordered(core, own, other, out, width):
    rest = out.shape[-1] - width
    lead = core[0] == 0
    out[..., :width] = jnp.where(lead, own[...], other[...])
    out[..., width:] = jnp.where(lead, other[..., :rest], own[..., :rest])


def block_of(width):
    return 256 if width % 256 == 0 else LANES


def mixed_out_kernel(swap, core, own, other, weight, *outs):
    units = outs[-1]
    count = own.shape[0]

    @pl.when(pl.program_id(0) == 0)
    def _():
        for at in range(count):
            ordered(core, own.at[at], other.at[swap[at]], units.at[at], own.shape[2])

    for at in range(count):
        outs[at][...] = dot(units[at], weight[...]).astype(bf16)


def mixed_out(core, swap, own, other, weight):
    count, rows, units = own.shape
    width = weight.shape[1]
    block = block_of(width)
    whole = lambda k, *s: (0, 0, 0)
    return pl.pallas_call(
        functools.partial(mixed_out_kernel, swap),
        grid_spec=pltpu.PrefetchScalarGridSpec(
            num_scalar_prefetch=1,
            grid=(width // block,),
            in_specs=[
                pl.BlockSpec((count, rows, units), whole),
                pl.BlockSpec((count, rows, units), whole),
                pl.BlockSpec((2 * units, block), lambda k, *s: (0, k)),
            ],
            out_specs=[pl.BlockSpec((rows, block), lambda k, *s: (0, k))] * count
            + [pl.BlockSpec((count, rows, 2 * units), whole)],
        ),
        out_shape=[jax.ShapeDtypeStruct((rows, width), bf16)] * count
        + [jax.ShapeDtypeStruct((count, rows, 2 * units), bf16)],
        compiler_params=params(24),
        cost_estimate=cost(4 * count * rows * units * width, 2 * count * rows * (width + 4 * units)),
        name="mixed_out",
    )(core, own, other, weight)


def hidden_kernel(members, place, *refs):
    own, other, grad_own, grad_other = (refs[k * members : (k + 1) * members] for k in range(4))
    gate_up, taken, down, down_taken = refs[4 * members : 4 * members + 4]
    outs = refs[4 * members + 4 :]
    for at in range(members):
        gate = dot(own[at][...], gate_up[0]) + dot(other[at][...], taken[0])
        up = dot(own[at][...], gate_up[1]) + dot(other[at][...], taken[1])
        grad = dot(grad_own[at][...], down[...], NT) + dot(grad_other[at][...], down_taken[...], NT)
        sigmoid = jax.nn.sigmoid(gate)
        silu = gate * sigmoid
        slope = sigmoid * (1.0 + gate * (1.0 - sigmoid))
        outs[at][0] = (grad * up * slope).astype(bf16)
        outs[at][1] = (grad * silu).astype(bf16)
        outs[at][2] = (silu * up).astype(bf16)


def hidden_pieces(group, place, own, other, grad_own, grad_other, gate_up, taken, down, down_taken):
    members = len(own)
    rows, width = own[0].shape
    units = gate_up.shape[2]
    block = block_of(units)
    rows_in = pl.BlockSpec((rows, width), lambda k, s: (0, 0), pipeline_mode=pl.Buffered(1))
    grads = [
        pl.BlockSpec(
            (rows, width),
            functools.partial(lambda at, k, s: (s[at], 0), at),
            pipeline_mode=pl.Buffered(1),
        )
        for at in group
    ]
    entry = pl.BlockSpec((2, width, block), lambda k, s: (0, 0, k))
    leave = pl.BlockSpec((block, width), lambda k, s: (k, 0))
    return pl.pallas_call(
        functools.partial(hidden_kernel, members),
        grid_spec=pltpu.PrefetchScalarGridSpec(
            num_scalar_prefetch=1,
            grid=(units // block,),
            in_specs=[rows_in] * (2 * members) + grads + grads + [entry, entry, leave, leave],
            out_specs=[pl.BlockSpec((3, rows, block), lambda k, s: (0, 0, k))] * members,
        ),
        out_shape=[jax.ShapeDtypeStruct((3, rows, units), bf16)] * members,
        compiler_params=params(40),
        cost_estimate=cost(
            12 * members * rows * width * units, 12 * width * units + 8 * members * rows * width
        ),
        name="hidden_pieces",
    )(
        place, *own, *other, *([grad_own] * members), *([grad_other] * members),
        gate_up, taken, down, down_taken,
    )


def down_grad_kernel(count, steps, core, place, *refs):
    own, other, grads = refs[:count], refs[count : 2 * count], refs[2 * count]
    first, second, units = refs[-3:]
    rows = own[0].shape[1]
    leading = pl.program_id(0) < steps
    mine = (core[0] == 0) == leading
    for at in range(count):
        units[row_range(place[at], rows), :] = jnp.where(mine, own[at][0], other[at][0])
    result = dot(units[...], grads[...], TN).astype(bf16)

    @pl.when(leading)
    def _():
        first[...] = result

    @pl.when(jnp.logical_not(leading))
    def _():
        second[...] = result


def down_grad_parts(core, place, own, other, grads, total):
    count = len(own)
    _, rows, half = own[0].shape
    width = grads.shape[1]
    block = 384
    steps = half // block
    rest = total - half
    piece = pl.BlockSpec(
        (1, rows, block), lambda k, *s: (2, 0, jnp.where(k < steps, k, k - steps))
    )
    return pl.pallas_call(
        functools.partial(down_grad_kernel, count, steps),
        grid_spec=pltpu.PrefetchScalarGridSpec(
            num_scalar_prefetch=2,
            grid=(steps + -(-rest // block),),
            in_specs=[piece] * (2 * count)
            + [pl.BlockSpec(grads.shape, lambda k, *s: (0, 0), pipeline_mode=pl.Buffered(1))],
            out_specs=[
                pl.BlockSpec((block, width), lambda k, *s: (jnp.minimum(k, steps - 1), 0)),
                pl.BlockSpec((block, width), lambda k, *s: (jnp.maximum(k - steps, 0), 0)),
            ],
            scratch_shapes=[pltpu.VMEM((count * rows, block), bf16)],
        ),
        out_shape=[
            jax.ShapeDtypeStruct((half, width), bf16),
            jax.ShapeDtypeStruct((rest, width), bf16),
        ],
        compiler_params=params(),
        cost_estimate=cost(
            2 * count * rows * total * width, 2 * count * rows * (width + 2 * half) + 2 * total * width
        ),
        name="down_grad_parts",
    )(core, place, *own, *other, grads)


def units_back_kernel(count, blocks, core, *refs):
    own, other, normed = refs[:count], refs[count : 2 * count], refs[2 * count : 3 * count]
    gate_up = refs[3 * count]
    parts = refs[3 * count + 1 : 4 * count + 1]
    sides = refs[4 * count + 1 : 4 * count + 5]
    gate, up, turned = refs[4 * count + 5 :]
    rows, half = own[0].shape[1:]
    step = pl.program_id(0)

    @pl.when(step == 0)
    def _():
        for at in range(count):
            span = pl.ds(at * rows, rows)
            for kind, units in ((0, gate), (1, up)):
                ordered(core, own[at].at[kind], other[at].at[kind], units.at[span], half)

    @pl.when(step < blocks)
    def _():
        result = (dot(gate[...], gate_up[0], NT) + dot(up[...], gate_up[1], NT)).astype(bf16)
        for at in range(count):
            parts[at][...] = result[at * rows : (at + 1) * rows]

    @pl.when(step >= blocks)
    def _():
        for at in range(count):
            turned[:, pl.ds(at * rows, rows)] = jnp.transpose(normed[at][...])
        for kind, units in ((0, gate), (1, up)):
            result = dot(turned[...], units[...]).astype(bf16)
            for side in range(2):

                @pl.when((step - blocks) // (blocks // 2) == side)
                def _():
                    sides[2 * kind + side][...] = result


def units_back(core, own, other, normed, gate_up):
    count = len(own)
    _, rows, half = own[0].shape
    _, width, total = gate_up.shape
    block = block_of(width)
    blocks = width // block
    once = pl.Buffered(1)

    def normed_at(k):
        return jnp.minimum(k, blocks - 1)

    def grad_at(k):
        return jnp.maximum(k - blocks, 0)

    sides = [
        pl.BlockSpec(
            (block, total),
            functools.partial(
                lambda side, k, s: (
                    jnp.clip(grad_at(k) - side * (blocks // 2), 0, blocks // 2 - 1),
                    0,
                ),
                side,
            ),
        )
        for _ in range(2)
        for side in range(2)
    ]
    result = pl.pallas_call(
        functools.partial(units_back_kernel, count, blocks),
        grid_spec=pltpu.PrefetchScalarGridSpec(
            num_scalar_prefetch=1,
            grid=(2 * blocks,),
            in_specs=[pl.BlockSpec((2, rows, half), lambda k, s: (0, 0, 0), pipeline_mode=once)]
            * (2 * count)
            + [pl.BlockSpec((rows, block), lambda k, s: (0, grad_at(k)))] * count
            + [pl.BlockSpec((2, block, total), lambda k, s: (0, normed_at(k), 0))],
            out_specs=[pl.BlockSpec((rows, block), lambda k, s: (0, normed_at(k)))] * count
            + sides,
            scratch_shapes=[
                pltpu.VMEM((count * rows, total), bf16),
                pltpu.VMEM((count * rows, total), bf16),
                pltpu.VMEM((block, count * rows), bf16),
            ],
        ),
        out_shape=[jax.ShapeDtypeStruct((rows, width), bf16)] * count
        + [jax.ShapeDtypeStruct((width // 2, total), bf16)] * 4,
        compiler_params=params(),
        cost_estimate=cost(
            8 * count * rows * width * total, 8 * width * total + 12 * count * rows * total
        ),
        name="units_back",
    )(core, *own, *other, *normed, gate_up)
    return result[:count], result[count:]


def down_out_kernel(count, core, *refs):
    own, other, down = refs[:count], refs[count : 2 * count], refs[2 * count]
    outs, units = refs[2 * count + 1 : -1], refs[-1]

    @pl.when(pl.program_id(0) == 0)
    def _():
        for at in range(count):
            ordered(core, own[at].at[0], other[at].at[0], units.at[at], own[at].shape[2])

    for at in range(count):
        outs[at][...] = dot(units[at], down[...]).astype(bf16)


def down_out(core, own, other, down):
    count = len(own)
    _, rows, half = own[0].shape
    total, width = down.shape
    block = block_of(width)
    piece = pl.BlockSpec((1, rows, half), lambda k, s: (2, 0, 0), pipeline_mode=pl.Buffered(1))
    return pl.pallas_call(
        functools.partial(down_out_kernel, count),
        grid_spec=pltpu.PrefetchScalarGridSpec(
            num_scalar_prefetch=1,
            grid=(width // block,),
            in_specs=[piece] * (2 * count) + [pl.BlockSpec((total, block), lambda k, s: (0, k))],
            out_specs=[pl.BlockSpec((rows, block), lambda k, s: (0, k))] * count,
            scratch_shapes=[pltpu.VMEM((count, rows, total), bf16)],
        ),
        out_shape=[jax.ShapeDtypeStruct((rows, width), bf16)] * count,
        compiler_params=params(),
        cost_estimate=cost(
            2 * count * rows * total * width, 2 * total * width + 4 * count * rows * total
        ),
        name="down_out",
    )(core, *own, *other, down)


def settle_kernel(middle, total, moved, *rest):
    rest[-1][0] = jnp.where(middle[0] == 1, total[...], moved[...]).astype(f32)


def settle(shape, index, start, block, clock, total, moved, before):
    rows, width = total.shape
    middle = clock(in_middle().astype(jnp.int32)[None])
    piece = pl.BlockSpec((block, width), lambda k, s: (k, 0))
    in_specs, args, aliases = [piece, piece], [total, moved], {}
    if before is not None:
        in_specs.append(pl.BlockSpec(memory_space=pl.ANY))
        args.append(before)
        aliases = {3: 0}
    return pl.pallas_call(
        settle_kernel,
        grid_spec=pltpu.PrefetchScalarGridSpec(
            num_scalar_prefetch=1,
            grid=(rows // block,),
            in_specs=in_specs,
            out_specs=pl.BlockSpec((1, block, width), lambda k, s: (index, start // block + k, 0)),
        ),
        out_shape=jax.ShapeDtypeStruct(shape, f32),
        input_output_aliases=aliases,
        compiler_params=params(16),
        cost_estimate=cost(0, 8 * rows * width),
        name="settle",
    )(middle, *args)


def weight_grad_kernel(pieces, kinds, parts, stacked, *refs):
    rows_in, units = refs[:pieces], refs[pieces : pieces + kinds]
    outs, rows = refs[pieces + kinds : -1], refs[-1]
    size = rows_in[0].shape[0]
    for at in range(pieces):
        rows[:, pl.ds(at * size, size)] = jnp.transpose(rows_in[at][...])
    steps = pl.num_programs(0) // parts
    for kind in range(kinds):
        array = units[kind][...]
        result = dot(rows[...], array.reshape(array.shape[-2:])).astype(bf16)
        if stacked:
            outs[0][kind] = result
            continue
        for at in range(parts):

            @pl.when(pl.program_id(0) // steps == at)
            def _():
                outs[kind * parts + at][...] = result


def weight_grads(rows, units, indices=(None,), parts=1, stacked=False):
    pieces, kinds = len(rows), len(units)
    size, width = rows[0].shape
    total, columns = units[0].shape[-2:]
    block = 256 if width // parts % 256 == 0 else LANES
    steps = width // block // parts
    specs = [
        pl.BlockSpec((total, columns), lambda k: (0, 0), pipeline_mode=pl.Buffered(1))
        if index is None
        else pl.BlockSpec(
            (1, total, columns),
            functools.partial(lambda at, k: (at, 0, 0), index),
            pipeline_mode=pl.Buffered(1),
        )
        for index in indices
    ]
    outs = [
        pl.BlockSpec(
            (block, columns),
            functools.partial(lambda at, k: (jnp.clip(k - at * steps, 0, steps - 1), 0), at),
        )
        for _ in range(kinds)
        for at in range(parts)
    ]
    shapes = [jax.ShapeDtypeStruct((width // parts, columns), bf16)] * (kinds * parts)
    if stacked:
        outs = [pl.BlockSpec((kinds, block, columns), lambda k: (0, k, 0))]
        shapes = [jax.ShapeDtypeStruct((kinds, width, columns), bf16)]
    return pl.pallas_call(
        functools.partial(weight_grad_kernel, pieces, kinds, parts, stacked),
        grid=(steps * parts,),
        in_specs=[pl.BlockSpec((size, block), lambda k: (0, k))] * pieces + specs,
        out_specs=outs,
        out_shape=shapes,
        scratch_shapes=[pltpu.VMEM((block, total), bf16)],
        compiler_params=params(),
        cost_estimate=cost(
            2 * total * width * columns * kinds,
            2 * (total * (width + columns * kinds) + width * columns * kinds),
        ),
        name="weight_grads",
    )(*rows, *units)


def mixed_grad_kernel(count, *refs):
    keep, taken, out = refs[-3:]
    for at in range(count):
        out[at] = (
            dot(refs[at][...], keep[...], NT) + dot(refs[count + at][...], taken[...], NT)
        ).astype(bf16)


def mixed_back(own, other, keep, taken):
    count = len(own)
    rows, width = own[0].shape
    units = keep.shape[0]
    return pl.pallas_call(
        functools.partial(mixed_grad_kernel, count),
        out_shape=jax.ShapeDtypeStruct((count, rows, units), bf16),
        compiler_params=params(),
        cost_estimate=cost(4 * count * rows * width * units, 4 * count * rows * width),
        name="mixed_back",
    )(*own, *other, keep, taken)


def project_back_kernel(swap, core, own, other, weight, *outs):
    units = outs[-1]
    count = own.shape[1]

    @pl.when(pl.program_id(0) == 0)
    def _():
        for kind in range(3):
            for at in range(count):
                ordered(
                    core,
                    own.at[kind, at],
                    other.at[kind, swap[at]],
                    units.at[kind, at],
                    own.shape[3],
                )

    for at in range(count):
        outs[at][...] = sum(
            dot(units[kind, at], weight[kind], NT) for kind in range(3)
        ).astype(bf16)


def project_back(core, swap, own, other, weight):
    _, count, rows, half = own.shape
    _, width, total = weight.shape
    block = block_of(width)
    whole = lambda k, *s: (0, 0, 0, 0)
    return pl.pallas_call(
        functools.partial(project_back_kernel, swap),
        grid_spec=pltpu.PrefetchScalarGridSpec(
            num_scalar_prefetch=1,
            grid=(width // block,),
            in_specs=[
                pl.BlockSpec((3, count, rows, half), whole),
                pl.BlockSpec((3, count, rows, half), whole),
                pl.BlockSpec((3, block, total), lambda k, *s: (0, k, 0)),
            ],
            out_specs=[pl.BlockSpec((rows, block), lambda k, *s: (0, k))] * count
            + [pl.BlockSpec((3, count, rows, total), whole)],
        ),
        out_shape=[jax.ShapeDtypeStruct((rows, width), bf16)] * count
        + [jax.ShapeDtypeStruct((3, count, rows, total), bf16)],
        compiler_params=params(),
        cost_estimate=cost(6 * count * rows * total * width, 2 * count * rows * (width + 6 * total)),
        name="project_back",
    )(core, own, other, weight)


def halves(weight, axis, width):
    lead = lax.slice_in_dim(weight, 0, width, axis=axis)
    rest = lax.slice_in_dim(weight, width, weight.shape[axis], axis=axis)
    pad = [(0, 0)] * weight.ndim
    pad[axis] = (0, width - rest.shape[axis])
    rest = jnp.pad(rest, pad)
    first = lax.axis_index("col") == 0
    return jnp.where(first, lead, rest), jnp.where(first, rest, lead)


def shards(
    block_input,
    norm1_gain,
    norm1_shift,
    qkv_weight,
    qkv_bias,
    out_weight,
    norm2_gain,
    norm2_shift,
    gate_up_weight,
    down_weight,
    output_grad,
):
    count = lax.axis_size("row")
    rows = block_input.shape[0]
    core = lax.axis_index("col").astype(jnp.int32)[None]
    place, swap = places()
    place = place.astype(jnp.int32)
    slot = inverse_places(place)
    half_units = out_weight.shape[0] // 2
    total_hidden = down_weight.shape[0]
    half_hidden = -(-total_hidden // (2 * LANES)) * LANES
    if grid_rows():
        groups = (((2,), 2), ((0, 1), 0), ((3,), 3))
    else:
        groups = tuple(((at,), at) for at in range(count))

    clock = Clock()
    inputs = block_input.astype(f32)
    gain_one = norm1_gain.astype(f32)
    gain_two = norm2_gain.astype(f32)
    split = {}

    def between(stats):
        split["keep"], split["send"] = halves(after(qkv_weight, stats), 2, half_units)
        return split["keep"]

    hat_one, inverse_one = normalize(inputs, between)
    normed_one = clock.mark((hat_one * gain_one + norm1_shift.astype(f32)).astype(bf16))

    one_own, fetch = gather_rows(normed_one)
    grad_own = None if grid_rows() else gather_whole(output_grad)
    qkv_keep = split["keep"]
    qkv_taken = sibling(split["send"])
    cosine, sine = rotary_tables(count, rows)
    bias = qkv_bias[:, None, :]
    qkv = None
    for group, index in groups:
        if qkv is not None and len(one_own) < count:
            grad_own = gather_whole(after(output_grad, one_own[0], one_own[1], clock.last))
            one_own += fetch(clock.last)
        others = [sibling(clock(one_own[swap[at]])) for at in group]
        qkv = clock.mark(
            project_pieces(
                index, group, count, place, [one_own[at] for at in group], others,
                qkv_keep, qkv_taken, clock(bias), cosine, sine, qkv,
            )
        )
        if group == groups[0][0]:
            gate_up_keep, gate_up_send = halves(clock(gate_up_weight), 2, half_hidden)
            clock.mark(gate_up_keep)
            down_keep, down_send = halves(clock(down_weight), 0, half_hidden)
            clock.mark(down_keep)
            out_keep, out_send = halves(clock(out_weight), 0, half_units)
            clock.mark(out_keep)
    gate_up_taken = sibling(clock(gate_up_send))
    down_taken = sibling(clock(down_send))
    out_taken = sibling(clock(out_send))
    mixed, kept, logsum = attend_forward(clock(slot), qkv)
    clock.mark(mixed)
    *branch, mixed_units = mixed_out(clock(core), swap, mixed, sibling(mixed), out_weight)
    clock.mark(branch[0])
    branch = scatter_rows(branch, clock)
    grad_other = sibling(clock(grad_own))
    after_rows = inputs + branch
    hat_two, inverse_two = normalize(after_rows)
    normed_two = clock.mark((hat_two * gain_two + norm2_shift.astype(f32)).astype(bf16))

    two_own, fetch = gather_rows(normed_two)
    mine, theirs = [None] * count, [None] * count
    for group, _ in groups:
        if group != groups[0][0] and len(two_own) < count:
            two_own += fetch(clock.last)
        results = hidden_pieces(
            group, clock(place),
            [two_own[at] for at in group],
            [sibling(clock(two_own[swap[at]])) for at in group],
            grad_own, grad_other, gate_up_keep, gate_up_taken, down_keep, down_taken,
        )
        clock.mark(results[0])
        for at, result in zip(group, results):
            mine[at] = result
        for at in group:
            theirs[at] = sibling(mine[swap[at]])

    sums = Line(clock)
    parts = down_grad_parts(clock(core), place, mine, theirs, grad_own, total_hidden)
    clock.mark(parts[0])
    sums.add(*parts)
    normed_parts, parts = units_back(clock(core), mine, theirs, two_own, gate_up_weight)
    clock.mark(normed_parts[0])
    sums.add(*parts)
    sums.join()
    forms = {
        "down": ((1,) + down_weight.shape, LANES),
        "gate_up": (gate_up_weight.shape, block_of(gate_up_weight.shape[1] // 2)),
        "out": ((1,) + out_weight.shape, block_of(out_weight.shape[0])),
        "qkv": (qkv_weight.shape, block_of(qkv_weight.shape[1])),
    }
    targets = [("down", 0, 0), ("down", 0, half_hidden)]
    half_width = gate_up_weight.shape[1] // 2
    targets += [("gate_up", kind, start) for kind in (0, 1) for start in (0, half_width)]
    targets += [("out", 0, 0)] + [("qkv", kind, 0) for kind in range(3)] + [("small", 0, 0)]
    settled = {}

    def settle_next():
        at = sums.settled
        name, part, start = targets[at]
        if name == "small":
            settled[name] = sums.small(at)
            sums.settled += 1
        else:
            shape, block = forms[name]
            settled[name] = sums.settle(shape, ((part, start),), block, settled.get(name))

    def tick():
        sums.join()
        sums.total_up()
        settle_next()

    normed_two_grad = clock.mark(scatter_rows(normed_parts, clock))
    after_grad = output_grad.astype(f32) + norm_back(
        normed_two_grad * gain_two, hat_two, inverse_two
    )
    branch_grad = clock.mark(after_grad.astype(bf16))
    branch_own, fetch = gather_rows(branch_grad)
    sums.join()
    down_parts = down_out(clock(core), mine, theirs, down_weight)
    clock.mark(down_parts[0])
    if len(branch_own) < count:
        branch_own += fetch(clock.last)
    branch_other = [sibling(branch_own[swap[at]]) for at in range(count)]
    sums.total_up()
    branch_rows = clock.mark(jnp.concatenate([clock(branch_own[0]), *branch_own[1:]], axis=0))
    mixed_grad = clock.mark(mixed_back(branch_own, branch_other, clock(out_keep), out_taken))
    sums.join()
    project_grad = clock.mark(
        attend_backward(clock(slot), place, qkv, mixed_grad, kept, logsum, cosine, sine)
    )
    project_other = sibling(project_grad)
    parts = weight_grads([mixed_units.reshape(count * rows, -1)], [clock(branch_rows)])
    clock.mark(parts[0])
    sums.add(*parts)
    sums.join()
    sums.total_up()
    if grid_rows():
        far = first_way(down_parts[3])
        near = first_way(down_parts[0])
        side = second_way(clock.mark(plus(down_parts[1], clock(far))))
    *one_parts, project_units = project_back(
        clock(core), swap, project_grad, project_other, qkv_weight
    )
    clock.mark(one_parts[0])
    if grid_rows():
        down = down_parts[2].astype(f32) + near.astype(f32) + clock(side).astype(f32)
    else:
        down = scatter_rows(down_parts, clock)
    block_output = clock.mark((after_rows + down).astype(bf16))
    sums.join()
    sums.total_up()
    settle_next()
    project_units = project_units.reshape(3, count * rows, -1)
    qkv_parts = weight_grads(one_own, [clock(project_units)] * 3, (0, 1, 2))
    clock.mark(qkv_parts[0])
    tick()
    normed_one_grad = clock.mark(scatter_rows(one_parts, clock))
    input_grad = after_grad + norm_back(normed_one_grad * gain_one, hat_one, inverse_one)
    gains = jnp.stack(
        [
            jnp.sum(normed_one_grad * hat_one, axis=0),
            jnp.sum(normed_one_grad, axis=0),
            jnp.sum(normed_two_grad * hat_two, axis=0),
            jnp.sum(normed_two_grad, axis=0),
        ]
    )
    width = gains.shape[1]
    gains = clock.mark(gains)
    sums.total_up()
    settle_next()
    gains = sum_rows(gains, clock)
    bias_grad = jnp.sum(clock(project_grad).astype(f32), axis=(1, 2))
    clock.mark(bias_grad)
    small = jnp.concatenate([gains.reshape(-1, LANES), bias_grad.reshape(-1, LANES)], axis=0)
    sums.add(*qkv_parts, small)
    input_grad = clock.mark(clock(input_grad))
    while len(sums.half) < len(targets) - 1 if line() else sums.settled < len(targets) - 4:
        tick()
    sums.join()
    sums.total_up()
    settle_next()
    sums.total_up()
    while sums.settled < len(targets):
        settle_next()
    small = settled["small"]
    gains = small[: 4 * width // LANES].reshape(4, width)
    bias_grad = small[4 * width // LANES :].reshape(bias_grad.shape)
    return (
        block_output,
        input_grad,
        gains[0],
        gains[1],
        settled["qkv"],
        bias_grad,
        settled["out"][0],
        gains[2],
        gains[3],
        settled["gate_up"],
        settled["down"][0],
    )


def inverse_places(place):
    spots = jnp.arange(place.shape[0])
    return jnp.sum(
        jnp.where(place[None, :] == spots[:, None], spots[None, :], 0), axis=1
    ).astype(jnp.int32)


def solution(mesh):
    placed = (
        P(("dp", "row"), "col"),
        P("col"),
        P("col"),
        P(None, "col", "row"),
        P(None, ("row", "col")),
        P("row", "col"),
        P("col"),
        P("col"),
        P(None, "col", "row"),
        P("row", "col"),
        P(("dp", "row"), "col"),
    )
    return jax.shard_map(
        shards,
        mesh=mesh,
        in_specs=placed,
        out_specs=(
            P(("dp", "row"), "col"),
            P(("dp", "row"), "col"),
            P("col"),
            P("col"),
            P(None, "col", "row"),
            P(None, ("row", "col")),
            P("row", "col"),
            P("col"),
            P("col"),
            P(None, "col", "row"),
            P("row", "col"),
        ),
        check_vma=False,
    )
```

```python
import functools

import jax
import jax.numpy as jnp
import numpy as np
from jax import lax
from jax.experimental import pallas as pl
from jax.experimental.pallas import tpu as pltpu
from jax.sharding import PartitionSpec as P

HD = 64
ROT = 16
LANES = 128

epsilon = 1e-05
base_rate = 10000.0
bf16 = jnp.bfloat16
f32 = jnp.float32

NN = (((1,), (0,)), ((), ()))
NT = (((1,), (1,)), ((), ()))
TN = (((0,), (0,)), ((), ()))


def dot(first, second, dims=NN):
    return lax.dot_general(first, second, dims, preferred_element_type=f32)


def row_permute(values, core_zero, core_one):
    pairs = [
        (row * 2 + core, (row ^ (core_one if core else core_zero)) * 2 + core)
        for row in range(4)
        for core in range(2)
    ]
    return lax.ppermute(values, ("row", "col"), pairs)


def first_way(values):
    return row_permute(values, 1, 2)


def second_way(values):
    return row_permute(values, 2, 1)


def sibling(values):
    return lax.ppermute(values, "col", [(0, 1), (1, 0)])


def grid_rows():
    return lax.axis_size("row") == 4


def places():
    row, core = lax.axis_index("row"), lax.axis_index("col")
    if grid_rows():
        one = jnp.where(core == 0, 1, 2)
        return jnp.stack([row ^ one, row ^ (3 - one), row, row ^ 3]), (1, 0, 2, 3)
    count = lax.axis_size("row")
    return jnp.arange(count), tuple(range(count))


def after(value, *earlier):
    return lax.optimization_barrier((value,) + earlier)[0]


def gather_rows(own):
    if grid_rows():
        near = first_way(own)
        side = second_way(own)
        return [near, side, own], lambda *earlier: [second_way(after(near, side, *earlier))]
    whole = lax.all_gather(own, "row", axis=0, tiled=True)
    return jnp.split(whole, lax.axis_size("row"), axis=0), lambda *earlier: []


def scatter_rows(parts, clock):
    if grid_rows():
        passing = first_way(parts[3])
        near = first_way(parts[0])
        side = second_way(clock.mark(plus(parts[1], clock(passing))))
        return parts[2].astype(f32) + near.astype(f32) + side.astype(f32)
    whole = jnp.concatenate(parts, axis=0)
    return lax.psum_scatter(whole, "row", scatter_dimension=0, tiled=True).astype(f32)


def line():
    return lax.axis_size("dp") == 4


def in_middle():
    place = lax.axis_index("dp")
    return (place == 1) | (place == 2)


def inward(part):
    return lax.ppermute(part, "dp", [(0, 1), (3, 2)])


def across(part):
    return lax.ppermute(part, "dp", [(1, 2), (2, 1)])


def outward(part):
    return lax.ppermute(part, "dp", [(1, 0), (2, 3)])


def plus(first, second):
    return (first.astype(f32) + second.astype(f32)).astype(first.dtype)


class Clock:
    def __init__(self):
        self.last = None

    def __call__(self, value):
        return value if self.last is None else after(value, self.last)

    def mark(self, value):
        self.last = value
        return value


class Line:
    def __init__(self, clock):
        self.clock = clock
        self.parts, self.inner, self.half, self.other, self.total, self.outer = ([] for _ in range(6))
        self.settled = 0

    def feed(self):
        at = len(self.inner)
        if at < len(self.parts) and at < len(self.half) + 2:
            part = self.parts[at]
            self.inner.append(inward(after(part, self.inner[at - 2]) if at >= 2 else part))

    def add(self, *parts):
        self.parts += parts
        if line():
            for _ in parts:
                self.feed()

    def join(self):
        if line():
            at = len(self.half)
            self.half.append(self.clock.mark(plus(self.parts[at], self.clock(self.inner[at]))))
            self.feed()
            self.other.append(across(self.half[at]))

    def total_up(self):
        if line():
            at = len(self.total)
            self.total.append(self.clock.mark(plus(self.half[at], self.clock(self.other[at]))))
            self.outer.append(outward(self.total[at]))

    def settle(self, shape, places, block, before=None):
        for index, start in places:
            at = self.settled
            self.settled += 1
            if line():
                before = self.clock.mark(
                    settle(shape, index, start, block, self.clock, self.total[at], self.outer[at], before)
                )
            else:
                value = lax.psum(self.parts[at], "dp").astype(f32)[None]
                before = jnp.zeros(shape, f32) if before is None else before
                before = lax.dynamic_update_slice(before, value, (index, start, 0))
        return before

    def small(self, at):
        if line():
            return jnp.where(in_middle(), self.total[at], self.outer[at])
        return lax.psum(self.parts[at], "dp")


def gather_whole(own):
    return lax.all_gather(own, "row", axis=0, tiled=True)


def scatter_whole(parts):
    return lax.psum_scatter(parts, "row", scatter_dimension=0, tiled=True).astype(f32)


def sum_rows(values, clock):
    if grid_rows():
        values = clock.mark(values + clock(first_way(values)))
        return clock.mark(values + clock(second_way(values)))
    return lax.psum(values, "row")


def width_pair(first, second, between=None):
    both = jnp.stack([first, second])
    moved = sibling(both)
    if between is not None:
        moved = after(moved, between(both))
    both = both + moved
    return both[0], both[1]


def normalize(values, between=None):
    width = values.shape[1] * lax.axis_size("col")
    totals, squares = width_pair(
        jnp.sum(values, axis=-1), jnp.sum(values * values, axis=-1), between
    )
    average = totals / width
    spread = squares / width - average * average
    inverse = lax.rsqrt(spread + epsilon)[:, None]
    return ((values - average[:, None]) * inverse, inverse)


def norm_back(scaled, normed_hat, inverse):
    width = normed_hat.shape[1] * lax.axis_size("col")
    first, second = width_pair(jnp.sum(scaled, axis=-1), jnp.sum(scaled * normed_hat, axis=-1))
    return inverse * (scaled - first[:, None] / width - normed_hat * second[:, None] / width)


def rotary_tables(count, rows):
    half_dims = ROT // 2
    lane = np.arange(LANES) % HD
    freqs = np.float32(base_rate) ** (-(2.0 * (lane % half_dims).astype(np.float32)) / np.float32(ROT))
    angles = np.arange(count * rows, dtype=np.float32)[:, None] * freqs.astype(np.float32)[None, :]
    turned = lane < ROT
    sign = np.where(lane < half_dims, -1.0, 1.0)
    cosine = np.where(turned, np.cos(angles.astype(np.float64)), 1.0)
    sine = np.where(turned, sign * np.sin(angles.astype(np.float64)), 0.0)
    shape = (count, rows, LANES)
    return jnp.asarray(cosine.reshape(shape), f32), jnp.asarray(sine.reshape(shape), f32)


def turn(values, cosine, sine):
    half_dims = ROT // 2
    lane = lax.broadcasted_iota(jnp.int32, values.shape, 1) % HD
    partner = jnp.where(
        lane < half_dims,
        pltpu.roll(values, LANES - half_dims, 1),
        pltpu.roll(values, half_dims, 1),
    )
    return values * cosine + partner * sine


def params(mib=60):
    return pltpu.CompilerParams(vmem_limit_bytes=mib << 20)


def cost(flops, moved, hard=0):
    return pl.CostEstimate(flops=int(flops), bytes_accessed=int(moved), transcendentals=int(hard))


def project_kernel(members, place, *refs):
    own, other = refs[:members], refs[members : 2 * members]
    keep, taken, bias = refs[2 * members : 2 * members + 3]
    cosine, sine = refs[2 * members + 3 : 3 * members + 3], refs[3 * members + 3 : 4 * members + 3]
    out = refs[-1]
    kind = pl.program_id(0)
    for at in range(members):
        result = dot(own[at][...], keep[0]) + dot(other[at][...], taken[0]) + bias[0].astype(f32)

        @pl.when(kind < 2)
        def _():
            for start in range(0, result.shape[1], LANES):
                part = slice(start, start + LANES)
                out[at, 0, :, part] = turn(result[:, part], cosine[at][0], sine[at][0]).astype(bf16)

        @pl.when(kind == 2)
        def _():
            out[at, 0] = result.astype(bf16)


def project_pieces(index, group, count, place, own, other, keep, taken, bias, cosine, sine, before):
    members = len(own)
    rows, width = own[0].shape
    units = keep.shape[2]
    piece = pl.BlockSpec((rows, width), lambda k, s: (0, 0), pipeline_mode=pl.Buffered(1))
    tables = [
        pl.BlockSpec((1, rows, LANES), functools.partial(lambda at, k, s: (s[at], 0, 0), at))
        for at in group
    ]
    weight = pl.BlockSpec((1, width, units), lambda k, s: (k, 0, 0))
    in_specs = [piece] * (2 * members) + [
        weight,
        weight,
        pl.BlockSpec((1, 1, units), lambda k, s: (k, 0, 0)),
        *tables,
        *tables,
    ]
    args = [*own, *other, keep, taken, bias] + [cosine] * members + [sine] * members
    aliases = {}
    if before is not None:
        aliases = {len(args) + 1: 0}
        in_specs.append(pl.BlockSpec(memory_space=pl.ANY))
        args.append(before)
    return pl.pallas_call(
        functools.partial(project_kernel, members),
        grid_spec=pltpu.PrefetchScalarGridSpec(
            num_scalar_prefetch=1,
            grid=(3,),
            in_specs=in_specs,
            out_specs=pl.BlockSpec((members, 1, rows, units), lambda k, s: (index, k, 0, 0)),
        ),
        out_shape=jax.ShapeDtypeStruct((count, 3, rows, units), bf16),
        input_output_aliases=aliases,
        compiler_params=params(24),
        cost_estimate=cost(
            12 * members * rows * width * units, 4 * members * rows * width + 12 * width * units
        ),
        name="project_pieces",
    )(place, *args)


def causal(rows):
    keys = lax.broadcasted_iota(jnp.int32, (rows, rows), 0)
    return keys <= lax.broadcasted_iota(jnp.int32, (rows, rows), 1)


def head_lanes(values, head):
    lane = lax.broadcasted_iota(jnp.int32, values.shape, 1)
    return jnp.where((lane >= head * HD) & (lane < (head + 1) * HD), values, jnp.zeros_like(values))


def walk(stop, body, carry):
    if isinstance(stop, int):
        for step in range(stop):
            carry = body(step, carry)
        return carry
    return lax.fori_loop(0, stop, body, carry)


def each(count, body):
    if count <= 4:
        for step in range(count):
            body(step)
    else:
        lax.fori_loop(0, count, lambda step, carry: (body(step), carry)[1], 0)


def row_range(step, rows):
    return pl.ds(step * rows if isinstance(step, int) else pl.multiple_of(step * rows, rows), rows)


def attend_kernel(slot, qkv, mixed, kept, logsum, scores):
    count, _, rows, _ = qkv.shape
    heads = LANES // HD
    scale = HD**-0.5

    def one(at):
        here = slot[at]
        query = qkv[here, 0] * jnp.asarray(scale, bf16)
        for head in range(heads):

            def look(past, highest):
                block = dot(head_lanes(qkv[slot[past], 1], head), query, NT)
                scores[row_range(past, rows), :] = block
                return jnp.maximum(highest, jnp.max(block, axis=0, keepdims=True))

            def add(past, carry):
                total, outs = carry
                weights = jnp.exp(scores[row_range(past, rows), :] - highest)
                total = total + jnp.sum(weights, axis=0, keepdims=True)
                value = jnp.transpose(qkv[slot[past], 2])[head * HD : (head + 1) * HD]
                return total, outs + dot(value, weights.astype(bf16))

            block = dot(head_lanes(qkv[here, 1], head), query, NT)
            block = jnp.where(causal(rows), block, -1e30)
            scores[row_range(at, rows), :] = block
            highest = walk(at, look, jnp.max(block, axis=0, keepdims=True))
            total, outs = walk(
                at + 1, add, (jnp.zeros((1, rows), f32), jnp.zeros((HD, rows), f32))
            )
            kept[0, here, pl.ds(head * HD, HD), :] = outs / total
            logsum[0, here, pl.ds(head, 1), :] = highest + jnp.log(total)
        mixed[here] = jnp.transpose(kept[0, here]).astype(bf16)

    each(count, one)


def attend_forward(slot, qkv):
    count, _, rows, units = qkv.shape
    pairs = units // LANES
    work = rows * rows * count * (count + 1) // 2 * units
    return pl.pallas_call(
        attend_kernel,
        grid_spec=pltpu.PrefetchScalarGridSpec(
            num_scalar_prefetch=1,
            grid=(pairs,),
            in_specs=[pl.BlockSpec((count, 3, rows, LANES), lambda p, s: (0, 0, 0, p))],
            out_specs=[
                pl.BlockSpec((count, rows, LANES), lambda p, s: (0, 0, p)),
                pl.BlockSpec((1, count, LANES, rows), lambda p, s: (p, 0, 0, 0)),
                pl.BlockSpec((1, count, 8, rows), lambda p, s: (p, 0, 0, 0)),
            ],
            scratch_shapes=[pltpu.VMEM((count * rows, rows), f32)],
        ),
        out_shape=[
            jax.ShapeDtypeStruct((count, rows, units), bf16),
            jax.ShapeDtypeStruct((pairs, count, LANES, rows), f32),
            jax.ShapeDtypeStruct((pairs, count, 8, rows), f32),
        ],
        compiler_params=params(40),
        cost_estimate=cost(16 * work, 16 * count * rows * units, work // HD),
        name="attend_forward",
    )(slot, qkv)


def attend_back_kernel(slot, place, qkv, grads, kept, logsum, cosine, sine, out, dq, dk, dv, inner):
    count, _, rows, _ = qkv.shape
    heads = LANES // HD
    scale = HD**-0.5
    dk[...] = jnp.zeros_like(dk)
    dv[...] = jnp.zeros_like(dv)

    def sums(at):
        product = jnp.transpose(grads[at].astype(f32)) * kept[0, at]
        for head in range(heads):
            part = product[head * HD : (head + 1) * HD]
            inner[at, pl.ds(head, 1), :] = jnp.sum(part, axis=0, keepdims=True)

    def one(at):
        here = slot[at]
        query = qkv[here, 0] * jnp.asarray(scale, bf16)
        grad = grads[here]
        for head in range(heads):
            query_head = head_lanes(query, head)
            grad_head = head_lanes(grad, head)

            def look(past, query_grad, last=False):
                there = slot[past]
                key = qkv[there, 1]
                block = dot(key, query_head, NT)
                weights = jnp.exp(block - logsum[0, here, pl.ds(head, 1), :])
                if last:
                    weights = jnp.where(causal(rows), weights, 0.0)
                moved = dot(qkv[there, 2], grad_head, NT)
                raw = (weights * (moved - inner[here, pl.ds(head, 1), :])).astype(bf16)
                dv[there] += dot(weights.astype(bf16), grad_head)
                dk[there] += dot(raw, query_head)
                turned = jnp.transpose(key)[head * HD : (head + 1) * HD]
                return query_grad + dot(turned, raw)

            query_grad = walk(at, look, jnp.zeros((HD, rows), f32))
            dq[pl.ds(head * HD, HD), :] = look(at, query_grad, True) * scale
        out[0, here] = turn(jnp.transpose(dq[...]), cosine[at], -sine[at]).astype(bf16)

    def finish(at):
        out[1, at] = turn(dk[at], cosine[place[at]], -sine[place[at]]).astype(bf16)
        out[2, at] = dv[at].astype(bf16)

    each(count, sums)
    each(count, one)
    each(count, finish)


def attend_backward(slot, place, qkv, grads, kept, logsum, cosine, sine):
    count, _, rows, units = qkv.shape
    pairs = units // LANES
    work = rows * rows * count * (count + 1) // 2 * units
    table = pl.BlockSpec((count, rows, LANES), lambda p, *s: (0, 0, 0))
    return pl.pallas_call(
        attend_back_kernel,
        grid_spec=pltpu.PrefetchScalarGridSpec(
            num_scalar_prefetch=2,
            grid=(pairs,),
            in_specs=[
                pl.BlockSpec((count, 3, rows, LANES), lambda p, *s: (0, 0, 0, p)),
                pl.BlockSpec((count, rows, LANES), lambda p, *s: (0, 0, p)),
                pl.BlockSpec((1, count, LANES, rows), lambda p, *s: (p, 0, 0, 0)),
                pl.BlockSpec((1, count, 8, rows), lambda p, *s: (p, 0, 0, 0)),
                table,
                table,
            ],
            out_specs=pl.BlockSpec((3, count, rows, LANES), lambda p, *s: (0, 0, 0, p)),
            scratch_shapes=[
                pltpu.VMEM((LANES, rows), f32),
                pltpu.VMEM((count, rows, LANES), f32),
                pltpu.VMEM((count, rows, LANES), f32),
                pltpu.VMEM((count, 8, rows), f32),
            ],
        ),
        out_shape=jax.ShapeDtypeStruct((3, count, rows, units), bf16),
        compiler_params=params(),
        cost_estimate=cost(40 * work, 24 * count * rows * units, work // HD),
        name="attend_backward",
    )(slot, place, qkv, grads, kept, logsum, cosine, sine)


def ordered(core, own, other, out, width):
    rest = out.shape[-1] - width
    lead = core[0] == 0
    out[..., :width] = jnp.where(lead, own[...], other[...])
    out[..., width:] = jnp.where(lead, other[..., :rest], own[..., :rest])


def block_of(width):
    return 256 if width % 256 == 0 else LANES


def mixed_out_kernel(swap, core, own, other, weight, *outs):
    units = outs[-1]
    count = own.shape[0]

    @pl.when(pl.program_id(0) == 0)
    def _():
        for at in range(count):
            ordered(core, own.at[at], other.at[swap[at]], units.at[at], own.shape[2])

    for at in range(count):
        outs[at][...] = dot(units[at], weight[...]).astype(bf16)


def mixed_out(core, swap, own, other, weight):
    count, rows, units = own.shape
    width = weight.shape[1]
    block = block_of(width)
    whole = lambda k, *s: (0, 0, 0)
    return pl.pallas_call(
        functools.partial(mixed_out_kernel, swap),
        grid_spec=pltpu.PrefetchScalarGridSpec(
            num_scalar_prefetch=1,
            grid=(width // block,),
            in_specs=[
                pl.BlockSpec((count, rows, units), whole),
                pl.BlockSpec((count, rows, units), whole),
                pl.BlockSpec((2 * units, block), lambda k, *s: (0, k)),
            ],
            out_specs=[pl.BlockSpec((rows, block), lambda k, *s: (0, k))] * count
            + [pl.BlockSpec((count, rows, 2 * units), whole)],
        ),
        out_shape=[jax.ShapeDtypeStruct((rows, width), bf16)] * count
        + [jax.ShapeDtypeStruct((count, rows, 2 * units), bf16)],
        compiler_params=params(24),
        cost_estimate=cost(4 * count * rows * units * width, 2 * count * rows * (width + 4 * units)),
        name="mixed_out",
    )(core, own, other, weight)


def hidden_kernel(members, place, *refs):
    own, other, grad_own, grad_other = (refs[k * members : (k + 1) * members] for k in range(4))
    gate_up, taken, down, down_taken = refs[4 * members : 4 * members + 4]
    outs = refs[4 * members + 4 :]
    for at in range(members):
        gate = dot(own[at][...], gate_up[0]) + dot(other[at][...], taken[0])
        up = dot(own[at][...], gate_up[1]) + dot(other[at][...], taken[1])
        grad = dot(grad_own[at][...], down[...], NT) + dot(grad_other[at][...], down_taken[...], NT)
        sigmoid = jax.nn.sigmoid(gate)
        silu = gate * sigmoid
        slope = sigmoid * (1.0 + gate * (1.0 - sigmoid))
        outs[at][0] = (grad * up * slope).astype(bf16)
        outs[at][1] = (grad * silu).astype(bf16)
        outs[at][2] = (silu * up).astype(bf16)


def hidden_pieces(group, place, own, other, grad_own, grad_other, gate_up, taken, down, down_taken):
    members = len(own)
    rows, width = own[0].shape
    units = gate_up.shape[2]
    block = block_of(units)
    rows_in = pl.BlockSpec((rows, width), lambda k, s: (0, 0), pipeline_mode=pl.Buffered(1))
    grads = [
        pl.BlockSpec(
            (rows, width),
            functools.partial(lambda at, k, s: (s[at], 0), at),
            pipeline_mode=pl.Buffered(1),
        )
        for at in group
    ]
    entry = pl.BlockSpec((2, width, block), lambda k, s: (0, 0, k))
    leave = pl.BlockSpec((block, width), lambda k, s: (k, 0))
    return pl.pallas_call(
        functools.partial(hidden_kernel, members),
        grid_spec=pltpu.PrefetchScalarGridSpec(
            num_scalar_prefetch=1,
            grid=(units // block,),
            in_specs=[rows_in] * (2 * members) + grads + grads + [entry, entry, leave, leave],
            out_specs=[pl.BlockSpec((3, rows, block), lambda k, s: (0, 0, k))] * members,
        ),
        out_shape=[jax.ShapeDtypeStruct((3, rows, units), bf16)] * members,
        compiler_params=params(40),
        cost_estimate=cost(
            12 * members * rows * width * units, 12 * width * units + 8 * members * rows * width
        ),
        name="hidden_pieces",
    )(
        place, *own, *other, *([grad_own] * members), *([grad_other] * members),
        gate_up, taken, down, down_taken,
    )


def down_grad_kernel(count, steps, core, place, *refs):
    own, other, grads = refs[:count], refs[count : 2 * count], refs[2 * count]
    first, second, units = refs[-3:]
    rows = own[0].shape[1]
    leading = pl.program_id(0) < steps
    mine = (core[0] == 0) == leading
    for at in range(count):
        units[row_range(place[at], rows), :] = jnp.where(mine, own[at][0], other[at][0])
    result = dot(units[...], grads[...], TN).astype(bf16)

    @pl.when(leading)
    def _():
        first[...] = result

    @pl.when(jnp.logical_not(leading))
    def _():
        second[...] = result


def down_grad_parts(core, place, own, other, grads, total):
    count = len(own)
    _, rows, half = own[0].shape
    width = grads.shape[1]
    block = 384
    steps = half // block
    rest = total - half
    piece = pl.BlockSpec(
        (1, rows, block), lambda k, *s: (2, 0, jnp.where(k < steps, k, k - steps))
    )
    return pl.pallas_call(
        functools.partial(down_grad_kernel, count, steps),
        grid_spec=pltpu.PrefetchScalarGridSpec(
            num_scalar_prefetch=2,
            grid=(steps + -(-rest // block),),
            in_specs=[piece] * (2 * count)
            + [pl.BlockSpec(grads.shape, lambda k, *s: (0, 0), pipeline_mode=pl.Buffered(1))],
            out_specs=[
                pl.BlockSpec((block, width), lambda k, *s: (jnp.minimum(k, steps - 1), 0)),
                pl.BlockSpec((block, width), lambda k, *s: (jnp.maximum(k - steps, 0), 0)),
            ],
            scratch_shapes=[pltpu.VMEM((count * rows, block), bf16)],
        ),
        out_shape=[
            jax.ShapeDtypeStruct((half, width), bf16),
            jax.ShapeDtypeStruct((rest, width), bf16),
        ],
        compiler_params=params(),
        cost_estimate=cost(
            2 * count * rows * total * width, 2 * count * rows * (width + 2 * half) + 2 * total * width
        ),
        name="down_grad_parts",
    )(core, place, *own, *other, grads)


def units_back_kernel(count, blocks, core, *refs):
    own, other, normed = refs[:count], refs[count : 2 * count], refs[2 * count : 3 * count]
    gate_up = refs[3 * count]
    parts = refs[3 * count + 1 : 4 * count + 1]
    sides = refs[4 * count + 1 : 4 * count + 5]
    gate, up, turned = refs[4 * count + 5 :]
    rows, half = own[0].shape[1:]
    step = pl.program_id(0)

    @pl.when(step == 0)
    def _():
        for at in range(count):
            span = pl.ds(at * rows, rows)
            for kind, units in ((0, gate), (1, up)):
                ordered(core, own[at].at[kind], other[at].at[kind], units.at[span], half)

    @pl.when(step < blocks)
    def _():
        result = (dot(gate[...], gate_up[0], NT) + dot(up[...], gate_up[1], NT)).astype(bf16)
        for at in range(count):
            parts[at][...] = result[at * rows : (at + 1) * rows]

    @pl.when(step >= blocks)
    def _():
        for at in range(count):
            turned[:, pl.ds(at * rows, rows)] = jnp.transpose(normed[at][...])
        for kind, units in ((0, gate), (1, up)):
            result = dot(turned[...], units[...]).astype(bf16)
            for side in range(2):

                @pl.when((step - blocks) // (blocks // 2) == side)
                def _():
                    sides[2 * kind + side][...] = result


def units_back(core, own, other, normed, gate_up):
    count = len(own)
    _, rows, half = own[0].shape
    _, width, total = gate_up.shape
    block = block_of(width)
    blocks = width // block
    once = pl.Buffered(1)

    def normed_at(k):
        return jnp.minimum(k, blocks - 1)

    def grad_at(k):
        return jnp.maximum(k - blocks, 0)

    sides = [
        pl.BlockSpec(
            (block, total),
            functools.partial(
                lambda side, k, s: (
                    jnp.clip(grad_at(k) - side * (blocks // 2), 0, blocks // 2 - 1),
                    0,
                ),
                side,
            ),
        )
        for _ in range(2)
        for side in range(2)
    ]
    result = pl.pallas_call(
        functools.partial(units_back_kernel, count, blocks),
        grid_spec=pltpu.PrefetchScalarGridSpec(
            num_scalar_prefetch=1,
            grid=(2 * blocks,),
            in_specs=[pl.BlockSpec((2, rows, half), lambda k, s: (0, 0, 0), pipeline_mode=once)]
            * (2 * count)
            + [pl.BlockSpec((rows, block), lambda k, s: (0, grad_at(k)))] * count
            + [pl.BlockSpec((2, block, total), lambda k, s: (0, normed_at(k), 0))],
            out_specs=[pl.BlockSpec((rows, block), lambda k, s: (0, normed_at(k)))] * count
            + sides,
            scratch_shapes=[
                pltpu.VMEM((count * rows, total), bf16),
                pltpu.VMEM((count * rows, total), bf16),
                pltpu.VMEM((block, count * rows), bf16),
            ],
        ),
        out_shape=[jax.ShapeDtypeStruct((rows, width), bf16)] * count
        + [jax.ShapeDtypeStruct((width // 2, total), bf16)] * 4,
        compiler_params=params(),
        cost_estimate=cost(
            8 * count * rows * width * total, 8 * width * total + 12 * count * rows * total
        ),
        name="units_back",
    )(core, *own, *other, *normed, gate_up)
    return result[:count], result[count:]


def down_out_kernel(count, core, *refs):
    own, other, down = refs[:count], refs[count : 2 * count], refs[2 * count]
    outs, units = refs[2 * count + 1 : -1], refs[-1]

    @pl.when(pl.program_id(0) == 0)
    def _():
        for at in range(count):
            ordered(core, own[at].at[0], other[at].at[0], units.at[at], own[at].shape[2])

    for at in range(count):
        outs[at][...] = dot(units[at], down[...]).astype(bf16)


def down_out(core, own, other, down):
    count = len(own)
    _, rows, half = own[0].shape
    total, width = down.shape
    block = block_of(width)
    piece = pl.BlockSpec((1, rows, half), lambda k, s: (2, 0, 0), pipeline_mode=pl.Buffered(1))
    return pl.pallas_call(
        functools.partial(down_out_kernel, count),
        grid_spec=pltpu.PrefetchScalarGridSpec(
            num_scalar_prefetch=1,
            grid=(width // block,),
            in_specs=[piece] * (2 * count) + [pl.BlockSpec((total, block), lambda k, s: (0, k))],
            out_specs=[pl.BlockSpec((rows, block), lambda k, s: (0, k))] * count,
            scratch_shapes=[pltpu.VMEM((count, rows, total), bf16)],
        ),
        out_shape=[jax.ShapeDtypeStruct((rows, width), bf16)] * count,
        compiler_params=params(),
        cost_estimate=cost(
            2 * count * rows * total * width, 2 * total * width + 4 * count * rows * total
        ),
        name="down_out",
    )(core, *own, *other, down)


def settle_kernel(middle, total, moved, *rest):
    rest[-1][0] = jnp.where(middle[0] == 1, total[...], moved[...]).astype(f32)


def settle(shape, index, start, block, clock, total, moved, before):
    rows, width = total.shape
    middle = clock(in_middle().astype(jnp.int32)[None])
    piece = pl.BlockSpec((block, width), lambda k, s: (k, 0))
    in_specs, args, aliases = [piece, piece], [total, moved], {}
    if before is not None:
        in_specs.append(pl.BlockSpec(memory_space=pl.ANY))
        args.append(before)
        aliases = {3: 0}
    return pl.pallas_call(
        settle_kernel,
        grid_spec=pltpu.PrefetchScalarGridSpec(
            num_scalar_prefetch=1,
            grid=(rows // block,),
            in_specs=in_specs,
            out_specs=pl.BlockSpec((1, block, width), lambda k, s: (index, start // block + k, 0)),
        ),
        out_shape=jax.ShapeDtypeStruct(shape, f32),
        input_output_aliases=aliases,
        compiler_params=params(16),
        cost_estimate=cost(0, 8 * rows * width),
        name="settle",
    )(middle, *args)


def weight_grad_kernel(pieces, kinds, parts, stacked, *refs):
    rows_in, units = refs[:pieces], refs[pieces : pieces + kinds]
    outs, rows = refs[pieces + kinds : -1], refs[-1]
    size = rows_in[0].shape[0]
    for at in range(pieces):
        rows[:, pl.ds(at * size, size)] = jnp.transpose(rows_in[at][...])
    steps = pl.num_programs(0) // parts
    for kind in range(kinds):
        array = units[kind][...]
        result = dot(rows[...], array.reshape(array.shape[-2:])).astype(bf16)
        if stacked:
            outs[0][kind] = result
            continue
        for at in range(parts):

            @pl.when(pl.program_id(0) // steps == at)
            def _():
                outs[kind * parts + at][...] = result


def weight_grads(rows, units, indices=(None,), parts=1, stacked=False):
    pieces, kinds = len(rows), len(units)
    size, width = rows[0].shape
    total, columns = units[0].shape[-2:]
    block = 256 if width // parts % 256 == 0 else LANES
    steps = width // block // parts
    specs = [
        pl.BlockSpec((total, columns), lambda k: (0, 0), pipeline_mode=pl.Buffered(1))
        if index is None
        else pl.BlockSpec(
            (1, total, columns),
            functools.partial(lambda at, k: (at, 0, 0), index),
            pipeline_mode=pl.Buffered(1),
        )
        for index in indices
    ]
    outs = [
        pl.BlockSpec(
            (block, columns),
            functools.partial(lambda at, k: (jnp.clip(k - at * steps, 0, steps - 1), 0), at),
        )
        for _ in range(kinds)
        for at in range(parts)
    ]
    shapes = [jax.ShapeDtypeStruct((width // parts, columns), bf16)] * (kinds * parts)
    if stacked:
        outs = [pl.BlockSpec((kinds, block, columns), lambda k: (0, k, 0))]
        shapes = [jax.ShapeDtypeStruct((kinds, width, columns), bf16)]
    return pl.pallas_call(
        functools.partial(weight_grad_kernel, pieces, kinds, parts, stacked),
        grid=(steps * parts,),
        in_specs=[pl.BlockSpec((size, block), lambda k: (0, k))] * pieces + specs,
        out_specs=outs,
        out_shape=shapes,
        scratch_shapes=[pltpu.VMEM((block, total), bf16)],
        compiler_params=params(),
        cost_estimate=cost(
            2 * total * width * columns * kinds,
            2 * (total * (width + columns * kinds) + width * columns * kinds),
        ),
        name="weight_grads",
    )(*rows, *units)


def mixed_grad_kernel(count, *refs):
    keep, taken, out = refs[-3:]
    for at in range(count):
        out[at] = (
            dot(refs[at][...], keep[...], NT) + dot(refs[count + at][...], taken[...], NT)
        ).astype(bf16)


def mixed_back(own, other, keep, taken):
    count = len(own)
    rows, width = own[0].shape
    units = keep.shape[0]
    return pl.pallas_call(
        functools.partial(mixed_grad_kernel, count),
        out_shape=jax.ShapeDtypeStruct((count, rows, units), bf16),
        compiler_params=params(),
        cost_estimate=cost(4 * count * rows * width * units, 4 * count * rows * width),
        name="mixed_back",
    )(*own, *other, keep, taken)


def project_back_kernel(swap, core, own, other, weight, *outs):
    units = outs[-1]
    count = own.shape[1]

    @pl.when(pl.program_id(0) == 0)
    def _():
        for kind in range(3):
            for at in range(count):
                ordered(
                    core,
                    own.at[kind, at],
                    other.at[kind, swap[at]],
                    units.at[kind, at],
                    own.shape[3],
                )

    for at in range(count):
        outs[at][...] = sum(
            dot(units[kind, at], weight[kind], NT) for kind in range(3)
        ).astype(bf16)


def project_back(core, swap, own, other, weight):
    _, count, rows, half = own.shape
    _, width, total = weight.shape
    block = block_of(width)
    whole = lambda k, *s: (0, 0, 0, 0)
    return pl.pallas_call(
        functools.partial(project_back_kernel, swap),
        grid_spec=pltpu.PrefetchScalarGridSpec(
            num_scalar_prefetch=1,
            grid=(width // block,),
            in_specs=[
                pl.BlockSpec((3, count, rows, half), whole),
                pl.BlockSpec((3, count, rows, half), whole),
                pl.BlockSpec((3, block, total), lambda k, *s: (0, k, 0)),
            ],
            out_specs=[pl.BlockSpec((rows, block), lambda k, *s: (0, k))] * count
            + [pl.BlockSpec((3, count, rows, total), whole)],
        ),
        out_shape=[jax.ShapeDtypeStruct((rows, width), bf16)] * count
        + [jax.ShapeDtypeStruct((3, count, rows, total), bf16)],
        compiler_params=params(),
        cost_estimate=cost(6 * count * rows * total * width, 2 * count * rows * (width + 6 * total)),
        name="project_back",
    )(core, own, other, weight)


def halves(weight, axis, width):
    lead = lax.slice_in_dim(weight, 0, width, axis=axis)
    rest = lax.slice_in_dim(weight, width, weight.shape[axis], axis=axis)
    pad = [(0, 0)] * weight.ndim
    pad[axis] = (0, width - rest.shape[axis])
    rest = jnp.pad(rest, pad)
    first = lax.axis_index("col") == 0
    return jnp.where(first, lead, rest), jnp.where(first, rest, lead)


def shards(
    block_input,
    norm1_gain,
    norm1_shift,
    qkv_weight,
    qkv_bias,
    out_weight,
    norm2_gain,
    norm2_shift,
    gate_up_weight,
    down_weight,
    output_grad,
):
    count = lax.axis_size("row")
    rows = block_input.shape[0]
    core = lax.axis_index("col").astype(jnp.int32)[None]
    place, swap = places()
    place = place.astype(jnp.int32)
    slot = inverse_places(place)
    half_units = out_weight.shape[0] // 2
    total_hidden = down_weight.shape[0]
    half_hidden = -(-total_hidden // (2 * LANES)) * LANES
    if grid_rows():
        groups = (((2,), 2), ((0, 1), 0), ((3,), 3))
    else:
        groups = tuple(((at,), at) for at in range(count))

    clock = Clock()
    inputs = block_input.astype(f32)
    gain_one = norm1_gain.astype(f32)
    gain_two = norm2_gain.astype(f32)
    split = {}

    def between(stats):
        split["keep"], split["send"] = halves(after(qkv_weight, stats), 2, half_units)
        return split["keep"]

    hat_one, inverse_one = normalize(inputs, between)
    normed_one = clock.mark((hat_one * gain_one + norm1_shift.astype(f32)).astype(bf16))

    one_own, fetch = gather_rows(normed_one)
    grad_own = None if grid_rows() else gather_whole(output_grad)
    qkv_keep = split["keep"]
    qkv_taken = sibling(split["send"])
    cosine, sine = rotary_tables(count, rows)
    bias = qkv_bias[:, None, :]
    qkv = None
    for group, index in groups:
        if qkv is not None and len(one_own) < count:
            grad_own = gather_whole(after(output_grad, one_own[0], one_own[1], clock.last))
            one_own += fetch(clock.last)
        others = [sibling(clock(one_own[swap[at]])) for at in group]
        qkv = clock.mark(
            project_pieces(
                index, group, count, place, [one_own[at] for at in group], others,
                qkv_keep, qkv_taken, clock(bias), cosine, sine, qkv,
            )
        )
        if group == groups[0][0]:
            gate_up_keep, gate_up_send = halves(clock(gate_up_weight), 2, half_hidden)
            clock.mark(gate_up_keep)
            down_keep, down_send = halves(clock(down_weight), 0, half_hidden)
            clock.mark(down_keep)
            out_keep, out_send = halves(clock(out_weight), 0, half_units)
            clock.mark(out_keep)
    gate_up_taken = sibling(clock(gate_up_send))
    down_taken = sibling(clock(down_send))
    out_taken = sibling(clock(out_send))
    mixed, kept, logsum = attend_forward(clock(slot), qkv)
    clock.mark(mixed)
    *branch, mixed_units = mixed_out(clock(core), swap, mixed, sibling(mixed), out_weight)
    clock.mark(branch[0])
    branch = scatter_rows(branch, clock)
    grad_other = sibling(clock(grad_own))
    after_rows = inputs + branch
    hat_two, inverse_two = normalize(after_rows)
    normed_two = clock.mark((hat_two * gain_two + norm2_shift.astype(f32)).astype(bf16))

    two_own, fetch = gather_rows(normed_two)
    mine, theirs = [None] * count, [None] * count
    for group, _ in groups:
        if group != groups[0][0] and len(two_own) < count:
            two_own += fetch(clock.last)
        results = hidden_pieces(
            group, clock(place),
            [two_own[at] for at in group],
            [sibling(clock(two_own[swap[at]])) for at in group],
            grad_own, grad_other, gate_up_keep, gate_up_taken, down_keep, down_taken,
        )
        clock.mark(results[0])
        for at, result in zip(group, results):
            mine[at] = result
        for at in group:
            theirs[at] = sibling(mine[swap[at]])

    sums = Line(clock)
    parts = down_grad_parts(clock(core), place, mine, theirs, grad_own, total_hidden)
    clock.mark(parts[0])
    sums.add(*parts)
    normed_parts, parts = units_back(clock(core), mine, theirs, two_own, gate_up_weight)
    clock.mark(normed_parts[0])
    sums.add(*parts)
    sums.join()
    forms = {
        "down": ((1,) + down_weight.shape, LANES),
        "gate_up": (gate_up_weight.shape, block_of(gate_up_weight.shape[1] // 2)),
        "out": ((1,) + out_weight.shape, block_of(out_weight.shape[0])),
        "qkv": (qkv_weight.shape, block_of(qkv_weight.shape[1])),
    }
    targets = [("down", 0, 0), ("down", 0, half_hidden)]
    half_width = gate_up_weight.shape[1] // 2
    targets += [("gate_up", kind, start) for kind in (0, 1) for start in (0, half_width)]
    targets += [("out", 0, 0)] + [("qkv", kind, 0) for kind in range(3)] + [("small", 0, 0)]
    settled = {}

    def settle_next():
        at = sums.settled
        name, part, start = targets[at]
        if name == "small":
            settled[name] = sums.small(at)
            sums.settled += 1
        else:
            shape, block = forms[name]
            settled[name] = sums.settle(shape, ((part, start),), block, settled.get(name))

    def tick():
        sums.join()
        sums.total_up()
        settle_next()

    normed_two_grad = clock.mark(scatter_rows(normed_parts, clock))
    after_grad = output_grad.astype(f32) + norm_back(
        normed_two_grad * gain_two, hat_two, inverse_two
    )
    branch_grad = clock.mark(after_grad.astype(bf16))
    branch_own, fetch = gather_rows(branch_grad)
    sums.join()
    down_parts = down_out(clock(core), mine, theirs, down_weight)
    clock.mark(down_parts[0])
    if len(branch_own) < count:
        branch_own += fetch(clock.last)
    branch_other = [sibling(branch_own[swap[at]]) for at in range(count)]
    sums.total_up()
    branch_rows = clock.mark(jnp.concatenate([clock(branch_own[0]), *branch_own[1:]], axis=0))
    mixed_grad = clock.mark(mixed_back(branch_own, branch_other, clock(out_keep), out_taken))
    sums.join()
    project_grad = clock.mark(
        attend_backward(clock(slot), place, qkv, mixed_grad, kept, logsum, cosine, sine)
    )
    project_other = sibling(project_grad)
    parts = weight_grads([mixed_units.reshape(count * rows, -1)], [clock(branch_rows)])
    clock.mark(parts[0])
    sums.add(*parts)
    sums.join()
    sums.total_up()
    if grid_rows():
        far = first_way(down_parts[3])
        near = first_way(down_parts[0])
        side = second_way(clock.mark(plus(down_parts[1], clock(far))))
    *one_parts, project_units = project_back(
        clock(core), swap, project_grad, project_other, qkv_weight
    )
    clock.mark(one_parts[0])
    if grid_rows():
        down = down_parts[2].astype(f32) + near.astype(f32) + clock(side).astype(f32)
    else:
        down = scatter_rows(down_parts, clock)
    block_output = clock.mark((after_rows + down).astype(bf16))
    sums.join()
    sums.total_up()
    settle_next()
    project_units = project_units.reshape(3, count * rows, -1)
    qkv_parts = weight_grads(one_own, [clock(project_units)] * 3, (0, 1, 2))
    clock.mark(qkv_parts[0])
    tick()
    settle_next()
    normed_one_grad = clock.mark(scatter_rows(one_parts, clock))
    input_grad = after_grad + norm_back(normed_one_grad * gain_one, hat_one, inverse_one)
    gains = jnp.stack(
        [
            jnp.sum(normed_one_grad * hat_one, axis=0),
            jnp.sum(normed_one_grad, axis=0),
            jnp.sum(normed_two_grad * hat_two, axis=0),
            jnp.sum(normed_two_grad, axis=0),
        ]
    )
    width = gains.shape[1]
    gains = clock.mark(gains)
    sums.total_up()
    settle_next()
    gains = sum_rows(gains, clock)
    bias_grad = jnp.sum(clock(project_grad).astype(f32), axis=(1, 2))
    clock.mark(bias_grad)
    small = jnp.concatenate([gains.reshape(-1, LANES), bias_grad.reshape(-1, LANES)], axis=0)
    sums.add(*qkv_parts, small)
    input_grad = clock.mark(clock(input_grad))
    while len(sums.half) < len(targets) - 1 if line() else sums.settled < len(targets) - 3:
        tick()
    sums.join()
    sums.total_up()
    settle_next()
    sums.total_up()
    while sums.settled < len(targets):
        settle_next()
    small = settled["small"]
    gains = small[: 4 * width // LANES].reshape(4, width)
    bias_grad = small[4 * width // LANES :].reshape(bias_grad.shape)
    return (
        block_output,
        input_grad,
        gains[0],
        gains[1],
        settled["qkv"],
        bias_grad,
        settled["out"][0],
        gains[2],
        gains[3],
        settled["gate_up"],
        settled["down"][0],
    )


def inverse_places(place):
    spots = jnp.arange(place.shape[0])
    return jnp.sum(
        jnp.where(place[None, :] == spots[:, None], spots[None, :], 0), axis=1
    ).astype(jnp.int32)


def solution(mesh):
    placed = (
        P(("dp", "row"), "col"),
        P("col"),
        P("col"),
        P(None, "col", "row"),
        P(None, ("row", "col")),
        P("row", "col"),
        P("col"),
        P("col"),
        P(None, "col", "row"),
        P("row", "col"),
        P(("dp", "row"), "col"),
    )
    return jax.shard_map(
        shards,
        mesh=mesh,
        in_specs=placed,
        out_specs=(
            P(("dp", "row"), "col"),
            P(("dp", "row"), "col"),
            P("col"),
            P("col"),
            P(None, "col", "row"),
            P(None, ("row", "col")),
            P("row", "col"),
            P("col"),
            P("col"),
            P(None, "col", "row"),
            P("row", "col"),
        ),
        check_vma=False,
    )
```

```python
import functools

import jax
import jax.numpy as jnp
import numpy as np
from jax import lax
from jax.experimental import pallas as pl
from jax.experimental.pallas import tpu as pltpu
from jax.sharding import PartitionSpec as P

HD = 64
ROT = 16
LANES = 128

epsilon = 1e-05
base_rate = 10000.0
bf16 = jnp.bfloat16
f32 = jnp.float32

NN = (((1,), (0,)), ((), ()))
NT = (((1,), (1,)), ((), ()))
TN = (((0,), (0,)), ((), ()))


def dot(first, second, dims=NN):
    return lax.dot_general(first, second, dims, preferred_element_type=f32)


def row_permute(values, core_zero, core_one):
    pairs = [
        (row * 2 + core, (row ^ (core_one if core else core_zero)) * 2 + core)
        for row in range(4)
        for core in range(2)
    ]
    return lax.ppermute(values, ("row", "col"), pairs)


def first_way(values):
    return row_permute(values, 1, 2)


def second_way(values):
    return row_permute(values, 2, 1)


def sibling(values):
    return lax.ppermute(values, "col", [(0, 1), (1, 0)])


def grid_rows():
    return lax.axis_size("row") == 4


def places():
    row, core = lax.axis_index("row"), lax.axis_index("col")
    if grid_rows():
        one = jnp.where(core == 0, 1, 2)
        return jnp.stack([row ^ one, row ^ (3 - one), row, row ^ 3]), (1, 0, 2, 3)
    count = lax.axis_size("row")
    return jnp.arange(count), tuple(range(count))


def after(value, *earlier):
    return lax.optimization_barrier((value,) + earlier)[0]


def gather_rows(own):
    if grid_rows():
        near = first_way(own)
        side = second_way(own)
        return [near, side, own], lambda *earlier: [second_way(after(near, side, *earlier))]
    whole = lax.all_gather(own, "row", axis=0, tiled=True)
    return jnp.split(whole, lax.axis_size("row"), axis=0), lambda *earlier: []


def scatter_rows(parts, clock):
    if grid_rows():
        passing = first_way(parts[3])
        near = first_way(parts[0])
        side = second_way(clock.mark(plus(parts[1], clock(passing))))
        return parts[2].astype(f32) + near.astype(f32) + side.astype(f32)
    whole = jnp.concatenate(parts, axis=0)
    return lax.psum_scatter(whole, "row", scatter_dimension=0, tiled=True).astype(f32)


def line():
    return lax.axis_size("dp") == 4


def in_middle():
    place = lax.axis_index("dp")
    return (place == 1) | (place == 2)


def inward(part):
    return lax.ppermute(part, "dp", [(0, 1), (3, 2)])


def across(part):
    return lax.ppermute(part, "dp", [(1, 2), (2, 1)])


def outward(part):
    return lax.ppermute(part, "dp", [(1, 0), (2, 3)])


def plus(first, second):
    return (first.astype(f32) + second.astype(f32)).astype(first.dtype)


class Clock:
    def __init__(self):
        self.last = None

    def __call__(self, value):
        return value if self.last is None else after(value, self.last)

    def mark(self, value):
        self.last = value
        return value


class Line:
    def __init__(self, clock):
        self.clock = clock
        self.parts, self.inner, self.half, self.other, self.total, self.outer = ([] for _ in range(6))
        self.settled = 0

    def feed(self):
        at = len(self.inner)
        if at < len(self.parts) and at < len(self.half) + 2:
            part = self.parts[at]
            self.inner.append(inward(after(part, self.inner[at - 2]) if at >= 2 else part))

    def add(self, *parts):
        self.parts += parts
        if line():
            for _ in parts:
                self.feed()

    def join(self):
        if line():
            at = len(self.half)
            self.half.append(self.clock.mark(plus(self.parts[at], self.clock(self.inner[at]))))
            self.feed()
            self.other.append(across(self.half[at]))

    def total_up(self):
        if line():
            at = len(self.total)
            self.total.append(self.clock.mark(plus(self.half[at], self.clock(self.other[at]))))
            self.outer.append(outward(self.total[at]))

    def settle(self, shape, places, block, before=None):
        for index, start in places:
            at = self.settled
            self.settled += 1
            if line():
                before = self.clock.mark(
                    settle(shape, index, start, block, self.clock, self.total[at], self.outer[at], before)
                )
            else:
                value = lax.psum(self.parts[at], "dp").astype(f32)[None]
                before = jnp.zeros(shape, f32) if before is None else before
                before = lax.dynamic_update_slice(before, value, (index, start, 0))
        return before

    def small(self, at):
        if line():
            return jnp.where(in_middle(), self.total[at], self.outer[at])
        return lax.psum(self.parts[at], "dp")


def gather_whole(own):
    return lax.all_gather(own, "row", axis=0, tiled=True)


def scatter_whole(parts):
    return lax.psum_scatter(parts, "row", scatter_dimension=0, tiled=True).astype(f32)


def sum_rows(values, clock):
    if grid_rows():
        values = clock.mark(values + clock(first_way(values)))
        return clock.mark(values + clock(second_way(values)))
    return lax.psum(values, "row")


def width_pair(first, second, between=None):
    both = jnp.stack([first, second])
    moved = sibling(both)
    if between is not None:
        moved = after(moved, between(both))
    both = both + moved
    return both[0], both[1]


def normalize(values, between=None):
    width = values.shape[1] * lax.axis_size("col")
    totals, squares = width_pair(
        jnp.sum(values, axis=-1), jnp.sum(values * values, axis=-1), between
    )
    average = totals / width
    spread = squares / width - average * average
    inverse = lax.rsqrt(spread + epsilon)[:, None]
    return ((values - average[:, None]) * inverse, inverse)


def norm_back(scaled, normed_hat, inverse):
    width = normed_hat.shape[1] * lax.axis_size("col")
    first, second = width_pair(jnp.sum(scaled, axis=-1), jnp.sum(scaled * normed_hat, axis=-1))
    return inverse * (scaled - first[:, None] / width - normed_hat * second[:, None] / width)


def rotary_tables(count, rows):
    half_dims = ROT // 2
    lane = np.arange(LANES) % HD
    freqs = np.float32(base_rate) ** (-(2.0 * (lane % half_dims).astype(np.float32)) / np.float32(ROT))
    angles = np.arange(count * rows, dtype=np.float32)[:, None] * freqs.astype(np.float32)[None, :]
    turned = lane < ROT
    sign = np.where(lane < half_dims, -1.0, 1.0)
    cosine = np.where(turned, np.cos(angles.astype(np.float64)), 1.0)
    sine = np.where(turned, sign * np.sin(angles.astype(np.float64)), 0.0)
    shape = (count, rows, LANES)
    return jnp.asarray(cosine.reshape(shape), f32), jnp.asarray(sine.reshape(shape), f32)


def turn(values, cosine, sine):
    half_dims = ROT // 2
    lane = lax.broadcasted_iota(jnp.int32, values.shape, 1) % HD
    partner = jnp.where(
        lane < half_dims,
        pltpu.roll(values, LANES - half_dims, 1),
        pltpu.roll(values, half_dims, 1),
    )
    return values * cosine + partner * sine


def params(mib=60):
    return pltpu.CompilerParams(vmem_limit_bytes=mib << 20)


def cost(flops, moved, hard=0):
    return pl.CostEstimate(flops=int(flops), bytes_accessed=int(moved), transcendentals=int(hard))


def project_kernel(members, place, *refs):
    own, other = refs[:members], refs[members : 2 * members]
    keep, taken, bias = refs[2 * members : 2 * members + 3]
    cosine, sine = refs[2 * members + 3 : 3 * members + 3], refs[3 * members + 3 : 4 * members + 3]
    out = refs[-1]
    kind = pl.program_id(0)
    for at in range(members):
        result = dot(own[at][...], keep[0]) + dot(other[at][...], taken[0]) + bias[0].astype(f32)

        @pl.when(kind < 2)
        def _():
            for start in range(0, result.shape[1], LANES):
                part = slice(start, start + LANES)
                out[at, 0, :, part] = turn(result[:, part], cosine[at][0], sine[at][0]).astype(bf16)

        @pl.when(kind == 2)
        def _():
            out[at, 0] = result.astype(bf16)


def project_pieces(index, group, count, place, own, other, keep, taken, bias, cosine, sine, before):
    members = len(own)
    rows, width = own[0].shape
    units = keep.shape[2]
    piece = pl.BlockSpec((rows, width), lambda k, s: (0, 0), pipeline_mode=pl.Buffered(1))
    tables = [
        pl.BlockSpec((1, rows, LANES), functools.partial(lambda at, k, s: (s[at], 0, 0), at))
        for at in group
    ]
    weight = pl.BlockSpec((1, width, units), lambda k, s: (k, 0, 0))
    in_specs = [piece] * (2 * members) + [
        weight,
        weight,
        pl.BlockSpec((1, 1, units), lambda k, s: (k, 0, 0)),
        *tables,
        *tables,
    ]
    args = [*own, *other, keep, taken, bias] + [cosine] * members + [sine] * members
    aliases = {}
    if before is not None:
        aliases = {len(args) + 1: 0}
        in_specs.append(pl.BlockSpec(memory_space=pl.ANY))
        args.append(before)
    return pl.pallas_call(
        functools.partial(project_kernel, members),
        grid_spec=pltpu.PrefetchScalarGridSpec(
            num_scalar_prefetch=1,
            grid=(3,),
            in_specs=in_specs,
            out_specs=pl.BlockSpec((members, 1, rows, units), lambda k, s: (index, k, 0, 0)),
        ),
        out_shape=jax.ShapeDtypeStruct((count, 3, rows, units), bf16),
        input_output_aliases=aliases,
        compiler_params=params(24),
        cost_estimate=cost(
            12 * members * rows * width * units, 4 * members * rows * width + 12 * width * units
        ),
        name="project_pieces",
    )(place, *args)


def causal(rows):
    keys = lax.broadcasted_iota(jnp.int32, (rows, rows), 0)
    return keys <= lax.broadcasted_iota(jnp.int32, (rows, rows), 1)


def head_lanes(values, head):
    lane = lax.broadcasted_iota(jnp.int32, values.shape, 1)
    return jnp.where((lane >= head * HD) & (lane < (head + 1) * HD), values, jnp.zeros_like(values))


def walk(stop, body, carry):
    if isinstance(stop, int):
        for step in range(stop):
            carry = body(step, carry)
        return carry
    return lax.fori_loop(0, stop, body, carry)


def each(count, body):
    if count <= 4:
        for step in range(count):
            body(step)
    else:
        lax.fori_loop(0, count, lambda step, carry: (body(step), carry)[1], 0)


def row_range(step, rows):
    return pl.ds(step * rows if isinstance(step, int) else pl.multiple_of(step * rows, rows), rows)


def attend_kernel(slot, qkv, mixed, kept, logsum, scores):
    count, _, rows, _ = qkv.shape
    heads = LANES // HD
    scale = HD**-0.5

    def one(at):
        here = slot[at]
        query = qkv[here, 0] * jnp.asarray(scale, bf16)
        for head in range(heads):

            def look(past, highest):
                block = dot(head_lanes(qkv[slot[past], 1], head), query, NT)
                scores[row_range(past, rows), :] = block
                return jnp.maximum(highest, jnp.max(block, axis=0, keepdims=True))

            def add(past, carry):
                total, outs = carry
                weights = jnp.exp(scores[row_range(past, rows), :] - highest)
                total = total + jnp.sum(weights, axis=0, keepdims=True)
                value = jnp.transpose(qkv[slot[past], 2])[head * HD : (head + 1) * HD]
                return total, outs + dot(value, weights.astype(bf16))

            block = dot(head_lanes(qkv[here, 1], head), query, NT)
            block = jnp.where(causal(rows), block, -1e30)
            scores[row_range(at, rows), :] = block
            highest = walk(at, look, jnp.max(block, axis=0, keepdims=True))
            total, outs = walk(
                at + 1, add, (jnp.zeros((1, rows), f32), jnp.zeros((HD, rows), f32))
            )
            kept[0, here, pl.ds(head * HD, HD), :] = outs / total
            logsum[0, here, pl.ds(head, 1), :] = highest + jnp.log(total)
        mixed[here] = jnp.transpose(kept[0, here]).astype(bf16)

    each(count, one)


def attend_forward(slot, qkv):
    count, _, rows, units = qkv.shape
    pairs = units // LANES
    work = rows * rows * count * (count + 1) // 2 * units
    return pl.pallas_call(
        attend_kernel,
        grid_spec=pltpu.PrefetchScalarGridSpec(
            num_scalar_prefetch=1,
            grid=(pairs,),
            in_specs=[pl.BlockSpec((count, 3, rows, LANES), lambda p, s: (0, 0, 0, p))],
            out_specs=[
                pl.BlockSpec((count, rows, LANES), lambda p, s: (0, 0, p)),
                pl.BlockSpec((1, count, LANES, rows), lambda p, s: (p, 0, 0, 0)),
                pl.BlockSpec((1, count, 8, rows), lambda p, s: (p, 0, 0, 0)),
            ],
            scratch_shapes=[pltpu.VMEM((count * rows, rows), f32)],
        ),
        out_shape=[
            jax.ShapeDtypeStruct((count, rows, units), bf16),
            jax.ShapeDtypeStruct((pairs, count, LANES, rows), f32),
            jax.ShapeDtypeStruct((pairs, count, 8, rows), f32),
        ],
        compiler_params=params(40),
        cost_estimate=cost(16 * work, 16 * count * rows * units, work // HD),
        name="attend_forward",
    )(slot, qkv)


def attend_back_kernel(slot, place, qkv, grads, kept, logsum, cosine, sine, out, dq, dk, dv, inner):
    count, _, rows, _ = qkv.shape
    heads = LANES // HD
    scale = HD**-0.5
    dk[...] = jnp.zeros_like(dk)
    dv[...] = jnp.zeros_like(dv)

    def sums(at):
        product = jnp.transpose(grads[at].astype(f32)) * kept[0, at]
        for head in range(heads):
            part = product[head * HD : (head + 1) * HD]
            inner[at, pl.ds(head, 1), :] = jnp.sum(part, axis=0, keepdims=True)

    def one(at):
        here = slot[at]
        query = qkv[here, 0] * jnp.asarray(scale, bf16)
        grad = grads[here]
        for head in range(heads):
            query_head = head_lanes(query, head)
            grad_head = head_lanes(grad, head)

            def look(past, query_grad, last=False):
                there = slot[past]
                key = qkv[there, 1]
                block = dot(key, query_head, NT)
                weights = jnp.exp(block - logsum[0, here, pl.ds(head, 1), :])
                if last:
                    weights = jnp.where(causal(rows), weights, 0.0)
                moved = dot(qkv[there, 2], grad_head, NT)
                raw = (weights * (moved - inner[here, pl.ds(head, 1), :])).astype(bf16)
                dv[there] += dot(weights.astype(bf16), grad_head)
                dk[there] += dot(raw, query_head)
                turned = jnp.transpose(key)[head * HD : (head + 1) * HD]
                return query_grad + dot(turned, raw)

            query_grad = walk(at, look, jnp.zeros((HD, rows), f32))
            dq[pl.ds(head * HD, HD), :] = look(at, query_grad, True) * scale
        out[0, here] = turn(jnp.transpose(dq[...]), cosine[at], -sine[at]).astype(bf16)

    def finish(at):
        out[1, at] = turn(dk[at], cosine[place[at]], -sine[place[at]]).astype(bf16)
        out[2, at] = dv[at].astype(bf16)

    each(count, sums)
    each(count, one)
    each(count, finish)


def attend_backward(slot, place, qkv, grads, kept, logsum, cosine, sine):
    count, _, rows, units = qkv.shape
    pairs = units // LANES
    work = rows * rows * count * (count + 1) // 2 * units
    table = pl.BlockSpec((count, rows, LANES), lambda p, *s: (0, 0, 0))
    return pl.pallas_call(
        attend_back_kernel,
        grid_spec=pltpu.PrefetchScalarGridSpec(
            num_scalar_prefetch=2,
            grid=(pairs,),
            in_specs=[
                pl.BlockSpec((count, 3, rows, LANES), lambda p, *s: (0, 0, 0, p)),
                pl.BlockSpec((count, rows, LANES), lambda p, *s: (0, 0, p)),
                pl.BlockSpec((1, count, LANES, rows), lambda p, *s: (p, 0, 0, 0)),
                pl.BlockSpec((1, count, 8, rows), lambda p, *s: (p, 0, 0, 0)),
                table,
                table,
            ],
            out_specs=pl.BlockSpec((3, count, rows, LANES), lambda p, *s: (0, 0, 0, p)),
            scratch_shapes=[
                pltpu.VMEM((LANES, rows), f32),
                pltpu.VMEM((count, rows, LANES), f32),
                pltpu.VMEM((count, rows, LANES), f32),
                pltpu.VMEM((count, 8, rows), f32),
            ],
        ),
        out_shape=jax.ShapeDtypeStruct((3, count, rows, units), bf16),
        compiler_params=params(),
        cost_estimate=cost(40 * work, 24 * count * rows * units, work // HD),
        name="attend_backward",
    )(slot, place, qkv, grads, kept, logsum, cosine, sine)


def ordered(core, own, other, out, width):
    rest = out.shape[-1] - width
    lead = core[0] == 0
    out[..., :width] = jnp.where(lead, own[...], other[...])
    out[..., width:] = jnp.where(lead, other[..., :rest], own[..., :rest])


def block_of(width):
    return 256 if width % 256 == 0 else LANES


def mixed_out_kernel(swap, core, own, other, weight, *outs):
    units = outs[-1]
    count = own.shape[0]

    @pl.when(pl.program_id(0) == 0)
    def _():
        for at in range(count):
            ordered(core, own.at[at], other.at[swap[at]], units.at[at], own.shape[2])

    for at in range(count):
        outs[at][...] = dot(units[at], weight[...]).astype(bf16)


def mixed_out(core, swap, own, other, weight):
    count, rows, units = own.shape
    width = weight.shape[1]
    block = block_of(width)
    whole = lambda k, *s: (0, 0, 0)
    return pl.pallas_call(
        functools.partial(mixed_out_kernel, swap),
        grid_spec=pltpu.PrefetchScalarGridSpec(
            num_scalar_prefetch=1,
            grid=(width // block,),
            in_specs=[
                pl.BlockSpec((count, rows, units), whole),
                pl.BlockSpec((count, rows, units), whole),
                pl.BlockSpec((2 * units, block), lambda k, *s: (0, k)),
            ],
            out_specs=[pl.BlockSpec((rows, block), lambda k, *s: (0, k))] * count
            + [pl.BlockSpec((count, rows, 2 * units), whole)],
        ),
        out_shape=[jax.ShapeDtypeStruct((rows, width), bf16)] * count
        + [jax.ShapeDtypeStruct((count, rows, 2 * units), bf16)],
        compiler_params=params(24),
        cost_estimate=cost(4 * count * rows * units * width, 2 * count * rows * (width + 4 * units)),
        name="mixed_out",
    )(core, own, other, weight)


def hidden_kernel(members, place, *refs):
    own, other, grad_own, grad_other = (refs[k * members : (k + 1) * members] for k in range(4))
    gate_up, taken, down, down_taken = refs[4 * members : 4 * members + 4]
    outs = refs[4 * members + 4 :]
    for at in range(members):
        gate = dot(own[at][...], gate_up[0]) + dot(other[at][...], taken[0])
        up = dot(own[at][...], gate_up[1]) + dot(other[at][...], taken[1])
        grad = dot(grad_own[at][...], down[...], NT) + dot(grad_other[at][...], down_taken[...], NT)
        sigmoid = jax.nn.sigmoid(gate)
        silu = gate * sigmoid
        slope = sigmoid * (1.0 + gate * (1.0 - sigmoid))
        outs[at][0] = (grad * up * slope).astype(bf16)
        outs[at][1] = (grad * silu).astype(bf16)
        outs[at][2] = (silu * up).astype(bf16)


def hidden_pieces(group, place, own, other, grad_own, grad_other, gate_up, taken, down, down_taken):
    members = len(own)
    rows, width = own[0].shape
    units = gate_up.shape[2]
    block = block_of(units)
    rows_in = pl.BlockSpec((rows, width), lambda k, s: (0, 0), pipeline_mode=pl.Buffered(1))
    grads = [
        pl.BlockSpec(
            (rows, width),
            functools.partial(lambda at, k, s: (s[at], 0), at),
            pipeline_mode=pl.Buffered(1),
        )
        for at in group
    ]
    entry = pl.BlockSpec((2, width, block), lambda k, s: (0, 0, k))
    leave = pl.BlockSpec((block, width), lambda k, s: (k, 0))
    return pl.pallas_call(
        functools.partial(hidden_kernel, members),
        grid_spec=pltpu.PrefetchScalarGridSpec(
            num_scalar_prefetch=1,
            grid=(units // block,),
            in_specs=[rows_in] * (2 * members) + grads + grads + [entry, entry, leave, leave],
            out_specs=[pl.BlockSpec((3, rows, block), lambda k, s: (0, 0, k))] * members,
        ),
        out_shape=[jax.ShapeDtypeStruct((3, rows, units), bf16)] * members,
        compiler_params=params(40),
        cost_estimate=cost(
            12 * members * rows * width * units, 12 * width * units + 8 * members * rows * width
        ),
        name="hidden_pieces",
    )(
        place, *own, *other, *([grad_own] * members), *([grad_other] * members),
        gate_up, taken, down, down_taken,
    )


def down_grad_kernel(count, steps, core, place, *refs):
    own, other, grads = refs[:count], refs[count : 2 * count], refs[2 * count]
    first, second, units = refs[-3:]
    rows = own[0].shape[1]
    leading = pl.program_id(0) < steps
    mine = (core[0] == 0) == leading
    for at in range(count):
        units[row_range(place[at], rows), :] = jnp.where(mine, own[at][0], other[at][0])
    result = dot(units[...], grads[...], TN).astype(bf16)

    @pl.when(leading)
    def _():
        first[...] = result

    @pl.when(jnp.logical_not(leading))
    def _():
        second[...] = result


def down_grad_parts(core, place, own, other, grads, total):
    count = len(own)
    _, rows, half = own[0].shape
    width = grads.shape[1]
    block = 384
    steps = half // block
    rest = total - half
    piece = pl.BlockSpec(
        (1, rows, block), lambda k, *s: (2, 0, jnp.where(k < steps, k, k - steps))
    )
    return pl.pallas_call(
        functools.partial(down_grad_kernel, count, steps),
        grid_spec=pltpu.PrefetchScalarGridSpec(
            num_scalar_prefetch=2,
            grid=(steps + -(-rest // block),),
            in_specs=[piece] * (2 * count)
            + [pl.BlockSpec(grads.shape, lambda k, *s: (0, 0), pipeline_mode=pl.Buffered(1))],
            out_specs=[
                pl.BlockSpec((block, width), lambda k, *s: (jnp.minimum(k, steps - 1), 0)),
                pl.BlockSpec((block, width), lambda k, *s: (jnp.maximum(k - steps, 0), 0)),
            ],
            scratch_shapes=[pltpu.VMEM((count * rows, block), bf16)],
        ),
        out_shape=[
            jax.ShapeDtypeStruct((half, width), bf16),
            jax.ShapeDtypeStruct((rest, width), bf16),
        ],
        compiler_params=params(),
        cost_estimate=cost(
            2 * count * rows * total * width, 2 * count * rows * (width + 2 * half) + 2 * total * width
        ),
        name="down_grad_parts",
    )(core, place, *own, *other, grads)


def units_back_kernel(count, blocks, core, *refs):
    own, other, normed = refs[:count], refs[count : 2 * count], refs[2 * count : 3 * count]
    gate_up = refs[3 * count]
    parts = refs[3 * count + 1 : 4 * count + 1]
    sides = refs[4 * count + 1 : 4 * count + 5]
    gate, up, turned = refs[4 * count + 5 :]
    rows, half = own[0].shape[1:]
    step = pl.program_id(0)

    @pl.when(step == 0)
    def _():
        for at in range(count):
            span = pl.ds(at * rows, rows)
            for kind, units in ((0, gate), (1, up)):
                ordered(core, own[at].at[kind], other[at].at[kind], units.at[span], half)

    @pl.when(step < blocks)
    def _():
        result = (dot(gate[...], gate_up[0], NT) + dot(up[...], gate_up[1], NT)).astype(bf16)
        for at in range(count):
            parts[at][...] = result[at * rows : (at + 1) * rows]

    @pl.when(step >= blocks)
    def _():
        for at in range(count):
            turned[:, pl.ds(at * rows, rows)] = jnp.transpose(normed[at][...])
        for kind, units in ((0, gate), (1, up)):
            result = dot(turned[...], units[...]).astype(bf16)
            for side in range(2):

                @pl.when((step - blocks) // (blocks // 2) == side)
                def _():
                    sides[2 * kind + side][...] = result


def units_back(core, own, other, normed, gate_up):
    count = len(own)
    _, rows, half = own[0].shape
    _, width, total = gate_up.shape
    block = block_of(width)
    blocks = width // block
    once = pl.Buffered(1)

    def normed_at(k):
        return jnp.minimum(k, blocks - 1)

    def grad_at(k):
        return jnp.maximum(k - blocks, 0)

    sides = [
        pl.BlockSpec(
            (block, total),
            functools.partial(
                lambda side, k, s: (
                    jnp.clip(grad_at(k) - side * (blocks // 2), 0, blocks // 2 - 1),
                    0,
                ),
                side,
            ),
        )
        for _ in range(2)
        for side in range(2)
    ]
    result = pl.pallas_call(
        functools.partial(units_back_kernel, count, blocks),
        grid_spec=pltpu.PrefetchScalarGridSpec(
            num_scalar_prefetch=1,
            grid=(2 * blocks,),
            in_specs=[pl.BlockSpec((2, rows, half), lambda k, s: (0, 0, 0), pipeline_mode=once)]
            * (2 * count)
            + [pl.BlockSpec((rows, block), lambda k, s: (0, grad_at(k)))] * count
            + [pl.BlockSpec((2, block, total), lambda k, s: (0, normed_at(k), 0))],
            out_specs=[pl.BlockSpec((rows, block), lambda k, s: (0, normed_at(k)))] * count
            + sides,
            scratch_shapes=[
                pltpu.VMEM((count * rows, total), bf16),
                pltpu.VMEM((count * rows, total), bf16),
                pltpu.VMEM((block, count * rows), bf16),
            ],
        ),
        out_shape=[jax.ShapeDtypeStruct((rows, width), bf16)] * count
        + [jax.ShapeDtypeStruct((width // 2, total), bf16)] * 4,
        compiler_params=params(),
        cost_estimate=cost(
            8 * count * rows * width * total, 8 * width * total + 12 * count * rows * total
        ),
        name="units_back",
    )(core, *own, *other, *normed, gate_up)
    return result[:count], result[count:]


def down_out_kernel(count, core, *refs):
    own, other, down = refs[:count], refs[count : 2 * count], refs[2 * count]
    outs, units = refs[2 * count + 1 : -1], refs[-1]

    @pl.when(pl.program_id(0) == 0)
    def _():
        for at in range(count):
            ordered(core, own[at].at[0], other[at].at[0], units.at[at], own[at].shape[2])

    for at in range(count):
        outs[at][...] = dot(units[at], down[...]).astype(bf16)


def down_out(core, own, other, down):
    count = len(own)
    _, rows, half = own[0].shape
    total, width = down.shape
    block = block_of(width)
    piece = pl.BlockSpec((1, rows, half), lambda k, s: (2, 0, 0), pipeline_mode=pl.Buffered(1))
    return pl.pallas_call(
        functools.partial(down_out_kernel, count),
        grid_spec=pltpu.PrefetchScalarGridSpec(
            num_scalar_prefetch=1,
            grid=(width // block,),
            in_specs=[piece] * (2 * count) + [pl.BlockSpec((total, block), lambda k, s: (0, k))],
            out_specs=[pl.BlockSpec((rows, block), lambda k, s: (0, k))] * count,
            scratch_shapes=[pltpu.VMEM((count, rows, total), bf16)],
        ),
        out_shape=[jax.ShapeDtypeStruct((rows, width), bf16)] * count,
        compiler_params=params(),
        cost_estimate=cost(
            2 * count * rows * total * width, 2 * total * width + 4 * count * rows * total
        ),
        name="down_out",
    )(core, *own, *other, down)


def settle_kernel(middle, total, moved, *rest):
    rest[-1][0] = jnp.where(middle[0] == 1, total[...], moved[...]).astype(f32)


def settle(shape, index, start, block, clock, total, moved, before):
    rows, width = total.shape
    middle = clock(in_middle().astype(jnp.int32)[None])
    piece = pl.BlockSpec((block, width), lambda k, s: (k, 0))
    in_specs, args, aliases = [piece, piece], [total, moved], {}
    if before is not None:
        in_specs.append(pl.BlockSpec(memory_space=pl.ANY))
        args.append(before)
        aliases = {3: 0}
    return pl.pallas_call(
        settle_kernel,
        grid_spec=pltpu.PrefetchScalarGridSpec(
            num_scalar_prefetch=1,
            grid=(rows // block,),
            in_specs=in_specs,
            out_specs=pl.BlockSpec((1, block, width), lambda k, s: (index, start // block + k, 0)),
        ),
        out_shape=jax.ShapeDtypeStruct(shape, f32),
        input_output_aliases=aliases,
        compiler_params=params(16),
        cost_estimate=cost(0, 8 * rows * width),
        name="settle",
    )(middle, *args)


def weight_grad_kernel(pieces, kinds, parts, stacked, *refs):
    rows_in, units = refs[:pieces], refs[pieces : pieces + kinds]
    outs, rows = refs[pieces + kinds : -1], refs[-1]
    size = rows_in[0].shape[0]
    for at in range(pieces):
        rows[:, pl.ds(at * size, size)] = jnp.transpose(rows_in[at][...])
    steps = pl.num_programs(0) // parts
    for kind in range(kinds):
        array = units[kind][...]
        result = dot(rows[...], array.reshape(array.shape[-2:])).astype(bf16)
        if stacked:
            outs[0][kind] = result
            continue
        for at in range(parts):

            @pl.when(pl.program_id(0) // steps == at)
            def _():
                outs[kind * parts + at][...] = result


def weight_grads(rows, units, indices=(None,), parts=1, stacked=False):
    pieces, kinds = len(rows), len(units)
    size, width = rows[0].shape
    total, columns = units[0].shape[-2:]
    block = 256 if width // parts % 256 == 0 else LANES
    steps = width // block // parts
    specs = [
        pl.BlockSpec((total, columns), lambda k: (0, 0), pipeline_mode=pl.Buffered(1))
        if index is None
        else pl.BlockSpec(
            (1, total, columns),
            functools.partial(lambda at, k: (at, 0, 0), index),
            pipeline_mode=pl.Buffered(1),
        )
        for index in indices
    ]
    outs = [
        pl.BlockSpec(
            (block, columns),
            functools.partial(lambda at, k: (jnp.clip(k - at * steps, 0, steps - 1), 0), at),
        )
        for _ in range(kinds)
        for at in range(parts)
    ]
    shapes = [jax.ShapeDtypeStruct((width // parts, columns), bf16)] * (kinds * parts)
    if stacked:
        outs = [pl.BlockSpec((kinds, block, columns), lambda k: (0, k, 0))]
        shapes = [jax.ShapeDtypeStruct((kinds, width, columns), bf16)]
    return pl.pallas_call(
        functools.partial(weight_grad_kernel, pieces, kinds, parts, stacked),
        grid=(steps * parts,),
        in_specs=[pl.BlockSpec((size, block), lambda k: (0, k))] * pieces + specs,
        out_specs=outs,
        out_shape=shapes,
        scratch_shapes=[pltpu.VMEM((block, total), bf16)],
        compiler_params=params(),
        cost_estimate=cost(
            2 * total * width * columns * kinds,
            2 * (total * (width + columns * kinds) + width * columns * kinds),
        ),
        name="weight_grads",
    )(*rows, *units)


def mixed_grad_kernel(count, *refs):
    keep, taken, out = refs[-3:]
    for at in range(count):
        out[at] = (
            dot(refs[at][...], keep[...], NT) + dot(refs[count + at][...], taken[...], NT)
        ).astype(bf16)


def mixed_back(own, other, keep, taken):
    count = len(own)
    rows, width = own[0].shape
    units = keep.shape[0]
    return pl.pallas_call(
        functools.partial(mixed_grad_kernel, count),
        out_shape=jax.ShapeDtypeStruct((count, rows, units), bf16),
        compiler_params=params(),
        cost_estimate=cost(4 * count * rows * width * units, 4 * count * rows * width),
        name="mixed_back",
    )(*own, *other, keep, taken)


def project_back_kernel(swap, core, own, other, weight, *outs):
    units = outs[-1]
    count = own.shape[1]

    @pl.when(pl.program_id(0) == 0)
    def _():
        for kind in range(3):
            for at in range(count):
                ordered(
                    core,
                    own.at[kind, at],
                    other.at[kind, swap[at]],
                    units.at[kind, at],
                    own.shape[3],
                )

    for at in range(count):
        outs[at][...] = sum(
            dot(units[kind, at], weight[kind], NT) for kind in range(3)
        ).astype(bf16)


def project_back(core, swap, own, other, weight):
    _, count, rows, half = own.shape
    _, width, total = weight.shape
    block = block_of(width)
    whole = lambda k, *s: (0, 0, 0, 0)
    return pl.pallas_call(
        functools.partial(project_back_kernel, swap),
        grid_spec=pltpu.PrefetchScalarGridSpec(
            num_scalar_prefetch=1,
            grid=(width // block,),
            in_specs=[
                pl.BlockSpec((3, count, rows, half), whole),
                pl.BlockSpec((3, count, rows, half), whole),
                pl.BlockSpec((3, block, total), lambda k, *s: (0, k, 0)),
            ],
            out_specs=[pl.BlockSpec((rows, block), lambda k, *s: (0, k))] * count
            + [pl.BlockSpec((3, count, rows, total), whole)],
        ),
        out_shape=[jax.ShapeDtypeStruct((rows, width), bf16)] * count
        + [jax.ShapeDtypeStruct((3, count, rows, total), bf16)],
        compiler_params=params(),
        cost_estimate=cost(6 * count * rows * total * width, 2 * count * rows * (width + 6 * total)),
        name="project_back",
    )(core, own, other, weight)


def halves(weight, axis, width):
    lead = lax.slice_in_dim(weight, 0, width, axis=axis)
    rest = lax.slice_in_dim(weight, width, weight.shape[axis], axis=axis)
    pad = [(0, 0)] * weight.ndim
    pad[axis] = (0, width - rest.shape[axis])
    rest = jnp.pad(rest, pad)
    first = lax.axis_index("col") == 0
    return jnp.where(first, lead, rest), jnp.where(first, rest, lead)


def shards(
    block_input,
    norm1_gain,
    norm1_shift,
    qkv_weight,
    qkv_bias,
    out_weight,
    norm2_gain,
    norm2_shift,
    gate_up_weight,
    down_weight,
    output_grad,
):
    count = lax.axis_size("row")
    rows = block_input.shape[0]
    core = lax.axis_index("col").astype(jnp.int32)[None]
    place, swap = places()
    place = place.astype(jnp.int32)
    slot = inverse_places(place)
    half_units = out_weight.shape[0] // 2
    total_hidden = down_weight.shape[0]
    half_hidden = -(-total_hidden // (2 * LANES)) * LANES
    if grid_rows():
        groups = (((2,), 2), ((0, 1), 0), ((3,), 3))
    else:
        groups = tuple(((at,), at) for at in range(count))

    clock = Clock()
    inputs = block_input.astype(f32)
    gain_one = norm1_gain.astype(f32)
    gain_two = norm2_gain.astype(f32)
    split = {}

    def between(stats):
        split["keep"], split["send"] = halves(after(qkv_weight, stats), 2, half_units)
        return split["keep"]

    hat_one, inverse_one = normalize(inputs, between)
    normed_one = clock.mark((hat_one * gain_one + norm1_shift.astype(f32)).astype(bf16))

    one_own, fetch = gather_rows(normed_one)
    grad_own = None if grid_rows() else gather_whole(output_grad)
    qkv_keep = split["keep"]
    qkv_taken = sibling(split["send"])
    cosine, sine = rotary_tables(count, rows)
    bias = qkv_bias[:, None, :]
    qkv = None
    for group, index in groups:
        if qkv is not None and len(one_own) < count:
            grad_own = gather_whole(after(output_grad, one_own[0], one_own[1], clock.last))
            one_own += fetch(clock.last)
        others = [sibling(clock(one_own[swap[at]])) for at in group]
        qkv = clock.mark(
            project_pieces(
                index, group, count, place, [one_own[at] for at in group], others,
                qkv_keep, qkv_taken, clock(bias), cosine, sine, qkv,
            )
        )
        if group == groups[0][0]:
            gate_up_keep, gate_up_send = halves(clock(gate_up_weight), 2, half_hidden)
            clock.mark(gate_up_keep)
            down_keep, down_send = halves(clock(down_weight), 0, half_hidden)
            clock.mark(down_keep)
            out_keep, out_send = halves(clock(out_weight), 0, half_units)
            clock.mark(out_keep)
    gate_up_taken = sibling(clock(gate_up_send))
    down_taken = sibling(clock(down_send))
    out_taken = sibling(clock(out_send))
    mixed, kept, logsum = attend_forward(clock(slot), qkv)
    clock.mark(mixed)
    *branch, mixed_units = mixed_out(clock(core), swap, mixed, sibling(mixed), out_weight)
    clock.mark(branch[0])
    branch = scatter_rows(branch, clock)
    grad_other = sibling(clock(grad_own))
    after_rows = inputs + branch
    hat_two, inverse_two = normalize(after_rows)
    normed_two = clock.mark((hat_two * gain_two + norm2_shift.astype(f32)).astype(bf16))

    two_own, fetch = gather_rows(normed_two)
    mine, theirs = [None] * count, [None] * count
    for group, _ in groups:
        if group != groups[0][0] and len(two_own) < count:
            two_own += fetch(clock.last)
        results = hidden_pieces(
            group, clock(place),
            [two_own[at] for at in group],
            [sibling(clock(two_own[swap[at]])) for at in group],
            grad_own, grad_other, gate_up_keep, gate_up_taken, down_keep, down_taken,
        )
        clock.mark(results[0])
        for at, result in zip(group, results):
            mine[at] = result
        for at in group:
            theirs[at] = sibling(mine[swap[at]])

    sums = Line(clock)
    parts = down_grad_parts(clock(core), place, mine, theirs, grad_own, total_hidden)
    clock.mark(parts[0])
    sums.add(*parts)
    normed_parts, parts = units_back(clock(core), mine, theirs, two_own, gate_up_weight)
    clock.mark(normed_parts[0])
    sums.add(*parts)
    sums.join()
    forms = {
        "down": ((1,) + down_weight.shape, LANES),
        "gate_up": (gate_up_weight.shape, block_of(gate_up_weight.shape[1] // 2)),
        "out": ((1,) + out_weight.shape, block_of(out_weight.shape[0])),
        "qkv": (qkv_weight.shape, block_of(qkv_weight.shape[1])),
    }
    targets = [("down", 0, 0), ("down", 0, half_hidden)]
    half_width = gate_up_weight.shape[1] // 2
    targets += [("gate_up", kind, start) for kind in (0, 1) for start in (0, half_width)]
    targets += [("out", 0, 0)] + [("qkv", kind, 0) for kind in range(3)] + [("small", 0, 0)]
    settled = {}

    def settle_next():
        at = sums.settled
        name, part, start = targets[at]
        if name == "small":
            settled[name] = sums.small(at)
            sums.settled += 1
        else:
            shape, block = forms[name]
            settled[name] = sums.settle(shape, ((part, start),), block, settled.get(name))

    def tick():
        sums.join()
        sums.total_up()
        settle_next()

    normed_two_grad = clock.mark(scatter_rows(normed_parts, clock))
    after_grad = output_grad.astype(f32) + norm_back(
        normed_two_grad * gain_two, hat_two, inverse_two
    )
    branch_grad = clock.mark(after_grad.astype(bf16))
    branch_own, fetch = gather_rows(branch_grad)
    sums.join()
    down_parts = down_out(clock(core), mine, theirs, down_weight)
    clock.mark(down_parts[0])
    if len(branch_own) < count:
        branch_own += fetch(clock.last)
    branch_other = [sibling(branch_own[swap[at]]) for at in range(count)]
    sums.total_up()
    branch_rows = clock.mark(jnp.concatenate([clock(branch_own[0]), *branch_own[1:]], axis=0))
    mixed_grad = clock.mark(mixed_back(branch_own, branch_other, clock(out_keep), out_taken))
    sums.join()
    project_grad = clock.mark(
        attend_backward(clock(slot), place, qkv, mixed_grad, kept, logsum, cosine, sine)
    )
    project_other = sibling(project_grad)
    settle_next()
    parts = weight_grads([mixed_units.reshape(count * rows, -1)], [clock(branch_rows)])
    clock.mark(parts[0])
    sums.add(*parts)
    sums.join()
    sums.total_up()
    if grid_rows():
        far = first_way(down_parts[3])
        near = first_way(down_parts[0])
        side = second_way(clock.mark(plus(down_parts[1], clock(far))))
    *one_parts, project_units = project_back(
        clock(core), swap, project_grad, project_other, qkv_weight
    )
    clock.mark(one_parts[0])
    if grid_rows():
        down = down_parts[2].astype(f32) + near.astype(f32) + clock(side).astype(f32)
    else:
        down = scatter_rows(down_parts, clock)
    block_output = clock.mark((after_rows + down).astype(bf16))
    sums.join()
    sums.total_up()
    settle_next()
    project_units = project_units.reshape(3, count * rows, -1)
    qkv_parts = weight_grads(one_own, [clock(project_units)] * 3, (0, 1, 2))
    clock.mark(qkv_parts[0])
    tick()
    normed_one_grad = clock.mark(scatter_rows(one_parts, clock))
    input_grad = after_grad + norm_back(normed_one_grad * gain_one, hat_one, inverse_one)
    gains = jnp.stack(
        [
            jnp.sum(normed_one_grad * hat_one, axis=0),
            jnp.sum(normed_one_grad, axis=0),
            jnp.sum(normed_two_grad * hat_two, axis=0),
            jnp.sum(normed_two_grad, axis=0),
        ]
    )
    width = gains.shape[1]
    gains = clock.mark(gains)
    sums.total_up()
    settle_next()
    gains = sum_rows(gains, clock)
    bias_grad = jnp.sum(clock(project_grad).astype(f32), axis=(1, 2))
    clock.mark(bias_grad)
    small = jnp.concatenate([gains.reshape(-1, LANES), bias_grad.reshape(-1, LANES)], axis=0)
    sums.add(*qkv_parts, small)
    input_grad = clock.mark(clock(input_grad))
    while len(sums.half) < len(targets) - 1 if line() else sums.settled < len(targets) - 3:
        tick()
    sums.join()
    sums.total_up()
    settle_next()
    sums.total_up()
    while sums.settled < len(targets):
        settle_next()
    small = settled["small"]
    gains = small[: 4 * width // LANES].reshape(4, width)
    bias_grad = small[4 * width // LANES :].reshape(bias_grad.shape)
    return (
        block_output,
        input_grad,
        gains[0],
        gains[1],
        settled["qkv"],
        bias_grad,
        settled["out"][0],
        gains[2],
        gains[3],
        settled["gate_up"],
        settled["down"][0],
    )


def inverse_places(place):
    spots = jnp.arange(place.shape[0])
    return jnp.sum(
        jnp.where(place[None, :] == spots[:, None], spots[None, :], 0), axis=1
    ).astype(jnp.int32)


def solution(mesh):
    placed = (
        P(("dp", "row"), "col"),
        P("col"),
        P("col"),
        P(None, "col", "row"),
        P(None, ("row", "col")),
        P("row", "col"),
        P("col"),
        P("col"),
        P(None, "col", "row"),
        P("row", "col"),
        P(("dp", "row"), "col"),
    )
    return jax.shard_map(
        shards,
        mesh=mesh,
        in_specs=placed,
        out_specs=(
            P(("dp", "row"), "col"),
            P(("dp", "row"), "col"),
            P("col"),
            P("col"),
            P(None, "col", "row"),
            P(None, ("row", "col")),
            P("row", "col"),
            P("col"),
            P("col"),
            P(None, "col", "row"),
            P("row", "col"),
        ),
        check_vma=False,
    )
```

```python
import functools

import jax
import jax.numpy as jnp
import numpy as np
from jax import lax
from jax.experimental import pallas as pl
from jax.experimental.pallas import tpu as pltpu
from jax.sharding import PartitionSpec as P

HD = 64
ROT = 16
LANES = 128

epsilon = 1e-05
base_rate = 10000.0
bf16 = jnp.bfloat16
f32 = jnp.float32

NN = (((1,), (0,)), ((), ()))
NT = (((1,), (1,)), ((), ()))
TN = (((0,), (0,)), ((), ()))


def dot(first, second, dims=NN):
    return lax.dot_general(first, second, dims, preferred_element_type=f32)


def row_permute(values, core_zero, core_one):
    pairs = [
        (row * 2 + core, (row ^ (core_one if core else core_zero)) * 2 + core)
        for row in range(4)
        for core in range(2)
    ]
    return lax.ppermute(values, ("row", "col"), pairs)


def first_way(values):
    return row_permute(values, 1, 2)


def second_way(values):
    return row_permute(values, 2, 1)


def sibling(values):
    return lax.ppermute(values, "col", [(0, 1), (1, 0)])


def grid_rows():
    return lax.axis_size("row") == 4


def places():
    row, core = lax.axis_index("row"), lax.axis_index("col")
    if grid_rows():
        one = jnp.where(core == 0, 1, 2)
        return jnp.stack([row ^ one, row ^ (3 - one), row, row ^ 3]), (1, 0, 2, 3)
    count = lax.axis_size("row")
    return jnp.arange(count), tuple(range(count))


def after(value, *earlier):
    return lax.optimization_barrier((value,) + earlier)[0]


def gather_rows(own):
    if grid_rows():
        near = first_way(own)
        side = second_way(own)
        return [near, side, own], lambda *earlier: [second_way(after(near, side, *earlier))]
    whole = lax.all_gather(own, "row", axis=0, tiled=True)
    return jnp.split(whole, lax.axis_size("row"), axis=0), lambda *earlier: []


def scatter_rows(parts, clock):
    if grid_rows():
        passing = first_way(parts[3])
        near = first_way(parts[0])
        side = second_way(clock.mark(plus(parts[1], clock(passing))))
        return parts[2].astype(f32) + near.astype(f32) + side.astype(f32)
    whole = jnp.concatenate(parts, axis=0)
    return lax.psum_scatter(whole, "row", scatter_dimension=0, tiled=True).astype(f32)


def line():
    return lax.axis_size("dp") == 4


def in_middle():
    place = lax.axis_index("dp")
    return (place == 1) | (place == 2)


def inward(part):
    return lax.ppermute(part, "dp", [(0, 1), (3, 2)])


def across(part):
    return lax.ppermute(part, "dp", [(1, 2), (2, 1)])


def outward(part):
    return lax.ppermute(part, "dp", [(1, 0), (2, 3)])


def plus(first, second):
    return (first.astype(f32) + second.astype(f32)).astype(first.dtype)


class Clock:
    def __init__(self):
        self.last = None

    def __call__(self, value):
        return value if self.last is None else after(value, self.last)

    def mark(self, value):
        self.last = value
        return value


class Line:
    def __init__(self, clock):
        self.clock = clock
        self.parts, self.inner, self.half, self.other, self.total, self.outer = ([] for _ in range(6))
        self.settled = 0

    def feed(self):
        at = len(self.inner)
        if at < len(self.parts) and at < len(self.half) + 2:
            part = self.parts[at]
            self.inner.append(inward(after(part, self.inner[at - 2]) if at >= 2 else part))

    def add(self, *parts):
        self.parts += parts
        if line():
            for _ in parts:
                self.feed()

    def join(self):
        if line():
            at = len(self.half)
            self.half.append(self.clock.mark(plus(self.parts[at], self.clock(self.inner[at]))))
            self.feed()
            self.other.append(across(self.half[at]))

    def total_up(self):
        if line():
            at = len(self.total)
            self.total.append(self.clock.mark(plus(self.half[at], self.clock(self.other[at]))))
            self.outer.append(outward(self.total[at]))

    def settle(self, shape, places, block, before=None):
        for index, start in places:
            at = self.settled
            self.settled += 1
            if line():
                before = self.clock.mark(
                    settle(shape, index, start, block, self.clock, self.total[at], self.outer[at], before)
                )
            else:
                value = lax.psum(self.parts[at], "dp").astype(f32)[None]
                before = jnp.zeros(shape, f32) if before is None else before
                before = lax.dynamic_update_slice(before, value, (index, start, 0))
        return before

    def small(self, at):
        if line():
            return jnp.where(in_middle(), self.total[at], self.outer[at])
        return lax.psum(self.parts[at], "dp")


def gather_whole(own):
    return lax.all_gather(own, "row", axis=0, tiled=True)


def scatter_whole(parts):
    return lax.psum_scatter(parts, "row", scatter_dimension=0, tiled=True).astype(f32)


def sum_rows(values, clock):
    if grid_rows():
        values = clock.mark(values + clock(first_way(values)))
        return clock.mark(values + clock(second_way(values)))
    return lax.psum(values, "row")


def width_pair(first, second, between=None):
    both = jnp.stack([first, second])
    moved = sibling(both)
    if between is not None:
        moved = after(moved, between(both))
    both = both + moved
    return both[0], both[1]


def normalize(values, between=None):
    width = values.shape[1] * lax.axis_size("col")
    totals, squares = width_pair(
        jnp.sum(values, axis=-1), jnp.sum(values * values, axis=-1), between
    )
    average = totals / width
    spread = squares / width - average * average
    inverse = lax.rsqrt(spread + epsilon)[:, None]
    return ((values - average[:, None]) * inverse, inverse)


def norm_back(scaled, normed_hat, inverse):
    width = normed_hat.shape[1] * lax.axis_size("col")
    first, second = width_pair(jnp.sum(scaled, axis=-1), jnp.sum(scaled * normed_hat, axis=-1))
    return inverse * (scaled - first[:, None] / width - normed_hat * second[:, None] / width)


def rotary_tables(count, rows):
    half_dims = ROT // 2
    lane = np.arange(LANES) % HD
    freqs = np.float32(base_rate) ** (-(2.0 * (lane % half_dims).astype(np.float32)) / np.float32(ROT))
    angles = np.arange(count * rows, dtype=np.float32)[:, None] * freqs.astype(np.float32)[None, :]
    turned = lane < ROT
    sign = np.where(lane < half_dims, -1.0, 1.0)
    cosine = np.where(turned, np.cos(angles.astype(np.float64)), 1.0)
    sine = np.where(turned, sign * np.sin(angles.astype(np.float64)), 0.0)
    shape = (count, rows, LANES)
    return jnp.asarray(cosine.reshape(shape), f32), jnp.asarray(sine.reshape(shape), f32)


def turn(values, cosine, sine):
    half_dims = ROT // 2
    lane = lax.broadcasted_iota(jnp.int32, values.shape, 1) % HD
    partner = jnp.where(
        lane < half_dims,
        pltpu.roll(values, LANES - half_dims, 1),
        pltpu.roll(values, half_dims, 1),
    )
    return values * cosine + partner * sine


def params(mib=60):
    return pltpu.CompilerParams(vmem_limit_bytes=mib << 20)


def cost(flops, moved, hard=0):
    return pl.CostEstimate(flops=int(flops), bytes_accessed=int(moved), transcendentals=int(hard))


def project_kernel(members, place, *refs):
    own, other = refs[:members], refs[members : 2 * members]
    keep, taken, bias = refs[2 * members : 2 * members + 3]
    cosine, sine = refs[2 * members + 3 : 3 * members + 3], refs[3 * members + 3 : 4 * members + 3]
    out = refs[-1]
    kind = pl.program_id(0)
    for at in range(members):
        result = dot(own[at][...], keep[0]) + dot(other[at][...], taken[0]) + bias[0].astype(f32)

        @pl.when(kind < 2)
        def _():
            for start in range(0, result.shape[1], LANES):
                part = slice(start, start + LANES)
                out[at, 0, :, part] = turn(result[:, part], cosine[at][0], sine[at][0]).astype(bf16)

        @pl.when(kind == 2)
        def _():
            out[at, 0] = result.astype(bf16)


def project_pieces(index, group, count, place, own, other, keep, taken, bias, cosine, sine, before):
    members = len(own)
    rows, width = own[0].shape
    units = keep.shape[2]
    piece = pl.BlockSpec((rows, width), lambda k, s: (0, 0), pipeline_mode=pl.Buffered(1))
    tables = [
        pl.BlockSpec((1, rows, LANES), functools.partial(lambda at, k, s: (s[at], 0, 0), at))
        for at in group
    ]
    weight = pl.BlockSpec((1, width, units), lambda k, s: (k, 0, 0))
    in_specs = [piece] * (2 * members) + [
        weight,
        weight,
        pl.BlockSpec((1, 1, units), lambda k, s: (k, 0, 0)),
        *tables,
        *tables,
    ]
    args = [*own, *other, keep, taken, bias] + [cosine] * members + [sine] * members
    aliases = {}
    if before is not None:
        aliases = {len(args) + 1: 0}
        in_specs.append(pl.BlockSpec(memory_space=pl.ANY))
        args.append(before)
    return pl.pallas_call(
        functools.partial(project_kernel, members),
        grid_spec=pltpu.PrefetchScalarGridSpec(
            num_scalar_prefetch=1,
            grid=(3,),
            in_specs=in_specs,
            out_specs=pl.BlockSpec((members, 1, rows, units), lambda k, s: (index, k, 0, 0)),
        ),
        out_shape=jax.ShapeDtypeStruct((count, 3, rows, units), bf16),
        input_output_aliases=aliases,
        compiler_params=params(24),
        cost_estimate=cost(
            12 * members * rows * width * units, 4 * members * rows * width + 12 * width * units
        ),
        name="project_pieces",
    )(place, *args)


def causal(rows):
    keys = lax.broadcasted_iota(jnp.int32, (rows, rows), 0)
    return keys <= lax.broadcasted_iota(jnp.int32, (rows, rows), 1)


def head_lanes(values, head):
    lane = lax.broadcasted_iota(jnp.int32, values.shape, 1)
    return jnp.where((lane >= head * HD) & (lane < (head + 1) * HD), values, jnp.zeros_like(values))


def walk(stop, body, carry):
    if isinstance(stop, int):
        for step in range(stop):
            carry = body(step, carry)
        return carry
    return lax.fori_loop(0, stop, body, carry)


def each(count, body):
    if count <= 4:
        for step in range(count):
            body(step)
    else:
        lax.fori_loop(0, count, lambda step, carry: (body(step), carry)[1], 0)


def row_range(step, rows):
    return pl.ds(step * rows if isinstance(step, int) else pl.multiple_of(step * rows, rows), rows)


def attend_kernel(slot, qkv, mixed, kept, logsum, scores):
    count, _, rows, _ = qkv.shape
    heads = LANES // HD
    scale = HD**-0.5

    def one(at):
        here = slot[at]
        query = qkv[here, 0] * jnp.asarray(scale, bf16)
        for head in range(heads):

            def look(past, highest):
                block = dot(head_lanes(qkv[slot[past], 1], head), query, NT)
                scores[row_range(past, rows), :] = block
                return jnp.maximum(highest, jnp.max(block, axis=0, keepdims=True))

            def add(past, carry):
                total, outs = carry
                weights = jnp.exp(scores[row_range(past, rows), :] - highest)
                total = total + jnp.sum(weights, axis=0, keepdims=True)
                value = jnp.transpose(qkv[slot[past], 2])[head * HD : (head + 1) * HD]
                return total, outs + dot(value, weights.astype(bf16))

            block = dot(head_lanes(qkv[here, 1], head), query, NT)
            block = jnp.where(causal(rows), block, -1e30)
            scores[row_range(at, rows), :] = block
            highest = walk(at, look, jnp.max(block, axis=0, keepdims=True))
            total, outs = walk(
                at + 1, add, (jnp.zeros((1, rows), f32), jnp.zeros((HD, rows), f32))
            )
            kept[0, here, pl.ds(head * HD, HD), :] = outs / total
            logsum[0, here, pl.ds(head, 1), :] = highest + jnp.log(total)
        mixed[here] = jnp.transpose(kept[0, here]).astype(bf16)

    each(count, one)


def attend_forward(slot, qkv):
    count, _, rows, units = qkv.shape
    pairs = units // LANES
    work = rows * rows * count * (count + 1) // 2 * units
    return pl.pallas_call(
        attend_kernel,
        grid_spec=pltpu.PrefetchScalarGridSpec(
            num_scalar_prefetch=1,
            grid=(pairs,),
            in_specs=[pl.BlockSpec((count, 3, rows, LANES), lambda p, s: (0, 0, 0, p))],
            out_specs=[
                pl.BlockSpec((count, rows, LANES), lambda p, s: (0, 0, p)),
                pl.BlockSpec((1, count, LANES, rows), lambda p, s: (p, 0, 0, 0)),
                pl.BlockSpec((1, count, 8, rows), lambda p, s: (p, 0, 0, 0)),
            ],
            scratch_shapes=[pltpu.VMEM((count * rows, rows), f32)],
        ),
        out_shape=[
            jax.ShapeDtypeStruct((count, rows, units), bf16),
            jax.ShapeDtypeStruct((pairs, count, LANES, rows), f32),
            jax.ShapeDtypeStruct((pairs, count, 8, rows), f32),
        ],
        compiler_params=params(40),
        cost_estimate=cost(16 * work, 16 * count * rows * units, work // HD),
        name="attend_forward",
    )(slot, qkv)


def attend_back_kernel(slot, place, qkv, grads, kept, logsum, cosine, sine, out, dq, dk, dv, inner):
    count, _, rows, _ = qkv.shape
    heads = LANES // HD
    scale = HD**-0.5
    dk[...] = jnp.zeros_like(dk)
    dv[...] = jnp.zeros_like(dv)

    def sums(at):
        product = jnp.transpose(grads[at].astype(f32)) * kept[0, at]
        for head in range(heads):
            part = product[head * HD : (head + 1) * HD]
            inner[at, pl.ds(head, 1), :] = jnp.sum(part, axis=0, keepdims=True)

    def one(at):
        here = slot[at]
        query = qkv[here, 0] * jnp.asarray(scale, bf16)
        grad = grads[here]
        for head in range(heads):
            query_head = head_lanes(query, head)
            grad_head = head_lanes(grad, head)

            def look(past, query_grad, last=False):
                there = slot[past]
                key = qkv[there, 1]
                block = dot(key, query_head, NT)
                weights = jnp.exp(block - logsum[0, here, pl.ds(head, 1), :])
                if last:
                    weights = jnp.where(causal(rows), weights, 0.0)
                moved = dot(qkv[there, 2], grad_head, NT)
                raw = (weights * (moved - inner[here, pl.ds(head, 1), :])).astype(bf16)
                dv[there] += dot(weights.astype(bf16), grad_head)
                dk[there] += dot(raw, query_head)
                turned = jnp.transpose(key)[head * HD : (head + 1) * HD]
                return query_grad + dot(turned, raw)

            query_grad = walk(at, look, jnp.zeros((HD, rows), f32))
            dq[pl.ds(head * HD, HD), :] = look(at, query_grad, True) * scale
        out[0, here] = turn(jnp.transpose(dq[...]), cosine[at], -sine[at]).astype(bf16)

    def finish(at):
        out[1, at] = turn(dk[at], cosine[place[at]], -sine[place[at]]).astype(bf16)
        out[2, at] = dv[at].astype(bf16)

    each(count, sums)
    each(count, one)
    each(count, finish)


def attend_backward(slot, place, qkv, grads, kept, logsum, cosine, sine):
    count, _, rows, units = qkv.shape
    pairs = units // LANES
    work = rows * rows * count * (count + 1) // 2 * units
    table = pl.BlockSpec((count, rows, LANES), lambda p, *s: (0, 0, 0))
    return pl.pallas_call(
        attend_back_kernel,
        grid_spec=pltpu.PrefetchScalarGridSpec(
            num_scalar_prefetch=2,
            grid=(pairs,),
            in_specs=[
                pl.BlockSpec((count, 3, rows, LANES), lambda p, *s: (0, 0, 0, p)),
                pl.BlockSpec((count, rows, LANES), lambda p, *s: (0, 0, p)),
                pl.BlockSpec((1, count, LANES, rows), lambda p, *s: (p, 0, 0, 0)),
                pl.BlockSpec((1, count, 8, rows), lambda p, *s: (p, 0, 0, 0)),
                table,
                table,
            ],
            out_specs=pl.BlockSpec((3, count, rows, LANES), lambda p, *s: (0, 0, 0, p)),
            scratch_shapes=[
                pltpu.VMEM((LANES, rows), f32),
                pltpu.VMEM((count, rows, LANES), f32),
                pltpu.VMEM((count, rows, LANES), f32),
                pltpu.VMEM((count, 8, rows), f32),
            ],
        ),
        out_shape=jax.ShapeDtypeStruct((3, count, rows, units), bf16),
        compiler_params=params(),
        cost_estimate=cost(40 * work, 24 * count * rows * units, work // HD),
        name="attend_backward",
    )(slot, place, qkv, grads, kept, logsum, cosine, sine)


def ordered(core, own, other, out, width):
    rest = out.shape[-1] - width
    lead = core[0] == 0
    out[..., :width] = jnp.where(lead, own[...], other[...])
    out[..., width:] = jnp.where(lead, other[..., :rest], own[..., :rest])


def block_of(width):
    return 256 if width % 256 == 0 else LANES


def mixed_out_kernel(swap, core, own, other, weight, *outs):
    units = outs[-1]
    count = own.shape[0]

    @pl.when(pl.program_id(0) == 0)
    def _():
        for at in range(count):
            ordered(core, own.at[at], other.at[swap[at]], units.at[at], own.shape[2])

    for at in range(count):
        outs[at][...] = dot(units[at], weight[...]).astype(bf16)


def mixed_out(core, swap, own, other, weight):
    count, rows, units = own.shape
    width = weight.shape[1]
    block = block_of(width)
    whole = lambda k, *s: (0, 0, 0)
    return pl.pallas_call(
        functools.partial(mixed_out_kernel, swap),
        grid_spec=pltpu.PrefetchScalarGridSpec(
            num_scalar_prefetch=1,
            grid=(width // block,),
            in_specs=[
                pl.BlockSpec((count, rows, units), whole),
                pl.BlockSpec((count, rows, units), whole),
                pl.BlockSpec((2 * units, block), lambda k, *s: (0, k)),
            ],
            out_specs=[pl.BlockSpec((rows, block), lambda k, *s: (0, k))] * count
            + [pl.BlockSpec((count, rows, 2 * units), whole)],
        ),
        out_shape=[jax.ShapeDtypeStruct((rows, width), bf16)] * count
        + [jax.ShapeDtypeStruct((count, rows, 2 * units), bf16)],
        compiler_params=params(24),
        cost_estimate=cost(4 * count * rows * units * width, 2 * count * rows * (width + 4 * units)),
        name="mixed_out",
    )(core, own, other, weight)


def hidden_kernel(members, place, *refs):
    own, other, grad_own, grad_other = (refs[k * members : (k + 1) * members] for k in range(4))
    gate_up, taken, down, down_taken = refs[4 * members : 4 * members + 4]
    outs = refs[4 * members + 4 :]
    for at in range(members):
        gate = dot(own[at][...], gate_up[0]) + dot(other[at][...], taken[0])
        up = dot(own[at][...], gate_up[1]) + dot(other[at][...], taken[1])
        grad = dot(grad_own[at][...], down[...], NT) + dot(grad_other[at][...], down_taken[...], NT)
        sigmoid = jax.nn.sigmoid(gate)
        silu = gate * sigmoid
        slope = sigmoid * (1.0 + gate * (1.0 - sigmoid))
        outs[at][0] = (grad * up * slope).astype(bf16)
        outs[at][1] = (grad * silu).astype(bf16)
        outs[at][2] = (silu * up).astype(bf16)


def hidden_pieces(group, place, own, other, grad_own, grad_other, gate_up, taken, down, down_taken):
    members = len(own)
    rows, width = own[0].shape
    units = gate_up.shape[2]
    block = block_of(units)
    rows_in = pl.BlockSpec((rows, width), lambda k, s: (0, 0), pipeline_mode=pl.Buffered(1))
    grads = [
        pl.BlockSpec(
            (rows, width),
            functools.partial(lambda at, k, s: (s[at], 0), at),
            pipeline_mode=pl.Buffered(1),
        )
        for at in group
    ]
    entry = pl.BlockSpec((2, width, block), lambda k, s: (0, 0, k))
    leave = pl.BlockSpec((block, width), lambda k, s: (k, 0))
    return pl.pallas_call(
        functools.partial(hidden_kernel, members),
        grid_spec=pltpu.PrefetchScalarGridSpec(
            num_scalar_prefetch=1,
            grid=(units // block,),
            in_specs=[rows_in] * (2 * members) + grads + grads + [entry, entry, leave, leave],
            out_specs=[pl.BlockSpec((3, rows, block), lambda k, s: (0, 0, k))] * members,
        ),
        out_shape=[jax.ShapeDtypeStruct((3, rows, units), bf16)] * members,
        compiler_params=params(40),
        cost_estimate=cost(
            12 * members * rows * width * units, 12 * width * units + 8 * members * rows * width
        ),
        name="hidden_pieces",
    )(
        place, *own, *other, *([grad_own] * members), *([grad_other] * members),
        gate_up, taken, down, down_taken,
    )


def down_grad_kernel(count, steps, core, place, *refs):
    own, other, grads = refs[:count], refs[count : 2 * count], refs[2 * count]
    first, second, units = refs[-3:]
    rows = own[0].shape[1]
    leading = pl.program_id(0) < steps
    mine = (core[0] == 0) == leading
    for at in range(count):
        units[row_range(place[at], rows), :] = jnp.where(mine, own[at][0], other[at][0])
    result = dot(units[...], grads[...], TN).astype(bf16)

    @pl.when(leading)
    def _():
        first[...] = result

    @pl.when(jnp.logical_not(leading))
    def _():
        second[...] = result


def down_grad_parts(core, place, own, other, grads, total):
    count = len(own)
    _, rows, half = own[0].shape
    width = grads.shape[1]
    block = 384
    steps = half // block
    rest = total - half
    piece = pl.BlockSpec(
        (1, rows, block), lambda k, *s: (2, 0, jnp.where(k < steps, k, k - steps))
    )
    return pl.pallas_call(
        functools.partial(down_grad_kernel, count, steps),
        grid_spec=pltpu.PrefetchScalarGridSpec(
            num_scalar_prefetch=2,
            grid=(steps + -(-rest // block),),
            in_specs=[piece] * (2 * count)
            + [pl.BlockSpec(grads.shape, lambda k, *s: (0, 0), pipeline_mode=pl.Buffered(1))],
            out_specs=[
                pl.BlockSpec((block, width), lambda k, *s: (jnp.minimum(k, steps - 1), 0)),
                pl.BlockSpec((block, width), lambda k, *s: (jnp.maximum(k - steps, 0), 0)),
            ],
            scratch_shapes=[pltpu.VMEM((count * rows, block), bf16)],
        ),
        out_shape=[
            jax.ShapeDtypeStruct((half, width), bf16),
            jax.ShapeDtypeStruct((rest, width), bf16),
        ],
        compiler_params=params(),
        cost_estimate=cost(
            2 * count * rows * total * width, 2 * count * rows * (width + 2 * half) + 2 * total * width
        ),
        name="down_grad_parts",
    )(core, place, *own, *other, grads)


def units_back_kernel(count, blocks, core, *refs):
    own, other, normed = refs[:count], refs[count : 2 * count], refs[2 * count : 3 * count]
    gate_up = refs[3 * count]
    parts = refs[3 * count + 1 : 4 * count + 1]
    sides = refs[4 * count + 1 : 4 * count + 5]
    gate, up, turned = refs[4 * count + 5 :]
    rows, half = own[0].shape[1:]
    step = pl.program_id(0)

    @pl.when(step == 0)
    def _():
        for at in range(count):
            span = pl.ds(at * rows, rows)
            for kind, units in ((0, gate), (1, up)):
                ordered(core, own[at].at[kind], other[at].at[kind], units.at[span], half)

    @pl.when(step < blocks)
    def _():
        result = (dot(gate[...], gate_up[0], NT) + dot(up[...], gate_up[1], NT)).astype(bf16)
        for at in range(count):
            parts[at][...] = result[at * rows : (at + 1) * rows]

    @pl.when(step >= blocks)
    def _():
        for at in range(count):
            turned[:, pl.ds(at * rows, rows)] = jnp.transpose(normed[at][...])
        for kind, units in ((0, gate), (1, up)):
            result = dot(turned[...], units[...]).astype(bf16)
            for side in range(2):

                @pl.when((step - blocks) // (blocks // 2) == side)
                def _():
                    sides[2 * kind + side][...] = result


def units_back(core, own, other, normed, gate_up):
    count = len(own)
    _, rows, half = own[0].shape
    _, width, total = gate_up.shape
    block = block_of(width)
    blocks = width // block
    once = pl.Buffered(1)

    def normed_at(k):
        return jnp.minimum(k, blocks - 1)

    def grad_at(k):
        return jnp.maximum(k - blocks, 0)

    sides = [
        pl.BlockSpec(
            (block, total),
            functools.partial(
                lambda side, k, s: (
                    jnp.clip(grad_at(k) - side * (blocks // 2), 0, blocks // 2 - 1),
                    0,
                ),
                side,
            ),
        )
        for _ in range(2)
        for side in range(2)
    ]
    result = pl.pallas_call(
        functools.partial(units_back_kernel, count, blocks),
        grid_spec=pltpu.PrefetchScalarGridSpec(
            num_scalar_prefetch=1,
            grid=(2 * blocks,),
            in_specs=[pl.BlockSpec((2, rows, half), lambda k, s: (0, 0, 0), pipeline_mode=once)]
            * (2 * count)
            + [pl.BlockSpec((rows, block), lambda k, s: (0, grad_at(k)))] * count
            + [pl.BlockSpec((2, block, total), lambda k, s: (0, normed_at(k), 0))],
            out_specs=[pl.BlockSpec((rows, block), lambda k, s: (0, normed_at(k)))] * count
            + sides,
            scratch_shapes=[
                pltpu.VMEM((count * rows, total), bf16),
                pltpu.VMEM((count * rows, total), bf16),
                pltpu.VMEM((block, count * rows), bf16),
            ],
        ),
        out_shape=[jax.ShapeDtypeStruct((rows, width), bf16)] * count
        + [jax.ShapeDtypeStruct((width // 2, total), bf16)] * 4,
        compiler_params=params(),
        cost_estimate=cost(
            8 * count * rows * width * total, 8 * width * total + 12 * count * rows * total
        ),
        name="units_back",
    )(core, *own, *other, *normed, gate_up)
    return result[:count], result[count:]


def down_out_kernel(count, core, *refs):
    own, other, down = refs[:count], refs[count : 2 * count], refs[2 * count]
    outs, units = refs[2 * count + 1 : -1], refs[-1]

    @pl.when(pl.program_id(0) == 0)
    def _():
        for at in range(count):
            ordered(core, own[at].at[0], other[at].at[0], units.at[at], own[at].shape[2])

    for at in range(count):
        outs[at][...] = dot(units[at], down[...]).astype(bf16)


def down_out(core, own, other, down):
    count = len(own)
    _, rows, half = own[0].shape
    total, width = down.shape
    block = block_of(width)
    piece = pl.BlockSpec((1, rows, half), lambda k, s: (2, 0, 0), pipeline_mode=pl.Buffered(1))
    return pl.pallas_call(
        functools.partial(down_out_kernel, count),
        grid_spec=pltpu.PrefetchScalarGridSpec(
            num_scalar_prefetch=1,
            grid=(width // block,),
            in_specs=[piece] * (2 * count) + [pl.BlockSpec((total, block), lambda k, s: (0, k))],
            out_specs=[pl.BlockSpec((rows, block), lambda k, s: (0, k))] * count,
            scratch_shapes=[pltpu.VMEM((count, rows, total), bf16)],
        ),
        out_shape=[jax.ShapeDtypeStruct((rows, width), bf16)] * count,
        compiler_params=params(),
        cost_estimate=cost(
            2 * count * rows * total * width, 2 * total * width + 4 * count * rows * total
        ),
        name="down_out",
    )(core, *own, *other, down)


def settle_kernel(middle, total, moved, *rest):
    rest[-1][0] = jnp.where(middle[0] == 1, total[...], moved[...]).astype(f32)


def settle(shape, index, start, block, clock, total, moved, before):
    rows, width = total.shape
    middle = clock(in_middle().astype(jnp.int32)[None])
    piece = pl.BlockSpec((block, width), lambda k, s: (k, 0))
    in_specs, args, aliases = [piece, piece], [total, moved], {}
    if before is not None:
        in_specs.append(pl.BlockSpec(memory_space=pl.ANY))
        args.append(before)
        aliases = {3: 0}
    return pl.pallas_call(
        settle_kernel,
        grid_spec=pltpu.PrefetchScalarGridSpec(
            num_scalar_prefetch=1,
            grid=(rows // block,),
            in_specs=in_specs,
            out_specs=pl.BlockSpec((1, block, width), lambda k, s: (index, start // block + k, 0)),
        ),
        out_shape=jax.ShapeDtypeStruct(shape, f32),
        input_output_aliases=aliases,
        compiler_params=params(16),
        cost_estimate=cost(0, 8 * rows * width),
        name="settle",
    )(middle, *args)


def weight_grad_kernel(pieces, kinds, parts, stacked, *refs):
    rows_in, units = refs[:pieces], refs[pieces : pieces + kinds]
    outs, rows = refs[pieces + kinds : -1], refs[-1]
    size = rows_in[0].shape[0]
    for at in range(pieces):
        rows[:, pl.ds(at * size, size)] = jnp.transpose(rows_in[at][...])
    steps = pl.num_programs(0) // parts
    for kind in range(kinds):
        array = units[kind][...]
        result = dot(rows[...], array.reshape(array.shape[-2:])).astype(bf16)
        if stacked:
            outs[0][kind] = result
            continue
        for at in range(parts):

            @pl.when(pl.program_id(0) // steps == at)
            def _():
                outs[kind * parts + at][...] = result


def weight_grads(rows, units, indices=(None,), parts=1, stacked=False):
    pieces, kinds = len(rows), len(units)
    size, width = rows[0].shape
    total, columns = units[0].shape[-2:]
    block = 256 if width // parts % 256 == 0 else LANES
    steps = width // block // parts
    specs = [
        pl.BlockSpec((total, columns), lambda k: (0, 0), pipeline_mode=pl.Buffered(1))
        if index is None
        else pl.BlockSpec(
            (1, total, columns),
            functools.partial(lambda at, k: (at, 0, 0), index),
            pipeline_mode=pl.Buffered(1),
        )
        for index in indices
    ]
    outs = [
        pl.BlockSpec(
            (block, columns),
            functools.partial(lambda at, k: (jnp.clip(k - at * steps, 0, steps - 1), 0), at),
        )
        for _ in range(kinds)
        for at in range(parts)
    ]
    shapes = [jax.ShapeDtypeStruct((width // parts, columns), bf16)] * (kinds * parts)
    if stacked:
        outs = [pl.BlockSpec((kinds, block, columns), lambda k: (0, k, 0))]
        shapes = [jax.ShapeDtypeStruct((kinds, width, columns), bf16)]
    return pl.pallas_call(
        functools.partial(weight_grad_kernel, pieces, kinds, parts, stacked),
        grid=(steps * parts,),
        in_specs=[pl.BlockSpec((size, block), lambda k: (0, k))] * pieces + specs,
        out_specs=outs,
        out_shape=shapes,
        scratch_shapes=[pltpu.VMEM((block, total), bf16)],
        compiler_params=params(),
        cost_estimate=cost(
            2 * total * width * columns * kinds,
            2 * (total * (width + columns * kinds) + width * columns * kinds),
        ),
        name="weight_grads",
    )(*rows, *units)


def mixed_grad_kernel(count, *refs):
    keep, taken, out = refs[-3:]
    for at in range(count):
        out[at] = (
            dot(refs[at][...], keep[...], NT) + dot(refs[count + at][...], taken[...], NT)
        ).astype(bf16)


def mixed_back(own, other, keep, taken):
    count = len(own)
    rows, width = own[0].shape
    units = keep.shape[0]
    return pl.pallas_call(
        functools.partial(mixed_grad_kernel, count),
        out_shape=jax.ShapeDtypeStruct((count, rows, units), bf16),
        compiler_params=params(),
        cost_estimate=cost(4 * count * rows * width * units, 4 * count * rows * width),
        name="mixed_back",
    )(*own, *other, keep, taken)


def project_back_kernel(swap, core, own, other, weight, *outs):
    units = outs[-1]
    count = own.shape[1]

    @pl.when(pl.program_id(0) == 0)
    def _():
        for kind in range(3):
            for at in range(count):
                ordered(
                    core,
                    own.at[kind, at],
                    other.at[kind, swap[at]],
                    units.at[kind, at],
                    own.shape[3],
                )

    for at in range(count):
        outs[at][...] = sum(
            dot(units[kind, at], weight[kind], NT) for kind in range(3)
        ).astype(bf16)


def project_back(core, swap, own, other, weight):
    _, count, rows, half = own.shape
    _, width, total = weight.shape
    block = block_of(width)
    whole = lambda k, *s: (0, 0, 0, 0)
    return pl.pallas_call(
        functools.partial(project_back_kernel, swap),
        grid_spec=pltpu.PrefetchScalarGridSpec(
            num_scalar_prefetch=1,
            grid=(width // block,),
            in_specs=[
                pl.BlockSpec((3, count, rows, half), whole),
                pl.BlockSpec((3, count, rows, half), whole),
                pl.BlockSpec((3, block, total), lambda k, *s: (0, k, 0)),
            ],
            out_specs=[pl.BlockSpec((rows, block), lambda k, *s: (0, k))] * count
            + [pl.BlockSpec((3, count, rows, total), whole)],
        ),
        out_shape=[jax.ShapeDtypeStruct((rows, width), bf16)] * count
        + [jax.ShapeDtypeStruct((3, count, rows, total), bf16)],
        compiler_params=params(),
        cost_estimate=cost(6 * count * rows * total * width, 2 * count * rows * (width + 6 * total)),
        name="project_back",
    )(core, own, other, weight)


def halves(weight, axis, width):
    lead = lax.slice_in_dim(weight, 0, width, axis=axis)
    rest = lax.slice_in_dim(weight, width, weight.shape[axis], axis=axis)
    pad = [(0, 0)] * weight.ndim
    pad[axis] = (0, width - rest.shape[axis])
    rest = jnp.pad(rest, pad)
    first = lax.axis_index("col") == 0
    return jnp.where(first, lead, rest), jnp.where(first, rest, lead)


def shards(
    block_input,
    norm1_gain,
    norm1_shift,
    qkv_weight,
    qkv_bias,
    out_weight,
    norm2_gain,
    norm2_shift,
    gate_up_weight,
    down_weight,
    output_grad,
):
    count = lax.axis_size("row")
    rows = block_input.shape[0]
    core = lax.axis_index("col").astype(jnp.int32)[None]
    place, swap = places()
    place = place.astype(jnp.int32)
    slot = inverse_places(place)
    half_units = out_weight.shape[0] // 2
    total_hidden = down_weight.shape[0]
    half_hidden = -(-total_hidden // (2 * LANES)) * LANES
    if grid_rows():
        groups = (((2,), 2), ((0, 1), 0), ((3,), 3))
    else:
        groups = tuple(((at,), at) for at in range(count))

    clock = Clock()
    inputs = block_input.astype(f32)
    gain_one = norm1_gain.astype(f32)
    gain_two = norm2_gain.astype(f32)
    split = {}

    def between(stats):
        split["keep"], split["send"] = halves(after(qkv_weight, stats), 2, half_units)
        return split["keep"]

    hat_one, inverse_one = normalize(inputs, between)
    normed_one = clock.mark((hat_one * gain_one + norm1_shift.astype(f32)).astype(bf16))

    one_own, fetch = gather_rows(normed_one)
    grad_own = None if grid_rows() else gather_whole(output_grad)
    qkv_keep = split["keep"]
    qkv_taken = sibling(split["send"])
    cosine, sine = rotary_tables(count, rows)
    bias = qkv_bias[:, None, :]
    qkv = None
    for group, index in groups:
        if qkv is not None and len(one_own) < count:
            grad_own = gather_whole(after(output_grad, one_own[0], one_own[1], clock.last))
            one_own += fetch(clock.last)
        others = [sibling(clock(one_own[swap[at]])) for at in group]
        qkv = clock.mark(
            project_pieces(
                index, group, count, place, [one_own[at] for at in group], others,
                qkv_keep, qkv_taken, clock(bias), cosine, sine, qkv,
            )
        )
        if group == groups[0][0]:
            gate_up_keep, gate_up_send = halves(clock(gate_up_weight), 2, half_hidden)
            clock.mark(gate_up_keep)
            down_keep, down_send = halves(clock(down_weight), 0, half_hidden)
            clock.mark(down_keep)
            out_keep, out_send = halves(clock(out_weight), 0, half_units)
            clock.mark(out_keep)
    gate_up_taken = sibling(clock(gate_up_send))
    down_taken = sibling(clock(down_send))
    out_taken = sibling(clock(out_send))
    mixed, kept, logsum = attend_forward(clock(slot), qkv)
    clock.mark(mixed)
    *branch, mixed_units = mixed_out(clock(core), swap, mixed, sibling(mixed), out_weight)
    clock.mark(branch[0])
    branch = scatter_rows(branch, clock)
    grad_other = sibling(clock(grad_own))
    after_rows = inputs + branch
    hat_two, inverse_two = normalize(after_rows)
    normed_two = clock.mark((hat_two * gain_two + norm2_shift.astype(f32)).astype(bf16))

    two_own, fetch = gather_rows(normed_two)
    mine, theirs = [None] * count, [None] * count
    for group, _ in groups:
        if group != groups[0][0] and len(two_own) < count:
            two_own += fetch(clock.last)
        results = hidden_pieces(
            group, clock(place),
            [two_own[at] for at in group],
            [sibling(clock(two_own[swap[at]])) for at in group],
            grad_own, grad_other, gate_up_keep, gate_up_taken, down_keep, down_taken,
        )
        clock.mark(results[0])
        for at, result in zip(group, results):
            mine[at] = result
        for at in group:
            theirs[at] = sibling(mine[swap[at]])

    sums = Line(clock)
    parts = down_grad_parts(clock(core), place, mine, theirs, grad_own, total_hidden)
    clock.mark(parts[0])
    sums.add(*parts)
    normed_parts, parts = units_back(clock(core), mine, theirs, two_own, gate_up_weight)
    clock.mark(normed_parts[0])
    sums.add(*parts)
    sums.join()
    forms = {
        "down": ((1,) + down_weight.shape, LANES),
        "gate_up": (gate_up_weight.shape, block_of(gate_up_weight.shape[1] // 2)),
        "out": ((1,) + out_weight.shape, block_of(out_weight.shape[0])),
        "qkv": (qkv_weight.shape, block_of(qkv_weight.shape[1])),
    }
    targets = [("down", 0, 0), ("down", 0, half_hidden)]
    half_width = gate_up_weight.shape[1] // 2
    targets += [("gate_up", kind, start) for kind in (0, 1) for start in (0, half_width)]
    targets += [("out", 0, 0)] + [("qkv", kind, 0) for kind in range(3)] + [("small", 0, 0)]
    settled = {}

    def settle_next():
        at = sums.settled
        name, part, start = targets[at]
        if name == "small":
            settled[name] = sums.small(at)
            sums.settled += 1
        else:
            shape, block = forms[name]
            settled[name] = sums.settle(shape, ((part, start),), block, settled.get(name))

    def tick():
        sums.join()
        sums.total_up()
        settle_next()

    normed_two_grad = clock.mark(scatter_rows(normed_parts, clock))
    after_grad = output_grad.astype(f32) + norm_back(
        normed_two_grad * gain_two, hat_two, inverse_two
    )
    branch_grad = clock.mark(after_grad.astype(bf16))
    branch_own, fetch = gather_rows(branch_grad)
    sums.join()
    down_parts = down_out(clock(core), mine, theirs, down_weight)
    clock.mark(down_parts[0])
    if len(branch_own) < count:
        branch_own += fetch(clock.last)
    branch_other = [sibling(branch_own[swap[at]]) for at in range(count)]
    sums.total_up()
    branch_rows = clock.mark(jnp.concatenate([clock(branch_own[0]), *branch_own[1:]], axis=0))
    mixed_grad = clock.mark(mixed_back(branch_own, branch_other, clock(out_keep), out_taken))
    sums.join()
    sums.total_up()
    project_grad = clock.mark(
        attend_backward(clock(slot), place, qkv, mixed_grad, kept, logsum, cosine, sine)
    )
    project_other = sibling(project_grad)
    settle_next()
    parts = weight_grads([mixed_units.reshape(count * rows, -1)], [clock(branch_rows)])
    clock.mark(parts[0])
    sums.add(*parts)
    sums.join()
    if grid_rows():
        far = first_way(down_parts[3])
        near = first_way(down_parts[0])
        side = second_way(clock.mark(plus(down_parts[1], clock(far))))
    settle_next()
    *one_parts, project_units = project_back(
        clock(core), swap, project_grad, project_other, qkv_weight
    )
    clock.mark(one_parts[0])
    if grid_rows():
        down = down_parts[2].astype(f32) + near.astype(f32) + clock(side).astype(f32)
    else:
        down = scatter_rows(down_parts, clock)
    block_output = clock.mark((after_rows + down).astype(bf16))
    sums.join()
    sums.total_up()
    project_units = project_units.reshape(3, count * rows, -1)
    qkv_parts = weight_grads(one_own, [clock(project_units)] * 3, (0, 1, 2))
    clock.mark(qkv_parts[0])
    tick()
    normed_one_grad = clock.mark(scatter_rows(one_parts, clock))
    input_grad = after_grad + norm_back(normed_one_grad * gain_one, hat_one, inverse_one)
    gains = jnp.stack(
        [
            jnp.sum(normed_one_grad * hat_one, axis=0),
            jnp.sum(normed_one_grad, axis=0),
            jnp.sum(normed_two_grad * hat_two, axis=0),
            jnp.sum(normed_two_grad, axis=0),
        ]
    )
    width = gains.shape[1]
    gains = clock.mark(gains)
    sums.total_up()
    settle_next()
    gains = sum_rows(gains, clock)
    bias_grad = jnp.sum(clock(project_grad).astype(f32), axis=(1, 2))
    clock.mark(bias_grad)
    small = jnp.concatenate([gains.reshape(-1, LANES), bias_grad.reshape(-1, LANES)], axis=0)
    sums.add(*qkv_parts, small)
    input_grad = clock.mark(clock(input_grad))
    while len(sums.half) < len(targets) - 1 if line() else sums.settled < len(targets) - 3:
        tick()
    sums.join()
    sums.total_up()
    settle_next()
    sums.total_up()
    while sums.settled < len(targets):
        settle_next()
    small = settled["small"]
    gains = small[: 4 * width // LANES].reshape(4, width)
    bias_grad = small[4 * width // LANES :].reshape(bias_grad.shape)
    return (
        block_output,
        input_grad,
        gains[0],
        gains[1],
        settled["qkv"],
        bias_grad,
        settled["out"][0],
        gains[2],
        gains[3],
        settled["gate_up"],
        settled["down"][0],
    )


def inverse_places(place):
    spots = jnp.arange(place.shape[0])
    return jnp.sum(
        jnp.where(place[None, :] == spots[:, None], spots[None, :], 0), axis=1
    ).astype(jnp.int32)


def solution(mesh):
    placed = (
        P(("dp", "row"), "col"),
        P("col"),
        P("col"),
        P(None, "col", "row"),
        P(None, ("row", "col")),
        P("row", "col"),
        P("col"),
        P("col"),
        P(None, "col", "row"),
        P("row", "col"),
        P(("dp", "row"), "col"),
    )
    return jax.shard_map(
        shards,
        mesh=mesh,
        in_specs=placed,
        out_specs=(
            P(("dp", "row"), "col"),
            P(("dp", "row"), "col"),
            P("col"),
            P("col"),
            P(None, "col", "row"),
            P(None, ("row", "col")),
            P("row", "col"),
            P("col"),
            P("col"),
            P(None, "col", "row"),
            P("row", "col"),
        ),
        check_vma=False,
    )
```
